32 devices in a mesh: blk: 8 (over z, x), batch: 4 (over y, core).
Axes of the slice: x: 2, y: 2, z: 4, core: 2. Of those that a mesh axis runs over, the one named last changes fastest.
Arguments:
- queries: bfloat16 [4, 2048, 2048], P('batch', 'blk'), may hold values from -8 to 8
- keys: bfloat16 [4, 2048, 1024], P('batch', 'blk'), may hold values from -8 to 8
- values: bfloat16 [4, 2048, 1024], P('batch', 'blk'), may hold values from -6 to 6
- seg_ids: int32 [4, 2048], P('batch', 'blk'), may hold values from 0 to 6, as said below
- lengths: int32 [4, 7], P('batch'), may hold values from 32 to 512, as said below
- live: int32 [4, 8, 2], P('batch', 'blk'), may hold values from 0 to 1, as said below
- page_table: int32 [4, 7, 2], replicated, may hold values from 0 to 31, as said below
- pool: bfloat16 [32, 16, 2048], P('batch'), may hold values from -6 to 6
Outputs:
- attended: bfloat16 [4, 2048, 2048], P('batch', 'blk')
- cache_keys: bfloat16 [4, 2048, 1024], P('batch', 'blk')
The draws below stay inside these ranges and needn't reach their ends.
Inputs may be any that keep to these rules, and one draw needn't show every extreme that they name: Each stream's lengths sum to 2048; one of them is exactly 512, three lie between 384 and 480, and three between 32 and 128, in random order. seg_ids[b, t] is the prompt that token t falls in under lengths[b]: it never decreases and every prompt number appears. live[b, j, r - 1] is 1 exactly when j >= r and the first token of block j and the last token of block j - r have the same seg_ids. `page_table`: page p is held by index p // 8 of batch. Of one stream's 7 * 2 pages, at most 5 are held by any one index of batch, and exactly 5 by one of them in every stream.
All inputs are finite; a program needn't handle non-finite values.
Results may differ from the reference program's by a relative error of at most 0.0055.
The reference program's roundings to bfloat16 on the way count: a program that leaves them out, or rounds other values in their place, can miss the bound.
Values may be sent and summed in bfloat16 or wider, within the bound.
No kernel may reach another device: no remote copies, remote signals or barrier semaphores. Data moves between devices by JAX's collectives and lax.ppermute only.
A program may use at most 128 MiB of HBM per device.

```python
import math
import jax
import jax.numpy as jnp
from jax import lax

QUERY_HEADS = 16
KEY_VALUE_HEADS = 8
HEAD_SIZE = 128
BLOCK_TOKENS = 256
SEGS = 7
PAGE = 16
PAGES_SEG = 2
POOL_DEV = 8
KVW = 1024
PACKED_STREAMS = 4
STREAM_TOKENS = 2048
STEPS = 2
LONG = 512
PAGES = 32
CAP = 5
N_BLK = 8


def layout(key):
    short_key, order_key = jax.random.split(key)
    shorts = jax.random.randint(short_key, (PACKED_STREAMS, 3), LONG // 16, LONG // 4 + 1)
    seg_lengths = jnp.concatenate([jnp.full((PACKED_STREAMS, 1), LONG, jnp.int32), LONG - shorts, shorts], axis=1).astype(jnp.int32)
    orders = jax.vmap(lambda one_key: jax.random.permutation(one_key, SEGS))(jax.random.split(order_key, PACKED_STREAMS))
    seg_lengths = jnp.take_along_axis(seg_lengths, orders, axis=1).astype(jnp.int32)
    seg_ends = jnp.cumsum(seg_lengths, axis=1)
    token_index = jnp.arange(STREAM_TOKENS, dtype=jnp.int32)
    segment = jnp.sum((seg_ends[:, None, :] <= token_index[None, :, None]).astype(jnp.int32), axis=2).astype(jnp.int32)
    return (seg_lengths, segment)


def draw_lengths(key, part):
    return layout(jax.random.fold_in(key, 17))[0]


def draw_seg_ids(key, part):
    return layout(jax.random.fold_in(key, 17))[1]


def draw_live(key, part):
    segment = layout(jax.random.fold_in(key, 17))[1]
    block_total = STREAM_TOKENS // BLOCK_TOKENS
    blocks = segment.reshape(PACKED_STREAMS, block_total, BLOCK_TOKENS)
    first_seg = blocks[:, :, 0]
    last_seg = blocks[:, :, BLOCK_TOKENS - 1]
    distance = jnp.arange(1, STEPS + 1, dtype=jnp.int32)
    earlier = jnp.arange(block_total, dtype=jnp.int32)[:, None] - distance[None, :]
    earlier_last = jnp.take(last_seg, jnp.clip(earlier, 0, block_total - 1), axis=1)
    return ((earlier[None] >= 0) & (earlier_last == first_seg[:, :, None])).astype(jnp.int32)


def draw_page_table(key, part):
    page_total = SEGS * PAGES_SEG

    def one_stream(stream_key):
        key_one, key_two, key_three, key_four = jax.random.split(stream_key, 4)
        heavy = jax.random.randint(key_one, (), 0, PACKED_STREAMS)
        others = jnp.arange((PACKED_STREAMS - 1) * CAP, dtype=jnp.int32) // CAP
        others = others + (others >= heavy).astype(jnp.int32)
        others = jax.random.permutation(key_two, others)[:page_total - CAP]
        holders = jnp.concatenate([jnp.full((CAP,), heavy, jnp.int32), others])
        holders = jax.random.permutation(key_three, holders)
        inside = jax.random.randint(key_four, (page_total,), 0, POOL_DEV)
        return (holders * POOL_DEV + inside).reshape(SEGS, PAGES_SEG)
    return jax.vmap(one_stream)(jax.random.split(jax.random.fold_in(key, 29), PACKED_STREAMS)).astype(jnp.int32)


def base_field(key, tensor_shape):
    return jnp.clip(jax.random.normal(key, tensor_shape, jnp.float32), -8.0, 8.0)


def draw_queries(key, part):
    tensor_shape = (PACKED_STREAMS, STREAM_TOKENS, QUERY_HEADS * HEAD_SIZE)
    field = base_field(jax.random.fold_in(key, 41), tensor_shape)
    return field.astype(jnp.bfloat16)


def draw_keys(key, part):
    tensor_shape = (PACKED_STREAMS, STREAM_TOKENS, KEY_VALUE_HEADS * HEAD_SIZE)
    field = base_field(jax.random.fold_in(key, 43), tensor_shape)
    return field.astype(jnp.bfloat16)


def levels(key, dims, cuts, low, top_value):
    def one(axis_at, shards_of):
        heights = jax.random.uniform(jax.random.fold_in(jax.random.fold_in(key, 6), axis_at), (shards_of,), jnp.float32, low / len(cuts), top_value / len(cuts))
        return jnp.repeat(jnp.exp(heights), dims[axis_at] // shards_of).reshape((-1,) + (1,) * (len(dims) - axis_at - 1))

    loudness = one(*cuts[0])
    for cut in cuts[1:]:
        loudness = loudness * one(*cut)
    return loudness


def gaussian(rng, shape, scale, most, cuts=(), kind=jnp.bfloat16):
    values = scale * jax.random.normal(rng, shape, jnp.float32)
    if cuts:
        values = values * levels(rng, shape, cuts, -0.22, 0.18)
    return jnp.clip(values, -most, most).astype(kind)


def setup_inputs(seed: int = 0) -> dict:
    key_of = jax.random.split(jax.random.key(seed), 9)
    queries = draw_queries(jax.random.fold_in(key_of[8], 71), 0)
    keys = draw_keys(jax.random.fold_in(key_of[8], 71), 0)
    values = gaussian(key_of[2], (PACKED_STREAMS, STREAM_TOKENS, KVW), 1.0, 6.0, ((0, 4), (1, 8)))
    seg_ids = draw_seg_ids(jax.random.fold_in(key_of[8], 71), 0)
    lengths = draw_lengths(jax.random.fold_in(key_of[8], 71), 0)
    live = draw_live(jax.random.fold_in(key_of[8], 71), 0)
    page_table = draw_page_table(jax.random.fold_in(key_of[8], 71), 0)
    pool = gaussian(key_of[7], (PAGES, PAGE, 2 * KVW), 1.0, 6.0, ((0, 4),))
    return dict(queries=queries, keys=keys, values=values, seg_ids=seg_ids, lengths=lengths, live=live, page_table=page_table, pool=pool)


rope_base = 1000000.0

def apply_rotary(matrix, token_position, head_count):
    head_width = matrix.shape[-1] // head_count
    halfway = head_width // 2
    inverse = jnp.power(jnp.float32(rope_base), -2.0 * jnp.arange(halfway, dtype=jnp.float32) / head_width)
    angles = token_position.astype(jnp.float32)[:, None] * inverse[None, :]
    cosine = jnp.cos(angles)[:, None, :]
    sine_part = jnp.sin(angles)[:, None, :]
    split_heads = matrix.astype(jnp.float32).reshape(matrix.shape[0], head_count, head_width)
    leading = split_heads[..., :halfway]
    trailing = split_heads[..., halfway:]
    turned = jnp.concatenate([leading * cosine - trailing * sine_part, trailing * cosine + leading * sine_part], axis=-1)
    return turned.reshape(matrix.shape[0], head_count * head_width).astype(jnp.bfloat16)

def segment_of(indices, lengths):
    seg_ends = jnp.cumsum(lengths).astype(jnp.int32)
    return lax.optimization_barrier(jnp.sum((seg_ends[None, :] <= indices[:, None]).astype(jnp.int32), axis=1)).astype(jnp.int32)

def positions(segment, lengths, offset, prefix_len):
    starts = (jnp.cumsum(lengths) - lengths).astype(jnp.int32)
    labels = jnp.arange(lengths.shape[0], dtype=jnp.int32)
    own_start = lax.optimization_barrier(jnp.sum(jnp.where(segment[:, None] == labels[None, :], starts[None, :], 0), axis=1)).astype(jnp.int32)
    token_index = (offset + jnp.arange(segment.shape[0], dtype=jnp.int32)).astype(jnp.int32)
    return (prefix_len + token_index - own_start).astype(jnp.int32)

def reference(queries, keys, values, seg_ids, lengths, live, page_table, pool):
    stream_len = queries.shape[1]
    q_width = queries.shape[2]
    kv_width = keys.shape[2]
    query_groups = QUERY_HEADS // KEY_VALUE_HEADS
    prefix_len = PAGES_SEG * PAGE
    scaling = 1.0 / math.sqrt(HEAD_SIZE)
    span = (STEPS + 1) * BLOCK_TOKENS

    def one_stream(stream_index):
        segment = seg_ids[stream_index]
        own_lengths = lengths[stream_index]
        token_position = positions(segment, own_lengths, 0, prefix_len)
        query_rotated = apply_rotary(queries[stream_index], token_position, QUERY_HEADS)
        key_rotated = apply_rotary(keys[stream_index], token_position, KEY_VALUE_HEADS)
        page_list = page_table[stream_index].reshape(-1)
        prefix = pool[page_list].reshape(SEGS * prefix_len, 2 * kv_width)
        pre_keys = prefix[:, :kv_width]
        pre_values = prefix[:, kv_width:]
        pre_seg = (jnp.arange(SEGS * prefix_len, dtype=jnp.int32) // prefix_len).astype(jnp.int32)
        padded_keys = jnp.concatenate([jnp.zeros((STEPS * BLOCK_TOKENS, kv_width), jnp.bfloat16), key_rotated], axis=0)
        padded_values = jnp.concatenate([jnp.zeros((STEPS * BLOCK_TOKENS, kv_width), jnp.bfloat16), values[stream_index]], axis=0)
        live_rows = live[stream_index]

        def one_block(block_id):
            start = (block_id * BLOCK_TOKENS).astype(jnp.int32)
            query_block = lax.dynamic_slice_in_dim(query_rotated, start, BLOCK_TOKENS, 0)
            query_seg = lax.dynamic_slice_in_dim(segment, start, BLOCK_TOKENS, 0)
            query_idx = (start + jnp.arange(BLOCK_TOKENS, dtype=jnp.int32)).astype(jnp.int32)
            window_keys = lax.dynamic_slice_in_dim(padded_keys, start, span, 0)
            window_values = lax.dynamic_slice_in_dim(padded_values, start, span, 0)
            key_idx = ((block_id - STEPS) * BLOCK_TOKENS + jnp.arange(span, dtype=jnp.int32)).astype(jnp.int32)
            key_seg = segment_of(key_idx, own_lengths)
            block_live = jnp.concatenate([live_rows[block_id][::-1], jnp.ones((1,), jnp.int32)]).astype(jnp.int32)
            key_live = jnp.repeat(block_live, BLOCK_TOKENS)
            seen_pre = query_seg[:, None] == pre_seg[None, :]
            seen_win = (query_seg[:, None] == key_seg[None, :]) & (key_idx[None, :] <= query_idx[:, None])
            seen_win = seen_win & (key_idx[None, :] >= 0) & (key_live[None, :] > 0)
            seen = jnp.concatenate([seen_pre, seen_win], axis=1)
            joined_keys = jnp.concatenate([pre_keys, window_keys], axis=0)
            joined_values = jnp.concatenate([pre_values, window_values], axis=0)
            query_heads = query_block.astype(jnp.float32).reshape(BLOCK_TOKENS, KEY_VALUE_HEADS, query_groups, HEAD_SIZE)
            key_heads = joined_keys.astype(jnp.float32).reshape(-1, KEY_VALUE_HEADS, HEAD_SIZE)
            value_heads = joined_values.astype(jnp.float32).reshape(-1, KEY_VALUE_HEADS, HEAD_SIZE)
            score = jnp.einsum('thgd,uhd->hgtu', query_heads, key_heads) * scaling
            score = jnp.where(seen[None, None], score, -jnp.inf)
            highest = lax.optimization_barrier(jnp.max(score, axis=-1, keepdims=True))
            weight = jnp.exp(score - highest)
            total = lax.optimization_barrier(jnp.sum(weight, axis=-1))
            rounded = lax.optimization_barrier(weight.astype(jnp.bfloat16)).astype(jnp.float32)
            summed = jnp.einsum('hgtu,uhd->thgd', rounded, value_heads)
            result = summed / jnp.transpose(total, (2, 0, 1))[..., None]
            return result.reshape(BLOCK_TOKENS, q_width).astype(jnp.bfloat16)
        blocks = lax.map(one_block, jnp.arange(N_BLK, dtype=jnp.int32))
        return (blocks.reshape(stream_len, q_width), key_rotated)
    attended, cache_keys = lax.map(one_stream, jnp.arange(queries.shape[0], dtype=jnp.int32))
    return (attended, cache_keys)
```

```python
import math

import jax
import jax.numpy as jnp
import numpy as np
from jax import lax
from jax.experimental import pallas as pl
from jax.experimental.pallas import tpu as pltpu
from jax.sharding import PartitionSpec as P

QUERY_HEADS = 16
KEY_VALUE_HEADS = 8
HEAD_SIZE = 128
GROUP = QUERY_HEADS // KEY_VALUE_HEADS
HALF = HEAD_SIZE // 2
ROPE_BASE = 1000000.0
HIDDEN = -1e30
EXP2_SCALE = math.log2(math.e) / math.sqrt(HEAD_SIZE)

PIO2_A = float(np.float32(1.5703125))
PIO2_B = float(np.float32(4.837512969970703125e-4))
PIO2_C = float(np.float32(math.pi / 2 - 1.5703125 - 4.837512969970703125e-4))


def shifted(value, steps):
    count = lax.axis_size("blk")
    return lax.ppermute(value, "blk", [(source, source + steps) for source in range(count - steps)])


def sine_cosine(angle):
    turns = jnp.floor(angle * (2.0 / math.pi) + 0.5)
    rest = ((angle - turns * PIO2_A) - turns * PIO2_B) - turns * PIO2_C
    square = rest * rest
    sine = rest + rest * square * (
        -1.6666654611e-1 + square * (8.3321608736e-3 - square * 1.9515295891e-4)
    )
    cosine = 1.0 - 0.5 * square + square * square * (
        4.166664568298827e-2 + square * (-1.388731625493765e-3 + square * 2.443315711809948e-5)
    )
    quadrant = turns.astype(jnp.int32) & 3
    swapped = (quadrant & 1) == 1
    sine_out = jnp.where(swapped, cosine, sine)
    cosine_out = jnp.where(swapped, sine, cosine)
    sine_out = jnp.where(quadrant >= 2, -sine_out, sine_out)
    cosine_out = jnp.where((quadrant == 1) | (quadrant == 2), -cosine_out, cosine_out)
    return sine_out, cosine_out


def rotate(head, cosine, signed_sine):
    wide = head.astype(jnp.float32)
    return (wide * cosine + pltpu.roll(wide, HALF, 1) * signed_sine).astype(jnp.bfloat16)


def prepare_kernel(
    rows, steps, segs, prefix_len,
    lengths_ref, live_ref, freq_ref, q_ref, k_ref,
    q_out, k_out, cos_out, sin_out, bias_out,
):
    @pl.when(pl.program_id(0) == 0)
    def _():
        block_start = lax.axis_index("blk") * rows
        starts, ends = [], []
        total = jnp.int32(0)
        for seg in range(segs):
            starts.append(total)
            total = total + lengths_ref[0, seg]
            ends.append(total)

        def label_of(index):
            label = jnp.zeros(index.shape, jnp.int32)
            for seg in range(segs):
                label += (index >= ends[seg]).astype(jnp.int32)
            return label

        lane = lax.broadcasted_iota(jnp.int32, (rows, HEAD_SIZE), 1)
        row = lax.broadcasted_iota(jnp.int32, (rows, HEAD_SIZE), 0)
        for step in range(steps + 1):
            index = block_start - step * rows + row
            own_start = jnp.zeros(index.shape, jnp.int32)
            for seg in range(1, segs):
                own_start = jnp.where(index >= starts[seg], starts[seg], own_start)
            place = (prefix_len + index - own_start).astype(jnp.float32)
            sine, cosine = sine_cosine(place * freq_ref[...])
            cos_out[pl.ds(step * rows, rows), :] = cosine
            sin_out[pl.ds(step * rows, rows), :] = jnp.where(lane < HALF, -sine, sine)

        query_index = block_start + lax.broadcasted_iota(jnp.int32, (rows, rows), 0)
        query_label = label_of(query_index)
        offset = lax.broadcasted_iota(jnp.int32, (rows, rows), 1)
        for step in range(steps + 1):
            key_index = block_start - step * rows + offset
            seen = (label_of(key_index) == query_label) & (key_index <= query_index)
            if step > 0:
                seen = seen & (live_ref[0, 0, step - 1] > 0)
            bias_out[:, pl.ds(step * rows, rows)] = jnp.where(seen, 0.0, HIDDEN)
        width = segs * prefix_len
        spot = lax.broadcasted_iota(jnp.int32, (rows, width), 1)
        owner = jnp.zeros((rows, width), jnp.int32)
        for seg in range(1, segs):
            owner += (spot >= seg * prefix_len).astype(jnp.int32)
        wide_label = label_of(block_start + lax.broadcasted_iota(jnp.int32, (rows, width), 0))
        bias_out[:, pl.ds((steps + 1) * rows, width)] = jnp.where(owner == wide_label, 0.0, HIDDEN)

    cosine = cos_out[pl.ds(0, rows), :]
    signed_sine = sin_out[pl.ds(0, rows), :]
    for head in range(GROUP):
        columns = pl.ds(head * HEAD_SIZE, HEAD_SIZE)
        q_out[0, :, columns] = rotate(q_ref[0, :, columns], cosine, signed_sine)
    k_out[0] = rotate(k_ref[0], cosine, signed_sine)


def prepare(queries, keys, lengths, live, prefix_len):
    rows = queries.shape[1]
    steps = live.shape[2]
    segs = lengths.shape[1]
    table_rows = (steps + 1) * rows
    key_count = table_rows + segs * prefix_len
    exponent = -2.0 * np.arange(HALF) / HEAD_SIZE
    freq = np.tile(np.power(ROPE_BASE, exponent), 2).astype(np.float32)[None, :]
    whole = lambda head: (0, 0)
    by_head = lambda head: (0, 0, head)
    return pl.pallas_call(
        lambda *refs: prepare_kernel(rows, steps, segs, prefix_len, *refs),
        grid=(KEY_VALUE_HEADS,),
        in_specs=[
            pl.BlockSpec(memory_space=pltpu.SMEM),
            pl.BlockSpec(memory_space=pltpu.SMEM),
            pl.BlockSpec((1, HEAD_SIZE), whole),
            pl.BlockSpec((1, rows, GROUP * HEAD_SIZE), by_head),
            pl.BlockSpec((1, rows, HEAD_SIZE), by_head),
        ],
        out_specs=[
            pl.BlockSpec((1, rows, GROUP * HEAD_SIZE), by_head),
            pl.BlockSpec((1, rows, HEAD_SIZE), by_head),
            pl.BlockSpec((table_rows, HEAD_SIZE), whole),
            pl.BlockSpec((table_rows, HEAD_SIZE), whole),
            pl.BlockSpec((rows, key_count), whole),
        ],
        out_shape=[
            jax.ShapeDtypeStruct(queries.shape, jnp.bfloat16),
            jax.ShapeDtypeStruct(keys.shape, jnp.bfloat16),
            jax.ShapeDtypeStruct((table_rows, HEAD_SIZE), jnp.float32),
            jax.ShapeDtypeStruct((table_rows, HEAD_SIZE), jnp.float32),
            jax.ShapeDtypeStruct((rows, key_count), jnp.float32),
        ],
        compiler_params=pltpu.CompilerParams(vmem_limit_bytes=32 * 1024 * 1024),
        cost_estimate=pl.CostEstimate(flops=20_000_000, bytes_accessed=6_000_000, transcendentals=0),
        name="prepare",
    )(lengths, live, jnp.asarray(freq), queries, keys)


def attend_kernel(rows, steps, pages, kv_width, *refs):
    table_ref, pool_ref, cos_ref, sin_ref, bias_ref, q_ref, k_ref, v_ref = refs[:8]
    far_refs = refs[8 : 8 + 2 * steps]
    out_ref, k_all, v_all, paged, sem = refs[8 + 2 * steps :]
    head = pl.program_id(0)
    page_tokens = pool_ref.shape[1]
    prefix_rows = pages * page_tokens
    base = (steps + 1) * rows
    copies = [
        pltpu.make_async_copy(pool_ref.at[table_ref[page]], paged.at[page], sem.at[page])
        for page in range(pages)
    ]

    @pl.when(head == 0)
    def _():
        for copy in copies:
            copy.start()

    k_all[pl.ds(0, rows), :] = k_ref[0]
    v_all[pl.ds(0, rows), :] = v_ref[0]
    for step in range(1, steps + 1):
        span = pl.ds(step * rows, rows)
        k_all[span, :] = rotate(far_refs[2 * step - 2][0], cos_ref[span, :], sin_ref[span, :])
        v_all[span, :] = far_refs[2 * step - 1][0]

    @pl.when(head == 0)
    def _():
        for copy in copies:
            copy.wait()

    columns = pl.ds(pl.multiple_of(head * HEAD_SIZE, HEAD_SIZE), HEAD_SIZE)
    value_columns = pl.ds(pl.multiple_of(kv_width + head * HEAD_SIZE, HEAD_SIZE), HEAD_SIZE)
    k_all[pl.ds(base, prefix_rows), :] = paged[:, :, columns].reshape(prefix_rows, HEAD_SIZE)
    v_all[pl.ds(base, prefix_rows), :] = paged[:, :, value_columns].reshape(prefix_rows, HEAD_SIZE)

    query = jnp.concatenate(
        [q_ref[0, :, pl.ds(h * HEAD_SIZE, HEAD_SIZE)] for h in range(GROUP)], axis=0
    )
    score = lax.dot_general(
        query, k_all[...], (((1,), (1,)), ((), ())), preferred_element_type=jnp.float32
    )
    key_count = score.shape[1]
    score = (score.reshape(GROUP, rows, key_count) + bias_ref[...][None]).reshape(GROUP * rows, key_count)
    highest = jnp.max(score, axis=1, keepdims=True)
    weight = jnp.exp2((score - highest) * EXP2_SCALE)
    total = jnp.sum(weight, axis=1, keepdims=True)
    summed = jnp.dot(weight.astype(jnp.bfloat16), v_all[...], preferred_element_type=jnp.float32)
    result = (summed / total).astype(jnp.bfloat16)
    for h in range(GROUP):
        out_ref[0, :, pl.ds(h * HEAD_SIZE, HEAD_SIZE)] = result[h * rows : (h + 1) * rows]


def attend(table, pool, cosine, signed_sine, bias, query, key, value, far):
    rows = query.shape[1]
    steps = len(far) // 2
    pages = table.shape[0]
    kv_width = key.shape[2]
    whole = lambda head: (0, 0)
    by_head = lambda head: (0, 0, head)
    narrow = pl.BlockSpec((1, rows, HEAD_SIZE), by_head)
    wide = pl.BlockSpec((1, rows, GROUP * HEAD_SIZE), by_head)
    key_count = bias.shape[1]
    return pl.pallas_call(
        lambda *refs: attend_kernel(rows, steps, pages, kv_width, *refs),
        grid=(KEY_VALUE_HEADS,),
        in_specs=[
            pl.BlockSpec(memory_space=pltpu.SMEM),
            pl.BlockSpec(memory_space=pl.ANY),
            pl.BlockSpec(cosine.shape, whole),
            pl.BlockSpec(signed_sine.shape, whole),
            pl.BlockSpec(bias.shape, whole),
            wide,
            narrow,
            narrow,
        ]
        + [narrow] * len(far),
        out_specs=wide,
        out_shape=jax.ShapeDtypeStruct(query.shape, jnp.bfloat16),
        scratch_shapes=[
            pltpu.VMEM((key_count, HEAD_SIZE), jnp.bfloat16),
            pltpu.VMEM((key_count, HEAD_SIZE), jnp.bfloat16),
            pltpu.VMEM((pages,) + pool.shape[1:], jnp.bfloat16),
            pltpu.SemaphoreType.DMA((pages,)),
        ],
        compiler_params=pltpu.CompilerParams(vmem_limit_bytes=48 * 1024 * 1024),
        cost_estimate=pl.CostEstimate(
            flops=4 * rows * QUERY_HEADS * HEAD_SIZE * key_count,
            bytes_accessed=8_000_000,
            transcendentals=rows * QUERY_HEADS * key_count,
        ),
        name="attend",
    )(table, pool, cosine, signed_sine, bias, query, key, value, *far)


def per_device(queries, keys, values, seg_ids, lengths, live, page_table, pool):
    steps = live.shape[2]
    prefix_len = page_table.shape[2] * pool.shape[1]
    per_stream = page_table.shape[1] * page_table.shape[2]
    far = []
    for step in range(1, steps + 1):
        far += [shifted(keys, step), shifted(values, step)]
    all_pool = lax.all_gather(pool, "batch", axis=0, tiled=True)
    table = lax.dynamic_index_in_dim(
        page_table.reshape(page_table.shape[0], per_stream), lax.axis_index("batch"), 0, keepdims=False
    )
    query, key, cosine, signed_sine, bias = prepare(queries, keys, lengths, live, prefix_len)
    result = attend(table, all_pool, cosine, signed_sine, bias, query, key, values, far)
    return (result, key)


def solution(mesh):
    in_specs = (
        P("batch", "blk", None),
        P("batch", "blk", None),
        P("batch", "blk", None),
        P("batch", "blk"),
        P("batch", None),
        P("batch", "blk", None),
        P(),
        P("batch", None, None),
    )
    out_specs = (P("batch", "blk", None), P("batch", "blk", None))
    return jax.shard_map(
        per_device, mesh=mesh, in_specs=in_specs, out_specs=out_specs, check_vma=False
    )
```

```python
import math

import jax
import jax.numpy as jnp
import numpy as np
from jax import lax
from jax.experimental import pallas as pl
from jax.experimental.pallas import tpu as pltpu
from jax.sharding import PartitionSpec as P

QUERY_HEADS = 16
KEY_VALUE_HEADS = 8
HEAD_SIZE = 128
GROUP = QUERY_HEADS // KEY_VALUE_HEADS
HALF = HEAD_SIZE // 2
ROPE_BASE = 1000000.0
HIDDEN = -1e30
LANES = 128
ROW_TILE = 64
SOFTMAX_TILE = 32
EXP2_SCALE = math.log2(math.e) / math.sqrt(HEAD_SIZE)

PIO2_A = float(np.float32(1.5703125))
PIO2_B = float(np.float32(4.837512969970703125e-4))
PIO2_C = float(np.float32(math.pi / 2 - 1.5703125 - 4.837512969970703125e-4))


def shifted(value, steps):
    count = lax.axis_size("blk")
    return lax.ppermute(value, "blk", [(source, source + steps) for source in range(count - steps)])


def padded_keys(count):
    return -(-count // LANES) * LANES


def vmem_bytes(key_count):
    return 12 * 1024 * (1024 + key_count)


def sine_cosine(angle):
    turns = jnp.floor(angle * (2.0 / math.pi) + 0.5)
    rest = ((angle - turns * PIO2_A) - turns * PIO2_B) - turns * PIO2_C
    square = rest * rest
    sine = rest + rest * square * (
        -1.6666654611e-1 + square * (8.3321608736e-3 - square * 1.9515295891e-4)
    )
    cosine = 1.0 - 0.5 * square + square * square * (
        4.166664568298827e-2 + square * (-1.388731625493765e-3 + square * 2.443315711809948e-5)
    )
    quadrant = turns.astype(jnp.int32) & 3
    swapped = (quadrant & 1) == 1
    sine_out = jnp.where(swapped, cosine, sine)
    cosine_out = jnp.where(swapped, sine, cosine)
    sine_out = jnp.where(quadrant >= 2, -sine_out, sine_out)
    cosine_out = jnp.where((quadrant == 1) | (quadrant == 2), -cosine_out, cosine_out)
    return sine_out, cosine_out


def rotate(head, cosine, signed_sine):
    wide = head.astype(jnp.float32)
    return (wide * cosine + pltpu.roll(wide, HALF, 1) * signed_sine).astype(jnp.bfloat16)


def prepare_kernel(
    rows, steps, segs, prefix_len,
    lengths_ref, live_ref, freq_ref, q_ref, k_ref,
    q_out, k_out, cos_out, sin_out, bias_out,
):
    @pl.when(pl.program_id(0) == 0)
    def _():
        block_start = lax.axis_index("blk") * rows
        starts = [jnp.int32(0)]
        for seg in range(1, segs):
            starts.append(starts[-1] + lengths_ref[0, seg - 1])
        lane = lax.broadcasted_iota(jnp.int32, (ROW_TILE, LANES), 1)
        row = lax.broadcasted_iota(jnp.int32, (ROW_TILE, LANES), 0)
        freq = jnp.broadcast_to(freq_ref[...], (ROW_TILE, LANES))
        for step in range(steps + 1):
            for tile in range(0, rows, ROW_TILE):
                index = block_start + (tile - step * rows) + row
                own_start = jnp.zeros(index.shape, jnp.int32)
                for seg in range(1, segs):
                    own_start = jnp.where(index >= starts[seg], starts[seg], own_start)
                place = (prefix_len + index - own_start).astype(jnp.float32)
                sine, cosine = sine_cosine(place * freq)
                span = pl.ds(step * rows + tile, ROW_TILE)
                cos_out[span, :] = cosine
                sin_out[span, :] = jnp.where(lane < HALF, -sine, sine)
        for tile in range(0, rows, ROW_TILE):
            span = pl.ds(tile, ROW_TILE)
            query_index = block_start + tile + row
            own_start = jnp.zeros(query_index.shape, jnp.int32)
            first_page_token = jnp.zeros(query_index.shape, jnp.int32)
            for seg in range(1, segs):
                later = query_index >= starts[seg]
                own_start = jnp.where(later, starts[seg], own_start)
                first_page_token = jnp.where(later, seg * prefix_len, first_page_token)
            for step in range(steps + 1):
                limit = query_index
                if step > 0:
                    limit = jnp.where(live_ref[0, 0, step - 1] > 0, limit, -1)
                for column in range(0, rows, LANES):
                    key_index = block_start + (column - step * rows) + lane
                    seen = (key_index >= own_start) & (key_index <= limit)
                    place = pl.ds(step * rows + column, LANES)
                    bias_out[span, place] = jnp.where(seen, 0.0, HIDDEN)
            base = (steps + 1) * rows
            for column in range(0, bias_out.shape[1] - base, LANES):
                offset = column + lane - first_page_token
                seen = (offset >= 0) & (offset < prefix_len)
                bias_out[span, pl.ds(base + column, LANES)] = jnp.where(seen, 0.0, HIDDEN)

    for tile in range(0, rows, ROW_TILE):
        span = pl.ds(tile, ROW_TILE)
        cosine = cos_out[span, :]
        signed_sine = sin_out[span, :]
        for head in range(GROUP):
            columns = pl.ds(head * HEAD_SIZE, HEAD_SIZE)
            q_out[0, span, columns] = rotate(q_ref[0, span, columns], cosine, signed_sine)
        k_out[0, span, :] = rotate(k_ref[0, span, :], cosine, signed_sine)


def prepare(queries, keys, lengths, live, prefix_len):
    rows = queries.shape[1]
    steps = live.shape[2]
    segs = lengths.shape[1]
    table_rows = (steps + 1) * rows
    key_count = padded_keys(table_rows + segs * prefix_len)
    exponent = -2.0 * np.arange(HALF) / HEAD_SIZE
    freq = np.tile(np.power(ROPE_BASE, exponent), 2).astype(np.float32)[None, :]
    whole = lambda head: (0, 0)
    by_head = lambda head: (0, 0, head)
    return pl.pallas_call(
        lambda *refs: prepare_kernel(rows, steps, segs, prefix_len, *refs),
        grid=(KEY_VALUE_HEADS,),
        in_specs=[
            pl.BlockSpec(memory_space=pltpu.SMEM),
            pl.BlockSpec(memory_space=pltpu.SMEM),
            pl.BlockSpec((1, HEAD_SIZE), whole),
            pl.BlockSpec((1, rows, GROUP * HEAD_SIZE), by_head),
            pl.BlockSpec((1, rows, HEAD_SIZE), by_head),
        ],
        out_specs=[
            pl.BlockSpec((1, rows, GROUP * HEAD_SIZE), by_head),
            pl.BlockSpec((1, rows, HEAD_SIZE), by_head),
            pl.BlockSpec((table_rows, HEAD_SIZE), whole),
            pl.BlockSpec((table_rows, HEAD_SIZE), whole),
            pl.BlockSpec((rows, key_count), whole),
        ],
        out_shape=[
            jax.ShapeDtypeStruct(queries.shape, jnp.bfloat16),
            jax.ShapeDtypeStruct(keys.shape, jnp.bfloat16),
            jax.ShapeDtypeStruct((table_rows, HEAD_SIZE), jnp.float32),
            jax.ShapeDtypeStruct((table_rows, HEAD_SIZE), jnp.float32),
            jax.ShapeDtypeStruct((rows, key_count), jnp.float32),
        ],
        compiler_params=pltpu.CompilerParams(vmem_limit_bytes=vmem_bytes(key_count)),
        cost_estimate=pl.CostEstimate(flops=0, bytes_accessed=0, transcendentals=0),
        name="prepare",
    )(lengths, live, jnp.asarray(freq), queries, keys)


def attend_kernel(rows, steps, pages, kv_width, columns_count, *refs):
    table_ref, cos_ref, sin_ref, bias_ref, q_ref, k_ref, v_ref = refs[:7]
    shards, refs = refs[7 : 7 + columns_count], refs[columns_count - 2 :]
    far_keys = refs[9 : 9 + steps]
    swapped_value, passed_value = refs[9 + steps : 11 + steps]
    far_values = refs[11 + steps : 10 + 2 * steps]
    out_ref, k_all, v_all, paged, scores, weights, sem = refs[10 + 2 * steps :]
    head = pl.program_id(0)
    pool_rows, page_tokens = shards[0].shape[:2]
    prefix_rows = pages * page_tokens
    base = (steps + 1) * rows

    def page_copy(shard, place, page):
        return pltpu.make_async_copy(shard.at[place], paged.at[page], sem.at[page])

    @pl.when(head == 0)
    def _():
        column = lax.axis_index("batch")
        for page in range(pages):
            number = table_ref[column * pages + page]
            apart = lax.div(number, jnp.int32(pool_rows)) ^ column
            place = lax.rem(number, jnp.int32(pool_rows))
            for which, shard in enumerate(shards):

                @pl.when(apart == which)
                def _(shard=shard, place=place, page=page):
                    page_copy(shard, place, page).start()

        rest = k_all.shape[0] - base - prefix_rows
        if rest:
            blank = jnp.zeros((rest, HEAD_SIZE), jnp.bfloat16)
            k_all[pl.ds(base + prefix_rows, rest), :] = blank
            v_all[pl.ds(base + prefix_rows, rest), :] = blank

    even = lax.rem(lax.axis_index("blk"), 2) == 0
    k_all[pl.ds(0, rows), :] = k_ref[0]
    v_all[pl.ds(0, rows), :] = v_ref[0]
    for step in range(1, steps + 1):
        for tile in range(0, rows, ROW_TILE):
            span = pl.ds(step * rows + tile, ROW_TILE)
            k_all[span, :] = rotate(
                far_keys[step - 1][0, pl.ds(tile, ROW_TILE), :], cos_ref[span, :], sin_ref[span, :]
            )
        span = pl.ds(step * rows, rows)
        if step == 1:
            v_all[span, :] = jnp.where(even, passed_value[0], swapped_value[0])
        else:
            v_all[span, :] = far_values[step - 2][0]

    @pl.when(head == 0)
    def _():
        for page in range(pages):
            page_copy(shards[0], 0, page).wait()

    columns = pl.ds(pl.multiple_of(head * HEAD_SIZE, HEAD_SIZE), HEAD_SIZE)
    value_columns = pl.ds(pl.multiple_of(kv_width + head * HEAD_SIZE, HEAD_SIZE), HEAD_SIZE)
    k_all[pl.ds(base, prefix_rows), :] = paged[:, :, columns].reshape(prefix_rows, HEAD_SIZE)
    v_all[pl.ds(base, prefix_rows), :] = paged[:, :, value_columns].reshape(prefix_rows, HEAD_SIZE)

    query = jnp.concatenate(
        [q_ref[0, :, pl.ds(h * HEAD_SIZE, HEAD_SIZE)] for h in range(GROUP)], axis=0
    )
    scores[...] = lax.dot_general(
        query, k_all[...], (((1,), (1,)), ((), ())), preferred_element_type=jnp.float32
    )
    totals = []
    for h in range(GROUP):
        for tile in range(0, rows, SOFTMAX_TILE):
            span = pl.ds(h * rows + tile, SOFTMAX_TILE)
            score = scores[span, :] + bias_ref[pl.ds(tile, SOFTMAX_TILE), :]
            highest = jnp.max(score, axis=1, keepdims=True)
            weight = jnp.exp2((score - highest) * EXP2_SCALE)
            totals.append(jnp.sum(weight, axis=1, keepdims=True))
            weights[span, :] = weight.astype(jnp.bfloat16)
    summed = jnp.dot(weights[...], v_all[...], preferred_element_type=jnp.float32)
    for place, total in enumerate(totals):
        start = place * SOFTMAX_TILE
        h, tile = divmod(start, rows)
        result = summed[start : start + SOFTMAX_TILE] / total
        out_ref[0, pl.ds(tile, SOFTMAX_TILE), pl.ds(h * HEAD_SIZE, HEAD_SIZE)] = result.astype(
            jnp.bfloat16
        )


def attend(
    table, shards, cosine, signed_sine, bias, query, key, value, far_keys, first_values, far_values
):
    rows = query.shape[1]
    steps = len(far_keys)
    columns_count = len(shards)
    pages = table.shape[0] // columns_count
    kv_width = key.shape[2]
    whole = lambda head: (0, 0)
    by_head = lambda head: (0, 0, head)
    narrow = pl.BlockSpec((1, rows, HEAD_SIZE), by_head)
    wide = pl.BlockSpec((1, rows, GROUP * HEAD_SIZE), by_head)
    key_count = bias.shape[1]
    far = [*far_keys, *first_values, *far_values]
    return pl.pallas_call(
        lambda *refs: attend_kernel(rows, steps, pages, kv_width, columns_count, *refs),
        grid=(KEY_VALUE_HEADS,),
        in_specs=[
            pl.BlockSpec(memory_space=pltpu.SMEM),
            pl.BlockSpec(cosine.shape, whole),
            pl.BlockSpec(signed_sine.shape, whole),
            pl.BlockSpec(bias.shape, whole),
            wide,
            narrow,
            narrow,
        ]
        + [pl.BlockSpec(memory_space=pl.ANY)] * columns_count
        + [narrow] * len(far),
        out_specs=wide,
        out_shape=jax.ShapeDtypeStruct(query.shape, jnp.bfloat16),
        scratch_shapes=[
            pltpu.VMEM((key_count, HEAD_SIZE), jnp.bfloat16),
            pltpu.VMEM((key_count, HEAD_SIZE), jnp.bfloat16),
            pltpu.VMEM((pages,) + shards[0].shape[1:], jnp.bfloat16),
            pltpu.VMEM((GROUP * rows, key_count), jnp.float32),
            pltpu.VMEM((GROUP * rows, key_count), jnp.bfloat16),
            pltpu.SemaphoreType.DMA((pages,)),
        ],
        compiler_params=pltpu.CompilerParams(vmem_limit_bytes=vmem_bytes(key_count)),
        cost_estimate=pl.CostEstimate(
            flops=4 * rows * QUERY_HEADS * HEAD_SIZE * key_count,
            bytes_accessed=8_000_000,
            transcendentals=rows * QUERY_HEADS * key_count,
        ),
        name="attend",
    )(table, cosine, signed_sine, bias, query, key, value, *shards, *far)


def pool_shards(pool):
    count = lax.axis_size("batch")
    return [pool] + [
        lax.ppermute(pool, "batch", [(c, c ^ apart) for c in range(count)])
        for apart in range(1, count)
    ]


def per_device(queries, keys, values, seg_ids, lengths, live, page_table, pool):
    steps = live.shape[2]
    prefix_len = page_table.shape[2] * pool.shape[1]
    columns_count, blocks = lax.axis_size("batch"), lax.axis_size("blk")
    far_keys = [shifted(keys, 2), shifted(keys, 1)][::-1]
    swapped_value = lax.ppermute(values, "blk", [(j, j ^ 1) for j in range(blocks)])
    far_values = [shifted(values, 2)]
    for step in range(3, steps + 1):
        far_keys.append(shifted(keys, step))
        far_values.append(shifted(values, step))
    passed_value = lax.ppermute(
        swapped_value, "blk", [(j, j + 2) for j in range(0, blocks - 2, 2)]
    )
    shards = pool_shards(pool)
    query, key, cosine, signed_sine, bias = prepare(queries, keys, lengths, live, prefix_len)
    result = attend(
        page_table.reshape(-1), shards, cosine, signed_sine, bias,
        query, key, values, far_keys, [swapped_value, passed_value], far_values,
    )
    return (result, key)


def solution(mesh):
    in_specs = (
        P("batch", "blk", None),
        P("batch", "blk", None),
        P("batch", "blk", None),
        P("batch", "blk"),
        P("batch", None),
        P("batch", "blk", None),
        P(),
        P("batch", None, None),
    )
    out_specs = (P("batch", "blk", None), P("batch", "blk", None))
    return jax.shard_map(
        per_device, mesh=mesh, in_specs=in_specs, out_specs=out_specs, check_vma=False
    )
```

```python
import math

import jax
import jax.numpy as jnp
import numpy as np
from jax import lax
from jax.experimental import pallas as pl
from jax.experimental.pallas import tpu as pltpu
from jax.sharding import PartitionSpec as P

QUERY_HEADS = 16
KEY_VALUE_HEADS = 8
HEAD_SIZE = 128
GROUP = QUERY_HEADS // KEY_VALUE_HEADS
HALF = HEAD_SIZE // 2
ROPE_BASE = 1000000.0
HIDDEN = -1e30
LANES = 128
ROW_TILE = 64
SOFTMAX_TILE = 16
HEADS_PER_STEP = 2
PREPARE_STEPS = 2
EXP2_SCALE = math.log2(math.e) / math.sqrt(HEAD_SIZE)

PIO2_A = float(np.float32(1.5703125))
PIO2_B = float(np.float32(4.837512969970703125e-4))
PIO2_C = float(np.float32(math.pi / 2 - 1.5703125 - 4.837512969970703125e-4))


def shifted(value, steps):
    count = lax.axis_size("blk")
    return lax.ppermute(value, "blk", [(source, source + steps) for source in range(count - steps)])


def padded_keys(count):
    return -(-count // LANES) * LANES


def vmem_bytes(key_count):
    return 16 * 1024 * (1024 + key_count)


def sine_cosine(angle):
    turns = jnp.floor(angle * (2.0 / math.pi) + 0.5)
    rest = ((angle - turns * PIO2_A) - turns * PIO2_B) - turns * PIO2_C
    square = rest * rest
    sine = rest + rest * square * (
        -1.6666654611e-1 + square * (8.3321608736e-3 - square * 1.9515295891e-4)
    )
    cosine = 1.0 - 0.5 * square + square * square * (
        4.166664568298827e-2 + square * (-1.388731625493765e-3 + square * 2.443315711809948e-5)
    )
    quadrant = turns.astype(jnp.int32) & 3
    swapped = (quadrant & 1) == 1
    sine_out = jnp.where(swapped, cosine, sine)
    cosine_out = jnp.where(swapped, sine, cosine)
    sine_out = jnp.where(quadrant >= 2, -sine_out, sine_out)
    cosine_out = jnp.where((quadrant == 1) | (quadrant == 2), -cosine_out, cosine_out)
    return sine_out, cosine_out


def rotate(head, cosine, signed_sine):
    wide = head.astype(jnp.float32)
    return (wide * cosine + pltpu.roll(wide, HALF, 1) * signed_sine).astype(jnp.bfloat16)


def prepare_kernel(
    rows, steps, segs, prefix_len,
    lengths_ref, live_ref, freq_ref, q_ref, k_ref,
    q_out, k_out, cos_out, sin_out, bias_out,
):
    @pl.when(pl.program_id(0) == 0)
    def _():
        block_start = lax.axis_index("blk") * rows
        starts = [jnp.int32(0)]
        for seg in range(1, segs):
            starts.append(starts[-1] + lengths_ref[0, seg - 1])
        lane = lax.broadcasted_iota(jnp.int32, (ROW_TILE, LANES), 1)
        row = lax.broadcasted_iota(jnp.int32, (ROW_TILE, LANES), 0)
        freq = jnp.broadcast_to(freq_ref[...], (ROW_TILE, LANES))
        for step in range(steps + 1):
            for tile in range(0, rows, ROW_TILE):
                index = block_start + (tile - step * rows) + row
                own_start = jnp.zeros(index.shape, jnp.int32)
                for seg in range(1, segs):
                    own_start = jnp.where(index >= starts[seg], starts[seg], own_start)
                place = (prefix_len + index - own_start).astype(jnp.float32)
                sine, cosine = sine_cosine(place * freq)
                span = pl.ds(step * rows + tile, ROW_TILE)
                cos_out[span, :] = cosine
                sin_out[span, :] = jnp.where(lane < HALF, -sine, sine)
        for tile in range(0, rows, ROW_TILE):
            span = pl.ds(tile, ROW_TILE)
            query_index = block_start + tile + row
            own_start = jnp.zeros(query_index.shape, jnp.int32)
            first_page_token = jnp.zeros(query_index.shape, jnp.int32)
            for seg in range(1, segs):
                later = query_index >= starts[seg]
                own_start = jnp.where(later, starts[seg], own_start)
                first_page_token = jnp.where(later, seg * prefix_len, first_page_token)
            for step in range(steps + 1):
                limit = query_index
                if step > 0:
                    limit = jnp.where(live_ref[0, 0, step - 1] > 0, limit, -1)
                for column in range(0, rows, LANES):
                    key_index = block_start + (column - step * rows) + lane
                    seen = (key_index >= own_start) & (key_index <= limit)
                    place = pl.ds(step * rows + column, LANES)
                    bias_out[span, place] = jnp.where(seen, 0.0, HIDDEN)
            base = (steps + 1) * rows
            for column in range(0, bias_out.shape[1] - base, LANES):
                offset = column + lane - first_page_token
                seen = (offset >= 0) & (offset < prefix_len)
                bias_out[span, pl.ds(base + column, LANES)] = jnp.where(seen, 0.0, HIDDEN)

    for tile in range(0, rows, ROW_TILE):
        span = pl.ds(tile, ROW_TILE)
        cosine = cos_out[span, :]
        signed_sine = sin_out[span, :]
        for source, target in ((q_ref, q_out), (k_ref, k_out)):
            for start in range(0, source.shape[2], HEAD_SIZE):
                columns = pl.ds(start, HEAD_SIZE)
                target[0, span, columns] = rotate(source[0, span, columns], cosine, signed_sine)


def prepare(queries, keys, lengths, live, prefix_len):
    rows = queries.shape[1]
    steps = live.shape[2]
    segs = lengths.shape[1]
    table_rows = (steps + 1) * rows
    key_count = padded_keys(table_rows + segs * prefix_len)
    exponent = -2.0 * np.arange(HALF) / HEAD_SIZE
    freq = np.tile(np.power(ROPE_BASE, exponent), 2).astype(np.float32)[None, :]
    whole = lambda head: (0, 0)
    by_head = lambda head: (0, 0, head)
    return pl.pallas_call(
        lambda *refs: prepare_kernel(rows, steps, segs, prefix_len, *refs),
        grid=(PREPARE_STEPS,),
        in_specs=[
            pl.BlockSpec(memory_space=pltpu.SMEM),
            pl.BlockSpec(memory_space=pltpu.SMEM),
            pl.BlockSpec((1, HEAD_SIZE), whole),
            pl.BlockSpec((1, rows, queries.shape[2] // PREPARE_STEPS), by_head),
            pl.BlockSpec((1, rows, keys.shape[2] // PREPARE_STEPS), by_head),
        ],
        out_specs=[
            pl.BlockSpec((1, rows, queries.shape[2] // PREPARE_STEPS), by_head),
            pl.BlockSpec((1, rows, keys.shape[2] // PREPARE_STEPS), by_head),
            pl.BlockSpec((table_rows, HEAD_SIZE), whole),
            pl.BlockSpec((table_rows, HEAD_SIZE), whole),
            pl.BlockSpec((rows, key_count), whole),
        ],
        out_shape=[
            jax.ShapeDtypeStruct(queries.shape, jnp.bfloat16),
            jax.ShapeDtypeStruct(keys.shape, jnp.bfloat16),
            jax.ShapeDtypeStruct((table_rows, HEAD_SIZE), jnp.float32),
            jax.ShapeDtypeStruct((table_rows, HEAD_SIZE), jnp.float32),
            jax.ShapeDtypeStruct((rows, key_count), jnp.float32),
        ],
        compiler_params=pltpu.CompilerParams(vmem_limit_bytes=vmem_bytes(key_count)),
        cost_estimate=pl.CostEstimate(flops=0, bytes_accessed=0, transcendentals=0),
        name="prepare",
    )(lengths, live, jnp.asarray(freq), queries, keys)


def attend_kernel(rows, steps, pages, kv_width, columns_count, *refs):
    table_ref, cos_ref, sin_ref, bias_ref, q_ref, k_ref, v_ref = refs[:7]
    shards, refs = refs[7 : 7 + columns_count], refs[columns_count - 2 :]
    far_keys = refs[9 : 9 + steps]
    swapped_value, passed_value = refs[9 + steps : 11 + steps]
    far_values = refs[11 + steps : 10 + 2 * steps]
    out_ref, paged, sem = refs[10 + 2 * steps : 13 + 2 * steps]
    work = refs[13 + 2 * steps :]
    k_parts, v_parts, scores, weights = (
        work[i : i + HEADS_PER_STEP] for i in range(0, len(work), HEADS_PER_STEP)
    )
    group = pl.program_id(0)
    pool_rows, page_tokens = shards[0].shape[:2]
    prefix_rows = pages * page_tokens
    base = (steps + 1) * rows

    def page_copy(shard, place, page):
        return pltpu.make_async_copy(shard.at[place], paged.at[page], sem.at[page])

    @pl.when(group == 0)
    def _():
        column = lax.axis_index("batch")
        for page in range(pages):
            number = table_ref[column, page % table_ref.shape[1], page // table_ref.shape[1]]
            apart = lax.div(number, jnp.int32(pool_rows)) ^ column
            place = lax.rem(number, jnp.int32(pool_rows))
            for which, shard in enumerate(shards):

                @pl.when(apart == which)
                def _(shard=shard, place=place, page=page):
                    page_copy(shard, place, page).start()

        rest = k_parts[0].shape[0] - base - prefix_rows
        for k_all, v_all in zip(k_parts, v_parts):
            v_all[:, pl.ds(HEAD_SIZE, HEAD_SIZE)] = jnp.ones(k_all.shape, jnp.bfloat16)
            if rest:
                blank = jnp.zeros((rest, HEAD_SIZE), jnp.bfloat16)
                k_all[pl.ds(base + prefix_rows, rest), :] = blank
                v_all[pl.ds(base + prefix_rows, rest), pl.ds(0, HEAD_SIZE)] = blank

    even = lax.rem(lax.axis_index("blk"), 2) == 0
    for part in range(HEADS_PER_STEP):
        lanes = pl.ds(part * HEAD_SIZE, HEAD_SIZE)
        k_all, v_all = k_parts[part], v_parts[part]
        k_all[pl.ds(0, rows), :] = k_ref[0, :, lanes]
        v_all[pl.ds(0, rows), pl.ds(0, HEAD_SIZE)] = v_ref[0, :, lanes]
        for step in range(1, steps + 1):
            for tile in range(0, rows, ROW_TILE):
                span = pl.ds(step * rows + tile, ROW_TILE)
                k_all[span, :] = rotate(
                    far_keys[step - 1][0, pl.ds(tile, ROW_TILE), lanes],
                    cos_ref[span, :],
                    sin_ref[span, :],
                )
            if step == 1:
                value = jnp.where(even, passed_value[0, :, lanes], swapped_value[0, :, lanes])
            else:
                value = far_values[step - 2][0, :, lanes]
            v_all[pl.ds(step * rows, rows), pl.ds(0, HEAD_SIZE)] = value

    @pl.when(group == 0)
    def _():
        for page in range(pages):
            page_copy(shards[0], 0, page).wait()

    for part in range(HEADS_PER_STEP):
        start = (group * HEADS_PER_STEP + part) * HEAD_SIZE
        columns = pl.ds(pl.multiple_of(start, HEAD_SIZE), HEAD_SIZE)
        value_columns = pl.ds(pl.multiple_of(kv_width + start, HEAD_SIZE), HEAD_SIZE)
        span = pl.ds(base, prefix_rows)
        k_parts[part][span, :] = paged[:, :, columns].reshape(prefix_rows, HEAD_SIZE)
        v_parts[part][span, pl.ds(0, HEAD_SIZE)] = paged[:, :, value_columns].reshape(
            prefix_rows, HEAD_SIZE
        )

    for part in range(HEADS_PER_STEP):
        query = jnp.concatenate(
            [
                q_ref[0, :, pl.ds((part * GROUP + h) * HEAD_SIZE, HEAD_SIZE)]
                for h in range(GROUP)
            ],
            axis=0,
        )
        scores[part][...] = lax.dot_general(
            query, k_parts[part][...], (((1,), (1,)), ((), ())), preferred_element_type=jnp.float32
        )
    for part in range(HEADS_PER_STEP):
        for start in range(0, GROUP * rows, SOFTMAX_TILE):
            span = pl.ds(start, SOFTMAX_TILE)
            score = scores[part][span, :] + bias_ref[pl.ds(start % rows, SOFTMAX_TILE), :]
            highest = jnp.max(score, axis=1, keepdims=True)
            weight = jnp.exp2((score - highest) * EXP2_SCALE)
            weights[part][span, :] = weight.astype(jnp.bfloat16)
        summed = jnp.dot(weights[part][...], v_parts[part][...], preferred_element_type=jnp.float32)
        result = (summed[:, :HEAD_SIZE] / summed[:, HEAD_SIZE:]).astype(jnp.bfloat16)
        for h in range(GROUP):
            lanes = pl.ds((part * GROUP + h) * HEAD_SIZE, HEAD_SIZE)
            out_ref[0, :, lanes] = result[h * rows : (h + 1) * rows]


def attend(
    table, shards, cosine, signed_sine, bias, query, key, value, far_keys, first_values, far_values
):
    rows = query.shape[1]
    steps = len(far_keys)
    columns_count = len(shards)
    pages = table.shape[1] * table.shape[2]
    kv_width = key.shape[2]
    whole = lambda head: (0, 0)
    by_head = lambda head: (0, 0, head)
    narrow = pl.BlockSpec((1, rows, HEADS_PER_STEP * HEAD_SIZE), by_head)
    wide = pl.BlockSpec((1, rows, HEADS_PER_STEP * GROUP * HEAD_SIZE), by_head)
    key_count = bias.shape[1]
    far = [*far_keys, *first_values, *far_values]
    return pl.pallas_call(
        lambda *refs: attend_kernel(rows, steps, pages, kv_width, columns_count, *refs),
        grid=(KEY_VALUE_HEADS // HEADS_PER_STEP,),
        in_specs=[
            pl.BlockSpec(memory_space=pltpu.SMEM),
            pl.BlockSpec(cosine.shape, whole),
            pl.BlockSpec(signed_sine.shape, whole),
            pl.BlockSpec(bias.shape, whole),
            wide,
            narrow,
            narrow,
        ]
        + [pl.BlockSpec(memory_space=pl.ANY)] * columns_count
        + [narrow] * len(far),
        out_specs=wide,
        out_shape=jax.ShapeDtypeStruct(query.shape, jnp.bfloat16),
        scratch_shapes=[
            pltpu.VMEM((pages,) + shards[0].shape[1:], jnp.bfloat16),
            pltpu.SemaphoreType.DMA((pages,)),
        ]
        + [pltpu.VMEM((key_count, HEAD_SIZE), jnp.bfloat16)] * HEADS_PER_STEP
        + [pltpu.VMEM((key_count, 2 * HEAD_SIZE), jnp.bfloat16)] * HEADS_PER_STEP
        + [pltpu.VMEM((GROUP * rows, key_count), jnp.float32)] * HEADS_PER_STEP
        + [pltpu.VMEM((GROUP * rows, key_count), jnp.bfloat16)] * HEADS_PER_STEP,
        compiler_params=pltpu.CompilerParams(vmem_limit_bytes=vmem_bytes(key_count)),
        cost_estimate=pl.CostEstimate(
            flops=4 * rows * QUERY_HEADS * HEAD_SIZE * key_count,
            bytes_accessed=8_000_000,
            transcendentals=rows * QUERY_HEADS * key_count,
        ),
        name="attend",
    )(table, cosine, signed_sine, bias, query, key, value, *shards, *far)


def pool_shards(pool):
    count = lax.axis_size("batch")
    return [pool] + [
        lax.ppermute(pool, "batch", [(c, c ^ apart) for c in range(count)])
        for apart in range(1, count)
    ]


def per_device(queries, keys, values, seg_ids, lengths, live, page_table, pool):
    steps = live.shape[2]
    prefix_len = page_table.shape[2] * pool.shape[1]
    columns_count, blocks = lax.axis_size("batch"), lax.axis_size("blk")
    swapped_value = lax.ppermute(values, "blk", [(j, j ^ 1) for j in range(blocks)])
    far_keys = [shifted(keys, 2), shifted(keys, 1)][::-1]
    far_values = [shifted(values, 2)]
    for step in range(3, steps + 1):
        far_keys.append(shifted(keys, step))
        far_values.append(shifted(values, step))
    passed_value = lax.ppermute(
        swapped_value, "blk", [(j, j + 2) for j in range(0, blocks - 2, 2)]
    )
    shards = pool_shards(pool)
    query, key, cosine, signed_sine, bias = prepare(queries, keys, lengths, live, prefix_len)
    result = attend(
        jnp.swapaxes(page_table, 1, 2), shards, cosine, signed_sine, bias,
        query, key, values, far_keys, [swapped_value, passed_value], far_values,
    )
    return (result, key)


def solution(mesh):
    in_specs = (
        P("batch", "blk", None),
        P("batch", "blk", None),
        P("batch", "blk", None),
        P("batch", "blk"),
        P("batch", None),
        P("batch", "blk", None),
        P(),
        P("batch", None, None),
    )
    out_specs = (P("batch", "blk", None), P("batch", "blk", None))
    return jax.shard_map(
        per_device, mesh=mesh, in_specs=in_specs, out_specs=out_specs, check_vma=False
    )
```

```python
import math

import jax
import jax.numpy as jnp
import numpy as np
from jax import lax
from jax.experimental import pallas as pl
from jax.experimental.pallas import tpu as pltpu
from jax.sharding import PartitionSpec as P

QUERY_HEADS = 16
KEY_VALUE_HEADS = 8
HEAD_SIZE = 128
GROUP = QUERY_HEADS // KEY_VALUE_HEADS
HALF = HEAD_SIZE // 2
ROPE_BASE = 1000000.0
HIDDEN = -1e30
LANES = 128
ROW_TILE = 64
SOFTMAX_TILE = 16
HEADS_PER_STEP = 2
PREPARE_STEPS = 2


def cost(flops):
    return pl.CostEstimate(flops=flops, bytes_accessed=0, transcendentals=0)


PREPARE_COST = cost(0)
NEAR_COST = cost(0)
LAST_COST = cost(0)
EXP2_SCALE = math.log2(math.e) / math.sqrt(HEAD_SIZE)

PIO2_A = float(np.float32(1.5703125))
PIO2_B = float(np.float32(4.837512969970703125e-4))
PIO2_C = float(np.float32(math.pi / 2 - 1.5703125 - 4.837512969970703125e-4))


def shifted(value, steps):
    count = lax.axis_size("blk")
    return lax.ppermute(value, "blk", [(source, source + steps) for source in range(count - steps)])


def padded_keys(count):
    return -(-count // LANES) * LANES


def vmem_bytes(key_count):
    return 16 * 1024 * (1024 + key_count)


def sine_cosine(angle):
    turns = jnp.floor(angle * (2.0 / math.pi) + 0.5)
    rest = ((angle - turns * PIO2_A) - turns * PIO2_B) - turns * PIO2_C
    square = rest * rest
    sine = rest + rest * square * (
        -1.6666654611e-1 + square * (8.3321608736e-3 - square * 1.9515295891e-4)
    )
    cosine = 1.0 - 0.5 * square + square * square * (
        4.166664568298827e-2 + square * (-1.388731625493765e-3 + square * 2.443315711809948e-5)
    )
    quadrant = turns.astype(jnp.int32) & 3
    swapped = (quadrant & 1) == 1
    sine_out = jnp.where(swapped, cosine, sine)
    cosine_out = jnp.where(swapped, sine, cosine)
    sine_out = jnp.where(quadrant >= 2, -sine_out, sine_out)
    cosine_out = jnp.where((quadrant == 1) | (quadrant == 2), -cosine_out, cosine_out)
    return sine_out, cosine_out


def rotate(head, cosine, signed_sine):
    wide = head.astype(jnp.float32)
    return (wide * cosine + pltpu.roll(wide, HALF, 1) * signed_sine).astype(jnp.bfloat16)


def prepare_kernel(
    rows, steps, segs, prefix_len,
    lengths_ref, live_ref, freq_ref, q_ref, k_ref,
    q_out, k_out, cos_out, sin_out, near_bias, last_bias, cos_own, sin_own,
):
    @pl.when(pl.program_id(0) == 0)
    def _():
        block_start = lax.axis_index("blk") * rows
        starts = [jnp.int32(0)]
        for seg in range(1, segs):
            starts.append(starts[-1] + lengths_ref[0, seg - 1])
        lane = lax.broadcasted_iota(jnp.int32, (ROW_TILE, LANES), 1)
        row = lax.broadcasted_iota(jnp.int32, (ROW_TILE, LANES), 0)
        freq = jnp.broadcast_to(freq_ref[...], (ROW_TILE, LANES))
        for step in range(steps + 1):
            for tile in range(0, rows, ROW_TILE):
                index = block_start + (tile - step * rows) + row
                own_start = jnp.zeros(index.shape, jnp.int32)
                for seg in range(1, segs):
                    own_start = jnp.where(index >= starts[seg], starts[seg], own_start)
                place = (prefix_len + index - own_start).astype(jnp.float32)
                sine, cosine = sine_cosine(place * freq)
                sine = jnp.where(lane < HALF, -sine, sine)
                if step == 0:
                    cos_own[pl.ds(tile, ROW_TILE), :] = cosine
                    sin_own[pl.ds(tile, ROW_TILE), :] = sine
                else:
                    span = pl.ds((step - 1) * rows + tile, ROW_TILE)
                    cos_out[span, :] = cosine
                    sin_out[span, :] = sine
        for tile in range(0, rows, ROW_TILE):
            span = pl.ds(tile, ROW_TILE)
            query_index = block_start + tile + row
            own_start = jnp.zeros(query_index.shape, jnp.int32)
            first_page_token = jnp.zeros(query_index.shape, jnp.int32)
            for seg in range(1, segs):
                later = query_index >= starts[seg]
                own_start = jnp.where(later, starts[seg], own_start)
                first_page_token = jnp.where(later, seg * prefix_len, first_page_token)
            for step in range(steps + 1):
                limit = query_index
                if step > 0:
                    limit = jnp.where(live_ref[0, 0, step - 1] > 0, limit, -1)
                for column in range(0, rows, LANES):
                    key_index = block_start + (column - step * rows) + lane
                    seen = (key_index >= own_start) & (key_index <= limit)
                    bias = jnp.where(seen, 0.0, HIDDEN)
                    if step == 1:
                        last_bias[span, pl.ds(column, LANES)] = bias
                    else:
                        place = max(step - 1, 0) * rows + column
                        near_bias[span, pl.ds(place, LANES)] = bias
            base = steps * rows
            for column in range(0, near_bias.shape[1] - base, LANES):
                offset = column + lane - first_page_token
                seen = (offset >= 0) & (offset < prefix_len)
                near_bias[span, pl.ds(base + column, LANES)] = jnp.where(seen, 0.0, HIDDEN)

    for tile in range(0, rows, ROW_TILE):
        span = pl.ds(tile, ROW_TILE)
        cosine = cos_own[span, :]
        signed_sine = sin_own[span, :]
        for source, target in ((q_ref, q_out), (k_ref, k_out)):
            for start in range(0, source.shape[2], HEAD_SIZE):
                columns = pl.ds(start, HEAD_SIZE)
                target[0, span, columns] = rotate(source[0, span, columns], cosine, signed_sine)


def prepare(queries, keys, lengths, live, prefix_len):
    rows = queries.shape[1]
    steps = live.shape[2]
    segs = lengths.shape[1]
    far_rows = steps * rows
    near_keys = padded_keys(far_rows + segs * prefix_len)
    exponent = -2.0 * np.arange(HALF) / HEAD_SIZE
    freq = np.tile(np.power(ROPE_BASE, exponent), 2).astype(np.float32)[None, :]
    whole = lambda part: (0, 0)
    by_part = lambda part: (0, 0, part)
    wide = pl.BlockSpec((1, rows, queries.shape[2] // PREPARE_STEPS), by_part)
    narrow = pl.BlockSpec((1, rows, keys.shape[2] // PREPARE_STEPS), by_part)
    table = jax.ShapeDtypeStruct((far_rows, HEAD_SIZE), jnp.float32)
    shapes = [
        jax.ShapeDtypeStruct(queries.shape, jnp.bfloat16),
        jax.ShapeDtypeStruct(keys.shape, jnp.bfloat16),
        table,
        table,
        jax.ShapeDtypeStruct((rows, near_keys), jnp.float32),
        jax.ShapeDtypeStruct((rows, rows), jnp.float32),
    ]
    return pl.pallas_call(
        lambda *refs: prepare_kernel(rows, steps, segs, prefix_len, *refs),
        grid=(PREPARE_STEPS,),
        in_specs=[
            pl.BlockSpec(memory_space=pltpu.SMEM),
            pl.BlockSpec(memory_space=pltpu.SMEM),
            pl.BlockSpec((1, HEAD_SIZE), whole),
            wide,
            narrow,
        ],
        out_specs=[wide, narrow] + [pl.BlockSpec(shape.shape, whole) for shape in shapes[2:]],
        out_shape=shapes,
        scratch_shapes=[pltpu.VMEM((rows, HEAD_SIZE), jnp.float32)] * 2,
        compiler_params=pltpu.CompilerParams(vmem_limit_bytes=vmem_bytes(near_keys + far_rows)),
        cost_estimate=PREPARE_COST,
        name="prepare",
    )(lengths, live, jnp.asarray(freq), queries, keys)


def stacked_queries(q_ref, part):
    return jnp.concatenate(
        [q_ref[0, :, pl.ds((part * GROUP + h) * HEAD_SIZE, HEAD_SIZE)] for h in range(GROUP)],
        axis=0,
    )


def rotate_rows(target, first, source, lanes, cos_ref, sin_ref, table_first):
    rows = source.shape[1]
    for tile in range(0, rows, ROW_TILE):
        table = pl.ds(table_first + tile, ROW_TILE)
        target[pl.ds(first + tile, ROW_TILE), :] = rotate(
            source[0, pl.ds(tile, ROW_TILE), lanes], cos_ref[table, :], sin_ref[table, :]
        )


def near_kernel(rows, steps, pages, kv_width, columns_count, *refs):
    table_ref, bias_ref, cos_ref, sin_ref, q_ref, k_ref, v_ref = refs[:7]
    shards, refs = refs[7 : 7 + columns_count], refs[7 + columns_count :]
    far_refs, refs = refs[: 2 * steps - 2], refs[2 * steps - 2 :]
    sum_ref, stat_ref, paged, sem = refs[:4]
    work = refs[4:]
    k_parts, v_parts, scores, weights, tops = (
        work[i : i + HEADS_PER_STEP] for i in range(0, len(work), HEADS_PER_STEP)
    )
    group = pl.program_id(0)
    pool_rows, page_tokens = shards[0].shape[:2]
    prefix_rows = pages * page_tokens
    base = steps * rows

    def page_copy(shard, place, page):
        return pltpu.make_async_copy(shard.at[place], paged.at[page], sem.at[page])

    @pl.when(group == 0)
    def _():
        column = lax.axis_index("batch")
        seg_pages = table_ref.shape[1]
        for page in range(pages):
            number = table_ref[column, page % seg_pages, page // seg_pages]
            apart = lax.div(number, jnp.int32(pool_rows)) ^ column
            place = lax.rem(number, jnp.int32(pool_rows))
            for which, shard in enumerate(shards):

                @pl.when(apart == which)
                def _(shard=shard, place=place, page=page):
                    page_copy(shard, place, page).start()

        rest = k_parts[0].shape[0] - base - prefix_rows
        for k_all, v_all in zip(k_parts, v_parts):
            v_all[:, pl.ds(HEAD_SIZE, HEAD_SIZE)] = jnp.ones(k_all.shape, jnp.bfloat16)
            if rest:
                blank = jnp.zeros((rest, HEAD_SIZE), jnp.bfloat16)
                k_all[pl.ds(base + prefix_rows, rest), :] = blank
                v_all[pl.ds(base + prefix_rows, rest), pl.ds(0, HEAD_SIZE)] = blank
        stat_ref[...] = jnp.zeros(stat_ref.shape, jnp.float32)

    for part in range(HEADS_PER_STEP):
        lanes = pl.ds(part * HEAD_SIZE, HEAD_SIZE)
        k_parts[part][pl.ds(0, rows), :] = k_ref[0, :, lanes]
        v_parts[part][pl.ds(0, rows), pl.ds(0, HEAD_SIZE)] = v_ref[0, :, lanes]
        for step in range(1, steps):
            far_key, far_value = far_refs[2 * step - 2 : 2 * step]
            rotate_rows(k_parts[part], step * rows, far_key, lanes, cos_ref, sin_ref, step * rows)
            v_parts[part][pl.ds(step * rows, rows), pl.ds(0, HEAD_SIZE)] = far_value[0, :, lanes]

    @pl.when(group == 0)
    def _():
        for page in range(pages):
            page_copy(shards[0], 0, page).wait()

    for part in range(HEADS_PER_STEP):
        start = (group * HEADS_PER_STEP + part) * HEAD_SIZE
        columns = pl.ds(pl.multiple_of(start, HEAD_SIZE), HEAD_SIZE)
        value_columns = pl.ds(pl.multiple_of(kv_width + start, HEAD_SIZE), HEAD_SIZE)
        span = pl.ds(base, prefix_rows)
        k_parts[part][span, :] = paged[:, :, columns].reshape(prefix_rows, HEAD_SIZE)
        v_parts[part][span, pl.ds(0, HEAD_SIZE)] = paged[:, :, value_columns].reshape(
            prefix_rows, HEAD_SIZE
        )

    for part in range(HEADS_PER_STEP):
        scores[part][...] = lax.dot_general(
            stacked_queries(q_ref, part), k_parts[part][...], (((1,), (1,)), ((), ())),
            preferred_element_type=jnp.float32,
        )
    lane = lax.broadcasted_iota(jnp.int32, (rows, LANES), 1)
    for part in range(HEADS_PER_STEP):
        for start in range(0, GROUP * rows, SOFTMAX_TILE):
            span = pl.ds(start, SOFTMAX_TILE)
            score = scores[part][span, :] + bias_ref[pl.ds(start % rows, SOFTMAX_TILE), :]
            highest = jnp.max(score, axis=1, keepdims=True)
            weight = jnp.exp2((score - highest) * EXP2_SCALE)
            weights[part][span, :] = weight.astype(jnp.bfloat16)
            tops[part][span, :] = jnp.broadcast_to(highest, (SOFTMAX_TILE, LANES))
        summed = jnp.dot(weights[part][...], v_parts[part][...], preferred_element_type=jnp.float32)
        for h in range(GROUP):
            own = part * GROUP + h
            head = group * (HEADS_PER_STEP * GROUP) + own
            span = slice(h * rows, (h + 1) * rows)
            sum_ref[:, pl.ds(own * HEAD_SIZE, HEAD_SIZE)] = summed[span, :HEAD_SIZE]
            stat_ref[...] = jnp.where(
                lane == head,
                tops[part][span, :],
                jnp.where(lane == QUERY_HEADS + head, summed[span, HEAD_SIZE:], stat_ref[...]),
            )


def near(table, shards, bias, cosine, signed_sine, query, key, value, far_both):
    rows, q_width = query.shape[1:]
    columns_count = len(shards)
    steps = 1 + len(far_both)
    pages = table.shape[1] * table.shape[2]
    key_count = bias.shape[1]
    whole = lambda group: (0, 0)
    by_group = lambda group: (0, 0, group)
    narrow = pl.BlockSpec((1, rows, HEADS_PER_STEP * HEAD_SIZE), by_group)
    narrow_value = pl.BlockSpec(
        (1, rows, HEADS_PER_STEP * HEAD_SIZE), lambda group: (1, 0, group)
    )
    wide = HEADS_PER_STEP * GROUP * HEAD_SIZE
    arrived = [both for both in far_both for _ in range(2)]
    return pl.pallas_call(
        lambda *refs: near_kernel(rows, steps, pages, key.shape[2], columns_count, *refs),
        grid=(KEY_VALUE_HEADS // HEADS_PER_STEP,),
        in_specs=[
            pl.BlockSpec(memory_space=pltpu.SMEM),
            pl.BlockSpec(bias.shape, whole),
            pl.BlockSpec(cosine.shape, whole),
            pl.BlockSpec(cosine.shape, whole),
            pl.BlockSpec((1, rows, wide), by_group),
            narrow,
            narrow,
        ]
        + [pl.BlockSpec(memory_space=pl.ANY)] * columns_count
        + [narrow, narrow_value] * len(far_both),
        out_specs=[
            pl.BlockSpec((rows, wide), lambda group: (0, group)),
            pl.BlockSpec((rows, LANES), whole),
        ],
        out_shape=[
            jax.ShapeDtypeStruct((rows, q_width), jnp.float32),
            jax.ShapeDtypeStruct((rows, LANES), jnp.float32),
        ],
        scratch_shapes=[
            pltpu.VMEM((pages,) + shards[0].shape[1:], jnp.bfloat16),
            pltpu.SemaphoreType.DMA((pages,)),
        ]
        + [pltpu.VMEM((key_count, HEAD_SIZE), jnp.bfloat16)] * HEADS_PER_STEP
        + [pltpu.VMEM((key_count, 2 * HEAD_SIZE), jnp.bfloat16)] * HEADS_PER_STEP
        + [pltpu.VMEM((GROUP * rows, key_count), jnp.float32)] * HEADS_PER_STEP
        + [pltpu.VMEM((GROUP * rows, key_count), jnp.bfloat16)] * HEADS_PER_STEP
        + [pltpu.VMEM((GROUP * rows, LANES), jnp.float32)] * HEADS_PER_STEP,
        compiler_params=pltpu.CompilerParams(vmem_limit_bytes=vmem_bytes(key_count)),
        cost_estimate=NEAR_COST,
        name="near",
    )(table, bias, cosine, signed_sine, query, key, value, *shards, *arrived)


def last_kernel(
    rows, cos_ref, sin_ref, bias_ref, stat_ref, sum_ref, q_ref, key_ref, swapped_value,
    passed_value, out_ref, *work,
):
    k_parts, v_parts, scores, weights, shrinks = (
        work[i : i + HEADS_PER_STEP] for i in range(0, len(work), HEADS_PER_STEP)
    )
    group = pl.program_id(0)
    even = lax.rem(lax.axis_index("blk"), 2) == 0

    @pl.when(group == 0)
    def _():
        for v_all in v_parts:
            v_all[:, pl.ds(HEAD_SIZE, HEAD_SIZE)] = jnp.ones((rows, HEAD_SIZE), jnp.bfloat16)

    for part in range(HEADS_PER_STEP):
        lanes = pl.ds(part * HEAD_SIZE, HEAD_SIZE)
        rotate_rows(k_parts[part], 0, key_ref, lanes, cos_ref, sin_ref, 0)
        v_parts[part][:, pl.ds(0, HEAD_SIZE)] = jnp.where(
            even, passed_value[0, :, lanes], swapped_value[0, :, lanes]
        )

    for part in range(HEADS_PER_STEP):
        scores[part][...] = lax.dot_general(
            stacked_queries(q_ref, part), k_parts[part][...], (((1,), (1,)), ((), ())),
            preferred_element_type=jnp.float32,
        )
    lane = lax.broadcasted_iota(jnp.int32, (SOFTMAX_TILE, LANES), 1)
    for part in range(HEADS_PER_STEP):
        for start in range(0, GROUP * rows, SOFTMAX_TILE):
            span = pl.ds(start, SOFTMAX_TILE)
            row_span = pl.ds(start % rows, SOFTMAX_TILE)
            head = group * (HEADS_PER_STEP * GROUP) + part * GROUP + start // rows
            score = scores[part][span, :] + bias_ref[row_span, :]
            stat = stat_ref[row_span, :]
            near_top = jnp.sum(jnp.where(lane == head, stat, 0.0), axis=1, keepdims=True)
            near_total = jnp.sum(
                jnp.where(lane == QUERY_HEADS + head, stat, 0.0), axis=1, keepdims=True
            )
            highest = jnp.maximum(jnp.max(score, axis=1, keepdims=True), near_top)
            weight = jnp.exp2((score - highest) * EXP2_SCALE)
            weights[part][span, :] = weight.astype(jnp.bfloat16)
            shrink = jnp.exp2((near_top - highest) * EXP2_SCALE)
            shrinks[part][span, pl.ds(0, LANES)] = jnp.broadcast_to(shrink, (SOFTMAX_TILE, LANES))
            shrinks[part][span, pl.ds(LANES, LANES)] = jnp.broadcast_to(
                shrink * near_total, (SOFTMAX_TILE, LANES)
            )
        summed = jnp.dot(weights[part][...], v_parts[part][...], preferred_element_type=jnp.float32)
        for h in range(GROUP):
            lanes = pl.ds((part * GROUP + h) * HEAD_SIZE, HEAD_SIZE)
            span = slice(h * rows, (h + 1) * rows)
            above = sum_ref[:, lanes] * shrinks[part][span, :LANES] + summed[span, :HEAD_SIZE]
            below = shrinks[part][span, LANES:] + summed[span, HEAD_SIZE:]
            out_ref[0, :, lanes] = (above / below).astype(jnp.bfloat16)


def last(cosine, signed_sine, bias, stat, sums, query, key, swapped_value, passed_value):
    rows = query.shape[1]
    whole = lambda group: (0, 0)
    by_group = lambda group: (0, 0, group)
    width = HEADS_PER_STEP * GROUP * HEAD_SIZE
    wide = pl.BlockSpec((1, rows, width), by_group)
    narrow = pl.BlockSpec((1, rows, HEADS_PER_STEP * HEAD_SIZE), by_group)
    table = pl.BlockSpec((rows, HEAD_SIZE), whole)
    return pl.pallas_call(
        lambda *refs: last_kernel(rows, *refs),
        grid=(KEY_VALUE_HEADS // HEADS_PER_STEP,),
        in_specs=[
            table,
            table,
            pl.BlockSpec(bias.shape, whole),
            pl.BlockSpec(stat.shape, whole),
            pl.BlockSpec((rows, width), lambda group: (0, group)),
            wide,
            narrow,
            narrow,
            narrow,
        ],
        out_specs=wide,
        out_shape=jax.ShapeDtypeStruct(query.shape, jnp.bfloat16),
        scratch_shapes=[pltpu.VMEM((rows, HEAD_SIZE), jnp.bfloat16)] * HEADS_PER_STEP
        + [pltpu.VMEM((rows, 2 * HEAD_SIZE), jnp.bfloat16)] * HEADS_PER_STEP
        + [pltpu.VMEM((GROUP * rows, rows), jnp.float32)] * HEADS_PER_STEP
        + [pltpu.VMEM((GROUP * rows, rows), jnp.bfloat16)] * HEADS_PER_STEP
        + [pltpu.VMEM((GROUP * rows, 2 * LANES), jnp.float32)] * HEADS_PER_STEP,
        compiler_params=pltpu.CompilerParams(vmem_limit_bytes=vmem_bytes(rows)),
        cost_estimate=LAST_COST,
        name="last",
    )(cosine, signed_sine, bias, stat, sums, query, key, swapped_value, passed_value)


def stack_kernel(first_ref, second_ref, out_ref, sem):
    copies = [
        pltpu.make_async_copy(source.at[0], out_ref.at[place], sem.at[place])
        for place, source in enumerate((first_ref, second_ref))
    ]
    for copy in copies:
        copy.start()
    for copy in copies:
        copy.wait()


def stacked(first, second):
    return pl.pallas_call(
        stack_kernel,
        in_specs=[pl.BlockSpec(memory_space=pltpu.HBM)] * 2,
        out_specs=pl.BlockSpec(memory_space=pltpu.HBM),
        out_shape=jax.ShapeDtypeStruct((2,) + first.shape[1:], first.dtype),
        scratch_shapes=[pltpu.SemaphoreType.DMA((2,))],
        cost_estimate=cost(0),
        name="stack",
    )(first, second)


def pool_shards(pool):
    count = lax.axis_size("batch")
    shards, bit = {0: pool}, count // 2
    while bit:
        for apart, shard in list(shards.items()):
            shards[apart ^ bit] = lax.ppermute(
                shard, "batch", [(c, c ^ bit) for c in range(count)]
            )
        bit //= 2
    return [shards[apart] for apart in range(count)]


def per_device(queries, keys, values, seg_ids, lengths, live, page_table, pool):
    steps = live.shape[2]
    prefix_len = page_table.shape[2] * pool.shape[1]
    blocks = lax.axis_size("blk")
    both = stacked(keys, values)
    far_both = [shifted(both, 2)]
    far_key = shifted(keys, 1)
    for step in range(3, steps + 1):
        far_both.append(shifted(both, step))
    pool, later_values, both = lax.optimization_barrier((pool, values, both))
    swapped_value = lax.ppermute(later_values, "blk", [(j, j ^ 1) for j in range(blocks)])
    query, key, cosine, signed_sine, near_bias, last_bias = prepare(
        queries, keys, lengths, live, prefix_len
    )
    passed_value = lax.ppermute(
        swapped_value, "blk", [(j, j + 2) for j in range(0, blocks - 2, 2)]
    )
    shards = pool_shards(pool)
    sums, stat = near(
        jnp.swapaxes(page_table, 1, 2), shards, near_bias, cosine, signed_sine,
        query, key, values, far_both,
    )
    result = last(
        cosine, signed_sine, last_bias, stat, sums, query, far_key, swapped_value, passed_value
    )
    return (result, key)


def solution(mesh):
    in_specs = (
        P("batch", "blk", None),
        P("batch", "blk", None),
        P("batch", "blk", None),
        P("batch", "blk"),
        P("batch", None),
        P("batch", "blk", None),
        P(),
        P("batch", None, None),
    )
    out_specs = (P("batch", "blk", None), P("batch", "blk", None))
    return jax.shard_map(
        per_device, mesh=mesh, in_specs=in_specs, out_specs=out_specs, check_vma=False
    )
```

```python
import math

import jax
import jax.numpy as jnp
import numpy as np
from jax import lax
from jax.experimental import pallas as pl
from jax.experimental.pallas import tpu as pltpu
from jax.sharding import PartitionSpec as P

QUERY_HEADS = 16
KEY_VALUE_HEADS = 8
HEAD_SIZE = 128
GROUP = QUERY_HEADS // KEY_VALUE_HEADS
HALF = HEAD_SIZE // 2
ROPE_BASE = 1000000.0
HIDDEN = -1e30
LANES = 128
ROW_TILE = 64
SOFTMAX_TILE = 16
HEADS_PER_STEP = 2
PREPARE_STEPS = 2


def cost(flops):
    return pl.CostEstimate(flops=flops, bytes_accessed=0, transcendentals=0)


PREPARE_COST = cost(0)
NEAR_COST = cost(0)
LAST_COST = cost(0)
EXP2_SCALE = math.log2(math.e) / math.sqrt(HEAD_SIZE)

PIO2_A = float(np.float32(1.5703125))
PIO2_B = float(np.float32(4.837512969970703125e-4))
PIO2_C = float(np.float32(math.pi / 2 - 1.5703125 - 4.837512969970703125e-4))


def shifted(value, steps):
    count = lax.axis_size("blk")
    return lax.ppermute(value, "blk", [(source, source + steps) for source in range(count - steps)])


def padded_keys(count):
    return -(-count // LANES) * LANES


def vmem_bytes(key_count):
    return 16 * 1024 * (1024 + key_count)


def sine_cosine(angle):
    turns = jnp.floor(angle * (2.0 / math.pi) + 0.5)
    rest = ((angle - turns * PIO2_A) - turns * PIO2_B) - turns * PIO2_C
    square = rest * rest
    sine = rest + rest * square * (
        -1.6666654611e-1 + square * (8.3321608736e-3 - square * 1.9515295891e-4)
    )
    cosine = 1.0 - 0.5 * square + square * square * (
        4.166664568298827e-2 + square * (-1.388731625493765e-3 + square * 2.443315711809948e-5)
    )
    quadrant = turns.astype(jnp.int32) & 3
    swapped = (quadrant & 1) == 1
    sine_out = jnp.where(swapped, cosine, sine)
    cosine_out = jnp.where(swapped, sine, cosine)
    sine_out = jnp.where(quadrant >= 2, -sine_out, sine_out)
    cosine_out = jnp.where((quadrant == 1) | (quadrant == 2), -cosine_out, cosine_out)
    return sine_out, cosine_out


def rotate(head, cosine, signed_sine):
    wide = head.astype(jnp.float32)
    return (wide * cosine + pltpu.roll(wide, HALF, 1) * signed_sine).astype(jnp.bfloat16)


def prepare_kernel(
    rows, steps, segs, prefix_len,
    lengths_ref, live_ref, freq_ref, q_ref, k_ref,
    q_out, k_out, cos_out, sin_out, near_bias, last_bias, cos_own, sin_own,
):
    @pl.when(pl.program_id(0) == 0)
    def _():
        block_start = lax.axis_index("blk") * rows
        starts = [jnp.int32(0)]
        for seg in range(1, segs):
            starts.append(starts[-1] + lengths_ref[0, seg - 1])
        lane = lax.broadcasted_iota(jnp.int32, (ROW_TILE, LANES), 1)
        row = lax.broadcasted_iota(jnp.int32, (ROW_TILE, LANES), 0)
        freq = jnp.broadcast_to(freq_ref[...], (ROW_TILE, LANES))
        for step in range(steps + 1):
            for tile in range(0, rows, ROW_TILE):
                index = block_start + (tile - step * rows) + row
                own_start = jnp.zeros(index.shape, jnp.int32)
                for seg in range(1, segs):
                    own_start = jnp.where(index >= starts[seg], starts[seg], own_start)
                place = (prefix_len + index - own_start).astype(jnp.float32)
                sine, cosine = sine_cosine(place * freq)
                sine = jnp.where(lane < HALF, -sine, sine)
                if step == 0:
                    cos_own[pl.ds(tile, ROW_TILE), :] = cosine
                    sin_own[pl.ds(tile, ROW_TILE), :] = sine
                else:
                    span = pl.ds((step - 1) * rows + tile, ROW_TILE)
                    cos_out[span, :] = cosine
                    sin_out[span, :] = sine
        for tile in range(0, rows, ROW_TILE):
            span = pl.ds(tile, ROW_TILE)
            query_index = block_start + tile + row
            own_start = jnp.zeros(query_index.shape, jnp.int32)
            first_page_token = jnp.zeros(query_index.shape, jnp.int32)
            for seg in range(1, segs):
                later = query_index >= starts[seg]
                own_start = jnp.where(later, starts[seg], own_start)
                first_page_token = jnp.where(later, seg * prefix_len, first_page_token)
            for step in range(steps + 1):
                limit = query_index
                if step > 0:
                    limit = jnp.where(live_ref[0, 0, step - 1] > 0, limit, -1)
                for column in range(0, rows, LANES):
                    key_index = block_start + (column - step * rows) + lane
                    seen = (key_index >= own_start) & (key_index <= limit)
                    bias = jnp.where(seen, 0.0, HIDDEN)
                    if step == 1:
                        last_bias[span, pl.ds(column, LANES)] = bias
                    else:
                        place = max(step - 1, 0) * rows + column
                        near_bias[span, pl.ds(place, LANES)] = bias
            base = steps * rows
            for column in range(0, near_bias.shape[1] - base, LANES):
                offset = column + lane - first_page_token
                seen = (offset >= 0) & (offset < prefix_len)
                near_bias[span, pl.ds(base + column, LANES)] = jnp.where(seen, 0.0, HIDDEN)

    for tile in range(0, rows, ROW_TILE):
        span = pl.ds(tile, ROW_TILE)
        cosine = cos_own[span, :]
        signed_sine = sin_own[span, :]
        for source, target in ((q_ref, q_out), (k_ref, k_out)):
            for start in range(0, source.shape[2], HEAD_SIZE):
                columns = pl.ds(start, HEAD_SIZE)
                target[0, span, columns] = rotate(source[0, span, columns], cosine, signed_sine)


def prepare(queries, keys, lengths, live, prefix_len):
    rows = queries.shape[1]
    steps = live.shape[2]
    segs = lengths.shape[1]
    far_rows = steps * rows
    near_keys = padded_keys(far_rows + segs * prefix_len)
    exponent = -2.0 * np.arange(HALF) / HEAD_SIZE
    freq = np.tile(np.power(ROPE_BASE, exponent), 2).astype(np.float32)[None, :]
    whole = lambda part: (0, 0)
    by_part = lambda part: (0, 0, part)
    wide = pl.BlockSpec((1, rows, queries.shape[2] // PREPARE_STEPS), by_part)
    narrow = pl.BlockSpec((1, rows, keys.shape[2] // PREPARE_STEPS), by_part)
    table = jax.ShapeDtypeStruct((far_rows, HEAD_SIZE), jnp.float32)
    shapes = [
        jax.ShapeDtypeStruct(queries.shape, jnp.bfloat16),
        jax.ShapeDtypeStruct(keys.shape, jnp.bfloat16),
        table,
        table,
        jax.ShapeDtypeStruct((rows, near_keys), jnp.float32),
        jax.ShapeDtypeStruct((rows, rows), jnp.float32),
    ]
    return pl.pallas_call(
        lambda *refs: prepare_kernel(rows, steps, segs, prefix_len, *refs),
        grid=(PREPARE_STEPS,),
        in_specs=[
            pl.BlockSpec(memory_space=pltpu.SMEM),
            pl.BlockSpec(memory_space=pltpu.SMEM),
            pl.BlockSpec((1, HEAD_SIZE), whole),
            wide,
            narrow,
        ],
        out_specs=[wide, narrow] + [pl.BlockSpec(shape.shape, whole) for shape in shapes[2:]],
        out_shape=shapes,
        scratch_shapes=[pltpu.VMEM((rows, HEAD_SIZE), jnp.float32)] * 2,
        compiler_params=pltpu.CompilerParams(vmem_limit_bytes=vmem_bytes(near_keys + far_rows)),
        cost_estimate=PREPARE_COST,
        name="prepare",
    )(lengths, live, jnp.asarray(freq), queries, keys)


def stacked_queries(q_ref, part):
    return jnp.concatenate(
        [q_ref[0, :, pl.ds((part * GROUP + h) * HEAD_SIZE, HEAD_SIZE)] for h in range(GROUP)],
        axis=0,
    )


def rotate_rows(target, first, source, lanes, cos_ref, sin_ref, table_first):
    rows = source.shape[1]
    for tile in range(0, rows, ROW_TILE):
        table = pl.ds(table_first + tile, ROW_TILE)
        target[pl.ds(first + tile, ROW_TILE), :] = rotate(
            source[0, pl.ds(tile, ROW_TILE), lanes], cos_ref[table, :], sin_ref[table, :]
        )


def near_kernel(rows, steps, pages, kv_width, columns_count, *refs):
    table_ref, bias_ref, cos_ref, sin_ref, q_ref, k_ref, v_ref = refs[:7]
    shards, refs = refs[7 : 7 + columns_count], refs[7 + columns_count :]
    far_refs, refs = refs[: 2 * steps - 2], refs[2 * steps - 2 :]
    sum_ref, stat_ref, paged, sem = refs[:4]
    work = refs[4:]
    k_parts, v_parts, scores, weights, tops = (
        work[i : i + HEADS_PER_STEP] for i in range(0, len(work), HEADS_PER_STEP)
    )
    group = pl.program_id(0)
    pool_rows, page_tokens = shards[0].shape[:2]
    prefix_rows = pages * page_tokens
    base = steps * rows

    def page_copy(shard, place, page):
        return pltpu.make_async_copy(shard.at[place], paged.at[page], sem.at[page])

    @pl.when(group == 0)
    def _():
        column = lax.axis_index("batch")
        seg_pages = table_ref.shape[1]
        for page in range(pages):
            number = table_ref[column, page % seg_pages, page // seg_pages]
            apart = lax.div(number, jnp.int32(pool_rows)) ^ column
            place = lax.rem(number, jnp.int32(pool_rows))
            for which, shard in enumerate(shards):

                @pl.when(apart == which)
                def _(shard=shard, place=place, page=page):
                    page_copy(shard, place, page).start()

        rest = k_parts[0].shape[0] - base - prefix_rows
        for k_all, v_all in zip(k_parts, v_parts):
            v_all[:, pl.ds(HEAD_SIZE, HEAD_SIZE)] = jnp.ones(k_all.shape, jnp.bfloat16)
            if rest:
                blank = jnp.zeros((rest, HEAD_SIZE), jnp.bfloat16)
                k_all[pl.ds(base + prefix_rows, rest), :] = blank
                v_all[pl.ds(base + prefix_rows, rest), pl.ds(0, HEAD_SIZE)] = blank
        stat_ref[...] = jnp.zeros(stat_ref.shape, jnp.float32)

    for part in range(HEADS_PER_STEP):
        lanes = pl.ds(part * HEAD_SIZE, HEAD_SIZE)
        k_parts[part][pl.ds(0, rows), :] = k_ref[0, :, lanes]
        v_parts[part][pl.ds(0, rows), pl.ds(0, HEAD_SIZE)] = v_ref[0, :, lanes]
        for step in range(1, steps):
            far_key, far_value = far_refs[2 * step - 2 : 2 * step]
            rotate_rows(k_parts[part], step * rows, far_key, lanes, cos_ref, sin_ref, step * rows)
            v_parts[part][pl.ds(step * rows, rows), pl.ds(0, HEAD_SIZE)] = far_value[0, :, lanes]

    @pl.when(group == 0)
    def _():
        for page in range(pages):
            page_copy(shards[0], 0, page).wait()

    for part in range(HEADS_PER_STEP):
        start = (group * HEADS_PER_STEP + part) * HEAD_SIZE
        columns = pl.ds(pl.multiple_of(start, HEAD_SIZE), HEAD_SIZE)
        value_columns = pl.ds(pl.multiple_of(kv_width + start, HEAD_SIZE), HEAD_SIZE)
        span = pl.ds(base, prefix_rows)
        k_parts[part][span, :] = paged[:, :, columns].reshape(prefix_rows, HEAD_SIZE)
        v_parts[part][span, pl.ds(0, HEAD_SIZE)] = paged[:, :, value_columns].reshape(
            prefix_rows, HEAD_SIZE
        )

    for part in range(HEADS_PER_STEP):
        scores[part][...] = lax.dot_general(
            stacked_queries(q_ref, part), k_parts[part][...], (((1,), (1,)), ((), ())),
            preferred_element_type=jnp.float32,
        )
    lane = lax.broadcasted_iota(jnp.int32, (rows, LANES), 1)
    for part in range(HEADS_PER_STEP):
        for start in range(0, GROUP * rows, SOFTMAX_TILE):
            span = pl.ds(start, SOFTMAX_TILE)
            score = scores[part][span, :] + bias_ref[pl.ds(start % rows, SOFTMAX_TILE), :]
            highest = jnp.max(score, axis=1, keepdims=True)
            weight = jnp.exp2((score - highest) * EXP2_SCALE)
            weights[part][span, :] = weight.astype(jnp.bfloat16)
            tops[part][span, :] = jnp.broadcast_to(highest, (SOFTMAX_TILE, LANES))
        summed = jnp.dot(weights[part][...], v_parts[part][...], preferred_element_type=jnp.float32)
        for h in range(GROUP):
            own = part * GROUP + h
            head = group * (HEADS_PER_STEP * GROUP) + own
            span = slice(h * rows, (h + 1) * rows)
            sum_ref[:, pl.ds(own * HEAD_SIZE, HEAD_SIZE)] = summed[span, :HEAD_SIZE]
            stat_ref[...] = jnp.where(
                lane == head,
                tops[part][span, :],
                jnp.where(lane == QUERY_HEADS + head, summed[span, HEAD_SIZE:], stat_ref[...]),
            )


def near(table, shards, bias, cosine, signed_sine, query, key, value, far):
    rows, q_width = query.shape[1:]
    columns_count = len(shards)
    steps = 1 + len(far) // 2
    pages = table.shape[1] * table.shape[2]
    key_count = bias.shape[1]
    whole = lambda group: (0, 0)
    by_group = lambda group: (0, 0, group)
    narrow = pl.BlockSpec((1, rows, HEADS_PER_STEP * HEAD_SIZE), by_group)
    wide = HEADS_PER_STEP * GROUP * HEAD_SIZE
    return pl.pallas_call(
        lambda *refs: near_kernel(rows, steps, pages, key.shape[2], columns_count, *refs),
        grid=(KEY_VALUE_HEADS // HEADS_PER_STEP,),
        in_specs=[
            pl.BlockSpec(memory_space=pltpu.SMEM),
            pl.BlockSpec(bias.shape, whole),
            pl.BlockSpec(cosine.shape, whole),
            pl.BlockSpec(cosine.shape, whole),
            pl.BlockSpec((1, rows, wide), by_group),
            narrow,
            narrow,
        ]
        + [pl.BlockSpec(memory_space=pl.ANY)] * columns_count
        + [narrow] * len(far),
        out_specs=[
            pl.BlockSpec((rows, wide), lambda group: (0, group)),
            pl.BlockSpec((rows, LANES), whole),
        ],
        out_shape=[
            jax.ShapeDtypeStruct((rows, q_width), jnp.float32),
            jax.ShapeDtypeStruct((rows, LANES), jnp.float32),
        ],
        scratch_shapes=[
            pltpu.VMEM((pages,) + shards[0].shape[1:], jnp.bfloat16),
            pltpu.SemaphoreType.DMA((pages,)),
        ]
        + [pltpu.VMEM((key_count, HEAD_SIZE), jnp.bfloat16)] * HEADS_PER_STEP
        + [pltpu.VMEM((key_count, 2 * HEAD_SIZE), jnp.bfloat16)] * HEADS_PER_STEP
        + [pltpu.VMEM((GROUP * rows, key_count), jnp.float32)] * HEADS_PER_STEP
        + [pltpu.VMEM((GROUP * rows, key_count), jnp.bfloat16)] * HEADS_PER_STEP
        + [pltpu.VMEM((GROUP * rows, LANES), jnp.float32)] * HEADS_PER_STEP,
        compiler_params=pltpu.CompilerParams(vmem_limit_bytes=vmem_bytes(key_count)),
        cost_estimate=NEAR_COST,
        name="near",
    )(table, bias, cosine, signed_sine, query, key, value, *shards, *far)


def last_kernel(
    rows, cos_ref, sin_ref, bias_ref, stat_ref, sum_ref, q_ref, key_ref, swapped_value,
    passed_value, out_ref, *work,
):
    k_parts, v_parts, scores, weights, shrinks = (
        work[i : i + HEADS_PER_STEP] for i in range(0, len(work), HEADS_PER_STEP)
    )
    group = pl.program_id(0)
    even = lax.rem(lax.axis_index("blk"), 2) == 0

    @pl.when(group == 0)
    def _():
        for v_all in v_parts:
            v_all[:, pl.ds(HEAD_SIZE, HEAD_SIZE)] = jnp.ones((rows, HEAD_SIZE), jnp.bfloat16)

    for part in range(HEADS_PER_STEP):
        lanes = pl.ds(part * HEAD_SIZE, HEAD_SIZE)
        rotate_rows(k_parts[part], 0, key_ref, lanes, cos_ref, sin_ref, 0)
        v_parts[part][:, pl.ds(0, HEAD_SIZE)] = jnp.where(
            even, passed_value[0, :, lanes], swapped_value[0, :, lanes]
        )

    for part in range(HEADS_PER_STEP):
        scores[part][...] = lax.dot_general(
            stacked_queries(q_ref, part), k_parts[part][...], (((1,), (1,)), ((), ())),
            preferred_element_type=jnp.float32,
        )
    lane = lax.broadcasted_iota(jnp.int32, (SOFTMAX_TILE, LANES), 1)
    for part in range(HEADS_PER_STEP):
        for start in range(0, GROUP * rows, SOFTMAX_TILE):
            span = pl.ds(start, SOFTMAX_TILE)
            row_span = pl.ds(start % rows, SOFTMAX_TILE)
            head = group * (HEADS_PER_STEP * GROUP) + part * GROUP + start // rows
            score = scores[part][span, :] + bias_ref[row_span, :]
            stat = stat_ref[row_span, :]
            near_top = jnp.sum(jnp.where(lane == head, stat, 0.0), axis=1, keepdims=True)
            near_total = jnp.sum(
                jnp.where(lane == QUERY_HEADS + head, stat, 0.0), axis=1, keepdims=True
            )
            highest = jnp.maximum(jnp.max(score, axis=1, keepdims=True), near_top)
            weight = jnp.exp2((score - highest) * EXP2_SCALE)
            weights[part][span, :] = weight.astype(jnp.bfloat16)
            shrink = jnp.exp2((near_top - highest) * EXP2_SCALE)
            shrinks[part][span, pl.ds(0, LANES)] = jnp.broadcast_to(shrink, (SOFTMAX_TILE, LANES))
            shrinks[part][span, pl.ds(LANES, LANES)] = jnp.broadcast_to(
                shrink * near_total, (SOFTMAX_TILE, LANES)
            )
        summed = jnp.dot(weights[part][...], v_parts[part][...], preferred_element_type=jnp.float32)
        for h in range(GROUP):
            lanes = pl.ds((part * GROUP + h) * HEAD_SIZE, HEAD_SIZE)
            span = slice(h * rows, (h + 1) * rows)
            above = sum_ref[:, lanes] * shrinks[part][span, :LANES] + summed[span, :HEAD_SIZE]
            below = shrinks[part][span, LANES:] + summed[span, HEAD_SIZE:]
            out_ref[0, :, lanes] = (above / below).astype(jnp.bfloat16)


def last(cosine, signed_sine, bias, stat, sums, query, key, swapped_value, passed_value):
    rows = query.shape[1]
    whole = lambda group: (0, 0)
    by_group = lambda group: (0, 0, group)
    width = HEADS_PER_STEP * GROUP * HEAD_SIZE
    wide = pl.BlockSpec((1, rows, width), by_group)
    narrow = pl.BlockSpec((1, rows, HEADS_PER_STEP * HEAD_SIZE), by_group)
    table = pl.BlockSpec((rows, HEAD_SIZE), whole)
    return pl.pallas_call(
        lambda *refs: last_kernel(rows, *refs),
        grid=(KEY_VALUE_HEADS // HEADS_PER_STEP,),
        in_specs=[
            table,
            table,
            pl.BlockSpec(bias.shape, whole),
            pl.BlockSpec(stat.shape, whole),
            pl.BlockSpec((rows, width), lambda group: (0, group)),
            wide,
            narrow,
            narrow,
            narrow,
        ],
        out_specs=wide,
        out_shape=jax.ShapeDtypeStruct(query.shape, jnp.bfloat16),
        scratch_shapes=[pltpu.VMEM((rows, HEAD_SIZE), jnp.bfloat16)] * HEADS_PER_STEP
        + [pltpu.VMEM((rows, 2 * HEAD_SIZE), jnp.bfloat16)] * HEADS_PER_STEP
        + [pltpu.VMEM((GROUP * rows, rows), jnp.float32)] * HEADS_PER_STEP
        + [pltpu.VMEM((GROUP * rows, rows), jnp.bfloat16)] * HEADS_PER_STEP
        + [pltpu.VMEM((GROUP * rows, 2 * LANES), jnp.float32)] * HEADS_PER_STEP,
        compiler_params=pltpu.CompilerParams(vmem_limit_bytes=vmem_bytes(rows)),
        cost_estimate=LAST_COST,
        name="last",
    )(cosine, signed_sine, bias, stat, sums, query, key, swapped_value, passed_value)


def pool_shards(pool, after):
    count = lax.axis_size("batch")
    shards, bit = {0: pool}, count // 2
    while bit:
        if len(shards) > 1:
            shards, after = lax.optimization_barrier((shards, after))
        for apart, shard in list(shards.items()):
            shards[apart ^ bit] = lax.ppermute(
                shard, "batch", [(c, c ^ bit) for c in range(count)]
            )
        bit //= 2
    return [shards[apart] for apart in range(count)]


def per_device(queries, keys, values, seg_ids, lengths, live, page_table, pool):
    steps = live.shape[2]
    prefix_len = page_table.shape[2] * pool.shape[1]
    blocks = lax.axis_size("blk")
    far = [shifted(keys, 2), shifted(values, 2)]
    far_key = shifted(keys, 1)
    for step in range(3, steps + 1):
        far += [shifted(keys, step), shifted(values, step)]
    swapped_value = lax.ppermute(values, "blk", [(j, j ^ 1) for j in range(blocks)])
    query, key, cosine, signed_sine, near_bias, last_bias = prepare(
        queries, keys, lengths, live, prefix_len
    )
    passed_value = lax.ppermute(
        swapped_value, "blk", [(j, j + 2) for j in range(0, blocks - 2, 2)]
    )
    shards = pool_shards(pool, cosine)
    sums, stat = near(
        jnp.swapaxes(page_table, 1, 2), shards, near_bias, cosine, signed_sine,
        query, key, values, far,
    )
    result = last(
        cosine, signed_sine, last_bias, stat, sums, query, far_key, swapped_value, passed_value
    )
    return (result, key)


def solution(mesh):
    in_specs = (
        P("batch", "blk", None),
        P("batch", "blk", None),
        P("batch", "blk", None),
        P("batch", "blk"),
        P("batch", None),
        P("batch", "blk", None),
        P(),
        P("batch", None, None),
    )
    out_specs = (P("batch", "blk", None), P("batch", "blk", None))
    return jax.shard_map(
        per_device, mesh=mesh, in_specs=in_specs, out_specs=out_specs, check_vma=False
    )
```

```python
import math

import jax
import jax.numpy as jnp
import numpy as np
from jax import lax
from jax.experimental import pallas as pl
from jax.experimental.pallas import tpu as pltpu
from jax.sharding import PartitionSpec as P

QUERY_HEADS = 16
KEY_VALUE_HEADS = 8
HEAD_SIZE = 128
GROUP = QUERY_HEADS // KEY_VALUE_HEADS
HALF = HEAD_SIZE // 2
ROPE_BASE = 1000000.0
HIDDEN = -1e30
LANES = 128
ROW_TILE = 64
SOFTMAX_TILE = 16
HEADS_PER_STEP = 2
PREPARE_STEPS = 2


def cost(flops):
    return pl.CostEstimate(flops=flops, bytes_accessed=0, transcendentals=0)


PREPARE_COST = cost(0)
NEAR_COST = cost(0)
LAST_COST = cost(0)
EXP2_SCALE = math.log2(math.e) / math.sqrt(HEAD_SIZE)

FREQ_POWERS = [float(ROPE_BASE ** (-(2**k) / HALF)) for k in range(HALF.bit_length() - 1)]

PIO2_A = float(np.float32(1.5703125))
PIO2_B = float(np.float32(4.837512969970703125e-4))
PIO2_C = float(np.float32(math.pi / 2 - 1.5703125 - 4.837512969970703125e-4))


def shifted(value, steps):
    count = lax.axis_size("blk")
    return lax.ppermute(value, "blk", [(source, source + steps) for source in range(count - steps)])


def padded_keys(count):
    return -(-count // LANES) * LANES


def vmem_bytes(key_count):
    return 16 * 1024 * (1024 + key_count)


def sine_cosine(angle):
    turns = jnp.floor(angle * (2.0 / math.pi) + 0.5)
    rest = ((angle - turns * PIO2_A) - turns * PIO2_B) - turns * PIO2_C
    square = rest * rest
    sine = rest + rest * square * (
        -1.6666654611e-1 + square * (8.3321608736e-3 - square * 1.9515295891e-4)
    )
    cosine = 1.0 - 0.5 * square + square * square * (
        4.166664568298827e-2 + square * (-1.388731625493765e-3 + square * 2.443315711809948e-5)
    )
    quadrant = turns.astype(jnp.int32) & 3
    swapped = (quadrant & 1) == 1
    sine_out = jnp.where(swapped, cosine, sine)
    cosine_out = jnp.where(swapped, sine, cosine)
    sine_out = jnp.where(quadrant >= 2, -sine_out, sine_out)
    cosine_out = jnp.where((quadrant == 1) | (quadrant == 2), -cosine_out, cosine_out)
    return sine_out, cosine_out


def rotate(head, cosine, signed_sine):
    wide = head.astype(jnp.float32)
    return (wide * cosine + pltpu.roll(wide, HALF, 1) * signed_sine).astype(jnp.bfloat16)


def prepare_kernel(
    rows, steps, segs, prefix_len,
    lengths_ref, live_ref, table_ref, q_ref, k_ref, v_ref, pool_ref,
    q_out, k_out, k_copy, v_copy, pool_copy, page_out, cos_out, sin_out, near_bias, last_bias,
    cos_own, sin_own,
):
    @pl.when(pl.program_id(0) == 0)
    def _():
        block_start = lax.axis_index("blk") * rows
        starts = [jnp.int32(0)]
        for seg in range(1, segs):
            starts.append(starts[-1] + lengths_ref[0, seg - 1])
        lane = lax.broadcasted_iota(jnp.int32, (ROW_TILE, LANES), 1)
        row = lax.broadcasted_iota(jnp.int32, (ROW_TILE, LANES), 0)
        freq = jnp.ones((ROW_TILE, LANES), jnp.float32)
        for bit, power in enumerate(FREQ_POWERS):
            freq = jnp.where((lane >> bit) & 1 == 1, freq * power, freq)
        column = lax.axis_index("batch")
        for seg in range(segs):
            for page in range(table_ref.shape[1]):
                page_out[seg * table_ref.shape[1] + page] = table_ref[column, page, seg]
        for step in range(steps + 1):
            for tile in range(0, rows, ROW_TILE):
                index = block_start + (tile - step * rows) + row
                own_start = jnp.zeros(index.shape, jnp.int32)
                for seg in range(1, segs):
                    own_start = jnp.where(index >= starts[seg], starts[seg], own_start)
                place = (prefix_len + index - own_start).astype(jnp.float32)
                sine, cosine = sine_cosine(place * freq)
                sine = jnp.where(lane < HALF, -sine, sine)
                if step == 0:
                    cos_own[pl.ds(tile, ROW_TILE), :] = cosine
                    sin_own[pl.ds(tile, ROW_TILE), :] = sine
                else:
                    span = pl.ds((step - 1) * rows + tile, ROW_TILE)
                    cos_out[span, :] = cosine
                    sin_out[span, :] = sine
        for tile in range(0, rows, ROW_TILE):
            span = pl.ds(tile, ROW_TILE)
            query_index = block_start + tile + row
            own_start = jnp.zeros(query_index.shape, jnp.int32)
            first_page_token = jnp.zeros(query_index.shape, jnp.int32)
            for seg in range(1, segs):
                later = query_index >= starts[seg]
                own_start = jnp.where(later, starts[seg], own_start)
                first_page_token = jnp.where(later, seg * prefix_len, first_page_token)
            for step in range(steps + 1):
                limit = query_index
                if step > 0:
                    limit = jnp.where(live_ref[0, 0, step - 1] > 0, limit, -1)
                for column in range(0, rows, LANES):
                    key_index = block_start + (column - step * rows) + lane
                    seen = (key_index >= own_start) & (key_index <= limit)
                    bias = jnp.where(seen, 0.0, HIDDEN)
                    if step == 1:
                        last_bias[span, pl.ds(column, LANES)] = bias
                    else:
                        place = max(step - 1, 0) * rows + column
                        near_bias[span, pl.ds(place, LANES)] = bias
            base = steps * rows
            for column in range(0, near_bias.shape[1] - base, LANES):
                offset = column + lane - first_page_token
                seen = (offset >= 0) & (offset < prefix_len)
                near_bias[span, pl.ds(base + column, LANES)] = jnp.where(seen, 0.0, HIDDEN)

    for tile in range(0, rows, ROW_TILE):
        span = pl.ds(tile, ROW_TILE)
        cosine = cos_own[span, :]
        signed_sine = sin_own[span, :]
        for source, target in ((q_ref, q_out), (k_ref, k_out)):
            for start in range(0, source.shape[2], HEAD_SIZE):
                columns = pl.ds(start, HEAD_SIZE)
                turned = rotate(source[0, span, columns], cosine, signed_sine)
                target[0, span, columns] = turned
                if source is k_ref:
                    k_copy[0, span, columns] = turned
    v_copy[...] = v_ref[...]
    pool_copy[...] = pool_ref[...]


def prepare(queries, keys, values, pool, lengths, live, page_table):
    rows = queries.shape[1]
    steps = live.shape[2]
    segs = lengths.shape[1]
    prefix_len = page_table.shape[2] * pool.shape[1]
    pages = page_table.shape[1] * page_table.shape[2]
    far_rows = steps * rows
    near_keys = padded_keys(far_rows + segs * prefix_len)
    whole = lambda part: (0, 0)
    by_part = lambda part: (0, 0, part)
    wide = pl.BlockSpec((1, rows, queries.shape[2] // PREPARE_STEPS), by_part)
    narrow = pl.BlockSpec((1, rows, keys.shape[2] // PREPARE_STEPS), by_part)
    some_pages = pl.BlockSpec(
        (pool.shape[0] // PREPARE_STEPS, *pool.shape[1:]), lambda part: (part, 0, 0)
    )
    table = jax.ShapeDtypeStruct((far_rows, HEAD_SIZE), jnp.float32)
    shapes = [
        jax.ShapeDtypeStruct(queries.shape, jnp.bfloat16),
        jax.ShapeDtypeStruct(keys.shape, jnp.bfloat16),
        jax.ShapeDtypeStruct(keys.shape, jnp.bfloat16),
        jax.ShapeDtypeStruct(values.shape, jnp.bfloat16),
        jax.ShapeDtypeStruct(pool.shape, jnp.bfloat16),
        jax.ShapeDtypeStruct((pages,), jnp.int32),
        table,
        table,
        jax.ShapeDtypeStruct((rows, near_keys), jnp.float32),
        jax.ShapeDtypeStruct((rows, rows), jnp.float32),
    ]
    return pl.pallas_call(
        lambda *refs: prepare_kernel(rows, steps, segs, prefix_len, *refs),
        grid=(PREPARE_STEPS,),
        in_specs=[
            pl.BlockSpec(memory_space=pltpu.SMEM),
            pl.BlockSpec(memory_space=pltpu.SMEM),
            pl.BlockSpec(memory_space=pltpu.SMEM),
            wide,
            narrow,
            narrow,
            some_pages,
        ],
        out_specs=[wide, narrow, narrow, narrow, some_pages, pl.BlockSpec(memory_space=pltpu.SMEM)]
        + [pl.BlockSpec(shape.shape, whole) for shape in shapes[6:]],
        out_shape=shapes,
        scratch_shapes=[pltpu.VMEM((rows, HEAD_SIZE), jnp.float32)] * 2,
        compiler_params=pltpu.CompilerParams(vmem_limit_bytes=vmem_bytes(near_keys + far_rows)),
        cost_estimate=PREPARE_COST,
        name="prepare",
    )(lengths, live, jnp.swapaxes(page_table, 1, 2), queries, keys, values, pool)


def stacked_queries(q_ref, part):
    return jnp.concatenate(
        [q_ref[0, :, pl.ds((part * GROUP + h) * HEAD_SIZE, HEAD_SIZE)] for h in range(GROUP)],
        axis=0,
    )


def rotate_rows(target, first, source, lanes, cos_ref, sin_ref, table_first):
    rows = source.shape[1]
    for tile in range(0, rows, ROW_TILE):
        table = pl.ds(table_first + tile, ROW_TILE)
        target[pl.ds(first + tile, ROW_TILE), :] = rotate(
            source[0, pl.ds(tile, ROW_TILE), lanes], cos_ref[table, :], sin_ref[table, :]
        )


def near_kernel(rows, steps, pages, kv_width, columns_count, *refs):
    table_ref, bias_ref, cos_ref, sin_ref, q_ref, k_ref, v_ref = refs[:7]
    shards, refs = refs[7 : 7 + columns_count], refs[7 + columns_count :]
    far_refs, refs = refs[: 2 * steps - 2], refs[2 * steps - 2 :]
    sum_ref, stat_ref, paged, sem = refs[:4]
    work = refs[4:]
    k_parts, v_parts, scores, weights, tops = (
        work[i : i + HEADS_PER_STEP] for i in range(0, len(work), HEADS_PER_STEP)
    )
    group = pl.program_id(0)
    pool_rows, page_tokens = shards[0].shape[:2]
    prefix_rows = pages * page_tokens
    base = steps * rows

    def page_copy(shard, place, page):
        return pltpu.make_async_copy(shard.at[place], paged.at[page], sem.at[page])

    @pl.when(group == 0)
    def _():
        column = lax.axis_index("batch")
        for page in range(pages):
            number = table_ref[page]
            apart = lax.div(number, jnp.int32(pool_rows)) ^ column
            place = lax.rem(number, jnp.int32(pool_rows))
            for which, shard in enumerate(shards):

                @pl.when(apart == which)
                def _(shard=shard, place=place, page=page):
                    page_copy(shard, place, page).start()

        rest = k_parts[0].shape[0] - base - prefix_rows
        for k_all, v_all in zip(k_parts, v_parts):
            v_all[:, pl.ds(HEAD_SIZE, HEAD_SIZE)] = jnp.ones(k_all.shape, jnp.bfloat16)
            if rest:
                blank = jnp.zeros((rest, HEAD_SIZE), jnp.bfloat16)
                k_all[pl.ds(base + prefix_rows, rest), :] = blank
                v_all[pl.ds(base + prefix_rows, rest), pl.ds(0, HEAD_SIZE)] = blank
        stat_ref[...] = jnp.zeros(stat_ref.shape, jnp.float32)

    for part in range(HEADS_PER_STEP):
        lanes = pl.ds(part * HEAD_SIZE, HEAD_SIZE)
        k_parts[part][pl.ds(0, rows), :] = k_ref[0, :, lanes]
        v_parts[part][pl.ds(0, rows), pl.ds(0, HEAD_SIZE)] = v_ref[0, :, lanes]
        for step in range(1, steps):
            far_key, far_value = far_refs[2 * step - 2 : 2 * step]
            rotate_rows(k_parts[part], step * rows, far_key, lanes, cos_ref, sin_ref, step * rows)
            v_parts[part][pl.ds(step * rows, rows), pl.ds(0, HEAD_SIZE)] = far_value[0, :, lanes]

    @pl.when(group == 0)
    def _():
        for page in range(pages):
            page_copy(shards[0], 0, page).wait()

    for part in range(HEADS_PER_STEP):
        start = (group * HEADS_PER_STEP + part) * HEAD_SIZE
        columns = pl.ds(pl.multiple_of(start, HEAD_SIZE), HEAD_SIZE)
        value_columns = pl.ds(pl.multiple_of(kv_width + start, HEAD_SIZE), HEAD_SIZE)
        span = pl.ds(base, prefix_rows)
        k_parts[part][span, :] = paged[:, :, columns].reshape(prefix_rows, HEAD_SIZE)
        v_parts[part][span, pl.ds(0, HEAD_SIZE)] = paged[:, :, value_columns].reshape(
            prefix_rows, HEAD_SIZE
        )

    for part in range(HEADS_PER_STEP):
        scores[part][...] = lax.dot_general(
            stacked_queries(q_ref, part), k_parts[part][...], (((1,), (1,)), ((), ())),
            preferred_element_type=jnp.float32,
        )
    lane = lax.broadcasted_iota(jnp.int32, (rows, LANES), 1)
    for part in range(HEADS_PER_STEP):
        for start in range(0, GROUP * rows, SOFTMAX_TILE):
            span = pl.ds(start, SOFTMAX_TILE)
            score = scores[part][span, :] + bias_ref[pl.ds(start % rows, SOFTMAX_TILE), :]
            highest = jnp.max(score, axis=1, keepdims=True)
            weight = jnp.exp2((score - highest) * EXP2_SCALE)
            weights[part][span, :] = weight.astype(jnp.bfloat16)
            tops[part][span, :] = jnp.broadcast_to(highest, (SOFTMAX_TILE, LANES))
        summed = jnp.dot(weights[part][...], v_parts[part][...], preferred_element_type=jnp.float32)
        for h in range(GROUP):
            own = part * GROUP + h
            head = group * (HEADS_PER_STEP * GROUP) + own
            span = slice(h * rows, (h + 1) * rows)
            sum_ref[:, pl.ds(own * HEAD_SIZE, HEAD_SIZE)] = summed[span, :HEAD_SIZE]
            stat_ref[...] = jnp.where(
                lane == head,
                tops[part][span, :],
                jnp.where(lane == QUERY_HEADS + head, summed[span, HEAD_SIZE:], stat_ref[...]),
            )


def near(table, shards, bias, cosine, signed_sine, query, key, value, far):
    rows, q_width = query.shape[1:]
    columns_count = len(shards)
    steps = 1 + len(far) // 2
    pages = table.shape[0]
    key_count = bias.shape[1]
    whole = lambda group: (0, 0)
    by_group = lambda group: (0, 0, group)
    narrow = pl.BlockSpec((1, rows, HEADS_PER_STEP * HEAD_SIZE), by_group)
    wide = HEADS_PER_STEP * GROUP * HEAD_SIZE
    return pl.pallas_call(
        lambda *refs: near_kernel(rows, steps, pages, key.shape[2], columns_count, *refs),
        grid=(KEY_VALUE_HEADS // HEADS_PER_STEP,),
        in_specs=[
            pl.BlockSpec(memory_space=pltpu.SMEM),
            pl.BlockSpec(bias.shape, whole),
            pl.BlockSpec(cosine.shape, whole),
            pl.BlockSpec(cosine.shape, whole),
            pl.BlockSpec((1, rows, wide), by_group),
            narrow,
            narrow,
        ]
        + [pl.BlockSpec(memory_space=pl.ANY)] * columns_count
        + [narrow] * len(far),
        out_specs=[
            pl.BlockSpec((rows, wide), lambda group: (0, group)),
            pl.BlockSpec((rows, LANES), whole),
        ],
        out_shape=[
            jax.ShapeDtypeStruct((rows, q_width), jnp.float32),
            jax.ShapeDtypeStruct((rows, LANES), jnp.float32),
        ],
        scratch_shapes=[
            pltpu.VMEM((pages,) + shards[0].shape[1:], jnp.bfloat16),
            pltpu.SemaphoreType.DMA((pages,)),
        ]
        + [pltpu.VMEM((key_count, HEAD_SIZE), jnp.bfloat16)] * HEADS_PER_STEP
        + [pltpu.VMEM((key_count, 2 * HEAD_SIZE), jnp.bfloat16)] * HEADS_PER_STEP
        + [pltpu.VMEM((GROUP * rows, key_count), jnp.float32)] * HEADS_PER_STEP
        + [pltpu.VMEM((GROUP * rows, key_count), jnp.bfloat16)] * HEADS_PER_STEP
        + [pltpu.VMEM((GROUP * rows, LANES), jnp.float32)] * HEADS_PER_STEP,
        compiler_params=pltpu.CompilerParams(vmem_limit_bytes=vmem_bytes(key_count)),
        cost_estimate=NEAR_COST,
        name="near",
    )(table, bias, cosine, signed_sine, query, key, value, *shards, *far)


def last_kernel(
    rows, cos_ref, sin_ref, bias_ref, stat_ref, sum_ref, q_ref, key_ref, swapped_value,
    passed_value, out_ref, *work,
):
    k_parts, v_parts, scores, weights, shrinks = (
        work[i : i + HEADS_PER_STEP] for i in range(0, len(work), HEADS_PER_STEP)
    )
    group = pl.program_id(0)
    even = lax.rem(lax.axis_index("blk"), 2) == 0

    @pl.when(group == 0)
    def _():
        for v_all in v_parts:
            v_all[:, pl.ds(HEAD_SIZE, HEAD_SIZE)] = jnp.ones((rows, HEAD_SIZE), jnp.bfloat16)

    for part in range(HEADS_PER_STEP):
        lanes = pl.ds(part * HEAD_SIZE, HEAD_SIZE)
        rotate_rows(k_parts[part], 0, key_ref, lanes, cos_ref, sin_ref, 0)
        v_parts[part][:, pl.ds(0, HEAD_SIZE)] = jnp.where(
            even, passed_value[0, :, lanes], swapped_value[0, :, lanes]
        )

    for part in range(HEADS_PER_STEP):
        scores[part][...] = lax.dot_general(
            stacked_queries(q_ref, part), k_parts[part][...], (((1,), (1,)), ((), ())),
            preferred_element_type=jnp.float32,
        )
    lane = lax.broadcasted_iota(jnp.int32, (SOFTMAX_TILE, LANES), 1)
    for part in range(HEADS_PER_STEP):
        for start in range(0, GROUP * rows, SOFTMAX_TILE):
            span = pl.ds(start, SOFTMAX_TILE)
            row_span = pl.ds(start % rows, SOFTMAX_TILE)
            head = group * (HEADS_PER_STEP * GROUP) + part * GROUP + start // rows
            score = scores[part][span, :] + bias_ref[row_span, :]
            stat = stat_ref[row_span, :]
            near_top = jnp.sum(jnp.where(lane == head, stat, 0.0), axis=1, keepdims=True)
            near_total = jnp.sum(
                jnp.where(lane == QUERY_HEADS + head, stat, 0.0), axis=1, keepdims=True
            )
            highest = jnp.maximum(jnp.max(score, axis=1, keepdims=True), near_top)
            weight = jnp.exp2((score - highest) * EXP2_SCALE)
            weights[part][span, :] = weight.astype(jnp.bfloat16)
            shrink = jnp.exp2((near_top - highest) * EXP2_SCALE)
            shrinks[part][span, pl.ds(0, LANES)] = jnp.broadcast_to(shrink, (SOFTMAX_TILE, LANES))
            shrinks[part][span, pl.ds(LANES, LANES)] = jnp.broadcast_to(
                shrink * near_total, (SOFTMAX_TILE, LANES)
            )
        summed = jnp.dot(weights[part][...], v_parts[part][...], preferred_element_type=jnp.float32)
        for h in range(GROUP):
            lanes = pl.ds((part * GROUP + h) * HEAD_SIZE, HEAD_SIZE)
            span = slice(h * rows, (h + 1) * rows)
            above = sum_ref[:, lanes] * shrinks[part][span, :LANES] + summed[span, :HEAD_SIZE]
            below = shrinks[part][span, LANES:] + summed[span, HEAD_SIZE:]
            out_ref[0, :, lanes] = (above / below).astype(jnp.bfloat16)


def last(cosine, signed_sine, bias, stat, sums, query, key, swapped_value, passed_value):
    rows = query.shape[1]
    whole = lambda group: (0, 0)
    by_group = lambda group: (0, 0, group)
    width = HEADS_PER_STEP * GROUP * HEAD_SIZE
    wide = pl.BlockSpec((1, rows, width), by_group)
    narrow = pl.BlockSpec((1, rows, HEADS_PER_STEP * HEAD_SIZE), by_group)
    table = pl.BlockSpec((rows, HEAD_SIZE), whole)
    return pl.pallas_call(
        lambda *refs: last_kernel(rows, *refs),
        grid=(KEY_VALUE_HEADS // HEADS_PER_STEP,),
        in_specs=[
            table,
            table,
            pl.BlockSpec(bias.shape, whole),
            pl.BlockSpec(stat.shape, whole),
            pl.BlockSpec((rows, width), lambda group: (0, group)),
            wide,
            narrow,
            narrow,
            narrow,
        ],
        out_specs=wide,
        out_shape=jax.ShapeDtypeStruct(query.shape, jnp.bfloat16),
        scratch_shapes=[pltpu.VMEM((rows, HEAD_SIZE), jnp.bfloat16)] * HEADS_PER_STEP
        + [pltpu.VMEM((rows, 2 * HEAD_SIZE), jnp.bfloat16)] * HEADS_PER_STEP
        + [pltpu.VMEM((GROUP * rows, rows), jnp.float32)] * HEADS_PER_STEP
        + [pltpu.VMEM((GROUP * rows, rows), jnp.bfloat16)] * HEADS_PER_STEP
        + [pltpu.VMEM((GROUP * rows, 2 * LANES), jnp.float32)] * HEADS_PER_STEP,
        compiler_params=pltpu.CompilerParams(vmem_limit_bytes=vmem_bytes(rows)),
        cost_estimate=LAST_COST,
        name="last",
    )(cosine, signed_sine, bias, stat, sums, query, key, swapped_value, passed_value)


def pool_shards(pool, after):
    count = lax.axis_size("batch")
    shards, bit = {0: pool}, count // 2
    while bit:
        if len(shards) > 1:
            shards, after = lax.optimization_barrier((shards, after))
        for apart, shard in list(shards.items()):
            shards[apart ^ bit] = lax.ppermute(
                shard, "batch", [(c, c ^ bit) for c in range(count)]
            )
        bit //= 2
    return [shards[apart] for apart in range(count)]


def per_device(queries, keys, values, seg_ids, lengths, live, page_table, pool):
    steps = live.shape[2]
    blocks = lax.axis_size("blk")
    far = [shifted(keys, 2), shifted(values, 2)]
    far_key = shifted(keys, 1)
    for step in range(3, steps + 1):
        far += [shifted(keys, step), shifted(values, step)]
    swapped_value = lax.ppermute(values, "blk", [(j, j ^ 1) for j in range(blocks)])
    (
        query, key, near_key, near_value, own_shard, table, cosine, signed_sine, near_bias, last_bias
    ) = prepare(queries, keys, values, pool, lengths, live, page_table)
    passed_value = lax.ppermute(
        swapped_value, "blk", [(j, j + 2) for j in range(0, blocks - 2, 2)]
    )
    shards = pool_shards(pool, cosine)
    sums, stat = near(
        table, [own_shard, *shards[1:]], near_bias, cosine, signed_sine,
        query, near_key, near_value, far,
    )
    result = last(
        cosine, signed_sine, last_bias, stat, sums, query, far_key, swapped_value, passed_value
    )
    return (result, key)


def solution(mesh):
    in_specs = (
        P("batch", "blk", None),
        P("batch", "blk", None),
        P("batch", "blk", None),
        P("batch", "blk"),
        P("batch", None),
        P("batch", "blk", None),
        P(),
        P("batch", None, None),
    )
    out_specs = (P("batch", "blk", None), P("batch", "blk", None))
    return jax.shard_map(
        per_device, mesh=mesh, in_specs=in_specs, out_specs=out_specs, check_vma=False
    )
```

```python
import math

import jax
import jax.numpy as jnp
import numpy as np
from jax import lax
from jax.experimental import pallas as pl
from jax.experimental.pallas import tpu as pltpu
from jax.sharding import PartitionSpec as P

QUERY_HEADS = 16
KEY_VALUE_HEADS = 8
HEAD_SIZE = 128
GROUP = QUERY_HEADS // KEY_VALUE_HEADS
HALF = HEAD_SIZE // 2
ROPE_BASE = 1000000.0
HIDDEN = -1e30
LANES = 128
ROW_TILE = 64
SOFTMAX_TILE = 16
HEADS_PER_STEP = 2
PREPARE_STEPS = 2


def cost(flops):
    return pl.CostEstimate(flops=flops, bytes_accessed=0, transcendentals=0)


PREPARE_COST = cost(0)
NEAR_COST = cost(0)
LAST_COST = cost(0)
EXP2_SCALE = math.log2(math.e) / math.sqrt(HEAD_SIZE)

FREQ_POWERS = [float(ROPE_BASE ** (-(2**k) / HALF)) for k in range(HALF.bit_length() - 1)]

PIO2_A = float(np.float32(1.5703125))
PIO2_B = float(np.float32(4.837512969970703125e-4))
PIO2_C = float(np.float32(math.pi / 2 - 1.5703125 - 4.837512969970703125e-4))


def shifted(value, steps):
    count = lax.axis_size("blk")
    return lax.ppermute(value, "blk", [(source, source + steps) for source in range(count - steps)])


def padded_keys(count):
    return -(-count // LANES) * LANES


def vmem_bytes(key_count):
    return 16 * 1024 * (1024 + key_count)


def sine_cosine(angle):
    turns = jnp.floor(angle * (2.0 / math.pi) + 0.5)
    rest = ((angle - turns * PIO2_A) - turns * PIO2_B) - turns * PIO2_C
    square = rest * rest
    sine = rest + rest * square * (
        -1.6666654611e-1 + square * (8.3321608736e-3 - square * 1.9515295891e-4)
    )
    cosine = 1.0 - 0.5 * square + square * square * (
        4.166664568298827e-2 + square * (-1.388731625493765e-3 + square * 2.443315711809948e-5)
    )
    quadrant = turns.astype(jnp.int32) & 3
    swapped = (quadrant & 1) == 1
    sine_out = jnp.where(swapped, cosine, sine)
    cosine_out = jnp.where(swapped, sine, cosine)
    sine_out = jnp.where(quadrant >= 2, -sine_out, sine_out)
    cosine_out = jnp.where((quadrant == 1) | (quadrant == 2), -cosine_out, cosine_out)
    return sine_out, cosine_out


def rotate(head, cosine, signed_sine):
    wide = head.astype(jnp.float32)
    return (wide * cosine + pltpu.roll(wide, HALF, 1) * signed_sine).astype(jnp.bfloat16)


def prepare_kernel(
    rows, steps, segs, prefix_len,
    lengths_ref, live_ref, table_ref, q_ref, k_ref, v_ref, pool_ref,
    q_out, k_out, k_copy, v_copy, pool_copy, page_out, cos_out, sin_out, near_bias, last_bias,
    cos_own, sin_own,
):
    @pl.when(pl.program_id(0) == 0)
    def _():
        block_start = lax.axis_index("blk") * rows
        starts = [jnp.int32(0)]
        for seg in range(1, segs):
            starts.append(starts[-1] + lengths_ref[0, seg - 1])
        lane = lax.broadcasted_iota(jnp.int32, (ROW_TILE, LANES), 1)
        row = lax.broadcasted_iota(jnp.int32, (ROW_TILE, LANES), 0)
        freq = jnp.ones((ROW_TILE, LANES), jnp.float32)
        for bit, power in enumerate(FREQ_POWERS):
            freq = jnp.where((lane >> bit) & 1 == 1, freq * power, freq)
        column = lax.axis_index("batch")
        for seg in range(segs):
            for page in range(table_ref.shape[1]):
                page_out[seg * table_ref.shape[1] + page] = table_ref[column, page, seg]
        for step in range(steps + 1):
            for tile in range(0, rows, ROW_TILE):
                index = block_start + (tile - step * rows) + row
                own_start = jnp.zeros(index.shape, jnp.int32)
                for seg in range(1, segs):
                    own_start = jnp.where(index >= starts[seg], starts[seg], own_start)
                place = (prefix_len + index - own_start).astype(jnp.float32)
                sine, cosine = sine_cosine(place * freq)
                sine = jnp.where(lane < HALF, -sine, sine)
                if step == 0:
                    cos_own[pl.ds(tile, ROW_TILE), :] = cosine
                    sin_own[pl.ds(tile, ROW_TILE), :] = sine
                else:
                    span = pl.ds((step - 1) * rows + tile, ROW_TILE)
                    cos_out[span, :] = cosine
                    sin_out[span, :] = sine
        for tile in range(0, rows, ROW_TILE):
            span = pl.ds(tile, ROW_TILE)
            query_index = block_start + tile + row
            own_start = jnp.zeros(query_index.shape, jnp.int32)
            first_page_token = jnp.zeros(query_index.shape, jnp.int32)
            for seg in range(1, segs):
                later = query_index >= starts[seg]
                own_start = jnp.where(later, starts[seg], own_start)
                first_page_token = jnp.where(later, seg * prefix_len, first_page_token)
            for step in range(steps + 1):
                limit = query_index
                if step > 0:
                    limit = jnp.where(live_ref[0, 0, step - 1] > 0, limit, -1)
                for column in range(0, rows, LANES):
                    key_index = block_start + (column - step * rows) + lane
                    seen = (key_index >= own_start) & (key_index <= limit)
                    bias = jnp.where(seen, 0.0, HIDDEN)
                    if step == 1:
                        last_bias[span, pl.ds(column, LANES)] = bias
                    else:
                        place = max(step - 1, 0) * rows + column
                        near_bias[span, pl.ds(place, LANES)] = bias
            base = steps * rows
            for column in range(0, near_bias.shape[1] - base, LANES):
                offset = column + lane - first_page_token
                seen = (offset >= 0) & (offset < prefix_len)
                near_bias[span, pl.ds(base + column, LANES)] = jnp.where(seen, 0.0, HIDDEN)

    for tile in range(0, rows, ROW_TILE):
        span = pl.ds(tile, ROW_TILE)
        cosine = cos_own[span, :]
        signed_sine = sin_own[span, :]
        for source, target in ((q_ref, q_out), (k_ref, k_out)):
            for start in range(0, source.shape[2], HEAD_SIZE):
                columns = pl.ds(start, HEAD_SIZE)
                turned = rotate(source[0, span, columns], cosine, signed_sine)
                target[0, span, columns] = turned
                if source is k_ref:
                    k_copy[0, span, columns] = turned
    v_copy[...] = v_ref[...]
    pool_copy[...] = pool_ref[...]


def prepare(queries, keys, values, pool, lengths, live, page_table):
    rows = queries.shape[1]
    steps = live.shape[2]
    segs = lengths.shape[1]
    prefix_len = page_table.shape[2] * pool.shape[1]
    pages = page_table.shape[1] * page_table.shape[2]
    far_rows = steps * rows
    near_keys = padded_keys(far_rows + segs * prefix_len)
    whole = lambda part: (0, 0)
    by_part = lambda part: (0, 0, part)
    wide = pl.BlockSpec((1, rows, queries.shape[2] // PREPARE_STEPS), by_part)
    narrow = pl.BlockSpec((1, rows, keys.shape[2] // PREPARE_STEPS), by_part)
    some_pages = pl.BlockSpec(
        (pool.shape[0] // PREPARE_STEPS, *pool.shape[1:]), lambda part: (part, 0, 0)
    )
    table = jax.ShapeDtypeStruct((far_rows, HEAD_SIZE), jnp.float32)
    shapes = [
        jax.ShapeDtypeStruct(queries.shape, jnp.bfloat16),
        jax.ShapeDtypeStruct(keys.shape, jnp.bfloat16),
        jax.ShapeDtypeStruct(keys.shape, jnp.bfloat16),
        jax.ShapeDtypeStruct(values.shape, jnp.bfloat16),
        jax.ShapeDtypeStruct(pool.shape, jnp.bfloat16),
        jax.ShapeDtypeStruct((pages,), jnp.int32),
        table,
        table,
        jax.ShapeDtypeStruct((rows, near_keys), jnp.float32),
        jax.ShapeDtypeStruct((rows, rows), jnp.float32),
    ]
    return pl.pallas_call(
        lambda *refs: prepare_kernel(rows, steps, segs, prefix_len, *refs),
        grid=(PREPARE_STEPS,),
        in_specs=[
            pl.BlockSpec(memory_space=pltpu.SMEM),
            pl.BlockSpec(memory_space=pltpu.SMEM),
            pl.BlockSpec(memory_space=pltpu.SMEM),
            wide,
            narrow,
            narrow,
            some_pages,
        ],
        out_specs=[wide, narrow, narrow, narrow, some_pages, pl.BlockSpec(memory_space=pltpu.SMEM)]
        + [pl.BlockSpec(shape.shape, whole) for shape in shapes[6:]],
        out_shape=shapes,
        scratch_shapes=[pltpu.VMEM((rows, HEAD_SIZE), jnp.float32)] * 2,
        compiler_params=pltpu.CompilerParams(vmem_limit_bytes=vmem_bytes(near_keys + far_rows)),
        cost_estimate=PREPARE_COST,
        name="prepare",
    )(lengths, live, jnp.swapaxes(page_table, 1, 2), queries, keys, values, pool)


def stacked_queries(q_ref, part):
    return jnp.concatenate(
        [q_ref[0, :, pl.ds((part * GROUP + h) * HEAD_SIZE, HEAD_SIZE)] for h in range(GROUP)],
        axis=0,
    )


def rotate_rows(target, first, source, lanes, cos_ref, sin_ref, table_first):
    rows = source.shape[1]
    for tile in range(0, rows, ROW_TILE):
        table = pl.ds(table_first + tile, ROW_TILE)
        target[pl.ds(first + tile, ROW_TILE), :] = rotate(
            source[0, pl.ds(tile, ROW_TILE), lanes], cos_ref[table, :], sin_ref[table, :]
        )


def near_kernel(rows, steps, pages, kv_width, columns_count, *refs):
    table_ref, bias_ref, cos_ref, sin_ref, q_ref, k_ref, v_ref = refs[:7]
    shards, refs = refs[7 : 7 + columns_count], refs[7 + columns_count :]
    far_refs, refs = refs[: 2 * steps - 2], refs[2 * steps - 2 :]
    sum_ref, stat_ref, paged, sem = refs[:4]
    work = refs[4:]
    k_parts, v_parts, scores, weights, tops = (
        work[i : i + HEADS_PER_STEP] for i in range(0, len(work), HEADS_PER_STEP)
    )
    group = pl.program_id(0)
    pool_rows, page_tokens = shards[0].shape[:2]
    prefix_rows = pages * page_tokens
    base = steps * rows

    def page_copy(shard, place, page):
        return pltpu.make_async_copy(shard.at[place], paged.at[page], sem.at[page])

    @pl.when(group == 0)
    def _():
        column = lax.axis_index("batch")
        for page in range(pages):
            number = table_ref[page]
            apart = lax.div(number, jnp.int32(pool_rows)) ^ column
            place = lax.rem(number, jnp.int32(pool_rows))
            for which, shard in enumerate(shards):

                @pl.when(apart == which)
                def _(shard=shard, place=place, page=page):
                    page_copy(shard, place, page).start()

        rest = k_parts[0].shape[0] - base - prefix_rows
        for k_all, v_all in zip(k_parts, v_parts):
            v_all[:, pl.ds(HEAD_SIZE, HEAD_SIZE)] = jnp.ones(k_all.shape, jnp.bfloat16)
            if rest:
                blank = jnp.zeros((rest, HEAD_SIZE), jnp.bfloat16)
                k_all[pl.ds(base + prefix_rows, rest), :] = blank
                v_all[pl.ds(base + prefix_rows, rest), pl.ds(0, HEAD_SIZE)] = blank
        stat_ref[...] = jnp.zeros(stat_ref.shape, jnp.float32)

    for part in range(HEADS_PER_STEP):
        lanes = pl.ds(part * HEAD_SIZE, HEAD_SIZE)
        k_parts[part][pl.ds(0, rows), :] = k_ref[0, :, lanes]
        v_parts[part][pl.ds(0, rows), pl.ds(0, HEAD_SIZE)] = v_ref[0, :, lanes]
        for step in range(1, steps):
            far_key, far_value = far_refs[2 * step - 2 : 2 * step]
            rotate_rows(k_parts[part], step * rows, far_key, lanes, cos_ref, sin_ref, step * rows)
            v_parts[part][pl.ds(step * rows, rows), pl.ds(0, HEAD_SIZE)] = far_value[0, :, lanes]

    @pl.when(group == 0)
    def _():
        for page in range(pages):
            page_copy(shards[0], 0, page).wait()

    for part in range(HEADS_PER_STEP):
        start = (group * HEADS_PER_STEP + part) * HEAD_SIZE
        columns = pl.ds(pl.multiple_of(start, HEAD_SIZE), HEAD_SIZE)
        value_columns = pl.ds(pl.multiple_of(kv_width + start, HEAD_SIZE), HEAD_SIZE)
        span = pl.ds(base, prefix_rows)
        k_parts[part][span, :] = paged[:, :, columns].reshape(prefix_rows, HEAD_SIZE)
        v_parts[part][span, pl.ds(0, HEAD_SIZE)] = paged[:, :, value_columns].reshape(
            prefix_rows, HEAD_SIZE
        )

    for part in range(HEADS_PER_STEP):
        scores[part][...] = lax.dot_general(
            stacked_queries(q_ref, part), k_parts[part][...], (((1,), (1,)), ((), ())),
            preferred_element_type=jnp.float32,
        )
    lane = lax.broadcasted_iota(jnp.int32, (rows, LANES), 1)
    for part in range(HEADS_PER_STEP):
        for start in range(0, GROUP * rows, SOFTMAX_TILE):
            span = pl.ds(start, SOFTMAX_TILE)
            score = scores[part][span, :] + bias_ref[pl.ds(start % rows, SOFTMAX_TILE), :]
            highest = jnp.max(score, axis=1, keepdims=True)
            weight = jnp.exp2((score - highest) * EXP2_SCALE)
            weights[part][span, :] = weight.astype(jnp.bfloat16)
            tops[part][span, :] = jnp.broadcast_to(highest, (SOFTMAX_TILE, LANES))
        summed = jnp.dot(weights[part][...], v_parts[part][...], preferred_element_type=jnp.float32)
        for h in range(GROUP):
            own = part * GROUP + h
            head = group * (HEADS_PER_STEP * GROUP) + own
            span = slice(h * rows, (h + 1) * rows)
            sum_ref[:, pl.ds(own * HEAD_SIZE, HEAD_SIZE)] = summed[span, :HEAD_SIZE]
            stat_ref[...] = jnp.where(
                lane == head,
                tops[part][span, :],
                jnp.where(lane == QUERY_HEADS + head, summed[span, HEAD_SIZE:], stat_ref[...]),
            )


def near(table, shards, bias, cosine, signed_sine, query, key, value, far):
    rows, q_width = query.shape[1:]
    columns_count = len(shards)
    steps = 1 + len(far) // 2
    pages = table.shape[0]
    key_count = bias.shape[1]
    whole = lambda group: (0, 0)
    by_group = lambda group: (0, 0, group)
    narrow = pl.BlockSpec((1, rows, HEADS_PER_STEP * HEAD_SIZE), by_group)
    wide = HEADS_PER_STEP * GROUP * HEAD_SIZE
    return pl.pallas_call(
        lambda *refs: near_kernel(rows, steps, pages, key.shape[2], columns_count, *refs),
        grid=(KEY_VALUE_HEADS // HEADS_PER_STEP,),
        in_specs=[
            pl.BlockSpec(memory_space=pltpu.SMEM),
            pl.BlockSpec(bias.shape, whole),
            pl.BlockSpec(cosine.shape, whole),
            pl.BlockSpec(cosine.shape, whole),
            pl.BlockSpec((1, rows, wide), by_group),
            narrow,
            narrow,
        ]
        + [pl.BlockSpec(memory_space=pl.ANY)] * columns_count
        + [narrow] * len(far),
        out_specs=[
            pl.BlockSpec((rows, wide), lambda group: (0, group)),
            pl.BlockSpec((rows, LANES), whole),
        ],
        out_shape=[
            jax.ShapeDtypeStruct((rows, q_width), jnp.float32),
            jax.ShapeDtypeStruct((rows, LANES), jnp.float32),
        ],
        scratch_shapes=[
            pltpu.VMEM((pages,) + shards[0].shape[1:], jnp.bfloat16),
            pltpu.SemaphoreType.DMA((pages,)),
        ]
        + [pltpu.VMEM((key_count, HEAD_SIZE), jnp.bfloat16)] * HEADS_PER_STEP
        + [pltpu.VMEM((key_count, 2 * HEAD_SIZE), jnp.bfloat16)] * HEADS_PER_STEP
        + [pltpu.VMEM((GROUP * rows, key_count), jnp.float32)] * HEADS_PER_STEP
        + [pltpu.VMEM((GROUP * rows, key_count), jnp.bfloat16)] * HEADS_PER_STEP
        + [pltpu.VMEM((GROUP * rows, LANES), jnp.float32)] * HEADS_PER_STEP,
        compiler_params=pltpu.CompilerParams(vmem_limit_bytes=vmem_bytes(key_count)),
        cost_estimate=NEAR_COST,
        name="near",
    )(table, bias, cosine, signed_sine, query, key, value, *shards, *far)


def last_kernel(
    rows, cos_ref, sin_ref, bias_ref, stat_ref, sum_ref, q_ref, key_ref, swapped_value,
    passed_value, direct_value, out_ref, *work,
):
    k_parts, v_parts, scores, weights, shrinks = (
        work[i : i + HEADS_PER_STEP] for i in range(0, len(work), HEADS_PER_STEP)
    )
    group = pl.program_id(0)
    even = lax.rem(lax.axis_index("blk"), 2) == 0

    @pl.when(group == 0)
    def _():
        for v_all in v_parts:
            v_all[:, pl.ds(HEAD_SIZE, HEAD_SIZE)] = jnp.ones((rows, HEAD_SIZE), jnp.bfloat16)

    for part in range(HEADS_PER_STEP):
        lanes = pl.ds(part * HEAD_SIZE, HEAD_SIZE)
        rotate_rows(k_parts[part], 0, key_ref, lanes, cos_ref, sin_ref, 0)
        half = rows // 2
        v_parts[part][pl.ds(0, half), pl.ds(0, HEAD_SIZE)] = jnp.where(
            even, passed_value[0, :, lanes], swapped_value[0, :, lanes]
        )
        v_parts[part][pl.ds(half, half), pl.ds(0, HEAD_SIZE)] = direct_value[0, :, lanes]

    for part in range(HEADS_PER_STEP):
        scores[part][...] = lax.dot_general(
            stacked_queries(q_ref, part), k_parts[part][...], (((1,), (1,)), ((), ())),
            preferred_element_type=jnp.float32,
        )
    lane = lax.broadcasted_iota(jnp.int32, (SOFTMAX_TILE, LANES), 1)
    for part in range(HEADS_PER_STEP):
        for start in range(0, GROUP * rows, SOFTMAX_TILE):
            span = pl.ds(start, SOFTMAX_TILE)
            row_span = pl.ds(start % rows, SOFTMAX_TILE)
            head = group * (HEADS_PER_STEP * GROUP) + part * GROUP + start // rows
            score = scores[part][span, :] + bias_ref[row_span, :]
            stat = stat_ref[row_span, :]
            near_top = jnp.sum(jnp.where(lane == head, stat, 0.0), axis=1, keepdims=True)
            near_total = jnp.sum(
                jnp.where(lane == QUERY_HEADS + head, stat, 0.0), axis=1, keepdims=True
            )
            highest = jnp.maximum(jnp.max(score, axis=1, keepdims=True), near_top)
            weight = jnp.exp2((score - highest) * EXP2_SCALE)
            weights[part][span, :] = weight.astype(jnp.bfloat16)
            shrink = jnp.exp2((near_top - highest) * EXP2_SCALE)
            shrinks[part][span, pl.ds(0, LANES)] = jnp.broadcast_to(shrink, (SOFTMAX_TILE, LANES))
            shrinks[part][span, pl.ds(LANES, LANES)] = jnp.broadcast_to(
                shrink * near_total, (SOFTMAX_TILE, LANES)
            )
        summed = jnp.dot(weights[part][...], v_parts[part][...], preferred_element_type=jnp.float32)
        for h in range(GROUP):
            lanes = pl.ds((part * GROUP + h) * HEAD_SIZE, HEAD_SIZE)
            span = slice(h * rows, (h + 1) * rows)
            above = sum_ref[:, lanes] * shrinks[part][span, :LANES] + summed[span, :HEAD_SIZE]
            below = shrinks[part][span, LANES:] + summed[span, HEAD_SIZE:]
            out_ref[0, :, lanes] = (above / below).astype(jnp.bfloat16)


def last(
    cosine, signed_sine, bias, stat, sums, query, key, swapped_value, passed_value, direct_value
):
    rows = query.shape[1]
    whole = lambda group: (0, 0)
    by_group = lambda group: (0, 0, group)
    width = HEADS_PER_STEP * GROUP * HEAD_SIZE
    wide = pl.BlockSpec((1, rows, width), by_group)
    narrow = pl.BlockSpec((1, rows, HEADS_PER_STEP * HEAD_SIZE), by_group)
    half = pl.BlockSpec((1, rows // 2, HEADS_PER_STEP * HEAD_SIZE), by_group)
    table = pl.BlockSpec((rows, HEAD_SIZE), whole)
    return pl.pallas_call(
        lambda *refs: last_kernel(rows, *refs),
        grid=(KEY_VALUE_HEADS // HEADS_PER_STEP,),
        in_specs=[
            table,
            table,
            pl.BlockSpec(bias.shape, whole),
            pl.BlockSpec(stat.shape, whole),
            pl.BlockSpec((rows, width), lambda group: (0, group)),
            wide,
            narrow,
            half,
            half,
            half,
        ],
        out_specs=wide,
        out_shape=jax.ShapeDtypeStruct(query.shape, jnp.bfloat16),
        scratch_shapes=[pltpu.VMEM((rows, HEAD_SIZE), jnp.bfloat16)] * HEADS_PER_STEP
        + [pltpu.VMEM((rows, 2 * HEAD_SIZE), jnp.bfloat16)] * HEADS_PER_STEP
        + [pltpu.VMEM((GROUP * rows, rows), jnp.float32)] * HEADS_PER_STEP
        + [pltpu.VMEM((GROUP * rows, rows), jnp.bfloat16)] * HEADS_PER_STEP
        + [pltpu.VMEM((GROUP * rows, 2 * LANES), jnp.float32)] * HEADS_PER_STEP,
        compiler_params=pltpu.CompilerParams(vmem_limit_bytes=vmem_bytes(rows)),
        cost_estimate=LAST_COST,
        name="last",
    )(
        cosine, signed_sine, bias, stat, sums, query, key, swapped_value, passed_value, direct_value
    )


def pool_shards(pool, after):
    count = lax.axis_size("batch")
    shards, bit = {0: pool}, count // 2
    while bit:
        if len(shards) > 1:
            shards, after = lax.optimization_barrier((shards, after))
        for apart, shard in list(shards.items()):
            shards[apart ^ bit] = lax.ppermute(
                shard, "batch", [(c, c ^ bit) for c in range(count)]
            )
        bit //= 2
    return [shards[apart] for apart in range(count)]


def per_device(queries, keys, values, seg_ids, lengths, live, page_table, pool):
    steps = live.shape[2]
    blocks = lax.axis_size("blk")
    far = [shifted(keys, 2), shifted(values, 2)]
    for step in range(3, steps + 1):
        far += [shifted(keys, step), shifted(values, step)]
    half = values.shape[1] // 2
    swap = [(j, j ^ 1) for j in range(blocks)]
    even = lax.rem(lax.axis_index("blk"), 2) == 0
    swapped_value = lax.ppermute(values[:, :half], "blk", swap)
    direct_value = shifted(values[:, half:], 1)
    (
        query, key, near_key, near_value, own_shard, table, cosine, signed_sine, near_bias, last_bias
    ) = prepare(queries, keys, values, pool, lengths, live, page_table)
    far_key = lax.ppermute(jnp.where(even, keys, far[0]), "blk", swap)
    shards = pool_shards(pool, cosine)
    shards[1:], swapped_value = lax.optimization_barrier((shards[1:], swapped_value))
    passed_value = lax.ppermute(
        swapped_value, "blk", [(j, j + 2) for j in range(0, blocks - 2, 2)]
    )
    sums, stat = near(
        table, [own_shard, *shards[1:]], near_bias, cosine, signed_sine,
        query, near_key, near_value, far,
    )
    result = last(
        cosine, signed_sine, last_bias, stat, sums, query, far_key, swapped_value, passed_value,
        direct_value,
    )
    return (result, key)


def solution(mesh):
    in_specs = (
        P("batch", "blk", None),
        P("batch", "blk", None),
        P("batch", "blk", None),
        P("batch", "blk"),
        P("batch", None),
        P("batch", "blk", None),
        P(),
        P("batch", None, None),
    )
    out_specs = (P("batch", "blk", None), P("batch", "blk", None))
    return jax.shard_map(
        per_device, mesh=mesh, in_specs=in_specs, out_specs=out_specs, check_vma=False
    )
```

```python
import math

import jax
import jax.numpy as jnp
import numpy as np
from jax import lax
from jax.experimental import pallas as pl
from jax.experimental.pallas import tpu as pltpu
from jax.sharding import PartitionSpec as P

QUERY_HEADS = 16
KEY_VALUE_HEADS = 8
HEAD_SIZE = 128
GROUP = QUERY_HEADS // KEY_VALUE_HEADS
HALF = HEAD_SIZE // 2
ROPE_BASE = 1000000.0
HIDDEN = -1e30
LANES = 128
ROW_TILE = 64
SOFTMAX_TILE = 16
HEADS_PER_STEP = 2
PREPARE_STEPS = 2


def cost(flops):
    return pl.CostEstimate(flops=flops, bytes_accessed=0, transcendentals=0)


PREPARE_COST = cost(0)
NEAR_COST = cost(0)
LAST_COST = cost(0)
EXP2_SCALE = math.log2(math.e) / math.sqrt(HEAD_SIZE)

FREQ_POWERS = [float(ROPE_BASE ** (-(2**k) / HALF)) for k in range(HALF.bit_length() - 1)]

PIO2_A = float(np.float32(1.5703125))
PIO2_B = float(np.float32(4.837512969970703125e-4))
PIO2_C = float(np.float32(math.pi / 2 - 1.5703125 - 4.837512969970703125e-4))


def shifted(value, steps):
    count = lax.axis_size("blk")
    return lax.ppermute(value, "blk", [(source, source + steps) for source in range(count - steps)])


def padded_keys(count):
    return -(-count // LANES) * LANES


def vmem_bytes(key_count):
    return 16 * 1024 * (1024 + key_count)


def sine_cosine(angle):
    turns = jnp.floor(angle * (2.0 / math.pi) + 0.5)
    rest = ((angle - turns * PIO2_A) - turns * PIO2_B) - turns * PIO2_C
    square = rest * rest
    sine = rest + rest * square * (
        -1.6666654611e-1 + square * (8.3321608736e-3 - square * 1.9515295891e-4)
    )
    cosine = 1.0 - 0.5 * square + square * square * (
        4.166664568298827e-2 + square * (-1.388731625493765e-3 + square * 2.443315711809948e-5)
    )
    quadrant = turns.astype(jnp.int32) & 3
    swapped = (quadrant & 1) == 1
    sine_out = jnp.where(swapped, cosine, sine)
    cosine_out = jnp.where(swapped, sine, cosine)
    sine_out = jnp.where(quadrant >= 2, -sine_out, sine_out)
    cosine_out = jnp.where((quadrant == 1) | (quadrant == 2), -cosine_out, cosine_out)
    return sine_out, cosine_out


def rotate(head, cosine, signed_sine):
    wide = head.astype(jnp.float32)
    return (wide * cosine + pltpu.roll(wide, HALF, 1) * signed_sine).astype(jnp.bfloat16)


def prepare_kernel(
    rows, steps, segs, prefix_len,
    table_shape, integers_ref, q_ref, k_ref, v_ref, pool_ref,
    q_out, k_out, k_copy, v_copy, pool_copy, page_out, cos_out, sin_out, near_bias, last_bias,
    cos_own, sin_own,
):
    @pl.when(pl.program_id(0) == 0)
    def _():
        block_start = lax.axis_index("blk") * rows
        starts = [jnp.int32(0)]
        for seg in range(1, segs):
            starts.append(starts[-1] + integers_ref[seg - 1])
        lane = lax.broadcasted_iota(jnp.int32, (ROW_TILE, LANES), 1)
        row = lax.broadcasted_iota(jnp.int32, (ROW_TILE, LANES), 0)
        freq = jnp.ones((ROW_TILE, LANES), jnp.float32)
        for bit, power in enumerate(FREQ_POWERS):
            freq = jnp.where((lane >> bit) & 1 == 1, freq * power, freq)
        column = lax.axis_index("batch")
        seg_pages = table_shape[2]
        first = segs + steps + column * segs * seg_pages
        for page in range(segs * seg_pages):
            seg, place = divmod(page, seg_pages)
            page_out[page] = integers_ref[first + place * segs + seg]
        for step in range(steps + 1):
            for tile in range(0, rows, ROW_TILE):
                index = block_start + (tile - step * rows) + row
                own_start = jnp.zeros(index.shape, jnp.int32)
                for seg in range(1, segs):
                    own_start = jnp.where(index >= starts[seg], starts[seg], own_start)
                place = (prefix_len + index - own_start).astype(jnp.float32)
                sine, cosine = sine_cosine(place * freq)
                sine = jnp.where(lane < HALF, -sine, sine)
                if step == 0:
                    cos_own[pl.ds(tile, ROW_TILE), :] = cosine
                    sin_own[pl.ds(tile, ROW_TILE), :] = sine
                else:
                    span = pl.ds((step - 1) * rows + tile, ROW_TILE)
                    cos_out[span, :] = cosine
                    sin_out[span, :] = sine
        for tile in range(0, rows, ROW_TILE):
            span = pl.ds(tile, ROW_TILE)
            query_index = block_start + tile + row
            own_start = jnp.zeros(query_index.shape, jnp.int32)
            first_page_token = jnp.zeros(query_index.shape, jnp.int32)
            for seg in range(1, segs):
                later = query_index >= starts[seg]
                own_start = jnp.where(later, starts[seg], own_start)
                first_page_token = jnp.where(later, seg * prefix_len, first_page_token)
            for step in range(steps + 1):
                limit = query_index
                if step > 0:
                    limit = jnp.where(integers_ref[segs + step - 1] > 0, limit, -1)
                for column in range(0, rows, LANES):
                    key_index = block_start + (column - step * rows) + lane
                    seen = (key_index >= own_start) & (key_index <= limit)
                    bias = jnp.where(seen, 0.0, HIDDEN)
                    if step == 1:
                        last_bias[span, pl.ds(column, LANES)] = bias
                    else:
                        place = max(step - 1, 0) * rows + column
                        near_bias[span, pl.ds(place, LANES)] = bias
            base = steps * rows
            for column in range(0, near_bias.shape[1] - base, LANES):
                offset = column + lane - first_page_token
                seen = (offset >= 0) & (offset < prefix_len)
                near_bias[span, pl.ds(base + column, LANES)] = jnp.where(seen, 0.0, HIDDEN)

    for tile in range(0, rows, ROW_TILE):
        span = pl.ds(tile, ROW_TILE)
        cosine = cos_own[span, :]
        signed_sine = sin_own[span, :]
        for source, target in ((q_ref, q_out), (k_ref, k_out)):
            for start in range(0, source.shape[2], HEAD_SIZE):
                columns = pl.ds(start, HEAD_SIZE)
                turned = rotate(source[0, span, columns], cosine, signed_sine)
                target[0, span, columns] = turned
                if source is k_ref:
                    k_copy[0, span, columns] = turned
    v_copy[...] = v_ref[...]
    pool_copy[...] = pool_ref[...]


def prepare(queries, keys, values, pool, integers, segs, steps, table_shape):
    rows = queries.shape[1]
    prefix_len = table_shape[2] * pool.shape[1]
    pages = table_shape[1] * table_shape[2]
    far_rows = steps * rows
    near_keys = padded_keys(far_rows + segs * prefix_len)
    whole = lambda part: (0, 0)
    by_part = lambda part: (0, 0, part)
    wide = pl.BlockSpec((1, rows, queries.shape[2] // PREPARE_STEPS), by_part)
    narrow = pl.BlockSpec((1, rows, keys.shape[2] // PREPARE_STEPS), by_part)
    some_pages = pl.BlockSpec(
        (pool.shape[0] // PREPARE_STEPS, *pool.shape[1:]), lambda part: (part, 0, 0)
    )
    table = jax.ShapeDtypeStruct((far_rows, HEAD_SIZE), jnp.float32)
    shapes = [
        jax.ShapeDtypeStruct(queries.shape, jnp.bfloat16),
        jax.ShapeDtypeStruct(keys.shape, jnp.bfloat16),
        jax.ShapeDtypeStruct(keys.shape, jnp.bfloat16),
        jax.ShapeDtypeStruct(values.shape, jnp.bfloat16),
        jax.ShapeDtypeStruct(pool.shape, jnp.bfloat16),
        jax.ShapeDtypeStruct((pages,), jnp.int32),
        table,
        table,
        jax.ShapeDtypeStruct((rows, near_keys), jnp.float32),
        jax.ShapeDtypeStruct((rows, rows), jnp.float32),
    ]
    return pl.pallas_call(
        lambda *refs: prepare_kernel(rows, steps, segs, prefix_len, table_shape, *refs),
        grid=(PREPARE_STEPS,),
        in_specs=[
            pl.BlockSpec(memory_space=pltpu.SMEM),
            wide,
            narrow,
            narrow,
            some_pages,
        ],
        out_specs=[wide, narrow, narrow, narrow, some_pages, pl.BlockSpec(memory_space=pltpu.SMEM)]
        + [pl.BlockSpec(shape.shape, whole) for shape in shapes[6:]],
        out_shape=shapes,
        scratch_shapes=[pltpu.VMEM((rows, HEAD_SIZE), jnp.float32)] * 2,
        compiler_params=pltpu.CompilerParams(vmem_limit_bytes=vmem_bytes(near_keys + far_rows)),
        cost_estimate=PREPARE_COST,
        name="prepare",
    )(integers, queries, keys, values, pool)


def split_work(work):
    counts = [HEADS_PER_STEP] * 2 + [HEADS_PER_STEP * GROUP] * 3
    return [work[sum(counts[:i]) : sum(counts[: i + 1])] for i in range(len(counts))]


def rotate_rows(target, first, source, lanes, cos_ref, sin_ref, table_first):
    rows = source.shape[1]
    for tile in range(0, rows, ROW_TILE):
        table = pl.ds(table_first + tile, ROW_TILE)
        target[pl.ds(first + tile, ROW_TILE), :] = rotate(
            source[0, pl.ds(tile, ROW_TILE), lanes], cos_ref[table, :], sin_ref[table, :]
        )


def near_kernel(rows, steps, pages, kv_width, columns_count, *refs):
    table_ref, bias_ref, cos_ref, sin_ref, q_ref, k_ref, v_ref = refs[:7]
    shards, refs = refs[7 : 7 + columns_count], refs[7 + columns_count :]
    far_refs, refs = refs[: 2 * steps - 2], refs[2 * steps - 2 :]
    sum_ref, stat_ref, paged, sem = refs[:4]
    work = refs[4:]
    k_parts, v_parts, scores, weights, tops = split_work(work)
    group = pl.program_id(0)
    pool_rows, page_tokens = shards[0].shape[:2]
    prefix_rows = pages * page_tokens
    base = steps * rows

    def page_copy(shard, place, page):
        return pltpu.make_async_copy(shard.at[place], paged.at[page], sem.at[page])

    @pl.when(group == 0)
    def _():
        column = lax.axis_index("batch")
        for page in range(pages):
            number = table_ref[page]
            apart = lax.div(number, jnp.int32(pool_rows)) ^ column
            place = lax.rem(number, jnp.int32(pool_rows))
            for which, shard in enumerate(shards):

                @pl.when(apart == which)
                def _(shard=shard, place=place, page=page):
                    page_copy(shard, place, page).start()

        rest = k_parts[0].shape[0] - base - prefix_rows
        for k_all, v_all in zip(k_parts, v_parts):
            v_all[:, pl.ds(HEAD_SIZE, HEAD_SIZE)] = jnp.ones(k_all.shape, jnp.bfloat16)
            if rest:
                blank = jnp.zeros((rest, HEAD_SIZE), jnp.bfloat16)
                k_all[pl.ds(base + prefix_rows, rest), :] = blank
                v_all[pl.ds(base + prefix_rows, rest), pl.ds(0, HEAD_SIZE)] = blank
        stat_ref[...] = jnp.zeros(stat_ref.shape, jnp.float32)

    for part in range(HEADS_PER_STEP):
        lanes = pl.ds(part * HEAD_SIZE, HEAD_SIZE)
        k_parts[part][pl.ds(0, rows), :] = k_ref[0, :, lanes]
        v_parts[part][pl.ds(0, rows), pl.ds(0, HEAD_SIZE)] = v_ref[0, :, lanes]
        for step in range(1, steps):
            far_key, far_value = far_refs[2 * step - 2 : 2 * step]
            rotate_rows(k_parts[part], step * rows, far_key, lanes, cos_ref, sin_ref, step * rows)
            v_parts[part][pl.ds(step * rows, rows), pl.ds(0, HEAD_SIZE)] = far_value[0, :, lanes]

    @pl.when(group == 0)
    def _():
        for page in range(pages):
            page_copy(shards[0], 0, page).wait()

    for part in range(HEADS_PER_STEP):
        start = (group * HEADS_PER_STEP + part) * HEAD_SIZE
        columns = pl.ds(pl.multiple_of(start, HEAD_SIZE), HEAD_SIZE)
        value_columns = pl.ds(pl.multiple_of(kv_width + start, HEAD_SIZE), HEAD_SIZE)
        span = pl.ds(base, prefix_rows)
        k_parts[part][span, :] = paged[:, :, columns].reshape(prefix_rows, HEAD_SIZE)
        v_parts[part][span, pl.ds(0, HEAD_SIZE)] = paged[:, :, value_columns].reshape(
            prefix_rows, HEAD_SIZE
        )

    units = HEADS_PER_STEP * GROUP

    def score_unit(unit):
        query = q_ref[0, :, pl.ds(unit * HEAD_SIZE, HEAD_SIZE)]
        scores[unit][...] = lax.dot_general(
            query, k_parts[unit // GROUP][...], (((1,), (1,)), ((), ())),
            preferred_element_type=jnp.float32,
        )

    score_unit(0)
    lane = lax.broadcasted_iota(jnp.int32, (rows, LANES), 1)
    stat = stat_ref[...]
    for unit in range(units):
        if unit + 1 < units:
            score_unit(unit + 1)
        for start in range(0, rows, SOFTMAX_TILE):
            span = pl.ds(start, SOFTMAX_TILE)
            score = scores[unit][span, :] + bias_ref[span, :]
            highest = jnp.max(score, axis=1, keepdims=True)
            weight = jnp.exp2((score - highest) * EXP2_SCALE)
            weights[unit][span, :] = weight.astype(jnp.bfloat16)
            tops[unit][span, :] = jnp.broadcast_to(highest, (SOFTMAX_TILE, LANES))
        summed = jnp.dot(
            weights[unit][...], v_parts[unit // GROUP][...], preferred_element_type=jnp.float32
        )
        head = group * units + unit
        sum_ref[:, pl.ds(unit * HEAD_SIZE, HEAD_SIZE)] = summed[:, :HEAD_SIZE]
        stat = jnp.where(lane == QUERY_HEADS + head, summed[:, HEAD_SIZE:], stat)
        stat = jnp.where(lane == head, tops[unit][...], stat)
    stat_ref[...] = stat


def near(table, shards, bias, cosine, signed_sine, query, key, value, far):
    rows, q_width = query.shape[1:]
    columns_count = len(shards)
    steps = 1 + len(far) // 2
    pages = table.shape[0]
    key_count = bias.shape[1]
    whole = lambda group: (0, 0)
    by_group = lambda group: (0, 0, group)
    narrow = pl.BlockSpec((1, rows, HEADS_PER_STEP * HEAD_SIZE), by_group)
    wide = HEADS_PER_STEP * GROUP * HEAD_SIZE
    return pl.pallas_call(
        lambda *refs: near_kernel(rows, steps, pages, key.shape[2], columns_count, *refs),
        grid=(KEY_VALUE_HEADS // HEADS_PER_STEP,),
        in_specs=[
            pl.BlockSpec(memory_space=pltpu.SMEM),
            pl.BlockSpec(bias.shape, whole),
            pl.BlockSpec(cosine.shape, whole),
            pl.BlockSpec(cosine.shape, whole),
            pl.BlockSpec((1, rows, wide), by_group),
            narrow,
            narrow,
        ]
        + [pl.BlockSpec(memory_space=pl.ANY)] * columns_count
        + [narrow] * len(far),
        out_specs=[
            pl.BlockSpec((rows, wide), lambda group: (0, group)),
            pl.BlockSpec((rows, LANES), whole),
        ],
        out_shape=[
            jax.ShapeDtypeStruct((rows, q_width), jnp.float32),
            jax.ShapeDtypeStruct((rows, LANES), jnp.float32),
        ],
        scratch_shapes=[
            pltpu.VMEM((pages,) + shards[0].shape[1:], jnp.bfloat16),
            pltpu.SemaphoreType.DMA((pages,)),
        ]
        + [pltpu.VMEM((key_count, HEAD_SIZE), jnp.bfloat16)] * HEADS_PER_STEP
        + [pltpu.VMEM((key_count, 2 * HEAD_SIZE), jnp.bfloat16)] * HEADS_PER_STEP
        + [pltpu.VMEM((rows, key_count), jnp.float32)] * HEADS_PER_STEP * GROUP
        + [pltpu.VMEM((rows, key_count), jnp.bfloat16)] * HEADS_PER_STEP * GROUP
        + [pltpu.VMEM((rows, LANES), jnp.float32)] * HEADS_PER_STEP * GROUP,
        compiler_params=pltpu.CompilerParams(vmem_limit_bytes=vmem_bytes(key_count)),
        cost_estimate=NEAR_COST,
        name="near",
    )(table, bias, cosine, signed_sine, query, key, value, *shards, *far)


def last_kernel(
    rows, cos_ref, sin_ref, bias_ref, stat_ref, sum_ref, q_ref, key_ref, swapped_value,
    passed_value, out_ref, *work,
):
    k_parts, v_parts, scores, weights, shrinks = split_work(work)
    group = pl.program_id(0)
    even = lax.rem(lax.axis_index("blk"), 2) == 0

    @pl.when(group == 0)
    def _():
        for v_all in v_parts:
            v_all[:, pl.ds(HEAD_SIZE, HEAD_SIZE)] = jnp.ones((rows, HEAD_SIZE), jnp.bfloat16)

    for part in range(HEADS_PER_STEP):
        lanes = pl.ds(part * HEAD_SIZE, HEAD_SIZE)
        rotate_rows(k_parts[part], 0, key_ref, lanes, cos_ref, sin_ref, 0)
        v_parts[part][:, pl.ds(0, HEAD_SIZE)] = jnp.where(
            even, passed_value[0, :, lanes], swapped_value[0, :, lanes]
        )

    units = HEADS_PER_STEP * GROUP

    def score_unit(unit):
        query = q_ref[0, :, pl.ds(unit * HEAD_SIZE, HEAD_SIZE)]
        scores[unit][...] = lax.dot_general(
            query, k_parts[unit // GROUP][...], (((1,), (1,)), ((), ())),
            preferred_element_type=jnp.float32,
        )

    score_unit(0)
    lane = lax.broadcasted_iota(jnp.int32, (SOFTMAX_TILE, LANES), 1)
    for unit in range(units):
        if unit + 1 < units:
            score_unit(unit + 1)
        head = group * units + unit
        lanes = pl.ds(unit * HEAD_SIZE, HEAD_SIZE)
        for start in range(0, rows, SOFTMAX_TILE):
            span = pl.ds(start, SOFTMAX_TILE)
            score = scores[unit][span, :] + bias_ref[span, :]
            stat = stat_ref[span, :]
            near_top = jnp.sum(jnp.where(lane == head, stat, 0.0), axis=1, keepdims=True)
            near_total = jnp.sum(
                jnp.where(lane == QUERY_HEADS + head, stat, 0.0), axis=1, keepdims=True
            )
            highest = jnp.maximum(jnp.max(score, axis=1, keepdims=True), near_top)
            weight = jnp.exp2((score - highest) * EXP2_SCALE)
            weights[unit][span, :] = weight.astype(jnp.bfloat16)
            shrink = jnp.exp2((near_top - highest) * EXP2_SCALE)
            shrinks[unit][span, pl.ds(0, LANES)] = jnp.broadcast_to(shrink, (SOFTMAX_TILE, LANES))
            shrinks[unit][span, pl.ds(LANES, LANES)] = jnp.broadcast_to(
                shrink * near_total, (SOFTMAX_TILE, LANES)
            )
        summed = jnp.dot(
            weights[unit][...], v_parts[unit // GROUP][...], preferred_element_type=jnp.float32
        )
        above = sum_ref[:, lanes] * shrinks[unit][:, :LANES] + summed[:, :HEAD_SIZE]
        below = shrinks[unit][:, LANES:] + summed[:, HEAD_SIZE:]
        out_ref[0, :, lanes] = (above / below).astype(jnp.bfloat16)


def last(cosine, signed_sine, bias, stat, sums, query, key, swapped_value, passed_value):
    rows = query.shape[1]
    whole = lambda group: (0, 0)
    by_group = lambda group: (0, 0, group)
    width = HEADS_PER_STEP * GROUP * HEAD_SIZE
    wide = pl.BlockSpec((1, rows, width), by_group)
    narrow = pl.BlockSpec((1, rows, HEADS_PER_STEP * HEAD_SIZE), by_group)
    table = pl.BlockSpec((rows, HEAD_SIZE), whole)
    return pl.pallas_call(
        lambda *refs: last_kernel(rows, *refs),
        grid=(KEY_VALUE_HEADS // HEADS_PER_STEP,),
        in_specs=[
            table,
            table,
            pl.BlockSpec(bias.shape, whole),
            pl.BlockSpec(stat.shape, whole),
            pl.BlockSpec((rows, width), lambda group: (0, group)),
            wide,
            narrow,
            narrow,
            narrow,
        ],
        out_specs=wide,
        out_shape=jax.ShapeDtypeStruct(query.shape, jnp.bfloat16),
        scratch_shapes=[pltpu.VMEM((rows, HEAD_SIZE), jnp.bfloat16)] * HEADS_PER_STEP
        + [pltpu.VMEM((rows, 2 * HEAD_SIZE), jnp.bfloat16)] * HEADS_PER_STEP
        + [pltpu.VMEM((rows, rows), jnp.float32)] * HEADS_PER_STEP * GROUP
        + [pltpu.VMEM((rows, rows), jnp.bfloat16)] * HEADS_PER_STEP * GROUP
        + [pltpu.VMEM((rows, 2 * LANES), jnp.float32)] * HEADS_PER_STEP * GROUP,
        compiler_params=pltpu.CompilerParams(vmem_limit_bytes=vmem_bytes(rows)),
        cost_estimate=LAST_COST,
        name="last",
    )(cosine, signed_sine, bias, stat, sums, query, key, swapped_value, passed_value)


def pool_shards(pool, after):
    count = lax.axis_size("batch")
    shards, bit = {0: pool}, count // 2
    while bit:
        if len(shards) > 1:
            shards, after = lax.optimization_barrier((shards, after))
        for apart, shard in list(shards.items()):
            shards[apart ^ bit] = lax.ppermute(
                shard, "batch", [(c, c ^ bit) for c in range(count)]
            )
        bit //= 2
    return [shards[apart] for apart in range(count)]


def per_device(queries, keys, values, seg_ids, lengths, live, page_table, pool):
    steps = live.shape[2]
    blocks = lax.axis_size("blk")
    far = [shifted(keys, 2), shifted(values, 2)]
    for step in range(3, steps + 1):
        far += [shifted(keys, step), shifted(values, step)]
    swap = [(j, j ^ 1) for j in range(blocks)]
    even = lax.rem(lax.axis_index("blk"), 2) == 0
    swapped_value = lax.ppermute(values, "blk", swap)
    integers = jnp.concatenate([lengths.ravel(), live.ravel(), jnp.swapaxes(page_table, 1, 2).ravel()])
    (
        query, key, near_key, near_value, own_shard, table, cosine, signed_sine, near_bias, last_bias
    ) = prepare(queries, keys, values, pool, integers, lengths.shape[1], steps, page_table.shape)
    far_key = lax.ppermute(jnp.where(even, keys, far[0]), "blk", swap)
    passed_value = lax.ppermute(
        swapped_value, "blk", [(j, j + 2) for j in range(0, blocks - 2, 2)]
    )
    shards = pool_shards(pool, (cosine, far[0]))
    sums, stat = near(
        table, [own_shard, *shards[1:]], near_bias, cosine, signed_sine,
        query, near_key, near_value, far,
    )
    result = last(
        cosine, signed_sine, last_bias, stat, sums, query, far_key, swapped_value, passed_value
    )
    return (result, key)


def solution(mesh):
    in_specs = (
        P("batch", "blk", None),
        P("batch", "blk", None),
        P("batch", "blk", None),
        P("batch", "blk"),
        P("batch", None),
        P("batch", "blk", None),
        P(),
        P("batch", None, None),
    )
    out_specs = (P("batch", "blk", None), P("batch", "blk", None))
    return jax.shard_map(
        per_device, mesh=mesh, in_specs=in_specs, out_specs=out_specs, check_vma=False
    )
```

```python
import math

import jax
import jax.numpy as jnp
import numpy as np
from jax import lax
from jax.experimental import pallas as pl
from jax.experimental.pallas import tpu as pltpu
from jax.sharding import PartitionSpec as P

QUERY_HEADS = 16
KEY_VALUE_HEADS = 8
HEAD_SIZE = 128
GROUP = QUERY_HEADS // KEY_VALUE_HEADS
HALF = HEAD_SIZE // 2
ROPE_BASE = 1000000.0
HIDDEN = -1e30
LANES = 128
ROW_TILE = 64
SOFTMAX_TILE = 16
HEADS_PER_STEP = 2
PREPARE_STEPS = 2


def cost(flops):
    return pl.CostEstimate(flops=flops, bytes_accessed=0, transcendentals=0)


PREPARE_COST = cost(0)
NEAR_COST = cost(0)
LAST_COST = cost(0)
EXP2_SCALE = math.log2(math.e) / math.sqrt(HEAD_SIZE)

FREQ_POWERS = [float(ROPE_BASE ** (-(2**k) / HALF)) for k in range(HALF.bit_length() - 1)]

PIO2_A = float(np.float32(1.5703125))
PIO2_B = float(np.float32(4.837512969970703125e-4))
PIO2_C = float(np.float32(math.pi / 2 - 1.5703125 - 4.837512969970703125e-4))


def shifted(value, steps):
    count = lax.axis_size("blk")
    return lax.ppermute(value, "blk", [(source, source + steps) for source in range(count - steps)])


def padded_keys(count):
    return -(-count // LANES) * LANES


def vmem_bytes(key_count):
    return 16 * 1024 * (1024 + key_count)


def sine_cosine(angle):
    turns = jnp.floor(angle * (2.0 / math.pi) + 0.5)
    rest = ((angle - turns * PIO2_A) - turns * PIO2_B) - turns * PIO2_C
    square = rest * rest
    sine = rest + rest * square * (
        -1.6666654611e-1 + square * (8.3321608736e-3 - square * 1.9515295891e-4)
    )
    cosine = 1.0 - 0.5 * square + square * square * (
        4.166664568298827e-2 + square * (-1.388731625493765e-3 + square * 2.443315711809948e-5)
    )
    quadrant = turns.astype(jnp.int32) & 3
    swapped = (quadrant & 1) == 1
    sine_out = jnp.where(swapped, cosine, sine)
    cosine_out = jnp.where(swapped, sine, cosine)
    sine_out = jnp.where(quadrant >= 2, -sine_out, sine_out)
    cosine_out = jnp.where((quadrant == 1) | (quadrant == 2), -cosine_out, cosine_out)
    return sine_out, cosine_out


def rotate(head, cosine, signed_sine):
    wide = head.astype(jnp.float32)
    return (wide * cosine + pltpu.roll(wide, HALF, 1) * signed_sine).astype(jnp.bfloat16)


def prepare_kernel(
    rows, steps, segs, prefix_len,
    table_shape, integers_ref, q_ref, k_ref, v_ref, pool_ref,
    q_out, k_out, k_copy, v_copy, pool_copy, page_out, cos_out, sin_out, near_bias, last_bias,
    cos_own, sin_own,
):
    @pl.when(pl.program_id(0) == 0)
    def _():
        block_start = lax.axis_index("blk") * rows
        starts = [jnp.int32(0)]
        for seg in range(1, segs):
            starts.append(starts[-1] + integers_ref[seg - 1])
        lane = lax.broadcasted_iota(jnp.int32, (ROW_TILE, LANES), 1)
        row = lax.broadcasted_iota(jnp.int32, (ROW_TILE, LANES), 0)
        freq = jnp.ones((ROW_TILE, LANES), jnp.float32)
        for bit, power in enumerate(FREQ_POWERS):
            freq = jnp.where((lane >> bit) & 1 == 1, freq * power, freq)
        column = lax.axis_index("batch")
        seg_pages = table_shape[2]
        first = segs + steps + column * segs * seg_pages
        for page in range(segs * seg_pages):
            seg, place = divmod(page, seg_pages)
            page_out[page] = integers_ref[first + place * segs + seg]
        for step in range(steps + 1):
            for tile in range(0, rows, ROW_TILE):
                index = block_start + (tile - step * rows) + row
                own_start = jnp.zeros(index.shape, jnp.int32)
                for seg in range(1, segs):
                    own_start = jnp.where(index >= starts[seg], starts[seg], own_start)
                place = (prefix_len + index - own_start).astype(jnp.float32)
                sine, cosine = sine_cosine(place * freq)
                sine = jnp.where(lane < HALF, -sine, sine)
                if step == 0:
                    cos_own[pl.ds(tile, ROW_TILE), :] = cosine
                    sin_own[pl.ds(tile, ROW_TILE), :] = sine
                else:
                    span = pl.ds((step - 1) * rows + tile, ROW_TILE)
                    cos_out[span, :] = cosine
                    sin_out[span, :] = sine
        for tile in range(0, rows, ROW_TILE):
            span = pl.ds(tile, ROW_TILE)
            query_index = block_start + tile + row
            own_start = jnp.zeros(query_index.shape, jnp.int32)
            first_page_token = jnp.zeros(query_index.shape, jnp.int32)
            for seg in range(1, segs):
                later = query_index >= starts[seg]
                own_start = jnp.where(later, starts[seg], own_start)
                first_page_token = jnp.where(later, seg * prefix_len, first_page_token)
            for step in range(steps + 1):
                limit = query_index
                if step > 0:
                    limit = jnp.where(integers_ref[segs + step - 1] > 0, limit, -1)
                for column in range(0, rows, LANES):
                    key_index = block_start + (column - step * rows) + lane
                    seen = (key_index >= own_start) & (key_index <= limit)
                    bias = jnp.where(seen, 0.0, HIDDEN)
                    if step == 1:
                        last_bias[span, pl.ds(column, LANES)] = bias
                    else:
                        place = max(step - 1, 0) * rows + column
                        near_bias[span, pl.ds(place, LANES)] = bias
            base = steps * rows
            for column in range(0, near_bias.shape[1] - base, LANES):
                offset = column + lane - first_page_token
                seen = (offset >= 0) & (offset < prefix_len)
                near_bias[span, pl.ds(base + column, LANES)] = jnp.where(seen, 0.0, HIDDEN)

    for tile in range(0, rows, ROW_TILE):
        span = pl.ds(tile, ROW_TILE)
        cosine = cos_own[span, :]
        signed_sine = sin_own[span, :]
        for source, target in ((q_ref, q_out), (k_ref, k_out)):
            for start in range(0, source.shape[2], HEAD_SIZE):
                columns = pl.ds(start, HEAD_SIZE)
                turned = rotate(source[0, span, columns], cosine, signed_sine)
                target[0, span, columns] = turned
                if source is k_ref:
                    k_copy[0, span, columns] = turned
    v_copy[...] = v_ref[...]
    pool_copy[...] = pool_ref[...]


def prepare(queries, keys, values, pool, integers, segs, steps, table_shape):
    rows = queries.shape[1]
    prefix_len = table_shape[2] * pool.shape[1]
    pages = table_shape[1] * table_shape[2]
    far_rows = steps * rows
    near_keys = padded_keys(far_rows + segs * prefix_len)
    whole = lambda part: (0, 0)
    by_part = lambda part: (0, 0, part)
    wide = pl.BlockSpec((1, rows, queries.shape[2] // PREPARE_STEPS), by_part)
    narrow = pl.BlockSpec((1, rows, keys.shape[2] // PREPARE_STEPS), by_part)
    some_pages = pl.BlockSpec(
        (pool.shape[0] // PREPARE_STEPS, *pool.shape[1:]), lambda part: (part, 0, 0)
    )
    table = jax.ShapeDtypeStruct((far_rows, HEAD_SIZE), jnp.float32)
    shapes = [
        jax.ShapeDtypeStruct(queries.shape, jnp.bfloat16),
        jax.ShapeDtypeStruct(keys.shape, jnp.bfloat16),
        jax.ShapeDtypeStruct(keys.shape, jnp.bfloat16),
        jax.ShapeDtypeStruct(values.shape, jnp.bfloat16),
        jax.ShapeDtypeStruct(pool.shape, jnp.bfloat16),
        jax.ShapeDtypeStruct((pages,), jnp.int32),
        table,
        table,
        jax.ShapeDtypeStruct((rows, near_keys), jnp.float32),
        jax.ShapeDtypeStruct((rows, rows), jnp.float32),
    ]
    return pl.pallas_call(
        lambda *refs: prepare_kernel(rows, steps, segs, prefix_len, table_shape, *refs),
        grid=(PREPARE_STEPS,),
        in_specs=[
            pl.BlockSpec(memory_space=pltpu.SMEM),
            wide,
            narrow,
            narrow,
            some_pages,
        ],
        out_specs=[wide, narrow, narrow, narrow, some_pages, pl.BlockSpec(memory_space=pltpu.SMEM)]
        + [pl.BlockSpec(shape.shape, whole) for shape in shapes[6:]],
        out_shape=shapes,
        scratch_shapes=[pltpu.VMEM((rows, HEAD_SIZE), jnp.float32)] * 2,
        compiler_params=pltpu.CompilerParams(vmem_limit_bytes=vmem_bytes(near_keys + far_rows)),
        cost_estimate=PREPARE_COST,
        name="prepare",
    )(integers, queries, keys, values, pool)


def stacked_queries(q_ref, part):
    return jnp.concatenate(
        [q_ref[0, :, pl.ds((part * GROUP + h) * HEAD_SIZE, HEAD_SIZE)] for h in range(GROUP)],
        axis=0,
    )


def rotate_rows(target, first, source, lanes, cos_ref, sin_ref, table_first):
    rows = source.shape[1]
    for tile in range(0, rows, ROW_TILE):
        table = pl.ds(table_first + tile, ROW_TILE)
        target[pl.ds(first + tile, ROW_TILE), :] = rotate(
            source[0, pl.ds(tile, ROW_TILE), lanes], cos_ref[table, :], sin_ref[table, :]
        )


def near_kernel(rows, steps, pages, kv_width, columns_count, *refs):
    table_ref, bias_ref, cos_ref, sin_ref, q_ref, k_ref, v_ref = refs[:7]
    shards, refs = refs[7 : 7 + columns_count], refs[7 + columns_count :]
    far_refs, refs = refs[: 2 * steps - 2], refs[2 * steps - 2 :]
    sum_ref, stat_ref, paged, sem = refs[:4]
    work = refs[4:]
    k_parts, v_parts, scores, weights, tops = (
        work[i : i + HEADS_PER_STEP] for i in range(0, len(work), HEADS_PER_STEP)
    )
    group = pl.program_id(0)
    pool_rows, page_tokens = shards[0].shape[:2]
    prefix_rows = pages * page_tokens
    base = steps * rows

    def page_copy(shard, place, page):
        return pltpu.make_async_copy(shard.at[place], paged.at[page], sem.at[page])

    @pl.when(group == 0)
    def _():
        column = lax.axis_index("batch")
        for page in range(pages):
            number = table_ref[page]
            apart = lax.div(number, jnp.int32(pool_rows)) ^ column
            place = lax.rem(number, jnp.int32(pool_rows))
            for which, shard in enumerate(shards):

                @pl.when(apart == which)
                def _(shard=shard, place=place, page=page):
                    page_copy(shard, place, page).start()

        rest = k_parts[0].shape[0] - base - prefix_rows
        for k_all, v_all in zip(k_parts, v_parts):
            v_all[:, pl.ds(HEAD_SIZE, HEAD_SIZE)] = jnp.ones(k_all.shape, jnp.bfloat16)
            if rest:
                blank = jnp.zeros((rest, HEAD_SIZE), jnp.bfloat16)
                k_all[pl.ds(base + prefix_rows, rest), :] = blank
                v_all[pl.ds(base + prefix_rows, rest), pl.ds(0, HEAD_SIZE)] = blank
        stat_ref[...] = jnp.zeros(stat_ref.shape, jnp.float32)

    for part in range(HEADS_PER_STEP):
        lanes = pl.ds(part * HEAD_SIZE, HEAD_SIZE)
        k_parts[part][pl.ds(0, rows), :] = k_ref[0, :, lanes]
        v_parts[part][pl.ds(0, rows), pl.ds(0, HEAD_SIZE)] = v_ref[0, :, lanes]
        for step in range(1, steps):
            far_key, far_value = far_refs[2 * step - 2 : 2 * step]
            rotate_rows(k_parts[part], step * rows, far_key, lanes, cos_ref, sin_ref, step * rows)
            v_parts[part][pl.ds(step * rows, rows), pl.ds(0, HEAD_SIZE)] = far_value[0, :, lanes]

    @pl.when(group == 0)
    def _():
        for page in range(pages):
            page_copy(shards[0], 0, page).wait()

    for part in range(HEADS_PER_STEP):
        start = (group * HEADS_PER_STEP + part) * HEAD_SIZE
        columns = pl.ds(pl.multiple_of(start, HEAD_SIZE), HEAD_SIZE)
        value_columns = pl.ds(pl.multiple_of(kv_width + start, HEAD_SIZE), HEAD_SIZE)
        span = pl.ds(base, prefix_rows)
        k_parts[part][span, :] = paged[:, :, columns].reshape(prefix_rows, HEAD_SIZE)
        v_parts[part][span, pl.ds(0, HEAD_SIZE)] = paged[:, :, value_columns].reshape(
            prefix_rows, HEAD_SIZE
        )

    for part in range(HEADS_PER_STEP):
        scores[part][...] = lax.dot_general(
            stacked_queries(q_ref, part), k_parts[part][...], (((1,), (1,)), ((), ())),
            preferred_element_type=jnp.float32,
        )
    lane = lax.broadcasted_iota(jnp.int32, (rows, LANES), 1)
    for part in range(HEADS_PER_STEP):
        for start in range(0, GROUP * rows, SOFTMAX_TILE):
            span = pl.ds(start, SOFTMAX_TILE)
            score = scores[part][span, :] + bias_ref[pl.ds(start % rows, SOFTMAX_TILE), :]
            highest = jnp.max(score, axis=1, keepdims=True)
            weight = jnp.exp2((score - highest) * EXP2_SCALE)
            weights[part][span, :] = weight.astype(jnp.bfloat16)
            tops[part][span, :] = jnp.broadcast_to(highest, (SOFTMAX_TILE, LANES))
        summed = jnp.dot(weights[part][...], v_parts[part][...], preferred_element_type=jnp.float32)
        for h in range(GROUP):
            own = part * GROUP + h
            head = group * (HEADS_PER_STEP * GROUP) + own
            span = slice(h * rows, (h + 1) * rows)
            sum_ref[:, pl.ds(own * HEAD_SIZE, HEAD_SIZE)] = summed[span, :HEAD_SIZE]
            stat_ref[...] = jnp.where(
                lane == head,
                tops[part][span, :],
                jnp.where(lane == QUERY_HEADS + head, summed[span, HEAD_SIZE:], stat_ref[...]),
            )


def near(table, shards, bias, cosine, signed_sine, query, key, value, far):
    rows, q_width = query.shape[1:]
    columns_count = len(shards)
    steps = 1 + len(far) // 2
    pages = table.shape[0]
    key_count = bias.shape[1]
    whole = lambda group: (0, 0)
    by_group = lambda group: (0, 0, group)
    narrow = pl.BlockSpec((1, rows, HEADS_PER_STEP * HEAD_SIZE), by_group)
    wide = HEADS_PER_STEP * GROUP * HEAD_SIZE
    return pl.pallas_call(
        lambda *refs: near_kernel(rows, steps, pages, key.shape[2], columns_count, *refs),
        grid=(KEY_VALUE_HEADS // HEADS_PER_STEP,),
        in_specs=[
            pl.BlockSpec(memory_space=pltpu.SMEM),
            pl.BlockSpec(bias.shape, whole),
            pl.BlockSpec(cosine.shape, whole),
            pl.BlockSpec(cosine.shape, whole),
            pl.BlockSpec((1, rows, wide), by_group),
            narrow,
            narrow,
        ]
        + [pl.BlockSpec(memory_space=pl.ANY)] * columns_count
        + [narrow] * len(far),
        out_specs=[
            pl.BlockSpec((rows, wide), lambda group: (0, group)),
            pl.BlockSpec((rows, LANES), whole),
        ],
        out_shape=[
            jax.ShapeDtypeStruct((rows, q_width), jnp.float32),
            jax.ShapeDtypeStruct((rows, LANES), jnp.float32),
        ],
        scratch_shapes=[
            pltpu.VMEM((pages,) + shards[0].shape[1:], jnp.bfloat16),
            pltpu.SemaphoreType.DMA((pages,)),
        ]
        + [pltpu.VMEM((key_count, HEAD_SIZE), jnp.bfloat16)] * HEADS_PER_STEP
        + [pltpu.VMEM((key_count, 2 * HEAD_SIZE), jnp.bfloat16)] * HEADS_PER_STEP
        + [pltpu.VMEM((GROUP * rows, key_count), jnp.float32)] * HEADS_PER_STEP
        + [pltpu.VMEM((GROUP * rows, key_count), jnp.bfloat16)] * HEADS_PER_STEP
        + [pltpu.VMEM((GROUP * rows, LANES), jnp.float32)] * HEADS_PER_STEP,
        compiler_params=pltpu.CompilerParams(vmem_limit_bytes=vmem_bytes(key_count)),
        cost_estimate=NEAR_COST,
        name="near",
    )(table, bias, cosine, signed_sine, query, key, value, *shards, *far)


def last_kernel(
    rows, cos_ref, sin_ref, bias_ref, stat_ref, sum_ref, q_ref, key_ref, swapped_value,
    passed_value, direct_value, out_ref, *work,
):
    k_parts, v_parts, scores, weights, shrinks = (
        work[i : i + HEADS_PER_STEP] for i in range(0, len(work), HEADS_PER_STEP)
    )
    group = pl.program_id(0)
    even = lax.rem(lax.axis_index("blk"), 2) == 0

    @pl.when(group == 0)
    def _():
        for v_all in v_parts:
            v_all[:, pl.ds(HEAD_SIZE, HEAD_SIZE)] = jnp.ones((rows, HEAD_SIZE), jnp.bfloat16)

    for part in range(HEADS_PER_STEP):
        lanes = pl.ds(part * HEAD_SIZE, HEAD_SIZE)
        rotate_rows(k_parts[part], 0, key_ref, lanes, cos_ref, sin_ref, 0)
        start = 0
        for arrived in (passed_value, direct_value):
            span = pl.ds(start, arrived.shape[1])
            v_parts[part][span, pl.ds(0, HEAD_SIZE)] = jnp.where(
                even, arrived[0, :, lanes], swapped_value[0, span, lanes]
            )
            start += arrived.shape[1]

    for part in range(HEADS_PER_STEP):
        scores[part][...] = lax.dot_general(
            stacked_queries(q_ref, part), k_parts[part][...], (((1,), (1,)), ((), ())),
            preferred_element_type=jnp.float32,
        )
    lane = lax.broadcasted_iota(jnp.int32, (SOFTMAX_TILE, LANES), 1)
    for part in range(HEADS_PER_STEP):
        for start in range(0, GROUP * rows, SOFTMAX_TILE):
            span = pl.ds(start, SOFTMAX_TILE)
            row_span = pl.ds(start % rows, SOFTMAX_TILE)
            head = group * (HEADS_PER_STEP * GROUP) + part * GROUP + start // rows
            score = scores[part][span, :] + bias_ref[row_span, :]
            stat = stat_ref[row_span, :]
            near_top = jnp.sum(jnp.where(lane == head, stat, 0.0), axis=1, keepdims=True)
            near_total = jnp.sum(
                jnp.where(lane == QUERY_HEADS + head, stat, 0.0), axis=1, keepdims=True
            )
            highest = jnp.maximum(jnp.max(score, axis=1, keepdims=True), near_top)
            weight = jnp.exp2((score - highest) * EXP2_SCALE)
            weights[part][span, :] = weight.astype(jnp.bfloat16)
            shrink = jnp.exp2((near_top - highest) * EXP2_SCALE)
            shrinks[part][span, pl.ds(0, LANES)] = jnp.broadcast_to(shrink, (SOFTMAX_TILE, LANES))
            shrinks[part][span, pl.ds(LANES, LANES)] = jnp.broadcast_to(
                shrink * near_total, (SOFTMAX_TILE, LANES)
            )
        summed = jnp.dot(weights[part][...], v_parts[part][...], preferred_element_type=jnp.float32)
        for h in range(GROUP):
            lanes = pl.ds((part * GROUP + h) * HEAD_SIZE, HEAD_SIZE)
            span = slice(h * rows, (h + 1) * rows)
            above = sum_ref[:, lanes] * shrinks[part][span, :LANES] + summed[span, :HEAD_SIZE]
            below = shrinks[part][span, LANES:] + summed[span, HEAD_SIZE:]
            out_ref[0, :, lanes] = (above / below).astype(jnp.bfloat16)


def last(
    cosine, signed_sine, bias, stat, sums, query, key, swapped_value, passed_value, direct_value
):
    rows = query.shape[1]
    whole = lambda group: (0, 0)
    by_group = lambda group: (0, 0, group)
    width = HEADS_PER_STEP * GROUP * HEAD_SIZE
    wide = pl.BlockSpec((1, rows, width), by_group)
    narrow = pl.BlockSpec((1, rows, HEADS_PER_STEP * HEAD_SIZE), by_group)
    table = pl.BlockSpec((rows, HEAD_SIZE), whole)
    return pl.pallas_call(
        lambda *refs: last_kernel(rows, *refs),
        grid=(KEY_VALUE_HEADS // HEADS_PER_STEP,),
        in_specs=[
            table,
            table,
            pl.BlockSpec(bias.shape, whole),
            pl.BlockSpec(stat.shape, whole),
            pl.BlockSpec((rows, width), lambda group: (0, group)),
            wide,
            narrow,
            narrow,
            pl.BlockSpec((1, passed_value.shape[1], HEADS_PER_STEP * HEAD_SIZE), by_group),
            pl.BlockSpec((1, direct_value.shape[1], HEADS_PER_STEP * HEAD_SIZE), by_group),
        ],
        out_specs=wide,
        out_shape=jax.ShapeDtypeStruct(query.shape, jnp.bfloat16),
        scratch_shapes=[pltpu.VMEM((rows, HEAD_SIZE), jnp.bfloat16)] * HEADS_PER_STEP
        + [pltpu.VMEM((rows, 2 * HEAD_SIZE), jnp.bfloat16)] * HEADS_PER_STEP
        + [pltpu.VMEM((GROUP * rows, rows), jnp.float32)] * HEADS_PER_STEP
        + [pltpu.VMEM((GROUP * rows, rows), jnp.bfloat16)] * HEADS_PER_STEP
        + [pltpu.VMEM((GROUP * rows, 2 * LANES), jnp.float32)] * HEADS_PER_STEP,
        compiler_params=pltpu.CompilerParams(vmem_limit_bytes=vmem_bytes(rows)),
        cost_estimate=LAST_COST,
        name="last",
    )(
        cosine, signed_sine, bias, stat, sums, query, key, swapped_value, passed_value, direct_value
    )


def pool_shards(pool, after):
    count = lax.axis_size("batch")
    shards, bit = {0: pool}, count // 2
    while bit:
        if len(shards) > 1:
            shards, after = lax.optimization_barrier((shards, after))
        for apart, shard in list(shards.items()):
            shards[apart ^ bit] = lax.ppermute(
                shard, "batch", [(c, c ^ bit) for c in range(count)]
            )
        bit //= 2
    return [shards[apart] for apart in range(count)]


def per_device(queries, keys, values, seg_ids, lengths, live, page_table, pool):
    steps = live.shape[2]
    blocks = lax.axis_size("blk")
    far = [shifted(keys, 2), shifted(values, 2)]
    for step in range(3, steps + 1):
        far += [shifted(keys, step), shifted(values, step)]
    swap = [(j, j ^ 1) for j in range(blocks)]
    even = lax.rem(lax.axis_index("blk"), 2) == 0
    swapped_value = lax.ppermute(values, "blk", swap)
    integers = jnp.concatenate([lengths.ravel(), live.ravel(), jnp.swapaxes(page_table, 1, 2).ravel()])
    (
        query, key, near_key, near_value, own_shard, table, cosine, signed_sine, near_bias, last_bias
    ) = prepare(queries, keys, values, pool, integers, lengths.shape[1], steps, page_table.shape)
    far_key = lax.ppermute(jnp.where(even, keys, far[0]), "blk", swap)
    split = values.shape[1] * 3 // 4
    passed_value = lax.ppermute(
        swapped_value[:, :split], "blk", [(j, j + 2) for j in range(0, blocks - 2, 2)]
    )
    shards = pool_shards(pool, (cosine, far[0]))
    shards[1:], later_values = lax.optimization_barrier((shards[1:], values[:, split:]))
    direct_value = lax.ppermute(
        later_values, "blk", [(j, j + 1) for j in range(1, blocks - 1, 2)]
    )
    sums, stat = near(
        table, [own_shard, *shards[1:]], near_bias, cosine, signed_sine,
        query, near_key, near_value, far,
    )
    result = last(
        cosine, signed_sine, last_bias, stat, sums, query, far_key, swapped_value, passed_value,
        direct_value,
    )
    return (result, key)


def solution(mesh):
    in_specs = (
        P("batch", "blk", None),
        P("batch", "blk", None),
        P("batch", "blk", None),
        P("batch", "blk"),
        P("batch", None),
        P("batch", "blk", None),
        P(),
        P("batch", None, None),
    )
    out_specs = (P("batch", "blk", None), P("batch", "blk", None))
    return jax.shard_map(
        per_device, mesh=mesh, in_specs=in_specs, out_specs=out_specs, check_vma=False
    )
```

```python
import math

import jax
import jax.numpy as jnp
import numpy as np
from jax import lax
from jax.experimental import pallas as pl
from jax.experimental.pallas import tpu as pltpu
from jax.sharding import PartitionSpec as P

QUERY_HEADS = 16
KEY_VALUE_HEADS = 8
HEAD_SIZE = 128
GROUP = QUERY_HEADS // KEY_VALUE_HEADS
HALF = HEAD_SIZE // 2
ROPE_BASE = 1000000.0
HIDDEN = -1e30
LANES = 128
ROW_TILE = 64
SOFTMAX_TILE = 16
HEADS_PER_STEP = 2
PREPARE_STEPS = 2


def cost(flops):
    return pl.CostEstimate(flops=flops, bytes_accessed=0, transcendentals=0)


TABLES_COST = cost(2_000_000_000)
PREPARE_COST = cost(0)
OWN_COST = cost(0)
JOIN_COST = cost(0)
EXP2_SCALE = math.log2(math.e) / math.sqrt(HEAD_SIZE)

FREQ_POWERS = [float(ROPE_BASE ** (-(2**k) / HALF)) for k in range(HALF.bit_length() - 1)]

PIO2_A = float(np.float32(1.5703125))
PIO2_B = float(np.float32(4.837512969970703125e-4))
PIO2_C = float(np.float32(math.pi / 2 - 1.5703125 - 4.837512969970703125e-4))


def shifted(value, steps):
    count = lax.axis_size("blk")
    return lax.ppermute(value, "blk", [(source, source + steps) for source in range(count - steps)])


def padded_keys(count):
    return -(-count // LANES) * LANES


def vmem_bytes(key_count):
    return 16 * 1024 * (1024 + key_count)


def sine_cosine(angle):
    turns = jnp.floor(angle * (2.0 / math.pi) + 0.5)
    rest = ((angle - turns * PIO2_A) - turns * PIO2_B) - turns * PIO2_C
    square = rest * rest
    sine = rest + rest * square * (
        -1.6666654611e-1 + square * (8.3321608736e-3 - square * 1.9515295891e-4)
    )
    cosine = 1.0 - 0.5 * square + square * square * (
        4.166664568298827e-2 + square * (-1.388731625493765e-3 + square * 2.443315711809948e-5)
    )
    quadrant = turns.astype(jnp.int32) & 3
    swapped = (quadrant & 1) == 1
    sine_out = jnp.where(swapped, cosine, sine)
    cosine_out = jnp.where(swapped, sine, cosine)
    sine_out = jnp.where(quadrant >= 2, -sine_out, sine_out)
    cosine_out = jnp.where((quadrant == 1) | (quadrant == 2), -cosine_out, cosine_out)
    return sine_out, cosine_out


def rotate(head, cosine, signed_sine):
    wide = head.astype(jnp.float32)
    return (wide * cosine + pltpu.roll(wide, HALF, 1) * signed_sine).astype(jnp.bfloat16)


def tables_kernel(
    rows, steps, segs, prefix_len, table_shape, integers_ref,
    page_out, cos_own, sin_own, cos_last, sin_last, cos_far, sin_far, own_bias, last_bias, far_bias,
):
    block_start = lax.axis_index("blk") * rows
    starts = [jnp.int32(0)]
    for seg in range(1, segs):
        starts.append(starts[-1] + integers_ref[seg - 1])
    lane = lax.broadcasted_iota(jnp.int32, (ROW_TILE, LANES), 1)
    row = lax.broadcasted_iota(jnp.int32, (ROW_TILE, LANES), 0)
    freq = jnp.ones((ROW_TILE, LANES), jnp.float32)
    for bit, power in enumerate(FREQ_POWERS):
        freq = jnp.where((lane >> bit) & 1 == 1, freq * power, freq)
    column = lax.axis_index("batch")
    seg_pages = table_shape[2]
    first = segs + steps + column * segs * seg_pages
    for page in range(segs * seg_pages):
        seg, place = divmod(page, seg_pages)
        page_out[page] = integers_ref[first + place * segs + seg]
    for step in range(steps + 1):
        for tile in range(0, rows, ROW_TILE):
            index = block_start + (tile - step * rows) + row
            own_start = jnp.zeros(index.shape, jnp.int32)
            for seg in range(1, segs):
                own_start = jnp.where(index >= starts[seg], starts[seg], own_start)
            place = (prefix_len + index - own_start).astype(jnp.float32)
            sine, cosine = sine_cosine(place * freq)
            sine = jnp.where(lane < HALF, -sine, sine)
            cos_out, sin_out = ((cos_own, sin_own), (cos_last, sin_last), (cos_far, sin_far))[
                min(step, 2)
            ]
            span = pl.ds(max(step - 2, 0) * rows + tile, ROW_TILE)
            cos_out[span, :] = cosine
            sin_out[span, :] = sine
    for tile in range(0, rows, ROW_TILE):
        span = pl.ds(tile, ROW_TILE)
        query_index = block_start + tile + row
        own_start = jnp.zeros(query_index.shape, jnp.int32)
        first_page_token = jnp.zeros(query_index.shape, jnp.int32)
        for seg in range(1, segs):
            later = query_index >= starts[seg]
            own_start = jnp.where(later, starts[seg], own_start)
            first_page_token = jnp.where(later, seg * prefix_len, first_page_token)
        for step in range(steps + 1):
            limit = query_index
            if step > 0:
                limit = jnp.where(integers_ref[segs + step - 1] > 0, limit, -1)
            for column in range(0, rows, LANES):
                key_index = block_start + (column - step * rows) + lane
                seen = (key_index >= own_start) & (key_index <= limit)
                bias = jnp.where(seen, 0.0, HIDDEN)
                if step == 0:
                    own_bias[span, pl.ds(column, LANES)] = bias
                elif step == 1:
                    last_bias[span, pl.ds(column, LANES)] = bias
                else:
                    far_bias[span, pl.ds((step - 2) * rows + column, LANES)] = bias
        base = (steps - 1) * rows
        for column in range(0, far_bias.shape[1] - base, LANES):
            offset = column + lane - first_page_token
            seen = (offset >= 0) & (offset < prefix_len)
            far_bias[span, pl.ds(base + column, LANES)] = jnp.where(seen, 0.0, HIDDEN)


def tables(rows, pool_page, integers, segs, steps, table_shape):
    prefix_len = table_shape[2] * pool_page
    pages = table_shape[1] * table_shape[2]
    far_rows = (steps - 1) * rows
    far_keys = padded_keys(far_rows + segs * prefix_len)
    block = jax.ShapeDtypeStruct((rows, HEAD_SIZE), jnp.float32)
    far = jax.ShapeDtypeStruct((far_rows, HEAD_SIZE), jnp.float32)
    shapes = [
        jax.ShapeDtypeStruct((pages,), jnp.int32),
        *[block] * 4,
        far,
        far,
        *[jax.ShapeDtypeStruct((rows, rows), jnp.float32)] * 2,
        jax.ShapeDtypeStruct((rows, far_keys), jnp.float32),
    ]
    return pl.pallas_call(
        lambda *refs: tables_kernel(rows, steps, segs, prefix_len, table_shape, *refs),
        in_specs=[pl.BlockSpec(memory_space=pltpu.SMEM)],
        out_specs=[pl.BlockSpec(memory_space=pltpu.SMEM)]
        + [pl.BlockSpec(memory_space=pltpu.VMEM)] * (len(shapes) - 1),
        out_shape=shapes,
        compiler_params=pltpu.CompilerParams(vmem_limit_bytes=vmem_bytes(far_keys + far_rows)),
        cost_estimate=TABLES_COST,
        name="tables",
    )(integers)


def prepare_kernel(
    rows, cos_own, sin_own, q_ref, k_ref, v_ref, pool_ref, q_out, k_out, k_copy, v_copy, pool_copy
):
    for tile in range(0, rows, ROW_TILE):
        span = pl.ds(tile, ROW_TILE)
        cosine = cos_own[span, :]
        signed_sine = sin_own[span, :]
        for source, target in ((q_ref, q_out), (k_ref, k_out)):
            for start in range(0, source.shape[2], HEAD_SIZE):
                columns = pl.ds(start, HEAD_SIZE)
                turned = rotate(source[0, span, columns], cosine, signed_sine)
                target[0, span, columns] = turned
                if source is k_ref:
                    k_copy[0, span, columns] = turned
    v_copy[...] = v_ref[...]
    pool_copy[...] = pool_ref[...]


def prepare(cosine, signed_sine, queries, keys, values, pool):
    rows = queries.shape[1]
    whole = lambda part: (0, 0)
    by_part = lambda part: (0, 0, part)
    wide = pl.BlockSpec((1, rows, queries.shape[2] // PREPARE_STEPS), by_part)
    narrow = pl.BlockSpec((1, rows, keys.shape[2] // PREPARE_STEPS), by_part)
    some_pages = pl.BlockSpec(
        (pool.shape[0] // PREPARE_STEPS, *pool.shape[1:]), lambda part: (part, 0, 0)
    )
    table = pl.BlockSpec(cosine.shape, whole)
    return pl.pallas_call(
        lambda *refs: prepare_kernel(rows, *refs),
        grid=(PREPARE_STEPS,),
        in_specs=[table, table, wide, narrow, narrow, some_pages],
        out_specs=[wide, narrow, narrow, narrow, some_pages],
        out_shape=[
            jax.ShapeDtypeStruct(array.shape, array.dtype)
            for array in (queries, keys, keys, values, pool)
        ],
        compiler_params=pltpu.CompilerParams(vmem_limit_bytes=vmem_bytes(rows)),
        cost_estimate=PREPARE_COST,
        name="prepare",
    )(cosine, signed_sine, queries, keys, values, pool)


def stacked_queries(q_ref, part):
    return jnp.concatenate(
        [q_ref[0, :, pl.ds((part * GROUP + h) * HEAD_SIZE, HEAD_SIZE)] for h in range(GROUP)],
        axis=0,
    )


def rotate_rows(target, first, source, lanes, cos_ref, sin_ref):
    rows = source.shape[1]
    for tile in range(0, rows, ROW_TILE):
        span = pl.ds(first + tile, ROW_TILE)
        target[span, :] = rotate(
            source[0, pl.ds(tile, ROW_TILE), lanes], cos_ref[span, :], sin_ref[span, :]
        )


def own_kernel(rows, bias_ref, q_ref, k_ref, v_ref, mean_ref, level_ref, *work):
    k_parts, v_parts, scores, weights, tops = split_work(work)
    group = pl.program_id(0)

    @pl.when(group == 0)
    def _():
        fill_ones(v_parts)
        level_ref[...] = jnp.zeros(level_ref.shape, jnp.float32)

    for part in range(HEADS_PER_STEP):
        lanes = pl.ds(part * HEAD_SIZE, HEAD_SIZE)
        k_parts[part][...] = k_ref[0, :, lanes]
        v_parts[part][:, pl.ds(0, HEAD_SIZE)] = v_ref[0, :, lanes]

    for part in range(HEADS_PER_STEP):
        score_part(part, q_ref, k_parts, scores)
    lane = lax.broadcasted_iota(jnp.int32, (rows, LANES), 1)
    for part in range(HEADS_PER_STEP):
        for start in range(0, GROUP * rows, SOFTMAX_TILE):
            span = pl.ds(start, SOFTMAX_TILE)
            bias = bias_ref[pl.ds(start % rows, SOFTMAX_TILE), :]
            score = scores[part][span, :] * EXP2_SCALE + bias
            highest = jnp.max(score, axis=1, keepdims=True)
            weights[part][span, :] = jnp.exp2(score - highest).astype(jnp.bfloat16)
            tops[part][span, :] = jnp.broadcast_to(highest, (SOFTMAX_TILE, LANES))
        summed = jnp.dot(weights[part][...], v_parts[part][...], preferred_element_type=jnp.float32)
        total = summed[:, HEAD_SIZE:]
        store_part(part, group, rows, lane, summed[:, :HEAD_SIZE] / total,
                   tops[part][...] + jnp.log2(total), mean_ref, level_ref)


def fill_ones(v_parts):
    for v_all in v_parts:
        v_all[:, pl.ds(HEAD_SIZE, HEAD_SIZE)] = jnp.ones((v_all.shape[0], HEAD_SIZE), jnp.bfloat16)


def split_work(work):
    return [work[i : i + HEADS_PER_STEP] for i in range(0, len(work), HEADS_PER_STEP)]


def score_part(part, q_ref, k_parts, scores):
    scores[part][...] = lax.dot_general(
        stacked_queries(q_ref, part), k_parts[part][...], (((1,), (1,)), ((), ())),
        preferred_element_type=jnp.float32,
    )


def store_part(part, group, rows, lane, mean, level, mean_ref, level_ref):
    for h in range(GROUP):
        own = part * GROUP + h
        span = slice(h * rows, (h + 1) * rows)
        mean_ref[:, pl.ds(own * HEAD_SIZE, HEAD_SIZE)] = mean[span]
        head = group * (HEADS_PER_STEP * GROUP) + own
        level_ref[...] = jnp.where(lane == head, level[span], level_ref[...])


def work_shapes(rows, key_count):
    shapes = [
        pltpu.VMEM((key_count, HEAD_SIZE), jnp.bfloat16),
        pltpu.VMEM((key_count, 2 * HEAD_SIZE), jnp.bfloat16),
        pltpu.VMEM((GROUP * rows, key_count), jnp.float32),
        pltpu.VMEM((GROUP * rows, key_count), jnp.bfloat16),
        pltpu.VMEM((GROUP * rows, LANES), jnp.float32),
    ]
    return [shape for shape in shapes for _ in range(HEADS_PER_STEP)]


def attend_own(bias, query, key, value):
    rows, q_width = query.shape[1:]
    by_group = lambda group: (0, 0, group)
    narrow = pl.BlockSpec((1, rows, HEADS_PER_STEP * HEAD_SIZE), by_group)
    wide = HEADS_PER_STEP * GROUP * HEAD_SIZE
    return pl.pallas_call(
        lambda *refs: own_kernel(rows, *refs),
        grid=(KEY_VALUE_HEADS // HEADS_PER_STEP,),
        in_specs=[
            pl.BlockSpec(bias.shape, lambda group: (0, 0)),
            pl.BlockSpec((1, rows, wide), by_group),
            narrow,
            narrow,
        ],
        out_specs=[
            pl.BlockSpec((rows, wide), lambda group: (0, group)),
            pl.BlockSpec((rows, LANES), lambda group: (0, 0)),
        ],
        out_shape=[
            jax.ShapeDtypeStruct((rows, q_width), jnp.float32),
            jax.ShapeDtypeStruct((rows, LANES), jnp.float32),
        ],
        scratch_shapes=work_shapes(rows, rows),
        compiler_params=pltpu.CompilerParams(vmem_limit_bytes=vmem_bytes(rows)),
        cost_estimate=OWN_COST,
        name="own",
    )(bias, query, key, value)


def page_copies(start, table_ref, shards, paged, sem):
    pool_rows = shards[0].shape[0]
    column = lax.axis_index("batch")

    def copy(shard, place, page):
        return pltpu.make_async_copy(shard.at[place], paged.at[page], sem.at[page])

    for page in range(paged.shape[0]):
        if not start:
            copy(shards[0], 0, page).wait()
            continue
        number = table_ref[page]
        apart = lax.div(number, jnp.int32(pool_rows)) ^ column
        place = lax.rem(number, jnp.int32(pool_rows))
        for which, shard in enumerate(shards):

            @pl.when(apart == which)
            def _(shard=shard, place=place, page=page):
                copy(shard, place, page).start()


def join_heads(
    final, group, rows, k_parts, v_parts, scores, weights, tops,
    bias_ref, level_ref, mean_ref, q_ref, out_ref, level_out,
):
    for part in range(HEADS_PER_STEP):
        score_part(part, q_ref, k_parts, scores)
    lane = lax.broadcasted_iota(jnp.int32, (SOFTMAX_TILE, LANES), 1)
    wide_lane = lax.broadcasted_iota(jnp.int32, (rows, LANES), 1)
    for part in range(HEADS_PER_STEP):
        for start in range(0, GROUP * rows, SOFTMAX_TILE):
            span = pl.ds(start, SOFTMAX_TILE)
            row_span = pl.ds(start % rows, SOFTMAX_TILE)
            head = group * (HEADS_PER_STEP * GROUP) + part * GROUP + start // rows
            score = scores[part][span, :] * EXP2_SCALE + bias_ref[row_span, :]
            level = jnp.sum(
                jnp.where(lane == head, level_ref[row_span, :], 0.0), axis=1, keepdims=True
            )
            highest = jnp.maximum(jnp.max(score, axis=1, keepdims=True), level)
            weights[part][span, :] = jnp.exp2(score - highest).astype(jnp.bfloat16)
            if final:
                shrink = jnp.exp2(level - highest)
                tops[part][span, :] = jnp.broadcast_to(shrink, (SOFTMAX_TILE, LANES))
            else:
                tops[part][span, :] = jnp.where(lane < HALF, highest, level)
        summed = jnp.dot(weights[part][...], v_parts[part][...], preferred_element_type=jnp.float32)
        if final:
            shrink = tops[part][...]
        else:
            both = tops[part][...]
            turned = pltpu.roll(both, HALF, 1)
            low = lax.broadcasted_iota(jnp.int32, both.shape, 1) < HALF
            highest = jnp.where(low, both, turned)
            shrink = jnp.exp2(jnp.where(low, turned, both) - highest)
        total = summed[:, HEAD_SIZE:] + shrink
        before = jnp.concatenate(
            [mean_ref[:, pl.ds((part * GROUP + h) * HEAD_SIZE, HEAD_SIZE)] for h in range(GROUP)],
            axis=0,
        )
        mean = (before * shrink + summed[:, :HEAD_SIZE]) / total
        if final:
            for h in range(GROUP):
                lanes = pl.ds((part * GROUP + h) * HEAD_SIZE, HEAD_SIZE)
                out_ref[0, :, lanes] = mean[h * rows : (h + 1) * rows].astype(jnp.bfloat16)
        else:
            level = highest + jnp.log2(total)
            store_part(part, group, rows, wide_lane, mean, level, out_ref, level_out)


def far_kernel(rows, columns_count, blocks, kv_width, *refs):
    table_ref, cos_ref, sin_ref, bias_ref, level_ref, mean_ref, q_ref = refs[:7]
    shards, refs = refs[7 : 7 + columns_count], refs[7 + columns_count :]
    keys, values, refs = refs[:blocks], refs[blocks : 2 * blocks], refs[2 * blocks :]
    mean_out, level_out, paged, sem = refs[:4]
    work = split_work(refs[4:])
    k_parts, v_parts = work[:2]
    group = pl.program_id(0)
    prefix_rows = paged.shape[0] * paged.shape[1]
    base = blocks * rows

    @pl.when(group == 0)
    def _():
        page_copies(True, table_ref, shards, paged, sem)
        fill_ones(v_parts)
        level_out[...] = jnp.zeros(level_out.shape, jnp.float32)
        rest = k_parts[0].shape[0] - base - prefix_rows
        if rest:
            blank = jnp.zeros((rest, HEAD_SIZE), jnp.bfloat16)
            for k_all, v_all in zip(k_parts, v_parts):
                k_all[pl.ds(base + prefix_rows, rest), :] = blank
                v_all[pl.ds(base + prefix_rows, rest), pl.ds(0, HEAD_SIZE)] = blank

    for part in range(HEADS_PER_STEP):
        lanes = pl.ds(part * HEAD_SIZE, HEAD_SIZE)
        for block in range(blocks):
            rotate_rows(k_parts[part], block * rows, keys[block], lanes, cos_ref, sin_ref)
            span = pl.ds(block * rows, rows)
            v_parts[part][span, pl.ds(0, HEAD_SIZE)] = values[block][0, :, lanes]

    @pl.when(group == 0)
    def _():
        page_copies(False, table_ref, shards, paged, sem)

    for part in range(HEADS_PER_STEP):
        start = (group * HEADS_PER_STEP + part) * HEAD_SIZE
        columns = pl.ds(pl.multiple_of(start, HEAD_SIZE), HEAD_SIZE)
        value_columns = pl.ds(pl.multiple_of(kv_width + start, HEAD_SIZE), HEAD_SIZE)
        span = pl.ds(base, prefix_rows)
        k_parts[part][span, :] = paged[:, :, columns].reshape(prefix_rows, HEAD_SIZE)
        v_parts[part][span, pl.ds(0, HEAD_SIZE)] = paged[:, :, value_columns].reshape(
            prefix_rows, HEAD_SIZE
        )
    join_heads(
        False, group, rows, *work, bias_ref, level_ref, mean_ref, q_ref, mean_out, level_out
    )


def last_kernel(
    rows, cos_ref, sin_ref, bias_ref, level_ref, mean_ref, q_ref, key_ref, swapped_value,
    passed_value, direct_value, out_ref, *refs,
):
    work = split_work(refs)
    k_parts, v_parts = work[:2]
    group = pl.program_id(0)
    even = lax.rem(lax.axis_index("blk"), 2) == 0

    @pl.when(group == 0)
    def _():
        fill_ones(v_parts)

    for part in range(HEADS_PER_STEP):
        lanes = pl.ds(part * HEAD_SIZE, HEAD_SIZE)
        rotate_rows(k_parts[part], 0, key_ref, lanes, cos_ref, sin_ref)
        start = 0
        for arrived in (passed_value, direct_value):
            span = pl.ds(start, arrived.shape[1])
            v_parts[part][span, pl.ds(0, HEAD_SIZE)] = jnp.where(
                even, arrived[0, :, lanes], swapped_value[0, span, lanes]
            )
            start += arrived.shape[1]
    join_heads(True, group, rows, *work, bias_ref, level_ref, mean_ref, q_ref, out_ref, None)


def join(cosine, signed_sine, bias, level, mean, query, arrived, pages=None):
    rows = query.shape[1]
    whole = lambda group: (0, 0)
    by_group = lambda group: (0, 0, group)
    width = HEADS_PER_STEP * GROUP * HEAD_SIZE
    wide = pl.BlockSpec((1, rows, width), by_group)
    flat = pl.BlockSpec((rows, width), lambda group: (0, group))
    table = pl.BlockSpec(cosine.shape, whole)
    level_spec = pl.BlockSpec(level.shape, whole)
    in_specs = [table, table, pl.BlockSpec(bias.shape, whole), level_spec, flat, wide]
    arrived_specs = [
        pl.BlockSpec((1, array.shape[1], HEADS_PER_STEP * HEAD_SIZE), by_group)
        for array in arrived
    ]
    operands = [cosine, signed_sine, bias, level, mean, query]
    scratch = work_shapes(rows, bias.shape[1])
    if pages is None:
        kernel = lambda *refs: last_kernel(rows, *refs)
        out_specs, out_shape = wide, jax.ShapeDtypeStruct(query.shape, jnp.bfloat16)
    else:
        numbers, shards = pages
        kernel = lambda *refs: far_kernel(
            rows, len(shards), len(arrived) // 2, arrived[0].shape[2], *refs
        )
        in_specs = [
            pl.BlockSpec(memory_space=pltpu.SMEM),
            *in_specs,
            *[pl.BlockSpec(memory_space=pl.ANY)] * len(shards),
        ]
        operands = [numbers, *operands, *shards]
        out_specs = [flat, level_spec]
        out_shape = [
            jax.ShapeDtypeStruct(array.shape, jnp.float32) for array in (mean, level)
        ]
        scratch = [
            pltpu.VMEM(numbers.shape + shards[0].shape[1:], jnp.bfloat16),
            pltpu.SemaphoreType.DMA(numbers.shape),
        ] + scratch
    return pl.pallas_call(
        kernel,
        grid=(KEY_VALUE_HEADS // HEADS_PER_STEP,),
        in_specs=in_specs + arrived_specs,
        out_specs=out_specs,
        out_shape=out_shape,
        scratch_shapes=scratch,
        compiler_params=pltpu.CompilerParams(vmem_limit_bytes=vmem_bytes(bias.shape[1])),
        cost_estimate=JOIN_COST,
        name="last" if pages is None else "far",
    )(*operands, *arrived)


def pool_shards(pool, after):
    count = lax.axis_size("batch")

    def swapped(shard, bit):
        return lax.ppermute(shard, "batch", [(c, c ^ bit) for c in range(count)])

    bits = [count >> (step + 1) for step in range(count.bit_length() - 1)]
    shards = {0: pool, **{bit: swapped(pool, bit) for bit in bits}}
    shards, after = lax.optimization_barrier((shards, after))
    for bit in reversed(bits):
        for apart, shard in list(shards.items()):
            if apart ^ bit not in shards:
                shards[apart ^ bit] = swapped(shard, bit)
    return [shards[apart] for apart in range(count)]


def per_device(queries, keys, values, seg_ids, lengths, live, page_table, pool):
    steps = live.shape[2]
    blocks = lax.axis_size("blk")
    far = [shifted(keys, 2), shifted(values, 2)]
    for step in range(3, steps + 1):
        far += [shifted(keys, step), shifted(values, step)]
    swap = [(j, j ^ 1) for j in range(blocks)]
    even = lax.rem(lax.axis_index("blk"), 2) == 0
    swapped_value = lax.ppermute(values, "blk", swap)
    integers = jnp.concatenate([lengths.ravel(), live.ravel(), jnp.swapaxes(page_table, 1, 2).ravel()])
    (
        table, cos_own, sin_own, cos_last, sin_last, cos_far, sin_far, own_bias, last_bias, far_bias
    ) = tables(keys.shape[1], pool.shape[1], integers, lengths.shape[1], steps, page_table.shape)
    query, key, near_key, near_value, own_shard = prepare(
        cos_own, sin_own, queries, keys, values, pool
    )
    to_swap = jnp.where(even, keys, far[0])
    far_key = lax.ppermute(to_swap, "blk", swap)
    split = values.shape[1] * 3 // 4
    passed_value = lax.ppermute(
        swapped_value[:, :split], "blk", [(j, j + 2) for j in range(0, blocks - 2, 2)]
    )
    shards = pool_shards(pool, (near_key, to_swap))
    later_values = values[:, split:]
    direct_value = lax.ppermute(
        later_values, "blk", [(j, j + 1) for j in range(1, blocks - 1, 2)]
    )
    mean, level = attend_own(own_bias, query, near_key, near_value)
    mean, level = join(
        cos_far, sin_far, far_bias, level, mean, query, [*far[::2], *far[1::2]],
        pages=(table, [own_shard, *shards[1:]]),
    )
    result = join(
        cos_last, sin_last, last_bias, level, mean, query,
        [far_key, swapped_value, passed_value, direct_value],
    )
    return (result, key)


def solution(mesh):
    in_specs = (
        P("batch", "blk", None),
        P("batch", "blk", None),
        P("batch", "blk", None),
        P("batch", "blk"),
        P("batch", None),
        P("batch", "blk", None),
        P(),
        P("batch", None, None),
    )
    out_specs = (P("batch", "blk", None), P("batch", "blk", None))
    return jax.shard_map(
        per_device, mesh=mesh, in_specs=in_specs, out_specs=out_specs, check_vma=False
    )
```

```python
import math

import jax
import jax.numpy as jnp
import numpy as np
from jax import lax
from jax.experimental import pallas as pl
from jax.experimental.pallas import tpu as pltpu
from jax.sharding import PartitionSpec as P

QUERY_HEADS = 16
KEY_VALUE_HEADS = 8
HEAD_SIZE = 128
GROUP = QUERY_HEADS // KEY_VALUE_HEADS
HALF = HEAD_SIZE // 2
ROPE_BASE = 1000000.0
HIDDEN = -1e30
LANES = 128
ROW_TILE = 64
SOFTMAX_TILE = 16
HEADS_PER_STEP = 2
PREPARE_STEPS = 2


def cost(flops):
    return pl.CostEstimate(flops=flops, bytes_accessed=0, transcendentals=0)


TABLES_COST = cost(2_000_000_000)
PREPARE_COST = cost(0)
OWN_COST = cost(0)
FAR_COST = cost(0)
LAST_COST = cost(0)
EXP2_SCALE = math.log2(math.e) / math.sqrt(HEAD_SIZE)

FREQ_POWERS = [float(ROPE_BASE ** (-(2**k) / HALF)) for k in range(HALF.bit_length() - 1)]

PIO2_A = float(np.float32(1.5703125))
PIO2_B = float(np.float32(4.837512969970703125e-4))
PIO2_C = float(np.float32(math.pi / 2 - 1.5703125 - 4.837512969970703125e-4))


def shifted(value, steps):
    count = lax.axis_size("blk")
    return lax.ppermute(value, "blk", [(source, source + steps) for source in range(count - steps)])


def padded_keys(count):
    return -(-count // LANES) * LANES


def vmem_bytes(key_count):
    return 16 * 1024 * (1024 + key_count)


def sine_cosine(angle):
    turns = jnp.floor(angle * (2.0 / math.pi) + 0.5)
    rest = ((angle - turns * PIO2_A) - turns * PIO2_B) - turns * PIO2_C
    square = rest * rest
    sine = rest + rest * square * (
        -1.6666654611e-1 + square * (8.3321608736e-3 - square * 1.9515295891e-4)
    )
    cosine = 1.0 - 0.5 * square + square * square * (
        4.166664568298827e-2 + square * (-1.388731625493765e-3 + square * 2.443315711809948e-5)
    )
    quadrant = turns.astype(jnp.int32) & 3
    swapped = (quadrant & 1) == 1
    sine_out = jnp.where(swapped, cosine, sine)
    cosine_out = jnp.where(swapped, sine, cosine)
    sine_out = jnp.where(quadrant >= 2, -sine_out, sine_out)
    cosine_out = jnp.where((quadrant == 1) | (quadrant == 2), -cosine_out, cosine_out)
    return sine_out, cosine_out


def rotate(head, cosine, signed_sine):
    wide = head.astype(jnp.float32)
    return (wide * cosine + pltpu.roll(wide, HALF, 1) * signed_sine).astype(jnp.bfloat16)


def tables_kernel(
    rows, steps, segs, prefix_len, table_shape, integers_ref,
    page_out, cos_own, sin_own, cos_last, sin_last, cos_far, sin_far, own_bias, last_bias, far_bias,
):
    block_start = lax.axis_index("blk") * rows
    starts = [jnp.int32(0)]
    for seg in range(1, segs):
        starts.append(starts[-1] + integers_ref[seg - 1])
    lane = lax.broadcasted_iota(jnp.int32, (ROW_TILE, LANES), 1)
    row = lax.broadcasted_iota(jnp.int32, (ROW_TILE, LANES), 0)
    freq = jnp.ones((ROW_TILE, LANES), jnp.float32)
    for bit, power in enumerate(FREQ_POWERS):
        freq = jnp.where((lane >> bit) & 1 == 1, freq * power, freq)
    column = lax.axis_index("batch")
    seg_pages = table_shape[2]
    first = segs + steps + column * segs * seg_pages
    for page in range(segs * seg_pages):
        seg, place = divmod(page, seg_pages)
        page_out[page] = integers_ref[first + place * segs + seg]
    for step in range(steps + 1):
        for tile in range(0, rows, ROW_TILE):
            index = block_start + (tile - step * rows) + row
            own_start = jnp.zeros(index.shape, jnp.int32)
            for seg in range(1, segs):
                own_start = jnp.where(index >= starts[seg], starts[seg], own_start)
            place = (prefix_len + index - own_start).astype(jnp.float32)
            sine, cosine = sine_cosine(place * freq)
            sine = jnp.where(lane < HALF, -sine, sine)
            cos_out, sin_out = ((cos_own, sin_own), (cos_last, sin_last), (cos_far, sin_far))[
                min(step, 2)
            ]
            span = pl.ds(max(step - 2, 0) * rows + tile, ROW_TILE)
            cos_out[span, :] = cosine
            sin_out[span, :] = sine
    for tile in range(0, rows, ROW_TILE):
        span = pl.ds(tile, ROW_TILE)
        query_index = block_start + tile + row
        own_start = jnp.zeros(query_index.shape, jnp.int32)
        first_page_token = jnp.zeros(query_index.shape, jnp.int32)
        for seg in range(1, segs):
            later = query_index >= starts[seg]
            own_start = jnp.where(later, starts[seg], own_start)
            first_page_token = jnp.where(later, seg * prefix_len, first_page_token)
        for step in range(steps + 1):
            limit = query_index
            if step > 0:
                limit = jnp.where(integers_ref[segs + step - 1] > 0, limit, -1)
            for column in range(0, rows, LANES):
                key_index = block_start + (column - step * rows) + lane
                seen = (key_index >= own_start) & (key_index <= limit)
                bias = jnp.where(seen, 0.0, HIDDEN)
                if step == 0:
                    own_bias[span, pl.ds(column, LANES)] = bias
                elif step == 1:
                    last_bias[span, pl.ds(column, LANES)] = bias
                else:
                    far_bias[span, pl.ds((step - 2) * rows + column, LANES)] = bias
        base = (steps - 1) * rows
        for column in range(0, far_bias.shape[1] - base, LANES):
            offset = column + lane - first_page_token
            seen = (offset >= 0) & (offset < prefix_len)
            far_bias[span, pl.ds(base + column, LANES)] = jnp.where(seen, 0.0, HIDDEN)


def tables(rows, pool_page, integers, segs, steps, table_shape):
    prefix_len = table_shape[2] * pool_page
    pages = table_shape[1] * table_shape[2]
    far_rows = (steps - 1) * rows
    far_keys = padded_keys(far_rows + segs * prefix_len)
    block = jax.ShapeDtypeStruct((rows, HEAD_SIZE), jnp.float32)
    far = jax.ShapeDtypeStruct((far_rows, HEAD_SIZE), jnp.float32)
    shapes = [
        jax.ShapeDtypeStruct((pages,), jnp.int32),
        *[block] * 4,
        far,
        far,
        *[jax.ShapeDtypeStruct((rows, rows), jnp.float32)] * 2,
        jax.ShapeDtypeStruct((rows, far_keys), jnp.float32),
    ]
    return pl.pallas_call(
        lambda *refs: tables_kernel(rows, steps, segs, prefix_len, table_shape, *refs),
        in_specs=[pl.BlockSpec(memory_space=pltpu.SMEM)],
        out_specs=[pl.BlockSpec(memory_space=pltpu.SMEM)]
        + [pl.BlockSpec(memory_space=pltpu.VMEM)] * (len(shapes) - 1),
        out_shape=shapes,
        compiler_params=pltpu.CompilerParams(vmem_limit_bytes=vmem_bytes(far_keys + far_rows)),
        cost_estimate=TABLES_COST,
        name="tables",
    )(integers)


def prepare_kernel(
    rows, cos_own, sin_own, q_ref, k_ref, v_ref, pool_ref, q_out, k_out, k_copy, v_copy, pool_copy
):
    for tile in range(0, rows, ROW_TILE):
        span = pl.ds(tile, ROW_TILE)
        cosine = cos_own[span, :]
        signed_sine = sin_own[span, :]
        for source, target in ((q_ref, q_out), (k_ref, k_out)):
            for start in range(0, source.shape[2], HEAD_SIZE):
                columns = pl.ds(start, HEAD_SIZE)
                turned = rotate(source[0, span, columns], cosine, signed_sine)
                target[0, span, columns] = turned
                if source is k_ref:
                    k_copy[0, span, columns] = turned
    v_copy[...] = v_ref[...]
    pool_copy[...] = pool_ref[...]


def prepare(cosine, signed_sine, queries, keys, values, pool):
    rows = queries.shape[1]
    whole = lambda part: (0, 0)
    by_part = lambda part: (0, 0, part)
    wide = pl.BlockSpec((1, rows, queries.shape[2] // PREPARE_STEPS), by_part)
    narrow = pl.BlockSpec((1, rows, keys.shape[2] // PREPARE_STEPS), by_part)
    some_pages = pl.BlockSpec(
        (pool.shape[0] // PREPARE_STEPS, *pool.shape[1:]), lambda part: (part, 0, 0)
    )
    table = pl.BlockSpec(cosine.shape, whole)
    return pl.pallas_call(
        lambda *refs: prepare_kernel(rows, *refs),
        grid=(PREPARE_STEPS,),
        in_specs=[table, table, wide, narrow, narrow, some_pages],
        out_specs=[wide, narrow, narrow, narrow, some_pages],
        out_shape=[
            jax.ShapeDtypeStruct(array.shape, array.dtype)
            for array in (queries, keys, keys, values, pool)
        ],
        compiler_params=pltpu.CompilerParams(vmem_limit_bytes=vmem_bytes(rows)),
        cost_estimate=PREPARE_COST,
        name="prepare",
    )(cosine, signed_sine, queries, keys, values, pool)


def stacked_queries(q_ref, part):
    return jnp.concatenate(
        [q_ref[0, :, pl.ds((part * GROUP + h) * HEAD_SIZE, HEAD_SIZE)] for h in range(GROUP)],
        axis=0,
    )


def rotate_rows(target, first, source, lanes, cos_ref, sin_ref):
    rows = source.shape[1]
    for tile in range(0, rows, ROW_TILE):
        span = pl.ds(first + tile, ROW_TILE)
        target[span, :] = rotate(
            source[0, pl.ds(tile, ROW_TILE), lanes], cos_ref[span, :], sin_ref[span, :]
        )


def own_kernel(rows, bias_ref, q_ref, k_ref, v_ref, level_ref, mean_ref, *work):
    k_parts, v_parts, scores, weights, tops = split_work(work)
    group = pl.program_id(0)

    @pl.when(group == 0)
    def _():
        fill_ones(v_parts)
        level_ref[...] = jnp.zeros(level_ref.shape, jnp.float32)

    for part in range(HEADS_PER_STEP):
        lanes = pl.ds(part * HEAD_SIZE, HEAD_SIZE)
        k_parts[part][...] = k_ref[0, :, lanes]
        v_parts[part][:, pl.ds(0, HEAD_SIZE)] = v_ref[0, :, lanes]

    fresh_heads(group, rows, k_parts, v_parts, scores, weights, tops,
                bias_ref, q_ref, mean_ref, level_ref)


def fresh_heads(
    group, rows, k_parts, v_parts, scores, weights, tops, bias_ref, q_ref, mean_ref, level_ref
):
    for part in range(HEADS_PER_STEP):
        score_part(part, q_ref, k_parts, scores)
    lane = lax.broadcasted_iota(jnp.int32, (rows, LANES), 1)
    for part in range(HEADS_PER_STEP):
        for start in range(0, GROUP * rows, SOFTMAX_TILE):
            span = pl.ds(start, SOFTMAX_TILE)
            bias = bias_ref[pl.ds(start % rows, SOFTMAX_TILE), :]
            score = scores[part][span, :] * EXP2_SCALE + bias
            highest = jnp.max(score, axis=1, keepdims=True)
            weights[part][span, :] = jnp.exp2(score - highest).astype(jnp.bfloat16)
            tops[part][span, :] = jnp.broadcast_to(highest, (SOFTMAX_TILE, LANES))
        summed = jnp.dot(weights[part][...], v_parts[part][...], preferred_element_type=jnp.float32)
        total = summed[:, HEAD_SIZE:]
        mean = (summed[:, :HEAD_SIZE] / total).astype(jnp.bfloat16)
        level = tops[part][...] + jnp.log2(total)
        for h in range(GROUP):
            own = part * GROUP + h
            span = slice(h * rows, (h + 1) * rows)
            mean_ref[:, pl.ds(own * HEAD_SIZE, HEAD_SIZE)] = mean[span]
            head = group * (HEADS_PER_STEP * GROUP) + own
            level_ref[...] = jnp.where(lane == head, level[span], level_ref[...])


def fill_ones(v_parts):
    for v_all in v_parts:
        v_all[:, pl.ds(HEAD_SIZE, HEAD_SIZE)] = jnp.ones((v_all.shape[0], HEAD_SIZE), jnp.bfloat16)


def split_work(work):
    return [work[i : i + HEADS_PER_STEP] for i in range(0, len(work), HEADS_PER_STEP)]


def score_part(part, q_ref, k_parts, scores):
    scores[part][...] = lax.dot_general(
        stacked_queries(q_ref, part), k_parts[part][...], (((1,), (1,)), ((), ())),
        preferred_element_type=jnp.float32,
    )


def work_shapes(rows, key_count, numbers=1):
    shapes = [
        pltpu.VMEM((key_count, HEAD_SIZE), jnp.bfloat16),
        pltpu.VMEM((key_count, 2 * HEAD_SIZE), jnp.bfloat16),
        pltpu.VMEM((GROUP * rows, key_count), jnp.float32),
        pltpu.VMEM((GROUP * rows, key_count), jnp.bfloat16),
        pltpu.VMEM((GROUP * rows, numbers * LANES), jnp.float32),
    ]
    return [shape for shape in shapes for _ in range(HEADS_PER_STEP)]


def attend_own(bias, query, key, value):
    rows, q_width = query.shape[1:]
    return pl.pallas_call(
        lambda *refs: own_kernel(rows, *refs),
        grid=(KEY_VALUE_HEADS // HEADS_PER_STEP,),
        in_specs=[*whole_specs([bias]), *step_specs([query, key, value])],
        out_specs=mean_specs(rows),
        out_shape=mean_shapes(rows, q_width),
        scratch_shapes=work_shapes(rows, rows),
        compiler_params=pltpu.CompilerParams(vmem_limit_bytes=vmem_bytes(rows)),
        cost_estimate=OWN_COST,
        name="own",
    )(bias, query, key, value)


def page_copies(start, table_ref, shards, paged, sem):
    pool_rows = shards[0].shape[0]
    column = lax.axis_index("batch")

    def copy(shard, place, page):
        return pltpu.make_async_copy(shard.at[place], paged.at[page], sem.at[page])

    for page in range(paged.shape[0]):
        if not start:
            copy(shards[0], 0, page).wait()
            continue
        number = table_ref[page]
        apart = lax.div(number, jnp.int32(pool_rows)) ^ column
        place = lax.rem(number, jnp.int32(pool_rows))
        for which, shard in enumerate(shards):

            @pl.when(apart == which)
            def _(shard=shard, place=place, page=page):
                copy(shard, place, page).start()


def join_heads(
    group, rows, k_parts, v_parts, scores, weights, shrinks, bias_ref, levels, means, q_ref, out_ref
):
    for part in range(HEADS_PER_STEP):
        score_part(part, q_ref, k_parts, scores)
    lane = lax.broadcasted_iota(jnp.int32, (SOFTMAX_TILE, LANES), 1)
    for part in range(HEADS_PER_STEP):
        for start in range(0, GROUP * rows, SOFTMAX_TILE):
            span = pl.ds(start, SOFTMAX_TILE)
            row_span = pl.ds(start % rows, SOFTMAX_TILE)
            head = group * (HEADS_PER_STEP * GROUP) + part * GROUP + start // rows
            score = scores[part][span, :] * EXP2_SCALE + bias_ref[row_span, :]
            highest = jnp.max(score, axis=1, keepdims=True)
            before = [
                jnp.sum(jnp.where(lane == head, level[row_span, :], 0.0), axis=1, keepdims=True)
                for level in levels
            ]
            for level in before:
                highest = jnp.maximum(highest, level)
            weights[part][span, :] = jnp.exp2(score - highest).astype(jnp.bfloat16)
            for which, level in enumerate(before):
                shrinks[part][span, pl.ds(which * LANES, LANES)] = jnp.broadcast_to(
                    jnp.exp2(level - highest), (SOFTMAX_TILE, LANES)
                )
        summed = jnp.dot(weights[part][...], v_parts[part][...], preferred_element_type=jnp.float32)
        for h in range(GROUP):
            lanes = pl.ds((part * GROUP + h) * HEAD_SIZE, HEAD_SIZE)
            span = slice(h * rows, (h + 1) * rows)
            above, total = summed[span, :HEAD_SIZE], summed[span, HEAD_SIZE:]
            for which, mean in enumerate(means):
                shrink = shrinks[part][pl.ds(h * rows, rows), pl.ds(which * LANES, LANES)]
                above += mean[:, lanes].astype(jnp.float32) * shrink
                total += shrink
            out_ref[0, :, lanes] = (above / total).astype(jnp.bfloat16)


def far_kernel(rows, columns_count, blocks, kv_width, *refs):
    table_ref, cos_ref, sin_ref, bias_ref, q_ref = refs[:5]
    shards, refs = refs[5 : 5 + columns_count], refs[5 + columns_count :]
    keys, values, refs = refs[:blocks], refs[blocks : 2 * blocks], refs[2 * blocks :]
    level_out, mean_out, paged, sem = refs[:4]
    work = split_work(refs[4:])
    k_parts, v_parts = work[:2]
    group = pl.program_id(0)
    prefix_rows = paged.shape[0] * paged.shape[1]
    base = blocks * rows

    @pl.when(group == 0)
    def _():
        page_copies(True, table_ref, shards, paged, sem)
        fill_ones(v_parts)
        level_out[...] = jnp.zeros(level_out.shape, jnp.float32)
        rest = k_parts[0].shape[0] - base - prefix_rows
        if rest:
            blank = jnp.zeros((rest, HEAD_SIZE), jnp.bfloat16)
            for k_all, v_all in zip(k_parts, v_parts):
                k_all[pl.ds(base + prefix_rows, rest), :] = blank
                v_all[pl.ds(base + prefix_rows, rest), pl.ds(0, HEAD_SIZE)] = blank

    for part in range(HEADS_PER_STEP):
        lanes = pl.ds(part * HEAD_SIZE, HEAD_SIZE)
        for block in range(blocks):
            rotate_rows(k_parts[part], block * rows, keys[block], lanes, cos_ref, sin_ref)
            span = pl.ds(block * rows, rows)
            v_parts[part][span, pl.ds(0, HEAD_SIZE)] = values[block][0, :, lanes]

    @pl.when(group == 0)
    def _():
        page_copies(False, table_ref, shards, paged, sem)

    for part in range(HEADS_PER_STEP):
        start = (group * HEADS_PER_STEP + part) * HEAD_SIZE
        columns = pl.ds(pl.multiple_of(start, HEAD_SIZE), HEAD_SIZE)
        value_columns = pl.ds(pl.multiple_of(kv_width + start, HEAD_SIZE), HEAD_SIZE)
        span = pl.ds(base, prefix_rows)
        k_parts[part][span, :] = paged[:, :, columns].reshape(prefix_rows, HEAD_SIZE)
        v_parts[part][span, pl.ds(0, HEAD_SIZE)] = paged[:, :, value_columns].reshape(
            prefix_rows, HEAD_SIZE
        )
    fresh_heads(group, rows, *work, bias_ref, q_ref, mean_out, level_out)


def last_kernel(
    rows, cos_ref, sin_ref, bias_ref, q_ref, own_level, far_level, own_mean, far_mean,
    key_ref, swapped_value, passed_value, direct_value, out_ref, *refs,
):
    work = split_work(refs)
    k_parts, v_parts = work[:2]
    group = pl.program_id(0)
    even = lax.rem(lax.axis_index("blk"), 2) == 0

    @pl.when(group == 0)
    def _():
        fill_ones(v_parts)

    for part in range(HEADS_PER_STEP):
        lanes = pl.ds(part * HEAD_SIZE, HEAD_SIZE)
        rotate_rows(k_parts[part], 0, key_ref, lanes, cos_ref, sin_ref)
        start = 0
        for arrived in (passed_value, direct_value):
            span = pl.ds(start, arrived.shape[1])
            v_parts[part][span, pl.ds(0, HEAD_SIZE)] = jnp.where(
                even, arrived[0, :, lanes], swapped_value[0, span, lanes]
            )
            start += arrived.shape[1]
    levels, means = (own_level, far_level), (own_mean, far_mean)
    join_heads(group, rows, *work, bias_ref, levels, means, q_ref, out_ref)


def mean_shapes(rows, q_width):
    return [
        jax.ShapeDtypeStruct((rows, LANES), jnp.float32),
        jax.ShapeDtypeStruct((rows, q_width), jnp.bfloat16),
    ]


def mean_specs(rows):
    return [
        pl.BlockSpec((rows, LANES), lambda group: (0, 0)),
        pl.BlockSpec((rows, HEADS_PER_STEP * GROUP * HEAD_SIZE), lambda group: (0, group)),
    ]


def step_specs(arrays):
    groups = KEY_VALUE_HEADS // HEADS_PER_STEP
    return [
        pl.BlockSpec((1, array.shape[1], array.shape[2] // groups), lambda group: (0, 0, group))
        for array in arrays
    ]


def whole_specs(arrays):
    return [pl.BlockSpec(array.shape, lambda group: (0, 0)) for array in arrays]


def attend_far(cosine, signed_sine, bias, query, arrived, numbers, shards):
    rows, q_width = query.shape[1:]
    return pl.pallas_call(
        lambda *refs: far_kernel(
            rows, len(shards), len(arrived) // 2, arrived[0].shape[2], *refs
        ),
        grid=(KEY_VALUE_HEADS // HEADS_PER_STEP,),
        in_specs=[
            pl.BlockSpec(memory_space=pltpu.SMEM),
            *whole_specs([cosine, signed_sine, bias]),
            *step_specs([query]),
            *[pl.BlockSpec(memory_space=pl.ANY)] * len(shards),
            *step_specs(arrived),
        ],
        out_specs=mean_specs(rows),
        out_shape=mean_shapes(rows, q_width),
        scratch_shapes=[
            pltpu.VMEM(numbers.shape + shards[0].shape[1:], jnp.bfloat16),
            pltpu.SemaphoreType.DMA(numbers.shape),
            *work_shapes(rows, bias.shape[1]),
        ],
        compiler_params=pltpu.CompilerParams(vmem_limit_bytes=vmem_bytes(bias.shape[1])),
        cost_estimate=FAR_COST,
        name="far",
    )(numbers, cosine, signed_sine, bias, query, *shards, *arrived)


def attend_last(cosine, signed_sine, bias, query, own, far, arrived):
    rows = query.shape[1]
    levels, means = zip(own, far)
    return pl.pallas_call(
        lambda *refs: last_kernel(rows, *refs),
        grid=(KEY_VALUE_HEADS // HEADS_PER_STEP,),
        in_specs=[
            *whole_specs([cosine, signed_sine, bias]),
            *step_specs([query]),
            *mean_specs(rows)[:1] * 2,
            *mean_specs(rows)[1:] * 2,
            *step_specs(arrived),
        ],
        out_specs=step_specs([query])[0],
        out_shape=jax.ShapeDtypeStruct(query.shape, jnp.bfloat16),
        scratch_shapes=work_shapes(rows, bias.shape[1], 2),
        compiler_params=pltpu.CompilerParams(vmem_limit_bytes=vmem_bytes(bias.shape[1])),
        cost_estimate=LAST_COST,
        name="last",
    )(cosine, signed_sine, bias, query, *levels, *means, *arrived)


def pool_shards(pool, after):
    count = lax.axis_size("batch")

    def swapped(shard, bit):
        return lax.ppermute(shard, "batch", [(c, c ^ bit) for c in range(count)])

    bits = [count >> (step + 1) for step in range(count.bit_length() - 1)]
    shards = {0: pool, **{bit: swapped(pool, bit) for bit in bits}}
    shards, after = lax.optimization_barrier((shards, after))
    for bit in reversed(bits):
        for apart, shard in list(shards.items()):
            if apart ^ bit not in shards:
                shards[apart ^ bit] = swapped(shard, bit)
    return [shards[apart] for apart in range(count)]


def per_device(queries, keys, values, seg_ids, lengths, live, page_table, pool):
    steps = live.shape[2]
    blocks = lax.axis_size("blk")
    far = [shifted(keys, 2), shifted(values, 2)]
    for step in range(3, steps + 1):
        far += [shifted(keys, step), shifted(values, step)]
    swap = [(j, j ^ 1) for j in range(blocks)]
    even = lax.rem(lax.axis_index("blk"), 2) == 0
    swapped_value = lax.ppermute(values, "blk", swap)
    integers = jnp.concatenate([lengths.ravel(), live.ravel(), jnp.swapaxes(page_table, 1, 2).ravel()])
    (
        table, cos_own, sin_own, cos_last, sin_last, cos_far, sin_far, own_bias, last_bias, far_bias
    ) = tables(keys.shape[1], pool.shape[1], integers, lengths.shape[1], steps, page_table.shape)
    query, key, near_key, near_value, own_shard = prepare(
        cos_own, sin_own, queries, keys, values, pool
    )
    to_swap = jnp.where(even, keys, far[0])
    far_key = lax.ppermute(to_swap, "blk", swap)
    split = values.shape[1] * 5 // 8
    passed_value = lax.ppermute(
        swapped_value[:, :split], "blk", [(j, j + 2) for j in range(0, blocks - 2, 2)]
    )
    shards = pool_shards(pool, (near_key, to_swap, swapped_value))
    later_values = values[:, split:]
    direct_value = lax.ppermute(
        later_values, "blk", [(j, j + 1) for j in range(1, blocks - 1, 2)]
    )
    own = attend_own(own_bias, query, near_key, near_value)
    earlier = attend_far(
        cos_far, sin_far, far_bias, query, [*far[::2], *far[1::2]], table, [own_shard, *shards[1:]]
    )
    result = attend_last(
        cos_last, sin_last, last_bias, query, own, earlier,
        [far_key, swapped_value, passed_value, direct_value],
    )
    return (result, key)


def solution(mesh):
    in_specs = (
        P("batch", "blk", None),
        P("batch", "blk", None),
        P("batch", "blk", None),
        P("batch", "blk"),
        P("batch", None),
        P("batch", "blk", None),
        P(),
        P("batch", None, None),
    )
    out_specs = (P("batch", "blk", None), P("batch", "blk", None))
    return jax.shard_map(
        per_device, mesh=mesh, in_specs=in_specs, out_specs=out_specs, check_vma=False
    )
```

```python
import math

import jax
import jax.numpy as jnp
import numpy as np
from jax import lax
from jax.experimental import pallas as pl
from jax.experimental.pallas import tpu as pltpu
from jax.sharding import PartitionSpec as P

QUERY_HEADS = 16
KEY_VALUE_HEADS = 8
HEAD_SIZE = 128
GROUP = QUERY_HEADS // KEY_VALUE_HEADS
HALF = HEAD_SIZE // 2
ROPE_BASE = 1000000.0
HIDDEN = -1e30
LANES = 128
ROW_TILE = 64
SOFTMAX_TILE = 16
HEADS_PER_STEP = 2
PREPARE_STEPS = 2


def cost(flops):
    return pl.CostEstimate(flops=flops, bytes_accessed=0, transcendentals=0)


TABLES_COST = cost(2_000_000_000)
PREPARE_COST = cost(0)
OWN_COST = cost(0)
FAR_COST = cost(0)
LAST_COST = cost(0)
EXP2_SCALE = math.log2(math.e) / math.sqrt(HEAD_SIZE)

FREQ_POWERS = [float(ROPE_BASE ** (-(2**k) / HALF)) for k in range(HALF.bit_length() - 1)]

PIO2_A = float(np.float32(1.5703125))
PIO2_B = float(np.float32(4.837512969970703125e-4))
PIO2_C = float(np.float32(math.pi / 2 - 1.5703125 - 4.837512969970703125e-4))


def shifted(value, steps):
    count = lax.axis_size("blk")
    return lax.ppermute(value, "blk", [(source, source + steps) for source in range(count - steps)])


def padded_keys(count):
    return -(-count // LANES) * LANES


def vmem_bytes(key_count):
    return 16 * 1024 * (1024 + key_count)


def sine_cosine(angle):
    turns = jnp.floor(angle * (2.0 / math.pi) + 0.5)
    rest = ((angle - turns * PIO2_A) - turns * PIO2_B) - turns * PIO2_C
    square = rest * rest
    sine = rest + rest * square * (
        -1.6666654611e-1 + square * (8.3321608736e-3 - square * 1.9515295891e-4)
    )
    cosine = 1.0 - 0.5 * square + square * square * (
        4.166664568298827e-2 + square * (-1.388731625493765e-3 + square * 2.443315711809948e-5)
    )
    quadrant = turns.astype(jnp.int32) & 3
    swapped = (quadrant & 1) == 1
    sine_out = jnp.where(swapped, cosine, sine)
    cosine_out = jnp.where(swapped, sine, cosine)
    sine_out = jnp.where(quadrant >= 2, -sine_out, sine_out)
    cosine_out = jnp.where((quadrant == 1) | (quadrant == 2), -cosine_out, cosine_out)
    return sine_out, cosine_out


def half_turn():
    row = lax.broadcasted_iota(jnp.int32, (HEAD_SIZE, HEAD_SIZE), 0)
    column = lax.broadcasted_iota(jnp.int32, (HEAD_SIZE, HEAD_SIZE), 1)
    return jnp.where((row ^ HALF) == column, 1.0, 0.0).astype(jnp.bfloat16)


def rotate(source, lanes, turn, cos_ref, sin_ref, table_first, targets):
    rows = source.shape[1]
    turned = jnp.dot(source[0, :, lanes], turn, preferred_element_type=jnp.float32)
    for tile in range(0, rows, ROW_TILE):
        table = pl.ds(table_first + tile, ROW_TILE)
        wide = source[0, pl.ds(tile, ROW_TILE), lanes].astype(jnp.float32)
        result = wide * cos_ref[table, :] + turned[tile : tile + ROW_TILE] * sin_ref[table, :]
        for target in targets:
            target(pl.ds(tile, ROW_TILE), result.astype(jnp.bfloat16))


def tables_kernel(
    rows, steps, segs, prefix_len, table_shape, integers_ref,
    page_out, cos_own, sin_own, cos_last, sin_last, cos_far, sin_far, own_bias, last_bias, far_bias,
):
    block_start = lax.axis_index("blk") * rows
    starts = [jnp.int32(0)]
    for seg in range(1, segs):
        starts.append(starts[-1] + integers_ref[seg - 1])
    lane = lax.broadcasted_iota(jnp.int32, (ROW_TILE, LANES), 1)
    row = lax.broadcasted_iota(jnp.int32, (ROW_TILE, LANES), 0)
    freq = jnp.ones((ROW_TILE, LANES), jnp.float32)
    for bit, power in enumerate(FREQ_POWERS):
        freq = jnp.where((lane >> bit) & 1 == 1, freq * power, freq)
    column = lax.axis_index("batch")
    seg_pages = table_shape[2]
    first = segs + steps + column * segs * seg_pages
    for page in range(segs * seg_pages):
        seg, place = divmod(page, seg_pages)
        page_out[page] = integers_ref[first + place * segs + seg]
    for step in range(steps + 1):
        for tile in range(0, rows, ROW_TILE):
            index = block_start + (tile - step * rows) + row
            own_start = jnp.zeros(index.shape, jnp.int32)
            for seg in range(1, segs):
                own_start = jnp.where(index >= starts[seg], starts[seg], own_start)
            place = (prefix_len + index - own_start).astype(jnp.float32)
            sine, cosine = sine_cosine(place * freq)
            sine = jnp.where(lane < HALF, -sine, sine)
            cos_out, sin_out = ((cos_own, sin_own), (cos_last, sin_last), (cos_far, sin_far))[
                min(step, 2)
            ]
            span = pl.ds(max(step - 2, 0) * rows + tile, ROW_TILE)
            cos_out[span, :] = cosine
            sin_out[span, :] = sine
    for tile in range(0, rows, ROW_TILE):
        span = pl.ds(tile, ROW_TILE)
        query_index = block_start + tile + row
        own_start = jnp.zeros(query_index.shape, jnp.int32)
        first_page_token = jnp.zeros(query_index.shape, jnp.int32)
        for seg in range(1, segs):
            later = query_index >= starts[seg]
            own_start = jnp.where(later, starts[seg], own_start)
            first_page_token = jnp.where(later, seg * prefix_len, first_page_token)
        for step in range(steps + 1):
            limit = query_index
            if step > 0:
                limit = jnp.where(integers_ref[segs + step - 1] > 0, limit, -1)
            for column in range(0, rows, LANES):
                key_index = block_start + (column - step * rows) + lane
                seen = (key_index >= own_start) & (key_index <= limit)
                bias = jnp.where(seen, 0.0, HIDDEN)
                if step == 0:
                    own_bias[span, pl.ds(column, LANES)] = bias
                elif step == 1:
                    last_bias[span, pl.ds(column, LANES)] = bias
                else:
                    far_bias[span, pl.ds((step - 2) * rows + column, LANES)] = bias
        base = (steps - 1) * rows
        for column in range(0, far_bias.shape[1] - base, LANES):
            offset = column + lane - first_page_token
            seen = (offset >= 0) & (offset < prefix_len)
            far_bias[span, pl.ds(base + column, LANES)] = jnp.where(seen, 0.0, HIDDEN)


def tables(rows, pool_page, integers, segs, steps, table_shape):
    prefix_len = table_shape[2] * pool_page
    pages = table_shape[1] * table_shape[2]
    far_rows = (steps - 1) * rows
    far_keys = padded_keys(far_rows + segs * prefix_len)
    block = jax.ShapeDtypeStruct((rows, HEAD_SIZE), jnp.float32)
    far = jax.ShapeDtypeStruct((far_rows, HEAD_SIZE), jnp.float32)
    shapes = [
        jax.ShapeDtypeStruct((pages,), jnp.int32),
        *[block] * 4,
        far,
        far,
        *[jax.ShapeDtypeStruct((rows, rows), jnp.float32)] * 2,
        jax.ShapeDtypeStruct((rows, far_keys), jnp.float32),
    ]
    return pl.pallas_call(
        lambda *refs: tables_kernel(rows, steps, segs, prefix_len, table_shape, *refs),
        in_specs=[pl.BlockSpec(memory_space=pltpu.SMEM)],
        out_specs=[pl.BlockSpec(memory_space=pltpu.SMEM)]
        + [pl.BlockSpec(memory_space=pltpu.VMEM)] * (len(shapes) - 1),
        out_shape=shapes,
        compiler_params=pltpu.CompilerParams(vmem_limit_bytes=vmem_bytes(far_keys + far_rows)),
        cost_estimate=TABLES_COST,
        name="tables",
    )(integers)


def prepare_kernel(
    rows, cos_own, sin_own, q_ref, k_ref, v_ref, pool_ref, q_out, k_out, k_copy, v_copy, pool_copy
):
    turn = half_turn()
    for source, targets in ((q_ref, (q_out,)), (k_ref, (k_out, k_copy))):
        for start in range(0, source.shape[2], HEAD_SIZE):
            lanes = pl.ds(start, HEAD_SIZE)

            def writer(target, lanes=lanes):
                def write(span, values):
                    target[0, span, lanes] = values

                return write

            rotate(source, lanes, turn, cos_own, sin_own, 0, [writer(t) for t in targets])
    v_copy[...] = v_ref[...]
    pool_copy[...] = pool_ref[...]


def prepare(cosine, signed_sine, queries, keys, values, pool):
    rows = queries.shape[1]
    whole = lambda part: (0, 0)
    by_part = lambda part: (0, 0, part)
    wide = pl.BlockSpec((1, rows, queries.shape[2] // PREPARE_STEPS), by_part)
    narrow = pl.BlockSpec((1, rows, keys.shape[2] // PREPARE_STEPS), by_part)
    some_pages = pl.BlockSpec(
        (pool.shape[0] // PREPARE_STEPS, *pool.shape[1:]), lambda part: (part, 0, 0)
    )
    table = pl.BlockSpec(cosine.shape, whole)
    return pl.pallas_call(
        lambda *refs: prepare_kernel(rows, *refs),
        grid=(PREPARE_STEPS,),
        in_specs=[table, table, wide, narrow, narrow, some_pages],
        out_specs=[wide, narrow, narrow, narrow, some_pages],
        out_shape=[
            jax.ShapeDtypeStruct(array.shape, array.dtype)
            for array in (queries, keys, keys, values, pool)
        ],
        compiler_params=pltpu.CompilerParams(vmem_limit_bytes=vmem_bytes(rows)),
        cost_estimate=PREPARE_COST,
        name="prepare",
    )(cosine, signed_sine, queries, keys, values, pool)


def stacked_queries(q_ref, part):
    return jnp.concatenate(
        [q_ref[0, :, pl.ds((part * GROUP + h) * HEAD_SIZE, HEAD_SIZE)] for h in range(GROUP)],
        axis=0,
    )


def rotate_rows(target, first, source, lanes, turn, cos_ref, sin_ref):
    def write(span, values):
        target[pl.ds(first + span.start, span.size), :] = values

    rotate(source, lanes, turn, cos_ref, sin_ref, first, [write])


def own_kernel(rows, bias_ref, q_ref, k_ref, v_ref, level_ref, mean_ref, *work):
    k_parts, v_parts, scores, weights, tops = split_work(work)
    group = pl.program_id(0)

    @pl.when(group == 0)
    def _():
        fill_ones(v_parts)
        level_ref[...] = jnp.zeros(level_ref.shape, jnp.float32)

    for part in range(HEADS_PER_STEP):
        lanes = pl.ds(part * HEAD_SIZE, HEAD_SIZE)
        k_parts[part][...] = k_ref[0, :, lanes]
        v_parts[part][:, pl.ds(0, HEAD_SIZE)] = v_ref[0, :, lanes]

    score_parts(q_ref, k_parts, scores)
    fresh_heads(group, rows, v_parts, scores, weights, tops, bias_ref, mean_ref, level_ref, 0)


def fresh_heads(
    group, rows, v_parts, scores, weights, tops, bias_ref, mean_ref, level_ref, first_lane
):
    lane = lax.broadcasted_iota(jnp.int32, (rows, LANES), 1)
    for part in range(HEADS_PER_STEP):
        for start in range(0, GROUP * rows, SOFTMAX_TILE):
            span = pl.ds(start, SOFTMAX_TILE)
            bias = bias_ref[pl.ds(start % rows, SOFTMAX_TILE), :]
            score = scores[part][span, :] * EXP2_SCALE + bias
            highest = jnp.max(score, axis=1, keepdims=True)
            weights[part][span, :] = jnp.exp2(score - highest).astype(jnp.bfloat16)
            tops[part][span, :] = jnp.broadcast_to(highest, (SOFTMAX_TILE, LANES))
        summed = jnp.dot(weights[part][...], v_parts[part][...], preferred_element_type=jnp.float32)
        total = summed[:, HEAD_SIZE:]
        mean = (summed[:, :HEAD_SIZE] / total).astype(jnp.bfloat16)
        level = tops[part][...] + jnp.log2(total)
        for h in range(GROUP):
            own = part * GROUP + h
            span = slice(h * rows, (h + 1) * rows)
            mean_ref[:, pl.ds(own * HEAD_SIZE, HEAD_SIZE)] = mean[span]
            head = group * (HEADS_PER_STEP * GROUP) + own
            level_ref[...] = jnp.where(lane == first_lane + head, level[span], level_ref[...])


def fill_ones(v_parts):
    for v_all in v_parts:
        v_all[:, pl.ds(HEAD_SIZE, HEAD_SIZE)] = jnp.ones((v_all.shape[0], HEAD_SIZE), jnp.bfloat16)


def split_work(work):
    return [work[i : i + HEADS_PER_STEP] for i in range(0, len(work), HEADS_PER_STEP)]


def score_parts(q_ref, k_parts, scores, first=0, count=None):
    for part in range(HEADS_PER_STEP):
        span = pl.ds(first, k_parts[part].shape[0] - first if count is None else count)
        scores[part][:, span] = lax.dot_general(
            stacked_queries(q_ref, part), k_parts[part][span, :], (((1,), (1,)), ((), ())),
            preferred_element_type=jnp.float32,
        )


def work_shapes(rows, key_count, last=False):
    shapes = [
        pltpu.VMEM((key_count, HEAD_SIZE), jnp.bfloat16),
        pltpu.VMEM((key_count, 2 * HEAD_SIZE), jnp.bfloat16),
        pltpu.VMEM((GROUP * rows, key_count), jnp.float32),
        pltpu.VMEM((GROUP * rows, key_count), jnp.bfloat16),
        pltpu.VMEM((GROUP * rows, 2 * LANES), jnp.bfloat16)
        if last
        else pltpu.VMEM((GROUP * rows, LANES), jnp.float32),
    ]
    return [shape for shape in shapes for _ in range(HEADS_PER_STEP)]


def attend_own(bias, query, key, value):
    rows, q_width = query.shape[1:]
    return pl.pallas_call(
        lambda *refs: own_kernel(rows, *refs),
        grid=(KEY_VALUE_HEADS // HEADS_PER_STEP,),
        in_specs=[*whole_specs([bias]), *step_specs([query, key, value])],
        out_specs=mean_specs(rows),
        out_shape=mean_shapes(rows, q_width),
        scratch_shapes=work_shapes(rows, rows),
        compiler_params=pltpu.CompilerParams(vmem_limit_bytes=vmem_bytes(rows)),
        cost_estimate=OWN_COST,
        name="own",
    )(bias, query, key, value)


def page_copies(start, table_ref, shards, paged, sem):
    pool_rows = shards[0].shape[0]
    column = lax.axis_index("batch")

    def copy(shard, place, page):
        return pltpu.make_async_copy(shard.at[place], paged.at[page], sem.at[page])

    for page in range(paged.shape[0]):
        if not start:
            copy(shards[0], 0, page).wait()
            continue
        number = table_ref[page]
        apart = lax.div(number, jnp.int32(pool_rows)) ^ column
        place = lax.rem(number, jnp.int32(pool_rows))
        for which, shard in enumerate(shards):

            @pl.when(apart == which)
            def _(shard=shard, place=place, page=page):
                copy(shard, place, page).start()


def spread(parts):
    row = lax.broadcasted_iota(jnp.int32, (2 * LANES, parts * LANES), 0) & (LANES - 1)
    column = lax.broadcasted_iota(jnp.int32, (2 * LANES, parts * LANES), 1)
    first = (column // LANES) * QUERY_HEADS
    return jnp.where((row >= first) & (row < first + QUERY_HEADS), 1.0, 0.0).astype(jnp.bfloat16)


def join_heads(
    group, rows, k_parts, v_parts, scores, weights, early, bias_ref, levels, means, q_ref, out_ref
):
    score_parts(q_ref, k_parts, scores)
    lane = lax.broadcasted_iota(jnp.int32, (SOFTMAX_TILE, LANES), 1)
    to_lanes = spread(len(means))
    for part in range(HEADS_PER_STEP):
        for start in range(0, GROUP * rows, SOFTMAX_TILE):
            span = pl.ds(start, SOFTMAX_TILE)
            row_span = pl.ds(start % rows, SOFTMAX_TILE)
            head = group * (HEADS_PER_STEP * GROUP) + part * GROUP + start // rows
            score = scores[part][span, :] * EXP2_SCALE + bias_ref[row_span, :]
            level = sum(ref[row_span, :] for ref in levels)
            mine = (lane & (QUERY_HEADS - 1)) == head
            level = jnp.where(mine & (lane < len(means) * QUERY_HEADS), level, HIDDEN)
            highest = level
            for column in range(0, score.shape[1], LANES):
                highest = jnp.maximum(highest, score[:, column : column + LANES])
            highest = jnp.max(highest, axis=1, keepdims=True)
            weights[part][span, :] = jnp.exp2(score - highest).astype(jnp.bfloat16)
            before = jnp.exp2(level - highest)
            high = before.astype(jnp.bfloat16)
            early[part][span, pl.ds(0, LANES)] = high
            early[part][span, pl.ds(LANES, LANES)] = (
                before - high.astype(jnp.float32)
            ).astype(jnp.bfloat16)
        summed = jnp.dot(weights[part][...], v_parts[part][...], preferred_element_type=jnp.float32)
        shrinks = jnp.dot(early[part][...], to_lanes, preferred_element_type=jnp.float32)
        for h in range(GROUP):
            lanes = pl.ds((part * GROUP + h) * HEAD_SIZE, HEAD_SIZE)
            span = slice(h * rows, (h + 1) * rows)
            above, total = summed[span, :HEAD_SIZE], summed[span, HEAD_SIZE:]
            for which, mean in enumerate(means):
                shrink = shrinks[span, which * LANES : (which + 1) * LANES]
                above += mean[:, lanes].astype(jnp.float32) * shrink
                total += shrink
            out_ref[0, :, lanes] = (above / total).astype(jnp.bfloat16)


def far_kernel(rows, columns_count, blocks, kv_width, *refs):
    table_ref, cos_ref, sin_ref, bias_ref, q_ref = refs[:5]
    shards, refs = refs[5 : 5 + columns_count], refs[5 + columns_count :]
    keys, values, refs = refs[:blocks], refs[blocks : 2 * blocks], refs[2 * blocks :]
    level_out, mean_out, paged, sem = refs[:4]
    work = split_work(refs[4:])
    k_parts, v_parts = work[:2]
    group = pl.program_id(0)
    prefix_rows = paged.shape[0] * paged.shape[1]
    base = blocks * rows

    @pl.when(group == 0)
    def _():
        page_copies(True, table_ref, shards, paged, sem)
        fill_ones(v_parts)
        level_out[...] = jnp.zeros(level_out.shape, jnp.float32)
        rest = k_parts[0].shape[0] - base - prefix_rows
        if rest:
            blank = jnp.zeros((rest, HEAD_SIZE), jnp.bfloat16)
            for k_all, v_all in zip(k_parts, v_parts):
                k_all[pl.ds(base + prefix_rows, rest), :] = blank
                v_all[pl.ds(base + prefix_rows, rest), pl.ds(0, HEAD_SIZE)] = blank

    turn = half_turn()
    for part in range(HEADS_PER_STEP):
        lanes = pl.ds(part * HEAD_SIZE, HEAD_SIZE)
        for block in range(blocks):
            rotate_rows(k_parts[part], block * rows, keys[block], lanes, turn, cos_ref, sin_ref)
            span = pl.ds(block * rows, rows)
            v_parts[part][span, pl.ds(0, HEAD_SIZE)] = values[block][0, :, lanes]

    score_parts(q_ref, k_parts, work[2], 0, base)

    @pl.when(group == 0)
    def _():
        page_copies(False, table_ref, shards, paged, sem)

    for part in range(HEADS_PER_STEP):
        start = (group * HEADS_PER_STEP + part) * HEAD_SIZE
        columns = pl.ds(pl.multiple_of(start, HEAD_SIZE), HEAD_SIZE)
        value_columns = pl.ds(pl.multiple_of(kv_width + start, HEAD_SIZE), HEAD_SIZE)
        span = pl.ds(base, prefix_rows)
        k_parts[part][span, :] = paged[:, :, columns].reshape(prefix_rows, HEAD_SIZE)
        v_parts[part][span, pl.ds(0, HEAD_SIZE)] = paged[:, :, value_columns].reshape(
            prefix_rows, HEAD_SIZE
        )
    score_parts(q_ref, k_parts, work[2], base)
    fresh_heads(group, rows, *work[1:], bias_ref, mean_out, level_out, QUERY_HEADS)


def last_kernel(
    rows, cos_ref, sin_ref, bias_ref, q_ref, own_level, far_level, own_mean, far_mean,
    key_ref, swapped_value, passed_value, direct_value, out_ref, *refs,
):
    work = split_work(refs)
    k_parts, v_parts = work[:2]
    group = pl.program_id(0)
    even = lax.rem(lax.axis_index("blk"), 2) == 0

    @pl.when(group == 0)
    def _():
        fill_ones(v_parts)

    turn = half_turn()
    for part in range(HEADS_PER_STEP):
        lanes = pl.ds(part * HEAD_SIZE, HEAD_SIZE)
        rotate_rows(k_parts[part], 0, key_ref, lanes, turn, cos_ref, sin_ref)
        start = 0
        for arrived in (passed_value, direct_value):
            span = pl.ds(start, arrived.shape[1])
            v_parts[part][span, pl.ds(0, HEAD_SIZE)] = jnp.where(
                even, arrived[0, :, lanes], swapped_value[0, span, lanes]
            )
            start += arrived.shape[1]
    levels, means = (own_level, far_level), (own_mean, far_mean)
    join_heads(group, rows, *work, bias_ref, levels, means, q_ref, out_ref)


def mean_shapes(rows, q_width):
    return [
        jax.ShapeDtypeStruct((rows, LANES), jnp.float32),
        jax.ShapeDtypeStruct((rows, q_width), jnp.bfloat16),
    ]


def mean_specs(rows):
    return [
        pl.BlockSpec((rows, LANES), lambda group: (0, 0)),
        pl.BlockSpec((rows, HEADS_PER_STEP * GROUP * HEAD_SIZE), lambda group: (0, group)),
    ]


def step_specs(arrays):
    groups = KEY_VALUE_HEADS // HEADS_PER_STEP
    return [
        pl.BlockSpec((1, array.shape[1], array.shape[2] // groups), lambda group: (0, 0, group))
        for array in arrays
    ]


def whole_specs(arrays):
    return [pl.BlockSpec(array.shape, lambda group: (0, 0)) for array in arrays]


def attend_far(cosine, signed_sine, bias, query, arrived, numbers, shards):
    rows, q_width = query.shape[1:]
    return pl.pallas_call(
        lambda *refs: far_kernel(
            rows, len(shards), len(arrived) // 2, arrived[0].shape[2], *refs
        ),
        grid=(KEY_VALUE_HEADS // HEADS_PER_STEP,),
        in_specs=[
            pl.BlockSpec(memory_space=pltpu.SMEM),
            *whole_specs([cosine, signed_sine, bias]),
            *step_specs([query]),
            *[pl.BlockSpec(memory_space=pl.ANY)] * len(shards),
            *step_specs(arrived),
        ],
        out_specs=mean_specs(rows),
        out_shape=mean_shapes(rows, q_width),
        scratch_shapes=[
            pltpu.VMEM(numbers.shape + shards[0].shape[1:], jnp.bfloat16),
            pltpu.SemaphoreType.DMA(numbers.shape),
            *work_shapes(rows, bias.shape[1]),
        ],
        compiler_params=pltpu.CompilerParams(vmem_limit_bytes=vmem_bytes(bias.shape[1])),
        cost_estimate=FAR_COST,
        name="far",
    )(numbers, cosine, signed_sine, bias, query, *shards, *arrived)


def attend_last(cosine, signed_sine, bias, query, own, far, arrived):
    rows = query.shape[1]
    levels, means = zip(own, far)
    return pl.pallas_call(
        lambda *refs: last_kernel(rows, *refs),
        grid=(KEY_VALUE_HEADS // HEADS_PER_STEP,),
        in_specs=[
            *whole_specs([cosine, signed_sine, bias]),
            *step_specs([query]),
            *mean_specs(rows)[:1] * 2,
            *mean_specs(rows)[1:] * 2,
            *step_specs(arrived),
        ],
        out_specs=step_specs([query])[0],
        out_shape=jax.ShapeDtypeStruct(query.shape, jnp.bfloat16),
        scratch_shapes=work_shapes(rows, bias.shape[1], last=True),
        compiler_params=pltpu.CompilerParams(vmem_limit_bytes=vmem_bytes(bias.shape[1])),
        cost_estimate=LAST_COST,
        name="last",
    )(cosine, signed_sine, bias, query, *levels, *means, *arrived)


def pool_shards(pool, after):
    count = lax.axis_size("batch")

    def swapped(shard, bit):
        return lax.ppermute(shard, "batch", [(c, c ^ bit) for c in range(count)])

    bits = [count >> (step + 1) for step in range(count.bit_length() - 1)]
    shards = {0: pool, **{bit: swapped(pool, bit) for bit in bits}}
    shards, after = lax.optimization_barrier((shards, after))
    for bit in reversed(bits):
        for apart, shard in list(shards.items()):
            if apart ^ bit not in shards:
                shards[apart ^ bit] = swapped(shard, bit)
    return [shards[apart] for apart in range(count)]


def per_device(queries, keys, values, seg_ids, lengths, live, page_table, pool):
    steps = live.shape[2]
    blocks = lax.axis_size("blk")
    far = [shifted(keys, 2), shifted(values, 2)]
    for step in range(3, steps + 1):
        far += [shifted(keys, step), shifted(values, step)]
    swap = [(j, j ^ 1) for j in range(blocks)]
    even = lax.rem(lax.axis_index("blk"), 2) == 0
    swapped_value = lax.ppermute(values, "blk", swap)
    integers = jnp.concatenate([lengths.ravel(), live.ravel(), jnp.swapaxes(page_table, 1, 2).ravel()])
    (
        table, cos_own, sin_own, cos_last, sin_last, cos_far, sin_far, own_bias, last_bias, far_bias
    ) = tables(keys.shape[1], pool.shape[1], integers, lengths.shape[1], steps, page_table.shape)
    query, key, near_key, near_value, own_shard = prepare(
        cos_own, sin_own, queries, keys, values, pool
    )
    to_swap = jnp.where(even, keys, far[0])
    far_key = lax.ppermute(to_swap, "blk", swap)
    split = values.shape[1] * 3 // 4
    passed_value = lax.ppermute(
        swapped_value[:, :split], "blk", [(j, j + 2) for j in range(0, blocks - 2, 2)]
    )
    shards = pool_shards(pool, (near_key, to_swap, swapped_value))
    later_values = values[:, split:]
    direct_value = lax.ppermute(
        later_values, "blk", [(j, j + 1) for j in range(1, blocks - 1, 2)]
    )
    own = attend_own(own_bias, query, near_key, near_value)
    earlier = attend_far(
        cos_far, sin_far, far_bias, query, [*far[::2], *far[1::2]], table, [own_shard, *shards[1:]]
    )
    result = attend_last(
        cos_last, sin_last, last_bias, query, own, earlier,
        [far_key, swapped_value, passed_value, direct_value],
    )
    return (result, key)


def solution(mesh):
    in_specs = (
        P("batch", "blk", None),
        P("batch", "blk", None),
        P("batch", "blk", None),
        P("batch", "blk"),
        P("batch", None),
        P("batch", "blk", None),
        P(),
        P("batch", None, None),
    )
    out_specs = (P("batch", "blk", None), P("batch", "blk", None))
    return jax.shard_map(
        per_device, mesh=mesh, in_specs=in_specs, out_specs=out_specs, check_vma=False
    )
```

```python
import math

import jax
import jax.numpy as jnp
import numpy as np
from jax import lax
from jax.experimental import pallas as pl
from jax.experimental.pallas import tpu as pltpu
from jax.sharding import PartitionSpec as P

QUERY_HEADS = 16
KEY_VALUE_HEADS = 8
HEAD_SIZE = 128
GROUP = QUERY_HEADS // KEY_VALUE_HEADS
HALF = HEAD_SIZE // 2
ROPE_BASE = 1000000.0
HIDDEN = -1e30
LANES = 128
ROW_TILE = 64
SOFTMAX_TILE = 16
HEADS_PER_STEP = 2
PREPARE_STEPS = 2


def cost(flops):
    return pl.CostEstimate(flops=flops, bytes_accessed=0, transcendentals=0)


TABLES_COST = cost(2_000_000_000)
PREPARE_COST = cost(0)
OWN_COST = cost(0)
JOIN_COST = cost(0)
EXP2_SCALE = math.log2(math.e) / math.sqrt(HEAD_SIZE)

FREQ_POWERS = [float(ROPE_BASE ** (-(2**k) / HALF)) for k in range(HALF.bit_length() - 1)]

PIO2_A = float(np.float32(1.5703125))
PIO2_B = float(np.float32(4.837512969970703125e-4))
PIO2_C = float(np.float32(math.pi / 2 - 1.5703125 - 4.837512969970703125e-4))


def shifted(value, steps):
    count = lax.axis_size("blk")
    return lax.ppermute(value, "blk", [(source, source + steps) for source in range(count - steps)])


def padded_keys(count):
    return -(-count // LANES) * LANES


def vmem_bytes(key_count):
    return 16 * 1024 * (1024 + key_count)


def sine_cosine(angle):
    turns = jnp.floor(angle * (2.0 / math.pi) + 0.5)
    rest = ((angle - turns * PIO2_A) - turns * PIO2_B) - turns * PIO2_C
    square = rest * rest
    sine = rest + rest * square * (
        -1.6666654611e-1 + square * (8.3321608736e-3 - square * 1.9515295891e-4)
    )
    cosine = 1.0 - 0.5 * square + square * square * (
        4.166664568298827e-2 + square * (-1.388731625493765e-3 + square * 2.443315711809948e-5)
    )
    quadrant = turns.astype(jnp.int32) & 3
    swapped = (quadrant & 1) == 1
    sine_out = jnp.where(swapped, cosine, sine)
    cosine_out = jnp.where(swapped, sine, cosine)
    sine_out = jnp.where(quadrant >= 2, -sine_out, sine_out)
    cosine_out = jnp.where((quadrant == 1) | (quadrant == 2), -cosine_out, cosine_out)
    return sine_out, cosine_out


def rotate(head, cosine, signed_sine):
    wide = head.astype(jnp.float32)
    return (wide * cosine + pltpu.roll(wide, HALF, 1) * signed_sine).astype(jnp.bfloat16)


def tables_kernel(
    rows, steps, segs, prefix_len, table_shape, integers_ref,
    page_out, cos_own, sin_own, cos_last, sin_last, cos_far, sin_far, own_bias, last_bias, far_bias,
):
    block_start = lax.axis_index("blk") * rows
    starts = [jnp.int32(0)]
    for seg in range(1, segs):
        starts.append(starts[-1] + integers_ref[seg - 1])
    lane = lax.broadcasted_iota(jnp.int32, (ROW_TILE, LANES), 1)
    row = lax.broadcasted_iota(jnp.int32, (ROW_TILE, LANES), 0)
    freq = jnp.ones((ROW_TILE, LANES), jnp.float32)
    for bit, power in enumerate(FREQ_POWERS):
        freq = jnp.where((lane >> bit) & 1 == 1, freq * power, freq)
    column = lax.axis_index("batch")
    seg_pages = table_shape[2]
    first = segs + steps + column * segs * seg_pages
    for page in range(segs * seg_pages):
        seg, place = divmod(page, seg_pages)
        page_out[page] = integers_ref[first + place * segs + seg]
    for step in range(steps + 1):
        for tile in range(0, rows, ROW_TILE):
            index = block_start + (tile - step * rows) + row
            own_start = jnp.zeros(index.shape, jnp.int32)
            for seg in range(1, segs):
                own_start = jnp.where(index >= starts[seg], starts[seg], own_start)
            place = (prefix_len + index - own_start).astype(jnp.float32)
            sine, cosine = sine_cosine(place * freq)
            sine = jnp.where(lane < HALF, -sine, sine)
            cos_out, sin_out = ((cos_own, sin_own), (cos_last, sin_last), (cos_far, sin_far))[
                min(step, 2)
            ]
            span = pl.ds(max(step - 2, 0) * rows + tile, ROW_TILE)
            cos_out[span, :] = cosine
            sin_out[span, :] = sine
    for tile in range(0, rows, ROW_TILE):
        span = pl.ds(tile, ROW_TILE)
        query_index = block_start + tile + row
        own_start = jnp.zeros(query_index.shape, jnp.int32)
        first_page_token = jnp.zeros(query_index.shape, jnp.int32)
        for seg in range(1, segs):
            later = query_index >= starts[seg]
            own_start = jnp.where(later, starts[seg], own_start)
            first_page_token = jnp.where(later, seg * prefix_len, first_page_token)
        for step in range(steps + 1):
            limit = query_index
            if step > 0:
                limit = jnp.where(integers_ref[segs + step - 1] > 0, limit, -1)
            for column in range(0, rows, LANES):
                key_index = block_start + (column - step * rows) + lane
                seen = (key_index >= own_start) & (key_index <= limit)
                bias = jnp.where(seen, 0.0, HIDDEN)
                if step == 0:
                    own_bias[span, pl.ds(column, LANES)] = bias
                elif step == 1:
                    last_bias[span, pl.ds(column, LANES)] = bias
                else:
                    far_bias[span, pl.ds((step - 2) * rows + column, LANES)] = bias
        base = (steps - 1) * rows
        for column in range(0, far_bias.shape[1] - base, LANES):
            offset = column + lane - first_page_token
            seen = (offset >= 0) & (offset < prefix_len)
            far_bias[span, pl.ds(base + column, LANES)] = jnp.where(seen, 0.0, HIDDEN)


def tables(rows, pool_page, integers, segs, steps, table_shape):
    prefix_len = table_shape[2] * pool_page
    pages = table_shape[1] * table_shape[2]
    far_rows = (steps - 1) * rows
    far_keys = padded_keys(far_rows + segs * prefix_len)
    block = jax.ShapeDtypeStruct((rows, HEAD_SIZE), jnp.float32)
    far = jax.ShapeDtypeStruct((far_rows, HEAD_SIZE), jnp.float32)
    shapes = [
        jax.ShapeDtypeStruct((pages,), jnp.int32),
        *[block] * 4,
        far,
        far,
        *[jax.ShapeDtypeStruct((rows, rows), jnp.float32)] * 2,
        jax.ShapeDtypeStruct((rows, far_keys), jnp.float32),
    ]
    return pl.pallas_call(
        lambda *refs: tables_kernel(rows, steps, segs, prefix_len, table_shape, *refs),
        in_specs=[pl.BlockSpec(memory_space=pltpu.SMEM)],
        out_specs=[pl.BlockSpec(memory_space=pltpu.SMEM)]
        + [pl.BlockSpec(memory_space=pltpu.VMEM)] * (len(shapes) - 1),
        out_shape=shapes,
        compiler_params=pltpu.CompilerParams(vmem_limit_bytes=vmem_bytes(far_keys + far_rows)),
        cost_estimate=TABLES_COST,
        name="tables",
    )(integers)


def prepare_kernel(
    rows, cos_own, sin_own, q_ref, k_ref, v_ref, pool_ref, q_out, k_out, k_copy, v_copy, pool_copy
):
    for tile in range(0, rows, ROW_TILE):
        span = pl.ds(tile, ROW_TILE)
        cosine = cos_own[span, :]
        signed_sine = sin_own[span, :]
        for source, target in ((q_ref, q_out), (k_ref, k_out)):
            for start in range(0, source.shape[2], HEAD_SIZE):
                columns = pl.ds(start, HEAD_SIZE)
                turned = rotate(source[0, span, columns], cosine, signed_sine)
                target[0, span, columns] = turned
                if source is k_ref:
                    k_copy[0, span, columns] = turned
    v_copy[...] = v_ref[...]
    pool_copy[...] = pool_ref[...]


def prepare(cosine, signed_sine, queries, keys, values, pool):
    rows = queries.shape[1]
    whole = lambda part: (0, 0)
    by_part = lambda part: (0, 0, part)
    wide = pl.BlockSpec((1, rows, queries.shape[2] // PREPARE_STEPS), by_part)
    narrow = pl.BlockSpec((1, rows, keys.shape[2] // PREPARE_STEPS), by_part)
    some_pages = pl.BlockSpec(
        (pool.shape[0] // PREPARE_STEPS, *pool.shape[1:]), lambda part: (part, 0, 0)
    )
    table = pl.BlockSpec(cosine.shape, whole)
    return pl.pallas_call(
        lambda *refs: prepare_kernel(rows, *refs),
        grid=(PREPARE_STEPS,),
        in_specs=[table, table, wide, narrow, narrow, some_pages],
        out_specs=[wide, narrow, narrow, narrow, some_pages],
        out_shape=[
            jax.ShapeDtypeStruct(array.shape, array.dtype)
            for array in (queries, keys, keys, values, pool)
        ],
        compiler_params=pltpu.CompilerParams(vmem_limit_bytes=vmem_bytes(rows)),
        cost_estimate=PREPARE_COST,
        name="prepare",
    )(cosine, signed_sine, queries, keys, values, pool)


def stacked_queries(q_ref, part):
    return jnp.concatenate(
        [q_ref[0, :, pl.ds((part * GROUP + h) * HEAD_SIZE, HEAD_SIZE)] for h in range(GROUP)],
        axis=0,
    )


def rotate_rows(target, first, source, lanes, cos_ref, sin_ref):
    rows = source.shape[1]
    for tile in range(0, rows, ROW_TILE):
        span = pl.ds(first + tile, ROW_TILE)
        target[span, :] = rotate(
            source[0, pl.ds(tile, ROW_TILE), lanes], cos_ref[span, :], sin_ref[span, :]
        )


def own_kernel(rows, bias_ref, q_ref, k_ref, v_ref, mean_ref, level_ref, *work):
    k_parts, v_parts, scores, weights, tops = split_work(work)
    group = pl.program_id(0)

    @pl.when(group == 0)
    def _():
        fill_ones(v_parts)
        level_ref[...] = jnp.zeros(level_ref.shape, jnp.float32)

    for part in range(HEADS_PER_STEP):
        lanes = pl.ds(part * HEAD_SIZE, HEAD_SIZE)
        k_parts[part][...] = k_ref[0, :, lanes]
        v_parts[part][:, pl.ds(0, HEAD_SIZE)] = v_ref[0, :, lanes]

    for part in range(HEADS_PER_STEP):
        score_part(part, q_ref, k_parts, scores)
    lane = lax.broadcasted_iota(jnp.int32, (rows, LANES), 1)
    for part in range(HEADS_PER_STEP):
        for start in range(0, GROUP * rows, SOFTMAX_TILE):
            span = pl.ds(start, SOFTMAX_TILE)
            bias = bias_ref[pl.ds(start % rows, SOFTMAX_TILE), :]
            score = scores[part][span, :] * EXP2_SCALE + bias
            highest = jnp.max(score, axis=1, keepdims=True)
            weights[part][span, :] = jnp.exp2(score - highest).astype(jnp.bfloat16)
            tops[part][span, :] = jnp.broadcast_to(highest, (SOFTMAX_TILE, LANES))
        summed = jnp.dot(weights[part][...], v_parts[part][...], preferred_element_type=jnp.float32)
        total = summed[:, HEAD_SIZE:]
        store_part(part, group, rows, lane, summed[:, :HEAD_SIZE] / total,
                   tops[part][...] + jnp.log2(total), mean_ref, level_ref)


def fill_ones(v_parts):
    for v_all in v_parts:
        v_all[:, pl.ds(HEAD_SIZE, HEAD_SIZE)] = jnp.ones((v_all.shape[0], HEAD_SIZE), jnp.bfloat16)


def split_work(work):
    return [work[i : i + HEADS_PER_STEP] for i in range(0, len(work), HEADS_PER_STEP)]


def score_part(part, q_ref, k_parts, scores):
    scores[part][...] = lax.dot_general(
        stacked_queries(q_ref, part), k_parts[part][...], (((1,), (1,)), ((), ())),
        preferred_element_type=jnp.float32,
    )


def store_part(part, group, rows, lane, mean, level, mean_ref, level_ref):
    for h in range(GROUP):
        own = part * GROUP + h
        span = slice(h * rows, (h + 1) * rows)
        mean_ref[:, pl.ds(own * HEAD_SIZE, HEAD_SIZE)] = mean[span]
        head = group * (HEADS_PER_STEP * GROUP) + own
        level_ref[...] = jnp.where(lane == head, level[span], level_ref[...])


def work_shapes(rows, key_count):
    shapes = [
        pltpu.VMEM((key_count, HEAD_SIZE), jnp.bfloat16),
        pltpu.VMEM((key_count, 2 * HEAD_SIZE), jnp.bfloat16),
        pltpu.VMEM((GROUP * rows, key_count), jnp.float32),
        pltpu.VMEM((GROUP * rows, key_count), jnp.bfloat16),
        pltpu.VMEM((GROUP * rows, LANES), jnp.float32),
    ]
    return [shape for shape in shapes for _ in range(HEADS_PER_STEP)]


def attend_own(bias, query, key, value):
    rows, q_width = query.shape[1:]
    by_group = lambda group: (0, 0, group)
    narrow = pl.BlockSpec((1, rows, HEADS_PER_STEP * HEAD_SIZE), by_group)
    wide = HEADS_PER_STEP * GROUP * HEAD_SIZE
    return pl.pallas_call(
        lambda *refs: own_kernel(rows, *refs),
        grid=(KEY_VALUE_HEADS // HEADS_PER_STEP,),
        in_specs=[
            pl.BlockSpec(bias.shape, lambda group: (0, 0)),
            pl.BlockSpec((1, rows, wide), by_group),
            narrow,
            narrow,
        ],
        out_specs=[
            pl.BlockSpec((rows, wide), lambda group: (0, group)),
            pl.BlockSpec((rows, LANES), lambda group: (0, 0)),
        ],
        out_shape=[
            jax.ShapeDtypeStruct((rows, q_width), jnp.float32),
            jax.ShapeDtypeStruct((rows, LANES), jnp.float32),
        ],
        scratch_shapes=work_shapes(rows, rows),
        compiler_params=pltpu.CompilerParams(vmem_limit_bytes=vmem_bytes(rows)),
        cost_estimate=OWN_COST,
        name="own",
    )(bias, query, key, value)


def page_copies(start, table_ref, shards, paged, sem):
    pool_rows = shards[0].shape[0]
    column = lax.axis_index("batch")

    def copy(shard, place, page):
        return pltpu.make_async_copy(shard.at[place], paged.at[page], sem.at[page])

    for page in range(paged.shape[0]):
        if not start:
            copy(shards[0], 0, page).wait()
            continue
        number = table_ref[page]
        apart = lax.div(number, jnp.int32(pool_rows)) ^ column
        place = lax.rem(number, jnp.int32(pool_rows))
        for which, shard in enumerate(shards):

            @pl.when(apart == which)
            def _(shard=shard, place=place, page=page):
                copy(shard, place, page).start()


def join_heads(
    final, group, rows, k_parts, v_parts, scores, weights, tops,
    bias_ref, level_ref, mean_ref, q_ref, out_ref, level_out,
):
    for part in range(HEADS_PER_STEP):
        score_part(part, q_ref, k_parts, scores)
    lane = lax.broadcasted_iota(jnp.int32, (SOFTMAX_TILE, LANES), 1)
    wide_lane = lax.broadcasted_iota(jnp.int32, (rows, LANES), 1)
    for part in range(HEADS_PER_STEP):
        for start in range(0, GROUP * rows, SOFTMAX_TILE):
            span = pl.ds(start, SOFTMAX_TILE)
            row_span = pl.ds(start % rows, SOFTMAX_TILE)
            head = group * (HEADS_PER_STEP * GROUP) + part * GROUP + start // rows
            score = scores[part][span, :] * EXP2_SCALE + bias_ref[row_span, :]
            level = jnp.sum(
                jnp.where(lane == head, level_ref[row_span, :], 0.0), axis=1, keepdims=True
            )
            highest = jnp.maximum(jnp.max(score, axis=1, keepdims=True), level)
            weights[part][span, :] = jnp.exp2(score - highest).astype(jnp.bfloat16)
            if final:
                shrink = jnp.exp2(level - highest)
                tops[part][span, :] = jnp.broadcast_to(shrink, (SOFTMAX_TILE, LANES))
            else:
                tops[part][span, :] = jnp.where(lane < HALF, highest, level)
        summed = jnp.dot(weights[part][...], v_parts[part][...], preferred_element_type=jnp.float32)
        if final:
            shrink = tops[part][...]
        else:
            both = tops[part][...]
            turned = pltpu.roll(both, HALF, 1)
            low = lax.broadcasted_iota(jnp.int32, both.shape, 1) < HALF
            highest = jnp.where(low, both, turned)
            shrink = jnp.exp2(jnp.where(low, turned, both) - highest)
        total = summed[:, HEAD_SIZE:] + shrink
        before = jnp.concatenate(
            [mean_ref[:, pl.ds((part * GROUP + h) * HEAD_SIZE, HEAD_SIZE)] for h in range(GROUP)],
            axis=0,
        )
        mean = (before * shrink + summed[:, :HEAD_SIZE]) / total
        if final:
            for h in range(GROUP):
                lanes = pl.ds((part * GROUP + h) * HEAD_SIZE, HEAD_SIZE)
                out_ref[0, :, lanes] = mean[h * rows : (h + 1) * rows].astype(jnp.bfloat16)
        else:
            level = highest + jnp.log2(total)
            store_part(part, group, rows, wide_lane, mean, level, out_ref, level_out)


def far_kernel(rows, columns_count, blocks, kv_width, *refs):
    table_ref, cos_ref, sin_ref, bias_ref, level_ref, mean_ref, q_ref = refs[:7]
    shards, refs = refs[7 : 7 + columns_count], refs[7 + columns_count :]
    keys, values, refs = refs[:blocks], refs[blocks : 2 * blocks], refs[2 * blocks :]
    mean_out, level_out, paged, sem = refs[:4]
    work = split_work(refs[4:])
    k_parts, v_parts = work[:2]
    group = pl.program_id(0)
    prefix_rows = paged.shape[0] * paged.shape[1]
    base = blocks * rows

    @pl.when(group == 0)
    def _():
        page_copies(True, table_ref, shards, paged, sem)
        fill_ones(v_parts)
        level_out[...] = jnp.zeros(level_out.shape, jnp.float32)
        rest = k_parts[0].shape[0] - base - prefix_rows
        if rest:
            blank = jnp.zeros((rest, HEAD_SIZE), jnp.bfloat16)
            for k_all, v_all in zip(k_parts, v_parts):
                k_all[pl.ds(base + prefix_rows, rest), :] = blank
                v_all[pl.ds(base + prefix_rows, rest), pl.ds(0, HEAD_SIZE)] = blank

    for part in range(HEADS_PER_STEP):
        lanes = pl.ds(part * HEAD_SIZE, HEAD_SIZE)
        for block in range(blocks):
            rotate_rows(k_parts[part], block * rows, keys[block], lanes, cos_ref, sin_ref)
            span = pl.ds(block * rows, rows)
            v_parts[part][span, pl.ds(0, HEAD_SIZE)] = values[block][0, :, lanes]

    @pl.when(group == 0)
    def _():
        page_copies(False, table_ref, shards, paged, sem)

    for part in range(HEADS_PER_STEP):
        start = (group * HEADS_PER_STEP + part) * HEAD_SIZE
        columns = pl.ds(pl.multiple_of(start, HEAD_SIZE), HEAD_SIZE)
        value_columns = pl.ds(pl.multiple_of(kv_width + start, HEAD_SIZE), HEAD_SIZE)
        span = pl.ds(base, prefix_rows)
        k_parts[part][span, :] = paged[:, :, columns].reshape(prefix_rows, HEAD_SIZE)
        v_parts[part][span, pl.ds(0, HEAD_SIZE)] = paged[:, :, value_columns].reshape(
            prefix_rows, HEAD_SIZE
        )
    join_heads(
        False, group, rows, *work, bias_ref, level_ref, mean_ref, q_ref, mean_out, level_out
    )


def last_kernel(
    rows, cos_ref, sin_ref, bias_ref, level_ref, mean_ref, q_ref, key_ref, swapped_value,
    passed_value, direct_value, out_ref, *refs,
):
    work = split_work(refs)
    k_parts, v_parts = work[:2]
    group = pl.program_id(0)
    even = lax.rem(lax.axis_index("blk"), 2) == 0

    @pl.when(group == 0)
    def _():
        fill_ones(v_parts)

    for part in range(HEADS_PER_STEP):
        lanes = pl.ds(part * HEAD_SIZE, HEAD_SIZE)
        rotate_rows(k_parts[part], 0, key_ref, lanes, cos_ref, sin_ref)
        start = 0
        for arrived in (passed_value, direct_value):
            span = pl.ds(start, arrived.shape[1])
            v_parts[part][span, pl.ds(0, HEAD_SIZE)] = jnp.where(
                even, arrived[0, :, lanes], swapped_value[0, span, lanes]
            )
            start += arrived.shape[1]
    join_heads(True, group, rows, *work, bias_ref, level_ref, mean_ref, q_ref, out_ref, None)


def join(cosine, signed_sine, bias, level, mean, query, arrived, pages=None):
    rows = query.shape[1]
    whole = lambda group: (0, 0)
    by_group = lambda group: (0, 0, group)
    width = HEADS_PER_STEP * GROUP * HEAD_SIZE
    wide = pl.BlockSpec((1, rows, width), by_group)
    flat = pl.BlockSpec((rows, width), lambda group: (0, group))
    table = pl.BlockSpec(cosine.shape, whole)
    level_spec = pl.BlockSpec(level.shape, whole)
    in_specs = [table, table, pl.BlockSpec(bias.shape, whole), level_spec, flat, wide]
    arrived_specs = [
        pl.BlockSpec((1, array.shape[1], HEADS_PER_STEP * HEAD_SIZE), by_group)
        for array in arrived
    ]
    operands = [cosine, signed_sine, bias, level, mean, query]
    scratch = work_shapes(rows, bias.shape[1])
    if pages is None:
        kernel = lambda *refs: last_kernel(rows, *refs)
        out_specs, out_shape = wide, jax.ShapeDtypeStruct(query.shape, jnp.bfloat16)
    else:
        numbers, shards = pages
        kernel = lambda *refs: far_kernel(
            rows, len(shards), len(arrived) // 2, arrived[0].shape[2], *refs
        )
        in_specs = [
            pl.BlockSpec(memory_space=pltpu.SMEM),
            *in_specs,
            *[pl.BlockSpec(memory_space=pl.ANY)] * len(shards),
        ]
        operands = [numbers, *operands, *shards]
        out_specs = [flat, level_spec]
        out_shape = [
            jax.ShapeDtypeStruct(array.shape, jnp.float32) for array in (mean, level)
        ]
        scratch = [
            pltpu.VMEM(numbers.shape + shards[0].shape[1:], jnp.bfloat16),
            pltpu.SemaphoreType.DMA(numbers.shape),
        ] + scratch
    return pl.pallas_call(
        kernel,
        grid=(KEY_VALUE_HEADS // HEADS_PER_STEP,),
        in_specs=in_specs + arrived_specs,
        out_specs=out_specs,
        out_shape=out_shape,
        scratch_shapes=scratch,
        compiler_params=pltpu.CompilerParams(vmem_limit_bytes=vmem_bytes(bias.shape[1])),
        cost_estimate=JOIN_COST,
        name="last" if pages is None else "far",
    )(*operands, *arrived)


def pool_shards(pool, after):
    count = lax.axis_size("batch")

    def swapped(shard, bit):
        return lax.ppermute(shard, "batch", [(c, c ^ bit) for c in range(count)])

    bits = [count >> (step + 1) for step in range(count.bit_length() - 1)]
    shards = {0: pool, **{bit: swapped(pool, bit) for bit in bits}}
    shards, after = lax.optimization_barrier((shards, after))
    for bit in reversed(bits):
        for apart, shard in list(shards.items()):
            if apart ^ bit not in shards:
                shards[apart ^ bit] = swapped(shard, bit)
    return [shards[apart] for apart in range(count)]


def per_device(queries, keys, values, seg_ids, lengths, live, page_table, pool):
    steps = live.shape[2]
    blocks = lax.axis_size("blk")
    far = [shifted(keys, 2), shifted(values, 2)]
    for step in range(3, steps + 1):
        far += [shifted(keys, step), shifted(values, step)]
    swap = [(j, j ^ 1) for j in range(blocks)]
    even = lax.rem(lax.axis_index("blk"), 2) == 0
    swapped_value = lax.ppermute(values, "blk", swap)
    integers = jnp.concatenate([lengths.ravel(), live.ravel(), jnp.swapaxes(page_table, 1, 2).ravel()])
    (
        table, cos_own, sin_own, cos_last, sin_last, cos_far, sin_far, own_bias, last_bias, far_bias
    ) = tables(keys.shape[1], pool.shape[1], integers, lengths.shape[1], steps, page_table.shape)
    query, key, near_key, near_value, own_shard = prepare(
        cos_own, sin_own, queries, keys, values, pool
    )
    to_swap = jnp.where(even, keys, far[0])
    far_key = lax.ppermute(to_swap, "blk", swap)
    split = values.shape[1] * 3 // 4
    passed_value = lax.ppermute(
        swapped_value[:, :split], "blk", [(j, j + 2) for j in range(0, blocks - 2, 2)]
    )
    mean, level = attend_own(own_bias, query, near_key, near_value)
    shards = pool_shards(pool, (level, to_swap, swapped_value))
    later_values = values[:, split:]
    direct_value = lax.ppermute(
        later_values, "blk", [(j, j + 1) for j in range(1, blocks - 1, 2)]
    )
    mean, level = join(
        cos_far, sin_far, far_bias, level, mean, query, [*far[::2], *far[1::2]],
        pages=(table, [own_shard, *shards[1:]]),
    )
    result = join(
        cos_last, sin_last, last_bias, level, mean, query,
        [far_key, swapped_value, passed_value, direct_value],
    )
    return (result, key)


def solution(mesh):
    in_specs = (
        P("batch", "blk", None),
        P("batch", "blk", None),
        P("batch", "blk", None),
        P("batch", "blk"),
        P("batch", None),
        P("batch", "blk", None),
        P(),
        P("batch", None, None),
    )
    out_specs = (P("batch", "blk", None), P("batch", "blk", None))
    return jax.shard_map(
        per_device, mesh=mesh, in_specs=in_specs, out_specs=out_specs, check_vma=False
    )
```

```python
import math

import jax
import jax.numpy as jnp
import numpy as np
from jax import lax
from jax.experimental import pallas as pl
from jax.experimental.pallas import tpu as pltpu
from jax.sharding import PartitionSpec as P

QUERY_HEADS = 16
KEY_VALUE_HEADS = 8
HEAD_SIZE = 128
GROUP = QUERY_HEADS // KEY_VALUE_HEADS
HALF = HEAD_SIZE // 2
ROPE_BASE = 1000000.0
HIDDEN = -1e30
LANES = 128
ROW_TILE = 64
SOFTMAX_TILE = 16
HEADS_PER_STEP = 2
PREPARE_STEPS = 2


def cost(flops):
    return pl.CostEstimate(flops=flops, bytes_accessed=0, transcendentals=0)


TABLES_COST = cost(2_000_000_000)
PREPARE_COST = cost(0)
OWN_COST = cost(0)
JOIN_COST = cost(0)
EXP2_SCALE = math.log2(math.e) / math.sqrt(HEAD_SIZE)

FREQ_POWERS = [float(ROPE_BASE ** (-(2**k) / HALF)) for k in range(HALF.bit_length() - 1)]

PIO2_A = float(np.float32(1.5703125))
PIO2_B = float(np.float32(4.837512969970703125e-4))
PIO2_C = float(np.float32(math.pi / 2 - 1.5703125 - 4.837512969970703125e-4))


def shifted(value, steps):
    count = lax.axis_size("blk")
    return lax.ppermute(value, "blk", [(source, source + steps) for source in range(count - steps)])


def padded_keys(count):
    return -(-count // LANES) * LANES


def vmem_bytes(key_count):
    return 16 * 1024 * (1024 + key_count)


def sine_cosine(angle):
    turns = jnp.floor(angle * (2.0 / math.pi) + 0.5)
    rest = ((angle - turns * PIO2_A) - turns * PIO2_B) - turns * PIO2_C
    square = rest * rest
    sine = rest + rest * square * (
        -1.6666654611e-1 + square * (8.3321608736e-3 - square * 1.9515295891e-4)
    )
    cosine = 1.0 - 0.5 * square + square * square * (
        4.166664568298827e-2 + square * (-1.388731625493765e-3 + square * 2.443315711809948e-5)
    )
    quadrant = turns.astype(jnp.int32) & 3
    swapped = (quadrant & 1) == 1
    sine_out = jnp.where(swapped, cosine, sine)
    cosine_out = jnp.where(swapped, sine, cosine)
    sine_out = jnp.where(quadrant >= 2, -sine_out, sine_out)
    cosine_out = jnp.where((quadrant == 1) | (quadrant == 2), -cosine_out, cosine_out)
    return sine_out, cosine_out


def rotate(head, cosine, signed_sine):
    wide = head.astype(jnp.float32)
    return (wide * cosine + pltpu.roll(wide, HALF, 1) * signed_sine).astype(jnp.bfloat16)


def tables_kernel(
    rows, steps, segs, prefix_len, table_shape, integers_ref,
    page_out, cos_own, sin_own, cos_last, sin_last, cos_far, sin_far, own_bias, last_bias, far_bias,
):
    block_start = lax.axis_index("blk") * rows
    starts = [jnp.int32(0)]
    for seg in range(1, segs):
        starts.append(starts[-1] + integers_ref[seg - 1])
    lane = lax.broadcasted_iota(jnp.int32, (ROW_TILE, LANES), 1)
    row = lax.broadcasted_iota(jnp.int32, (ROW_TILE, LANES), 0)
    freq = jnp.ones((ROW_TILE, LANES), jnp.float32)
    for bit, power in enumerate(FREQ_POWERS):
        freq = jnp.where((lane >> bit) & 1 == 1, freq * power, freq)
    column = lax.axis_index("batch")
    seg_pages = table_shape[2]
    first = segs + steps + column * segs * seg_pages
    for page in range(segs * seg_pages):
        seg, place = divmod(page, seg_pages)
        page_out[page] = integers_ref[first + place * segs + seg]
    for step in range(steps + 1):
        for tile in range(0, rows, ROW_TILE):
            index = block_start + (tile - step * rows) + row
            own_start = jnp.zeros(index.shape, jnp.int32)
            for seg in range(1, segs):
                own_start = jnp.where(index >= starts[seg], starts[seg], own_start)
            place = (prefix_len + index - own_start).astype(jnp.float32)
            sine, cosine = sine_cosine(place * freq)
            sine = jnp.where(lane < HALF, -sine, sine)
            cos_out, sin_out = ((cos_own, sin_own), (cos_last, sin_last), (cos_far, sin_far))[
                min(step, 2)
            ]
            span = pl.ds(max(step - 2, 0) * rows + tile, ROW_TILE)
            cos_out[span, :] = cosine
            sin_out[span, :] = sine
    for tile in range(0, rows, ROW_TILE):
        span = pl.ds(tile, ROW_TILE)
        query_index = block_start + tile + row
        own_start = jnp.zeros(query_index.shape, jnp.int32)
        first_page_token = jnp.zeros(query_index.shape, jnp.int32)
        for seg in range(1, segs):
            later = query_index >= starts[seg]
            own_start = jnp.where(later, starts[seg], own_start)
            first_page_token = jnp.where(later, seg * prefix_len, first_page_token)
        for step in range(steps + 1):
            limit = query_index
            if step > 0:
                limit = jnp.where(integers_ref[segs + step - 1] > 0, limit, -1)
            for column in range(0, rows, LANES):
                key_index = block_start + (column - step * rows) + lane
                seen = (key_index >= own_start) & (key_index <= limit)
                bias = jnp.where(seen, 0.0, HIDDEN)
                if step == 0:
                    own_bias[span, pl.ds(column, LANES)] = bias
                elif step == 1:
                    last_bias[span, pl.ds(column, LANES)] = bias
                else:
                    far_bias[span, pl.ds((step - 2) * rows + column, LANES)] = bias
        base = (steps - 1) * rows
        for column in range(0, far_bias.shape[1] - base, LANES):
            offset = column + lane - first_page_token
            seen = (offset >= 0) & (offset < prefix_len)
            far_bias[span, pl.ds(base + column, LANES)] = jnp.where(seen, 0.0, HIDDEN)


def tables(rows, pool_page, integers, segs, steps, table_shape):
    prefix_len = table_shape[2] * pool_page
    pages = table_shape[1] * table_shape[2]
    far_rows = (steps - 1) * rows
    far_keys = padded_keys(far_rows + segs * prefix_len)
    block = jax.ShapeDtypeStruct((rows, HEAD_SIZE), jnp.float32)
    far = jax.ShapeDtypeStruct((far_rows, HEAD_SIZE), jnp.float32)
    shapes = [
        jax.ShapeDtypeStruct((pages,), jnp.int32),
        *[block] * 4,
        far,
        far,
        *[jax.ShapeDtypeStruct((rows, rows), jnp.float32)] * 2,
        jax.ShapeDtypeStruct((rows, far_keys), jnp.float32),
    ]
    return pl.pallas_call(
        lambda *refs: tables_kernel(rows, steps, segs, prefix_len, table_shape, *refs),
        in_specs=[pl.BlockSpec(memory_space=pltpu.SMEM)],
        out_specs=[pl.BlockSpec(memory_space=pltpu.SMEM)]
        + [pl.BlockSpec(memory_space=pltpu.VMEM)] * (len(shapes) - 1),
        out_shape=shapes,
        compiler_params=pltpu.CompilerParams(vmem_limit_bytes=vmem_bytes(far_keys + far_rows)),
        cost_estimate=TABLES_COST,
        name="tables",
    )(integers)


def prepare_kernel(
    rows, cos_own, sin_own, q_ref, k_ref, v_ref, pool_ref, q_out, k_out, k_copy, v_copy, pool_copy
):
    for tile in range(0, rows, ROW_TILE):
        span = pl.ds(tile, ROW_TILE)
        cosine = cos_own[span, :]
        signed_sine = sin_own[span, :]
        for source, target in ((q_ref, q_out), (k_ref, k_out)):
            for start in range(0, source.shape[2], HEAD_SIZE):
                columns = pl.ds(start, HEAD_SIZE)
                turned = rotate(source[0, span, columns], cosine, signed_sine)
                target[0, span, columns] = turned
                if source is k_ref:
                    k_copy[0, span, columns] = turned
    v_copy[...] = v_ref[...]
    pool_copy[...] = pool_ref[...]


def prepare(cosine, signed_sine, queries, keys, values, pool):
    rows = queries.shape[1]
    whole = lambda part: (0, 0)
    by_part = lambda part: (0, 0, part)
    wide = pl.BlockSpec((1, rows, queries.shape[2] // PREPARE_STEPS), by_part)
    narrow = pl.BlockSpec((1, rows, keys.shape[2] // PREPARE_STEPS), by_part)
    some_pages = pl.BlockSpec(
        (pool.shape[0] // PREPARE_STEPS, *pool.shape[1:]), lambda part: (part, 0, 0)
    )
    table = pl.BlockSpec(cosine.shape, whole)
    return pl.pallas_call(
        lambda *refs: prepare_kernel(rows, *refs),
        grid=(PREPARE_STEPS,),
        in_specs=[table, table, wide, narrow, narrow, some_pages],
        out_specs=[wide, narrow, narrow, narrow, some_pages],
        out_shape=[
            jax.ShapeDtypeStruct(array.shape, array.dtype)
            for array in (queries, keys, keys, values, pool)
        ],
        compiler_params=pltpu.CompilerParams(vmem_limit_bytes=vmem_bytes(rows)),
        cost_estimate=PREPARE_COST,
        name="prepare",
    )(cosine, signed_sine, queries, keys, values, pool)


def stacked_queries(q_ref, part):
    return jnp.concatenate(
        [q_ref[0, :, pl.ds((part * GROUP + h) * HEAD_SIZE, HEAD_SIZE)] for h in range(GROUP)],
        axis=0,
    )


def rotate_rows(target, first, source, lanes, cos_ref, sin_ref):
    rows = source.shape[1]
    for tile in range(0, rows, ROW_TILE):
        span = pl.ds(first + tile, ROW_TILE)
        target[span, :] = rotate(
            source[0, pl.ds(tile, ROW_TILE), lanes], cos_ref[span, :], sin_ref[span, :]
        )


def own_kernel(rows, bias_ref, q_ref, k_ref, v_ref, mean_ref, level_ref, *work):
    k_parts, v_parts, scores, weights, tops = split_work(work)
    group = pl.program_id(0)

    @pl.when(group == 0)
    def _():
        fill_ones(v_parts)

    for part in range(HEADS_PER_STEP):
        lanes = pl.ds(part * HEAD_SIZE, HEAD_SIZE)
        k_parts[part][...] = k_ref[0, :, lanes]
        v_parts[part][:, pl.ds(0, HEAD_SIZE)] = v_ref[0, :, lanes]

    for part in range(HEADS_PER_STEP):
        score_part(part, q_ref, k_parts, scores)
    for part in range(HEADS_PER_STEP):
        for start in range(0, GROUP * rows, SOFTMAX_TILE):
            span = pl.ds(start, SOFTMAX_TILE)
            bias = bias_ref[pl.ds(start % rows, SOFTMAX_TILE), :]
            score = scores[part][span, :] * EXP2_SCALE + bias
            highest = jnp.max(score, axis=1, keepdims=True)
            weights[part][span, :] = jnp.exp2(score - highest).astype(jnp.bfloat16)
            tops[part][span, :] = jnp.broadcast_to(highest, (SOFTMAX_TILE, LANES))
        summed = jnp.dot(weights[part][...], v_parts[part][...], preferred_element_type=jnp.float32)
        total = summed[:, HEAD_SIZE:]
        mean = summed[:, :HEAD_SIZE] / total
        store_part(part, rows, mean, tops[part][...] + jnp.log2(total), mean_ref, level_ref)


def fill_ones(v_parts):
    for v_all in v_parts:
        v_all[:, pl.ds(HEAD_SIZE, HEAD_SIZE)] = jnp.ones((v_all.shape[0], HEAD_SIZE), jnp.bfloat16)


def split_work(work):
    return [work[i : i + HEADS_PER_STEP] for i in range(0, len(work), HEADS_PER_STEP)]


def score_part(part, q_ref, k_parts, scores):
    scores[part][...] = lax.dot_general(
        stacked_queries(q_ref, part), k_parts[part][...], (((1,), (1,)), ((), ())),
        preferred_element_type=jnp.float32,
    )


def store_part(part, rows, mean, level, mean_ref, level_ref):
    for h in range(GROUP):
        lanes = pl.ds((part * GROUP + h) * HEAD_SIZE, HEAD_SIZE)
        span = slice(h * rows, (h + 1) * rows)
        mean_ref[:, lanes] = mean[span]
        level_ref[:, lanes] = level[span]


def work_shapes(rows, key_count):
    shapes = [
        pltpu.VMEM((key_count, HEAD_SIZE), jnp.bfloat16),
        pltpu.VMEM((key_count, 2 * HEAD_SIZE), jnp.bfloat16),
        pltpu.VMEM((GROUP * rows, key_count), jnp.float32),
        pltpu.VMEM((GROUP * rows, key_count), jnp.bfloat16),
        pltpu.VMEM((GROUP * rows, LANES), jnp.float32),
    ]
    return [shape for shape in shapes for _ in range(HEADS_PER_STEP)]


def attend_own(bias, query, key, value):
    rows, q_width = query.shape[1:]
    by_group = lambda group: (0, 0, group)
    narrow = pl.BlockSpec((1, rows, HEADS_PER_STEP * HEAD_SIZE), by_group)
    wide = HEADS_PER_STEP * GROUP * HEAD_SIZE
    return pl.pallas_call(
        lambda *refs: own_kernel(rows, *refs),
        grid=(KEY_VALUE_HEADS // HEADS_PER_STEP,),
        in_specs=[
            pl.BlockSpec(bias.shape, lambda group: (0, 0)),
            pl.BlockSpec((1, rows, wide), by_group),
            narrow,
            narrow,
        ],
        out_specs=[
            pl.BlockSpec((rows, wide), lambda group: (0, group)),
        ]
        * 2,
        out_shape=[jax.ShapeDtypeStruct((rows, q_width), jnp.float32)] * 2,
        scratch_shapes=work_shapes(rows, rows),
        compiler_params=pltpu.CompilerParams(vmem_limit_bytes=vmem_bytes(rows)),
        cost_estimate=OWN_COST,
        name="own",
    )(bias, query, key, value)


def page_copies(start, table_ref, pool_rows, places, shards, paged, sem):
    column = lax.axis_index("batch")

    def copy(shard, place, page):
        return pltpu.make_async_copy(shard.at[place], paged.at[page], sem.at[page])

    for page in range(paged.shape[0]):
        if not start:
            copy(shards[0], 0, page).wait()
            continue
        number = table_ref[page]
        apart = lax.div(number, jnp.int32(pool_rows)) ^ column
        place = lax.rem(number, jnp.int32(pool_rows))
        for (which, first), shard in zip(places, shards):
            inside = place - first

            @pl.when((apart == which) & (inside >= 0) & (inside < shard.shape[0]))
            def _(shard=shard, inside=inside, page=page):
                copy(shard, inside, page).start()


def join_heads(
    final, rows, k_parts, v_parts, scores, weights, tops,
    bias_ref, level_ref, mean_ref, q_ref, out_ref, level_out,
):
    for part in range(HEADS_PER_STEP):
        score_part(part, q_ref, k_parts, scores)
    for part in range(HEADS_PER_STEP):
        for start in range(0, GROUP * rows, SOFTMAX_TILE):
            span = pl.ds(start, SOFTMAX_TILE)
            row_span = pl.ds(start % rows, SOFTMAX_TILE)
            lanes = pl.ds((part * GROUP + start // rows) * HEAD_SIZE, HEAD_SIZE)
            score = scores[part][span, :] * EXP2_SCALE + bias_ref[row_span, :]
            highest = jnp.maximum(
                jnp.broadcast_to(jnp.max(score, axis=1, keepdims=True), (SOFTMAX_TILE, LANES)),
                level_ref[row_span, lanes],
            )
            for column in range(0, score.shape[1], LANES):
                piece = jnp.exp2(score[:, column : column + LANES] - highest)
                weights[part][span, pl.ds(column, LANES)] = piece.astype(jnp.bfloat16)
            tops[part][span, :] = highest
        summed = jnp.dot(weights[part][...], v_parts[part][...], preferred_element_type=jnp.float32)
        for h in range(GROUP):
            lanes = pl.ds((part * GROUP + h) * HEAD_SIZE, HEAD_SIZE)
            span = slice(h * rows, (h + 1) * rows)
            highest = tops[part][pl.ds(h * rows, rows), :]
            shrink = jnp.exp2(level_ref[:, lanes] - highest)
            total = summed[span, HEAD_SIZE:] + shrink
            mean = (mean_ref[:, lanes] * shrink + summed[span, :HEAD_SIZE]) / total
            if final:
                out_ref[0, :, lanes] = mean.astype(jnp.bfloat16)
            else:
                out_ref[:, lanes] = mean
                level_out[:, lanes] = highest + jnp.log2(total)


def far_kernel(rows, pool_rows, places, blocks, kv_width, *refs):
    table_ref, cos_ref, sin_ref, bias_ref, level_ref, mean_ref, q_ref = refs[:7]
    shards, refs = refs[7 : 7 + len(places)], refs[7 + len(places) :]
    keys, values, refs = refs[:blocks], refs[blocks : 2 * blocks], refs[2 * blocks :]
    mean_out, level_out, paged, sem = refs[:4]
    work = split_work(refs[4:])
    k_parts, v_parts = work[:2]
    group = pl.program_id(0)
    prefix_rows = paged.shape[0] * paged.shape[1]
    base = blocks * rows

    @pl.when(group == 0)
    def _():
        page_copies(True, table_ref, pool_rows, places, shards, paged, sem)
        fill_ones(v_parts)
        rest = k_parts[0].shape[0] - base - prefix_rows
        if rest:
            blank = jnp.zeros((rest, HEAD_SIZE), jnp.bfloat16)
            for k_all, v_all in zip(k_parts, v_parts):
                k_all[pl.ds(base + prefix_rows, rest), :] = blank
                v_all[pl.ds(base + prefix_rows, rest), pl.ds(0, HEAD_SIZE)] = blank

    for part in range(HEADS_PER_STEP):
        lanes = pl.ds(part * HEAD_SIZE, HEAD_SIZE)
        for block in range(blocks):
            rotate_rows(k_parts[part], block * rows, keys[block], lanes, cos_ref, sin_ref)
            span = pl.ds(block * rows, rows)
            v_parts[part][span, pl.ds(0, HEAD_SIZE)] = values[block][0, :, lanes]

    @pl.when(group == 0)
    def _():
        page_copies(False, table_ref, pool_rows, places, shards, paged, sem)

    for part in range(HEADS_PER_STEP):
        start = (group * HEADS_PER_STEP + part) * HEAD_SIZE
        columns = pl.ds(pl.multiple_of(start, HEAD_SIZE), HEAD_SIZE)
        value_columns = pl.ds(pl.multiple_of(kv_width + start, HEAD_SIZE), HEAD_SIZE)
        span = pl.ds(base, prefix_rows)
        k_parts[part][span, :] = paged[:, :, columns].reshape(prefix_rows, HEAD_SIZE)
        v_parts[part][span, pl.ds(0, HEAD_SIZE)] = paged[:, :, value_columns].reshape(
            prefix_rows, HEAD_SIZE
        )
    join_heads(False, rows, *work, bias_ref, level_ref, mean_ref, q_ref, mean_out, level_out)


def last_kernel(
    rows, cos_ref, sin_ref, bias_ref, level_ref, mean_ref, q_ref, key_ref, swapped_value,
    passed_value, direct_value, out_ref, *refs,
):
    work = split_work(refs)
    k_parts, v_parts = work[:2]
    group = pl.program_id(0)
    even = lax.rem(lax.axis_index("blk"), 2) == 0

    @pl.when(group == 0)
    def _():
        fill_ones(v_parts)

    for part in range(HEADS_PER_STEP):
        lanes = pl.ds(part * HEAD_SIZE, HEAD_SIZE)
        rotate_rows(k_parts[part], 0, key_ref, lanes, cos_ref, sin_ref)
        start = 0
        for arrived in (passed_value, direct_value):
            span = pl.ds(start, arrived.shape[1])
            v_parts[part][span, pl.ds(0, HEAD_SIZE)] = jnp.where(
                even, arrived[0, :, lanes], swapped_value[0, span, lanes]
            )
            start += arrived.shape[1]
    join_heads(True, rows, *work, bias_ref, level_ref, mean_ref, q_ref, out_ref, None)


def join(cosine, signed_sine, bias, level, mean, query, arrived, pages=None):
    rows = query.shape[1]
    whole = lambda group: (0, 0)
    by_group = lambda group: (0, 0, group)
    width = HEADS_PER_STEP * GROUP * HEAD_SIZE
    wide = pl.BlockSpec((1, rows, width), by_group)
    flat = pl.BlockSpec((rows, width), lambda group: (0, group))
    table = pl.BlockSpec(cosine.shape, whole)
    in_specs = [table, table, pl.BlockSpec(bias.shape, whole), flat, flat, wide]
    arrived_specs = [
        pl.BlockSpec((1, array.shape[1], HEADS_PER_STEP * HEAD_SIZE), by_group)
        for array in arrived
    ]
    operands = [cosine, signed_sine, bias, level, mean, query]
    scratch = work_shapes(rows, bias.shape[1])
    if pages is None:
        kernel = lambda *refs: last_kernel(rows, *refs)
        out_specs, out_shape = wide, jax.ShapeDtypeStruct(query.shape, jnp.bfloat16)
    else:
        numbers, found = pages
        places, shards = [shard[:2] for shard in found], [shard[2] for shard in found]
        kernel = lambda *refs: far_kernel(
            rows, shards[0].shape[0], places, len(arrived) // 2, arrived[0].shape[2], *refs
        )
        in_specs = [
            pl.BlockSpec(memory_space=pltpu.SMEM),
            *in_specs,
            *[pl.BlockSpec(memory_space=pl.ANY)] * len(shards),
        ]
        operands = [numbers, *operands, *shards]
        out_specs = [flat, flat]
        out_shape = [
            jax.ShapeDtypeStruct(array.shape, jnp.float32) for array in (mean, level)
        ]
        scratch = [
            pltpu.VMEM(numbers.shape + shards[0].shape[1:], jnp.bfloat16),
            pltpu.SemaphoreType.DMA(numbers.shape),
        ] + scratch
    return pl.pallas_call(
        kernel,
        grid=(KEY_VALUE_HEADS // HEADS_PER_STEP,),
        in_specs=in_specs + arrived_specs,
        out_specs=out_specs,
        out_shape=out_shape,
        scratch_shapes=scratch,
        compiler_params=pltpu.CompilerParams(vmem_limit_bytes=vmem_bytes(bias.shape[1])),
        cost_estimate=JOIN_COST,
        name="last" if pages is None else "far",
    )(*operands, *arrived)


def pool_shards(pool, after):
    count = lax.axis_size("batch")

    def swapped(shard, bit):
        return lax.ppermute(shard, "batch", [(c, c ^ bit) for c in range(count)])

    bits = [count >> (step + 1) for step in range(count.bit_length() - 1)]
    shards = {bit: swapped(pool, bit) for bit in bits}
    shards, after = lax.optimization_barrier((shards, after))
    shards = {apart: [shard] for apart, shard in shards.items()}
    for bit in reversed(bits):
        for apart, pieces in list(shards.items()):
            if apart ^ bit not in shards and apart != bit:
                if len(pieces) == 1:
                    middle = pool.shape[0] // 2
                    pieces = [pieces[0][:middle], pieces[0][middle:]]
                shards[apart ^ bit] = [swapped(piece, bit) for piece in pieces]
    found = []
    for apart, pieces in sorted(shards.items()):
        held = pool.shape[0] // len(pieces)
        found += [(apart, place * held, piece) for place, piece in enumerate(pieces)]
    return found


def per_device(queries, keys, values, seg_ids, lengths, live, page_table, pool):
    steps = live.shape[2]
    blocks = lax.axis_size("blk")
    far = [shifted(keys, 2), shifted(values, 2)]
    for step in range(3, steps + 1):
        far += [shifted(keys, step), shifted(values, step)]
    swap = [(j, j ^ 1) for j in range(blocks)]
    even = lax.rem(lax.axis_index("blk"), 2) == 0
    swapped_value = lax.ppermute(values, "blk", swap)
    integers = jnp.concatenate([lengths.ravel(), live.ravel(), jnp.swapaxes(page_table, 1, 2).ravel()])
    (
        table, cos_own, sin_own, cos_last, sin_last, cos_far, sin_far, own_bias, last_bias, far_bias
    ) = tables(keys.shape[1], pool.shape[1], integers, lengths.shape[1], steps, page_table.shape)
    query, key, near_key, near_value, own_shard = prepare(
        cos_own, sin_own, queries, keys, values, pool
    )
    to_swap = jnp.where(even, keys, far[0])
    far_key = lax.ppermute(to_swap, "blk", swap)
    split = values.shape[1] * 3 // 4
    passed_value = lax.ppermute(
        swapped_value[:, :split], "blk", [(j, j + 2) for j in range(0, blocks - 2, 2)]
    )
    mean, level = attend_own(own_bias, query, near_key, near_value)
    shards = pool_shards(pool, (level, to_swap, swapped_value))
    pieces, later_values = lax.optimization_barrier(
        ([shard[2] for shard in shards], values[:, split:])
    )
    shards = [(*shard[:2], piece) for shard, piece in zip(shards, pieces)]
    direct_value = lax.ppermute(
        later_values, "blk", [(j, j + 1) for j in range(1, blocks - 1, 2)]
    )
    mean, level = join(
        cos_far, sin_far, far_bias, level, mean, query, [*far[::2], *far[1::2]],
        pages=(table, [(0, 0, own_shard), *shards]),
    )
    result = join(
        cos_last, sin_last, last_bias, level, mean, query,
        [far_key, swapped_value, passed_value, direct_value],
    )
    return (result, key)


def solution(mesh):
    in_specs = (
        P("batch", "blk", None),
        P("batch", "blk", None),
        P("batch", "blk", None),
        P("batch", "blk"),
        P("batch", None),
        P("batch", "blk", None),
        P(),
        P("batch", None, None),
    )
    out_specs = (P("batch", "blk", None), P("batch", "blk", None))
    return jax.shard_map(
        per_device, mesh=mesh, in_specs=in_specs, out_specs=out_specs, check_vma=False
    )
```

```python
import math

import jax
import jax.numpy as jnp
import numpy as np
from jax import lax
from jax.experimental import pallas as pl
from jax.experimental.pallas import tpu as pltpu
from jax.sharding import PartitionSpec as P

QUERY_HEADS = 16
KEY_VALUE_HEADS = 8
HEAD_SIZE = 128
GROUP = QUERY_HEADS // KEY_VALUE_HEADS
HALF = HEAD_SIZE // 2
ROPE_BASE = 1000000.0
HIDDEN = -1e30
LANES = 128
ROW_TILE = 64
SOFTMAX_TILE = 16
HEADS_PER_STEP = 2
PREPARE_STEPS = 2


def cost(flops):
    return pl.CostEstimate(flops=flops, bytes_accessed=0, transcendentals=0)


TABLES_COST = cost(2_000_000_000)
PREPARE_COST = cost(0)
OWN_COST = cost(0)
JOIN_COST = cost(0)
EXP2_SCALE = math.log2(math.e) / math.sqrt(HEAD_SIZE)

FREQ_POWERS = [float(ROPE_BASE ** (-(2**k) / HALF)) for k in range(HALF.bit_length() - 1)]

PIO2_A = float(np.float32(1.5703125))
PIO2_B = float(np.float32(4.837512969970703125e-4))
PIO2_C = float(np.float32(math.pi / 2 - 1.5703125 - 4.837512969970703125e-4))


def shifted(value, steps):
    count = lax.axis_size("blk")
    return lax.ppermute(value, "blk", [(source, source + steps) for source in range(count - steps)])


def padded_keys(count):
    return -(-count // LANES) * LANES


def vmem_bytes(key_count):
    return 16 * 1024 * (1024 + key_count)


def sine_cosine(angle):
    turns = jnp.floor(angle * (2.0 / math.pi) + 0.5)
    rest = ((angle - turns * PIO2_A) - turns * PIO2_B) - turns * PIO2_C
    square = rest * rest
    sine = rest + rest * square * (
        -1.6666654611e-1 + square * (8.3321608736e-3 - square * 1.9515295891e-4)
    )
    cosine = 1.0 - 0.5 * square + square * square * (
        4.166664568298827e-2 + square * (-1.388731625493765e-3 + square * 2.443315711809948e-5)
    )
    quadrant = turns.astype(jnp.int32) & 3
    swapped = (quadrant & 1) == 1
    sine_out = jnp.where(swapped, cosine, sine)
    cosine_out = jnp.where(swapped, sine, cosine)
    sine_out = jnp.where(quadrant >= 2, -sine_out, sine_out)
    cosine_out = jnp.where((quadrant == 1) | (quadrant == 2), -cosine_out, cosine_out)
    return sine_out, cosine_out


def rotate(head, cosine, signed_sine):
    wide = head.astype(jnp.float32)
    return (wide * cosine + pltpu.roll(wide, HALF, 1) * signed_sine).astype(jnp.bfloat16)


def tables_kernel(
    rows, steps, segs, prefix_len, table_shape, integers_ref,
    page_out, cos_own, sin_own, cos_last, sin_last, cos_far, sin_far, own_bias, last_bias, far_bias,
):
    block_start = lax.axis_index("blk") * rows
    starts = [jnp.int32(0)]
    for seg in range(1, segs):
        starts.append(starts[-1] + integers_ref[seg - 1])
    lane = lax.broadcasted_iota(jnp.int32, (ROW_TILE, LANES), 1)
    row = lax.broadcasted_iota(jnp.int32, (ROW_TILE, LANES), 0)
    freq = jnp.ones((ROW_TILE, LANES), jnp.float32)
    for bit, power in enumerate(FREQ_POWERS):
        freq = jnp.where((lane >> bit) & 1 == 1, freq * power, freq)
    column = lax.axis_index("batch")
    seg_pages = table_shape[2]
    first = segs + steps + column * segs * seg_pages
    for page in range(segs * seg_pages):
        seg, place = divmod(page, seg_pages)
        page_out[page] = integers_ref[first + place * segs + seg]
    for step in range(steps + 1):
        for tile in range(0, rows, ROW_TILE):
            index = block_start + (tile - step * rows) + row
            own_start = jnp.zeros(index.shape, jnp.int32)
            for seg in range(1, segs):
                own_start = jnp.where(index >= starts[seg], starts[seg], own_start)
            place = (prefix_len + index - own_start).astype(jnp.float32)
            sine, cosine = sine_cosine(place * freq)
            sine = jnp.where(lane < HALF, -sine, sine)
            cos_out, sin_out = ((cos_own, sin_own), (cos_last, sin_last), (cos_far, sin_far))[
                min(step, 2)
            ]
            span = pl.ds(max(step - 2, 0) * rows + tile, ROW_TILE)
            cos_out[span, :] = cosine
            sin_out[span, :] = sine
    for tile in range(0, rows, ROW_TILE):
        span = pl.ds(tile, ROW_TILE)
        query_index = block_start + tile + row
        own_start = jnp.zeros(query_index.shape, jnp.int32)
        first_page_token = jnp.zeros(query_index.shape, jnp.int32)
        for seg in range(1, segs):
            later = query_index >= starts[seg]
            own_start = jnp.where(later, starts[seg], own_start)
            first_page_token = jnp.where(later, seg * prefix_len, first_page_token)
        for step in range(steps + 1):
            limit = query_index
            if step > 0:
                limit = jnp.where(integers_ref[segs + step - 1] > 0, limit, -1)
            for column in range(0, rows, LANES):
                key_index = block_start + (column - step * rows) + lane
                seen = (key_index >= own_start) & (key_index <= limit)
                bias = jnp.where(seen, 0.0, HIDDEN)
                if step == 0:
                    own_bias[span, pl.ds(column, LANES)] = bias
                elif step == 1:
                    last_bias[span, pl.ds(column, LANES)] = bias
                else:
                    far_bias[span, pl.ds((step - 2) * rows + column, LANES)] = bias
        base = (steps - 1) * rows
        for column in range(0, far_bias.shape[1] - base, LANES):
            offset = column + lane - first_page_token
            seen = (offset >= 0) & (offset < prefix_len)
            far_bias[span, pl.ds(base + column, LANES)] = jnp.where(seen, 0.0, HIDDEN)


def tables(rows, pool_page, integers, segs, steps, table_shape):
    prefix_len = table_shape[2] * pool_page
    pages = table_shape[1] * table_shape[2]
    far_rows = (steps - 1) * rows
    far_keys = padded_keys(far_rows + segs * prefix_len)
    block = jax.ShapeDtypeStruct((rows, HEAD_SIZE), jnp.float32)
    far = jax.ShapeDtypeStruct((far_rows, HEAD_SIZE), jnp.float32)
    shapes = [
        jax.ShapeDtypeStruct((pages,), jnp.int32),
        *[block] * 4,
        far,
        far,
        *[jax.ShapeDtypeStruct((rows, rows), jnp.float32)] * 2,
        jax.ShapeDtypeStruct((rows, far_keys), jnp.float32),
    ]
    return pl.pallas_call(
        lambda *refs: tables_kernel(rows, steps, segs, prefix_len, table_shape, *refs),
        in_specs=[pl.BlockSpec(memory_space=pltpu.SMEM)],
        out_specs=[pl.BlockSpec(memory_space=pltpu.SMEM)]
        + [pl.BlockSpec(memory_space=pltpu.VMEM)] * (len(shapes) - 1),
        out_shape=shapes,
        compiler_params=pltpu.CompilerParams(vmem_limit_bytes=vmem_bytes(far_keys + far_rows)),
        cost_estimate=TABLES_COST,
        name="tables",
    )(integers)


def prepare_kernel(
    rows, cos_own, sin_own, q_ref, k_ref, v_ref, pool_ref, q_out, k_out, k_copy, v_copy, pool_copy
):
    for tile in range(0, rows, ROW_TILE):
        span = pl.ds(tile, ROW_TILE)
        cosine = cos_own[span, :]
        signed_sine = sin_own[span, :]
        for source, target in ((q_ref, q_out), (k_ref, k_out)):
            for start in range(0, source.shape[2], HEAD_SIZE):
                columns = pl.ds(start, HEAD_SIZE)
                turned = rotate(source[0, span, columns], cosine, signed_sine)
                target[0, span, columns] = turned
                if source is k_ref:
                    k_copy[0, span, columns] = turned
    v_copy[...] = v_ref[...]
    pool_copy[...] = pool_ref[...]


def prepare(cosine, signed_sine, queries, keys, values, pool):
    rows = queries.shape[1]
    whole = lambda part: (0, 0)
    by_part = lambda part: (0, 0, part)
    wide = pl.BlockSpec((1, rows, queries.shape[2] // PREPARE_STEPS), by_part)
    narrow = pl.BlockSpec((1, rows, keys.shape[2] // PREPARE_STEPS), by_part)
    some_pages = pl.BlockSpec(
        (pool.shape[0] // PREPARE_STEPS, *pool.shape[1:]), lambda part: (part, 0, 0)
    )
    table = pl.BlockSpec(cosine.shape, whole)
    return pl.pallas_call(
        lambda *refs: prepare_kernel(rows, *refs),
        grid=(PREPARE_STEPS,),
        in_specs=[table, table, wide, narrow, narrow, some_pages],
        out_specs=[wide, narrow, narrow, narrow, some_pages],
        out_shape=[
            jax.ShapeDtypeStruct(array.shape, array.dtype)
            for array in (queries, keys, keys, values, pool)
        ],
        compiler_params=pltpu.CompilerParams(vmem_limit_bytes=vmem_bytes(rows)),
        cost_estimate=PREPARE_COST,
        name="prepare",
    )(cosine, signed_sine, queries, keys, values, pool)


def stacked_queries(q_ref, part):
    return jnp.concatenate(
        [q_ref[0, :, pl.ds((part * GROUP + h) * HEAD_SIZE, HEAD_SIZE)] for h in range(GROUP)],
        axis=0,
    )


def rotate_rows(target, first, source, lanes, cos_ref, sin_ref):
    rows = source.shape[1]
    for tile in range(0, rows, ROW_TILE):
        span = pl.ds(first + tile, ROW_TILE)
        target[span, :] = rotate(
            source[0, pl.ds(tile, ROW_TILE), lanes], cos_ref[span, :], sin_ref[span, :]
        )


def own_kernel(rows, bias_ref, q_ref, k_ref, v_ref, mean_ref, level_ref, *work):
    k_parts, v_parts, scores, weights, tops = split_work(work)
    group = pl.program_id(0)

    @pl.when(group == 0)
    def _():
        fill_ones(v_parts)
        level_ref[...] = jnp.zeros(level_ref.shape, jnp.float32)

    for part in range(HEADS_PER_STEP):
        lanes = pl.ds(part * HEAD_SIZE, HEAD_SIZE)
        k_parts[part][...] = k_ref[0, :, lanes]
        v_parts[part][:, pl.ds(0, HEAD_SIZE)] = v_ref[0, :, lanes]

    for part in range(HEADS_PER_STEP):
        score_part(part, q_ref, k_parts, scores)
    lane = lax.broadcasted_iota(jnp.int32, (rows, LANES), 1)
    for part in range(HEADS_PER_STEP):
        for start in range(0, GROUP * rows, SOFTMAX_TILE):
            span = pl.ds(start, SOFTMAX_TILE)
            bias = bias_ref[pl.ds(start % rows, SOFTMAX_TILE), :]
            score = scores[part][span, :] * EXP2_SCALE + bias
            highest = jnp.max(score, axis=1, keepdims=True)
            weights[part][span, :] = jnp.exp2(score - highest).astype(jnp.bfloat16)
            tops[part][span, :] = jnp.broadcast_to(highest, (SOFTMAX_TILE, LANES))
        summed = jnp.dot(weights[part][...], v_parts[part][...], preferred_element_type=jnp.float32)
        total = summed[:, HEAD_SIZE:]
        store_part(part, group, rows, lane, summed[:, :HEAD_SIZE] / total,
                   tops[part][...] + jnp.log2(total), mean_ref, level_ref)


def fill_ones(v_parts):
    for v_all in v_parts:
        v_all[:, pl.ds(HEAD_SIZE, HEAD_SIZE)] = jnp.ones((v_all.shape[0], HEAD_SIZE), jnp.bfloat16)


def split_work(work):
    return [work[i : i + HEADS_PER_STEP] for i in range(0, len(work), HEADS_PER_STEP)]


def score_part(part, q_ref, k_parts, scores):
    scores[part][...] = lax.dot_general(
        stacked_queries(q_ref, part), k_parts[part][...], (((1,), (1,)), ((), ())),
        preferred_element_type=jnp.float32,
    )


def store_part(part, group, rows, lane, mean, level, mean_ref, level_ref):
    for h in range(GROUP):
        own = part * GROUP + h
        span = slice(h * rows, (h + 1) * rows)
        mean_ref[:, pl.ds(own * HEAD_SIZE, HEAD_SIZE)] = mean[span].astype(jnp.bfloat16)
        head = group * (HEADS_PER_STEP * GROUP) + own
        level_ref[...] = jnp.where(lane == head, level[span], level_ref[...])


def work_shapes(rows, key_count):
    shapes = [
        pltpu.VMEM((key_count, HEAD_SIZE), jnp.bfloat16),
        pltpu.VMEM((key_count, 2 * HEAD_SIZE), jnp.bfloat16),
        pltpu.VMEM((GROUP * rows, key_count), jnp.float32),
        pltpu.VMEM((GROUP * rows, key_count), jnp.bfloat16),
        pltpu.VMEM((GROUP * rows, LANES), jnp.float32),
    ]
    return [shape for shape in shapes for _ in range(HEADS_PER_STEP)]


def attend_own(bias, query, key, value):
    rows, q_width = query.shape[1:]
    by_group = lambda group: (0, 0, group)
    narrow = pl.BlockSpec((1, rows, HEADS_PER_STEP * HEAD_SIZE), by_group)
    wide = HEADS_PER_STEP * GROUP * HEAD_SIZE
    return pl.pallas_call(
        lambda *refs: own_kernel(rows, *refs),
        grid=(KEY_VALUE_HEADS // HEADS_PER_STEP,),
        in_specs=[
            pl.BlockSpec(bias.shape, lambda group: (0, 0)),
            pl.BlockSpec((1, rows, wide), by_group),
            narrow,
            narrow,
        ],
        out_specs=[
            pl.BlockSpec((rows, wide), lambda group: (0, group)),
            pl.BlockSpec((rows, LANES), lambda group: (0, 0)),
        ],
        out_shape=[
            jax.ShapeDtypeStruct((rows, q_width), jnp.bfloat16),
            jax.ShapeDtypeStruct((rows, LANES), jnp.float32),
        ],
        scratch_shapes=work_shapes(rows, rows),
        compiler_params=pltpu.CompilerParams(vmem_limit_bytes=vmem_bytes(rows)),
        cost_estimate=OWN_COST,
        name="own",
    )(bias, query, key, value)


def page_copies(start, table_ref, pool_rows, places, shards, paged, sem):
    column = lax.axis_index("batch")

    def copy(shard, place, page):
        return pltpu.make_async_copy(shard.at[place], paged.at[page], sem.at[page])

    for page in range(paged.shape[0]):
        if not start:
            copy(shards[0], 0, page).wait()
            continue
        number = table_ref[page]
        apart = lax.div(number, jnp.int32(pool_rows)) ^ column
        place = lax.rem(number, jnp.int32(pool_rows))
        for (which, first), shard in zip(places, shards):
            inside = place - first

            @pl.when((apart == which) & (inside >= 0) & (inside < shard.shape[0]))
            def _(shard=shard, inside=inside, page=page):
                copy(shard, inside, page).start()


def join_heads(
    final, group, rows, k_parts, v_parts, scores, weights, tops,
    bias_ref, level_ref, mean_ref, q_ref, out_ref, level_out,
):
    for part in range(HEADS_PER_STEP):
        score_part(part, q_ref, k_parts, scores)
    lane = lax.broadcasted_iota(jnp.int32, (SOFTMAX_TILE, LANES), 1)
    wide_lane = lax.broadcasted_iota(jnp.int32, (rows, LANES), 1)
    for part in range(HEADS_PER_STEP):
        for start in range(0, GROUP * rows, SOFTMAX_TILE):
            span = pl.ds(start, SOFTMAX_TILE)
            row_span = pl.ds(start % rows, SOFTMAX_TILE)
            head = group * (HEADS_PER_STEP * GROUP) + part * GROUP + start // rows
            score = scores[part][span, :] * EXP2_SCALE + bias_ref[row_span, :]
            level = jnp.sum(
                jnp.where(lane == head, level_ref[row_span, :], 0.0), axis=1, keepdims=True
            )
            highest = jnp.maximum(jnp.max(score, axis=1, keepdims=True), level)
            weights[part][span, :] = jnp.exp2(score - highest).astype(jnp.bfloat16)
            if final:
                shrink = jnp.exp2(level - highest)
                tops[part][span, :] = jnp.broadcast_to(shrink, (SOFTMAX_TILE, LANES))
            else:
                tops[part][span, :] = jnp.where(lane < HALF, highest, level)
        summed = jnp.dot(weights[part][...], v_parts[part][...], preferred_element_type=jnp.float32)
        if final:
            shrink = tops[part][...]
        else:
            both = tops[part][...]
            turned = pltpu.roll(both, HALF, 1)
            low = lax.broadcasted_iota(jnp.int32, both.shape, 1) < HALF
            highest = jnp.where(low, both, turned)
            shrink = jnp.exp2(jnp.where(low, turned, both) - highest)
        total = summed[:, HEAD_SIZE:] + shrink
        before = jnp.concatenate(
            [mean_ref[:, pl.ds((part * GROUP + h) * HEAD_SIZE, HEAD_SIZE)] for h in range(GROUP)],
            axis=0,
        )
        mean = (before.astype(jnp.float32) * shrink + summed[:, :HEAD_SIZE]) / total
        if final:
            for h in range(GROUP):
                lanes = pl.ds((part * GROUP + h) * HEAD_SIZE, HEAD_SIZE)
                out_ref[0, :, lanes] = mean[h * rows : (h + 1) * rows].astype(jnp.bfloat16)
        else:
            level = highest + jnp.log2(total)
            store_part(part, group, rows, wide_lane, mean, level, out_ref, level_out)


def far_kernel(rows, pool_rows, places, blocks, kv_width, *refs):
    table_ref, cos_ref, sin_ref, bias_ref, level_ref, mean_ref, q_ref = refs[:7]
    shards, refs = refs[7 : 7 + len(places)], refs[7 + len(places) :]
    keys, values, refs = refs[:blocks], refs[blocks : 2 * blocks], refs[2 * blocks :]
    mean_out, level_out, paged, sem = refs[:4]
    work = split_work(refs[4:])
    k_parts, v_parts = work[:2]
    group = pl.program_id(0)
    prefix_rows = paged.shape[0] * paged.shape[1]
    base = blocks * rows

    @pl.when(group == 0)
    def _():
        page_copies(True, table_ref, pool_rows, places, shards, paged, sem)
        fill_ones(v_parts)
        level_out[...] = jnp.zeros(level_out.shape, jnp.float32)
        rest = k_parts[0].shape[0] - base - prefix_rows
        if rest:
            blank = jnp.zeros((rest, HEAD_SIZE), jnp.bfloat16)
            for k_all, v_all in zip(k_parts, v_parts):
                k_all[pl.ds(base + prefix_rows, rest), :] = blank
                v_all[pl.ds(base + prefix_rows, rest), pl.ds(0, HEAD_SIZE)] = blank

    for part in range(HEADS_PER_STEP):
        lanes = pl.ds(part * HEAD_SIZE, HEAD_SIZE)
        for block in range(blocks):
            rotate_rows(k_parts[part], block * rows, keys[block], lanes, cos_ref, sin_ref)
            span = pl.ds(block * rows, rows)
            v_parts[part][span, pl.ds(0, HEAD_SIZE)] = values[block][0, :, lanes]

    @pl.when(group == 0)
    def _():
        page_copies(False, table_ref, pool_rows, places, shards, paged, sem)

    for part in range(HEADS_PER_STEP):
        start = (group * HEADS_PER_STEP + part) * HEAD_SIZE
        columns = pl.ds(pl.multiple_of(start, HEAD_SIZE), HEAD_SIZE)
        value_columns = pl.ds(pl.multiple_of(kv_width + start, HEAD_SIZE), HEAD_SIZE)
        span = pl.ds(base, prefix_rows)
        k_parts[part][span, :] = paged[:, :, columns].reshape(prefix_rows, HEAD_SIZE)
        v_parts[part][span, pl.ds(0, HEAD_SIZE)] = paged[:, :, value_columns].reshape(
            prefix_rows, HEAD_SIZE
        )
    join_heads(
        False, group, rows, *work, bias_ref, level_ref, mean_ref, q_ref, mean_out, level_out
    )


def last_kernel(
    rows, cos_ref, sin_ref, bias_ref, level_ref, mean_ref, q_ref, key_ref, swapped_value,
    passed_value, direct_value, out_ref, *refs,
):
    work = split_work(refs)
    k_parts, v_parts = work[:2]
    group = pl.program_id(0)
    even = lax.rem(lax.axis_index("blk"), 2) == 0

    @pl.when(group == 0)
    def _():
        fill_ones(v_parts)

    for part in range(HEADS_PER_STEP):
        lanes = pl.ds(part * HEAD_SIZE, HEAD_SIZE)
        rotate_rows(k_parts[part], 0, key_ref, lanes, cos_ref, sin_ref)
        start = 0
        for arrived in (passed_value, direct_value):
            span = pl.ds(start, arrived.shape[1])
            v_parts[part][span, pl.ds(0, HEAD_SIZE)] = jnp.where(
                even, arrived[0, :, lanes], swapped_value[0, span, lanes]
            )
            start += arrived.shape[1]
    join_heads(True, group, rows, *work, bias_ref, level_ref, mean_ref, q_ref, out_ref, None)


def join(cosine, signed_sine, bias, level, mean, query, arrived, pages=None):
    rows = query.shape[1]
    whole = lambda group: (0, 0)
    by_group = lambda group: (0, 0, group)
    width = HEADS_PER_STEP * GROUP * HEAD_SIZE
    wide = pl.BlockSpec((1, rows, width), by_group)
    flat = pl.BlockSpec((rows, width), lambda group: (0, group))
    level_spec = pl.BlockSpec(level.shape, whole)
    table = pl.BlockSpec(cosine.shape, whole)
    in_specs = [table, table, pl.BlockSpec(bias.shape, whole), level_spec, flat, wide]
    arrived_specs = [
        pl.BlockSpec((1, array.shape[1], HEADS_PER_STEP * HEAD_SIZE), by_group)
        for array in arrived
    ]
    operands = [cosine, signed_sine, bias, level, mean, query]
    scratch = work_shapes(rows, bias.shape[1])
    if pages is None:
        kernel = lambda *refs: last_kernel(rows, *refs)
        out_specs, out_shape = wide, jax.ShapeDtypeStruct(query.shape, jnp.bfloat16)
    else:
        numbers, found = pages
        places, shards = [shard[:2] for shard in found], [shard[2] for shard in found]
        kernel = lambda *refs: far_kernel(
            rows, shards[0].shape[0], places, len(arrived) // 2, arrived[0].shape[2], *refs
        )
        in_specs = [
            pl.BlockSpec(memory_space=pltpu.SMEM),
            *in_specs,
            *[pl.BlockSpec(memory_space=pl.ANY)] * len(shards),
        ]
        operands = [numbers, *operands, *shards]
        out_specs = [flat, level_spec]
        out_shape = [
            jax.ShapeDtypeStruct(array.shape, array.dtype) for array in (mean, level)
        ]
        scratch = [
            pltpu.VMEM(numbers.shape + shards[0].shape[1:], jnp.bfloat16),
            pltpu.SemaphoreType.DMA(numbers.shape),
        ] + scratch
    return pl.pallas_call(
        kernel,
        grid=(KEY_VALUE_HEADS // HEADS_PER_STEP,),
        in_specs=in_specs + arrived_specs,
        out_specs=out_specs,
        out_shape=out_shape,
        scratch_shapes=scratch,
        compiler_params=pltpu.CompilerParams(vmem_limit_bytes=vmem_bytes(bias.shape[1])),
        cost_estimate=JOIN_COST,
        name="last" if pages is None else "far",
    )(*operands, *arrived)


def pool_shards(pool, after):
    count = lax.axis_size("batch")

    def swapped(shard, bit):
        return lax.ppermute(shard, "batch", [(c, c ^ bit) for c in range(count)])

    bits = [count >> (step + 1) for step in range(count.bit_length() - 1)]
    shards = {bit: swapped(pool, bit) for bit in bits}
    shards, after = lax.optimization_barrier((shards, after))
    shards = {apart: [shard] for apart, shard in shards.items()}
    for bit in reversed(bits):
        for apart, pieces in list(shards.items()):
            if apart ^ bit not in shards and apart != bit:
                if len(pieces) == 1:
                    middle = pool.shape[0] // 2
                    pieces = [pieces[0][:middle], pieces[0][middle:]]
                shards[apart ^ bit] = [swapped(piece, bit) for piece in pieces]
    found = []
    for apart, pieces in sorted(shards.items()):
        held = pool.shape[0] // len(pieces)
        found += [(apart, place * held, piece) for place, piece in enumerate(pieces)]
    return found


def per_device(queries, keys, values, seg_ids, lengths, live, page_table, pool):
    steps = live.shape[2]
    blocks = lax.axis_size("blk")
    far = [shifted(keys, 2), shifted(values, 2)]
    for step in range(3, steps + 1):
        far += [shifted(keys, step), shifted(values, step)]
    swap = [(j, j ^ 1) for j in range(blocks)]
    even = lax.rem(lax.axis_index("blk"), 2) == 0
    swapped_value = lax.ppermute(values, "blk", swap)
    integers = jnp.concatenate([lengths.ravel(), live.ravel(), jnp.swapaxes(page_table, 1, 2).ravel()])
    (
        table, cos_own, sin_own, cos_last, sin_last, cos_far, sin_far, own_bias, last_bias, far_bias
    ) = tables(keys.shape[1], pool.shape[1], integers, lengths.shape[1], steps, page_table.shape)
    query, key, near_key, near_value, own_shard = prepare(
        cos_own, sin_own, queries, keys, values, pool
    )
    to_swap = jnp.where(even, keys, far[0])
    far_key = lax.ppermute(to_swap, "blk", swap)
    split = values.shape[1] * 3 // 4
    passed_value = lax.ppermute(
        swapped_value[:, :split], "blk", [(j, j + 2) for j in range(0, blocks - 2, 2)]
    )
    mean, level = attend_own(own_bias, query, near_key, near_value)
    shards = pool_shards(pool, (level, to_swap, swapped_value))
    pieces, later_values = lax.optimization_barrier(
        ([shard[2] for shard in shards], values[:, split:])
    )
    shards = [(*shard[:2], piece) for shard, piece in zip(shards, pieces)]
    direct_value = lax.ppermute(
        later_values, "blk", [(j, j + 1) for j in range(1, blocks - 1, 2)]
    )
    mean, level = join(
        cos_far, sin_far, far_bias, level, mean, query, [*far[::2], *far[1::2]],
        pages=(table, [(0, 0, own_shard), *shards]),
    )
    result = join(
        cos_last, sin_last, last_bias, level, mean, query,
        [far_key, swapped_value, passed_value, direct_value],
    )
    return (result, key)


def solution(mesh):
    in_specs = (
        P("batch", "blk", None),
        P("batch", "blk", None),
        P("batch", "blk", None),
        P("batch", "blk"),
        P("batch", None),
        P("batch", "blk", None),
        P(),
        P("batch", None, None),
    )
    out_specs = (P("batch", "blk", None), P("batch", "blk", None))
    return jax.shard_map(
        per_device, mesh=mesh, in_specs=in_specs, out_specs=out_specs, check_vma=False
    )
```

```python
import math

import jax
import jax.numpy as jnp
import numpy as np
from jax import lax
from jax.experimental import pallas as pl
from jax.experimental.pallas import tpu as pltpu
from jax.sharding import PartitionSpec as P

QUERY_HEADS = 16
KEY_VALUE_HEADS = 8
HEAD_SIZE = 128
GROUP = QUERY_HEADS // KEY_VALUE_HEADS
HALF = HEAD_SIZE // 2
ROPE_BASE = 1000000.0
HIDDEN = -1e30
LANES = 128
ROW_TILE = 64
SOFTMAX_TILE = 16
HEADS_PER_STEP = 2
PREPARE_STEPS = 2


def cost(flops):
    return pl.CostEstimate(flops=flops, bytes_accessed=0, transcendentals=0)


TABLES_COST = cost(2_000_000_000)
PREPARE_COST = cost(0)
OWN_COST = cost(0)
JOIN_COST = cost(0)
GATHER_COST = cost(0)
EXP2_SCALE = math.log2(math.e) / math.sqrt(HEAD_SIZE)

FREQ_POWERS = [float(ROPE_BASE ** (-(2**k) / HALF)) for k in range(HALF.bit_length() - 1)]

PIO2_A = float(np.float32(1.5703125))
PIO2_B = float(np.float32(4.837512969970703125e-4))
PIO2_C = float(np.float32(math.pi / 2 - 1.5703125 - 4.837512969970703125e-4))


def shifted(value, steps):
    count = lax.axis_size("blk")
    return lax.ppermute(value, "blk", [(source, source + steps) for source in range(count - steps)])


def padded_keys(count):
    return -(-count // LANES) * LANES


def vmem_bytes(key_count):
    return 16 * 1024 * (1024 + key_count)


def sine_cosine(angle):
    turns = jnp.floor(angle * (2.0 / math.pi) + 0.5)
    rest = ((angle - turns * PIO2_A) - turns * PIO2_B) - turns * PIO2_C
    square = rest * rest
    sine = rest + rest * square * (
        -1.6666654611e-1 + square * (8.3321608736e-3 - square * 1.9515295891e-4)
    )
    cosine = 1.0 - 0.5 * square + square * square * (
        4.166664568298827e-2 + square * (-1.388731625493765e-3 + square * 2.443315711809948e-5)
    )
    quadrant = turns.astype(jnp.int32) & 3
    swapped = (quadrant & 1) == 1
    sine_out = jnp.where(swapped, cosine, sine)
    cosine_out = jnp.where(swapped, sine, cosine)
    sine_out = jnp.where(quadrant >= 2, -sine_out, sine_out)
    cosine_out = jnp.where((quadrant == 1) | (quadrant == 2), -cosine_out, cosine_out)
    return sine_out, cosine_out


def rotate(head, cosine, signed_sine):
    wide = head.astype(jnp.float32)
    return (wide * cosine + pltpu.roll(wide, HALF, 1) * signed_sine).astype(jnp.bfloat16)


def tables_kernel(
    rows, steps, segs, prefix_len, table_shape, integers_ref,
    page_out, cos_own, sin_own, cos_last, sin_last, cos_far, sin_far, own_bias, last_bias, far_bias,
):
    block_start = lax.axis_index("blk") * rows
    starts = [jnp.int32(0)]
    for seg in range(1, segs):
        starts.append(starts[-1] + integers_ref[seg - 1])
    lane = lax.broadcasted_iota(jnp.int32, (ROW_TILE, LANES), 1)
    row = lax.broadcasted_iota(jnp.int32, (ROW_TILE, LANES), 0)
    freq = jnp.ones((ROW_TILE, LANES), jnp.float32)
    for bit, power in enumerate(FREQ_POWERS):
        freq = jnp.where((lane >> bit) & 1 == 1, freq * power, freq)
    column = lax.axis_index("batch")
    seg_pages = table_shape[2]
    first = segs + steps + column * segs * seg_pages
    for page in range(segs * seg_pages):
        seg, place = divmod(page, seg_pages)
        page_out[page] = integers_ref[first + place * segs + seg]
    for step in range(steps + 1):
        for tile in range(0, rows, ROW_TILE):
            index = block_start + (tile - step * rows) + row
            own_start = jnp.zeros(index.shape, jnp.int32)
            for seg in range(1, segs):
                own_start = jnp.where(index >= starts[seg], starts[seg], own_start)
            place = (prefix_len + index - own_start).astype(jnp.float32)
            sine, cosine = sine_cosine(place * freq)
            sine = jnp.where(lane < HALF, -sine, sine)
            cos_out, sin_out = ((cos_own, sin_own), (cos_last, sin_last), (cos_far, sin_far))[
                min(step, 2)
            ]
            span = pl.ds(max(step - 2, 0) * rows + tile, ROW_TILE)
            cos_out[span, :] = cosine
            sin_out[span, :] = sine
    for tile in range(0, rows, ROW_TILE):
        span = pl.ds(tile, ROW_TILE)
        query_index = block_start + tile + row
        own_start = jnp.zeros(query_index.shape, jnp.int32)
        first_page_token = jnp.zeros(query_index.shape, jnp.int32)
        for seg in range(1, segs):
            later = query_index >= starts[seg]
            own_start = jnp.where(later, starts[seg], own_start)
            first_page_token = jnp.where(later, seg * prefix_len, first_page_token)
        for step in range(steps + 1):
            limit = query_index
            if step > 0:
                limit = jnp.where(integers_ref[segs + step - 1] > 0, limit, -1)
            for column in range(0, rows, LANES):
                key_index = block_start + (column - step * rows) + lane
                seen = (key_index >= own_start) & (key_index <= limit)
                bias = jnp.where(seen, 0.0, HIDDEN)
                if step == 0:
                    own_bias[span, pl.ds(column, LANES)] = bias
                elif step == 1:
                    last_bias[span, pl.ds(column, LANES)] = bias
                else:
                    far_bias[span, pl.ds((step - 2) * rows + column, LANES)] = bias
        base = (steps - 1) * rows
        for column in range(0, far_bias.shape[1] - base, LANES):
            offset = column + lane - first_page_token
            seen = (offset >= 0) & (offset < prefix_len)
            far_bias[span, pl.ds(base + column, LANES)] = jnp.where(seen, 0.0, HIDDEN)


def tables(rows, pool_page, integers, segs, steps, table_shape):
    prefix_len = table_shape[2] * pool_page
    pages = table_shape[1] * table_shape[2]
    far_rows = (steps - 1) * rows
    far_keys = padded_keys(far_rows + segs * prefix_len)
    block = jax.ShapeDtypeStruct((rows, HEAD_SIZE), jnp.float32)
    far = jax.ShapeDtypeStruct((far_rows, HEAD_SIZE), jnp.float32)
    shapes = [
        jax.ShapeDtypeStruct((pages,), jnp.int32),
        *[block] * 4,
        far,
        far,
        *[jax.ShapeDtypeStruct((rows, rows), jnp.float32)] * 2,
        jax.ShapeDtypeStruct((rows, far_keys), jnp.float32),
    ]
    return pl.pallas_call(
        lambda *refs: tables_kernel(rows, steps, segs, prefix_len, table_shape, *refs),
        in_specs=[pl.BlockSpec(memory_space=pltpu.SMEM)],
        out_specs=[pl.BlockSpec(memory_space=pltpu.SMEM)]
        + [pl.BlockSpec(memory_space=pltpu.VMEM)] * (len(shapes) - 1),
        out_shape=shapes,
        compiler_params=pltpu.CompilerParams(vmem_limit_bytes=vmem_bytes(far_keys + far_rows)),
        cost_estimate=TABLES_COST,
        name="tables",
    )(integers)


def prepare_kernel(
    rows, cos_own, sin_own, q_ref, k_ref, v_ref, pool_ref, q_out, k_out, k_copy, v_copy, pool_copy
):
    for tile in range(0, rows, ROW_TILE):
        span = pl.ds(tile, ROW_TILE)
        cosine = cos_own[span, :]
        signed_sine = sin_own[span, :]
        for source, target in ((q_ref, q_out), (k_ref, k_out)):
            for start in range(0, source.shape[2], HEAD_SIZE):
                columns = pl.ds(start, HEAD_SIZE)
                turned = rotate(source[0, span, columns], cosine, signed_sine)
                target[0, span, columns] = turned
                if source is k_ref:
                    k_copy[0, span, columns] = turned
    v_copy[...] = v_ref[...]
    pool_copy[...] = pool_ref[...]


def prepare(cosine, signed_sine, queries, keys, values, pool):
    rows = queries.shape[1]
    whole = lambda part: (0, 0)
    by_part = lambda part: (0, 0, part)
    wide = pl.BlockSpec((1, rows, queries.shape[2] // PREPARE_STEPS), by_part)
    narrow = pl.BlockSpec((1, rows, keys.shape[2] // PREPARE_STEPS), by_part)
    some_pages = pl.BlockSpec(
        (pool.shape[0] // PREPARE_STEPS, *pool.shape[1:]), lambda part: (part, 0, 0)
    )
    table = pl.BlockSpec(cosine.shape, whole)
    return pl.pallas_call(
        lambda *refs: prepare_kernel(rows, *refs),
        grid=(PREPARE_STEPS,),
        in_specs=[table, table, wide, narrow, narrow, some_pages],
        out_specs=[wide, narrow, narrow, narrow, some_pages],
        out_shape=[
            jax.ShapeDtypeStruct(array.shape, array.dtype)
            for array in (queries, keys, keys, values, pool)
        ],
        compiler_params=pltpu.CompilerParams(vmem_limit_bytes=vmem_bytes(rows)),
        cost_estimate=PREPARE_COST,
        name="prepare",
    )(cosine, signed_sine, queries, keys, values, pool)


def stacked_queries(q_ref, part):
    return jnp.concatenate(
        [q_ref[0, :, pl.ds((part * GROUP + h) * HEAD_SIZE, HEAD_SIZE)] for h in range(GROUP)],
        axis=0,
    )


def rotate_rows(target, first, source, lanes, cos_ref, sin_ref):
    rows = source.shape[1]
    for tile in range(0, rows, ROW_TILE):
        span = pl.ds(first + tile, ROW_TILE)
        target[span, :] = rotate(
            source[0, pl.ds(tile, ROW_TILE), lanes], cos_ref[span, :], sin_ref[span, :]
        )


def own_kernel(rows, bias_ref, q_ref, k_ref, v_ref, mean_ref, level_ref, *work):
    k_parts, v_parts, scores, weights, tops = split_work(work)
    group = pl.program_id(0)

    @pl.when(group == 0)
    def _():
        fill_ones(v_parts)
        level_ref[...] = jnp.zeros(level_ref.shape, jnp.float32)

    for part in range(HEADS_PER_STEP):
        lanes = pl.ds(part * HEAD_SIZE, HEAD_SIZE)
        k_parts[part][...] = k_ref[0, :, lanes]
        v_parts[part][:, pl.ds(0, HEAD_SIZE)] = v_ref[0, :, lanes]

    for part in range(HEADS_PER_STEP):
        score_part(part, q_ref, k_parts, scores)
    lane = lax.broadcasted_iota(jnp.int32, (rows, LANES), 1)
    for part in range(HEADS_PER_STEP):
        for start in range(0, GROUP * rows, SOFTMAX_TILE):
            span = pl.ds(start, SOFTMAX_TILE)
            bias = bias_ref[pl.ds(start % rows, SOFTMAX_TILE), :]
            score = scores[part][span, :] * EXP2_SCALE + bias
            highest = jnp.max(score, axis=1, keepdims=True)
            weights[part][span, :] = jnp.exp2(score - highest).astype(jnp.bfloat16)
            tops[part][span, :] = jnp.broadcast_to(highest, (SOFTMAX_TILE, LANES))
        summed = jnp.dot(weights[part][...], v_parts[part][...], preferred_element_type=jnp.float32)
        total = summed[:, HEAD_SIZE:]
        store_part(part, group, rows, lane, summed[:, :HEAD_SIZE] / total,
                   tops[part][...] + jnp.log2(total), mean_ref, level_ref)


def fill_ones(v_parts):
    for v_all in v_parts:
        v_all[:, pl.ds(HEAD_SIZE, HEAD_SIZE)] = jnp.ones((v_all.shape[0], HEAD_SIZE), jnp.bfloat16)


def split_work(work):
    return [work[i : i + HEADS_PER_STEP] for i in range(0, len(work), HEADS_PER_STEP)]


def score_part(part, q_ref, k_parts, scores):
    scores[part][...] = lax.dot_general(
        stacked_queries(q_ref, part), k_parts[part][...], (((1,), (1,)), ((), ())),
        preferred_element_type=jnp.float32,
    )


def store_part(part, group, rows, lane, mean, level, mean_ref, level_ref):
    for h in range(GROUP):
        own = part * GROUP + h
        span = slice(h * rows, (h + 1) * rows)
        mean_ref[:, pl.ds(own * HEAD_SIZE, HEAD_SIZE)] = mean[span]
        head = group * (HEADS_PER_STEP * GROUP) + own
        level_ref[...] = jnp.where(lane == head, level[span], level_ref[...])


def work_shapes(rows, key_count):
    shapes = [
        pltpu.VMEM((key_count, HEAD_SIZE), jnp.bfloat16),
        pltpu.VMEM((key_count, 2 * HEAD_SIZE), jnp.bfloat16),
        pltpu.VMEM((GROUP * rows, key_count), jnp.float32),
        pltpu.VMEM((GROUP * rows, key_count), jnp.bfloat16),
        pltpu.VMEM((GROUP * rows, LANES), jnp.float32),
    ]
    return [shape for shape in shapes for _ in range(HEADS_PER_STEP)]


def attend_own(bias, query, key, value):
    rows, q_width = query.shape[1:]
    by_group = lambda group: (0, 0, group)
    narrow = pl.BlockSpec((1, rows, HEADS_PER_STEP * HEAD_SIZE), by_group)
    wide = HEADS_PER_STEP * GROUP * HEAD_SIZE
    return pl.pallas_call(
        lambda *refs: own_kernel(rows, *refs),
        grid=(KEY_VALUE_HEADS // HEADS_PER_STEP,),
        in_specs=[
            pl.BlockSpec(bias.shape, lambda group: (0, 0)),
            pl.BlockSpec((1, rows, wide), by_group),
            narrow,
            narrow,
        ],
        out_specs=[
            pl.BlockSpec((rows, wide), lambda group: (0, group)),
            pl.BlockSpec((rows, LANES), lambda group: (0, 0)),
        ],
        out_shape=[
            jax.ShapeDtypeStruct((rows, q_width), jnp.float32),
            jax.ShapeDtypeStruct((rows, LANES), jnp.float32),
        ],
        scratch_shapes=work_shapes(rows, rows),
        compiler_params=pltpu.CompilerParams(vmem_limit_bytes=vmem_bytes(rows)),
        cost_estimate=OWN_COST,
        name="own",
    )(bias, query, key, value)


def gather_kernel(pool_rows, places, table_ref, *refs):
    *shards, paged, sem = refs
    column = lax.axis_index("batch")

    def copy(shard, place, page):
        return pltpu.make_async_copy(shard.at[place], paged.at[page], sem.at[page])

    for page in range(paged.shape[0]):
        number = table_ref[page]
        apart = lax.div(number, jnp.int32(pool_rows)) ^ column
        place = lax.rem(number, jnp.int32(pool_rows))
        for (which, first), shard in zip(places, shards):
            inside = place - first

            @pl.when((apart == which) & (inside >= 0) & (inside < shard.shape[0]))
            def _(shard=shard, inside=inside, page=page):
                copy(shard, inside, page).start()

    for page in range(paged.shape[0]):
        copy(shards[0], 0, page).wait()


def gather_pages(numbers, found):
    places, shards = [shard[:2] for shard in found], [shard[2] for shard in found]
    pool_rows = shards[0].shape[0]
    return pl.pallas_call(
        lambda *refs: gather_kernel(pool_rows, places, *refs),
        in_specs=[pl.BlockSpec(memory_space=pltpu.SMEM)]
        + [pl.BlockSpec(memory_space=pl.ANY)] * len(shards),
        out_specs=pl.BlockSpec(memory_space=pltpu.VMEM),
        out_shape=jax.ShapeDtypeStruct(numbers.shape + shards[0].shape[1:], jnp.bfloat16),
        scratch_shapes=[pltpu.SemaphoreType.DMA(numbers.shape)],
        compiler_params=pltpu.CompilerParams(vmem_limit_bytes=vmem_bytes(0)),
        cost_estimate=GATHER_COST,
        name="gather",
    )(numbers, *shards)


def join_heads(
    final, group, rows, k_parts, v_parts, scores, weights, tops,
    bias_ref, level_ref, mean_ref, q_ref, out_ref, level_out,
):
    for part in range(HEADS_PER_STEP):
        score_part(part, q_ref, k_parts, scores)
    lane = lax.broadcasted_iota(jnp.int32, (SOFTMAX_TILE, LANES), 1)
    wide_lane = lax.broadcasted_iota(jnp.int32, (rows, LANES), 1)
    for part in range(HEADS_PER_STEP):
        for start in range(0, GROUP * rows, SOFTMAX_TILE):
            span = pl.ds(start, SOFTMAX_TILE)
            row_span = pl.ds(start % rows, SOFTMAX_TILE)
            head = group * (HEADS_PER_STEP * GROUP) + part * GROUP + start // rows
            score = scores[part][span, :] * EXP2_SCALE + bias_ref[row_span, :]
            level = jnp.sum(
                jnp.where(lane == head, level_ref[row_span, :], 0.0), axis=1, keepdims=True
            )
            highest = jnp.maximum(jnp.max(score, axis=1, keepdims=True), level)
            weights[part][span, :] = jnp.exp2(score - highest).astype(jnp.bfloat16)
            if final:
                shrink = jnp.exp2(level - highest)
                tops[part][span, :] = jnp.broadcast_to(shrink, (SOFTMAX_TILE, LANES))
            else:
                tops[part][span, :] = jnp.where(lane < HALF, highest, level)
        summed = jnp.dot(weights[part][...], v_parts[part][...], preferred_element_type=jnp.float32)
        if final:
            shrink = tops[part][...]
        else:
            both = tops[part][...]
            turned = pltpu.roll(both, HALF, 1)
            low = lax.broadcasted_iota(jnp.int32, both.shape, 1) < HALF
            highest = jnp.where(low, both, turned)
            shrink = jnp.exp2(jnp.where(low, turned, both) - highest)
        total = summed[:, HEAD_SIZE:] + shrink
        before = jnp.concatenate(
            [mean_ref[:, pl.ds((part * GROUP + h) * HEAD_SIZE, HEAD_SIZE)] for h in range(GROUP)],
            axis=0,
        )
        mean = (before * shrink + summed[:, :HEAD_SIZE]) / total
        if final:
            for h in range(GROUP):
                lanes = pl.ds((part * GROUP + h) * HEAD_SIZE, HEAD_SIZE)
                out_ref[0, :, lanes] = mean[h * rows : (h + 1) * rows].astype(jnp.bfloat16)
        else:
            level = highest + jnp.log2(total)
            store_part(part, group, rows, wide_lane, mean, level, out_ref, level_out)


def far_kernel(
    rows, blocks, cos_ref, sin_ref, bias_ref, level_ref, mean_ref, q_ref, page_keys, page_values, *refs
):
    keys, values, refs = refs[:blocks], refs[blocks : 2 * blocks], refs[2 * blocks :]
    mean_out, level_out = refs[:2]
    work = split_work(refs[2:])
    k_parts, v_parts = work[:2]
    group = pl.program_id(0)
    prefix_rows = page_keys.shape[0] * page_keys.shape[1]
    base = blocks * rows

    @pl.when(group == 0)
    def _():
        fill_ones(v_parts)
        level_out[...] = jnp.zeros(level_out.shape, jnp.float32)
        rest = k_parts[0].shape[0] - base - prefix_rows
        if rest:
            blank = jnp.zeros((rest, HEAD_SIZE), jnp.bfloat16)
            for k_all, v_all in zip(k_parts, v_parts):
                k_all[pl.ds(base + prefix_rows, rest), :] = blank
                v_all[pl.ds(base + prefix_rows, rest), pl.ds(0, HEAD_SIZE)] = blank

    for part in range(HEADS_PER_STEP):
        lanes = pl.ds(part * HEAD_SIZE, HEAD_SIZE)
        for block in range(blocks):
            rotate_rows(k_parts[part], block * rows, keys[block], lanes, cos_ref, sin_ref)
            span = pl.ds(block * rows, rows)
            v_parts[part][span, pl.ds(0, HEAD_SIZE)] = values[block][0, :, lanes]
        span = pl.ds(base, prefix_rows)
        k_parts[part][span, :] = page_keys[:, :, lanes].reshape(prefix_rows, HEAD_SIZE)
        v_parts[part][span, pl.ds(0, HEAD_SIZE)] = page_values[:, :, lanes].reshape(
            prefix_rows, HEAD_SIZE
        )
    join_heads(
        False, group, rows, *work, bias_ref, level_ref, mean_ref, q_ref, mean_out, level_out
    )


def last_kernel(
    rows, cos_ref, sin_ref, bias_ref, level_ref, mean_ref, q_ref, key_ref, swapped_value,
    passed_value, direct_value, out_ref, *refs,
):
    work = split_work(refs)
    k_parts, v_parts = work[:2]
    group = pl.program_id(0)
    even = lax.rem(lax.axis_index("blk"), 2) == 0

    @pl.when(group == 0)
    def _():
        fill_ones(v_parts)

    for part in range(HEADS_PER_STEP):
        lanes = pl.ds(part * HEAD_SIZE, HEAD_SIZE)
        rotate_rows(k_parts[part], 0, key_ref, lanes, cos_ref, sin_ref)
        start = 0
        for arrived in (passed_value, direct_value):
            span = pl.ds(start, arrived.shape[1])
            v_parts[part][span, pl.ds(0, HEAD_SIZE)] = jnp.where(
                even, arrived[0, :, lanes], swapped_value[0, span, lanes]
            )
            start += arrived.shape[1]
    join_heads(True, group, rows, *work, bias_ref, level_ref, mean_ref, q_ref, out_ref, None)


def join(cosine, signed_sine, bias, level, mean, query, arrived, pages=None):
    rows = query.shape[1]
    whole = lambda group: (0, 0)
    by_group = lambda group: (0, 0, group)
    width = HEADS_PER_STEP * GROUP * HEAD_SIZE
    wide = pl.BlockSpec((1, rows, width), by_group)
    flat = pl.BlockSpec((rows, width), lambda group: (0, group))
    level_spec = pl.BlockSpec(level.shape, whole)
    table = pl.BlockSpec(cosine.shape, whole)
    in_specs = [table, table, pl.BlockSpec(bias.shape, whole), level_spec, flat, wide]
    arrived_specs = [
        pl.BlockSpec((1, array.shape[1], HEADS_PER_STEP * HEAD_SIZE), by_group)
        for array in arrived
    ]
    operands = [cosine, signed_sine, bias, level, mean, query]
    scratch = work_shapes(rows, bias.shape[1])
    if pages is None:
        kernel = lambda *refs: last_kernel(rows, *refs)
        out_specs, out_shape = wide, jax.ShapeDtypeStruct(query.shape, jnp.bfloat16)
    else:
        kernel = lambda *refs: far_kernel(rows, len(arrived) // 2, *refs)
        groups = KEY_VALUE_HEADS // HEADS_PER_STEP
        for first in (0, groups):
            in_specs.append(
                pl.BlockSpec(
                    (*pages.shape[:2], HEADS_PER_STEP * HEAD_SIZE),
                    lambda group, first=first: (0, 0, first + group),
                )
            )
            operands.append(pages)
        out_specs = [flat, level_spec]
        out_shape = [
            jax.ShapeDtypeStruct(array.shape, jnp.float32) for array in (mean, level)
        ]
    return pl.pallas_call(
        kernel,
        grid=(KEY_VALUE_HEADS // HEADS_PER_STEP,),
        in_specs=in_specs + arrived_specs,
        out_specs=out_specs,
        out_shape=out_shape,
        scratch_shapes=scratch,
        compiler_params=pltpu.CompilerParams(vmem_limit_bytes=vmem_bytes(bias.shape[1])),
        cost_estimate=JOIN_COST,
        name="last" if pages is None else "far",
    )(*operands, *arrived)


def pool_shards(pool, after):
    count = lax.axis_size("batch")

    def swapped(shard, bit):
        return lax.ppermute(shard, "batch", [(c, c ^ bit) for c in range(count)])

    bits = [count >> (step + 1) for step in range(count.bit_length() - 1)]
    shards = {bit: swapped(pool, bit) for bit in bits}
    shards, after = lax.optimization_barrier((shards, after))
    shards = {apart: [shard] for apart, shard in shards.items()}
    for bit in reversed(bits):
        for apart, pieces in list(shards.items()):
            if apart ^ bit not in shards and apart != bit:
                if len(pieces) == 1:
                    middle = pool.shape[0] // 2
                    pieces = [pieces[0][:middle], pieces[0][middle:]]
                shards[apart ^ bit] = [swapped(piece, bit) for piece in pieces]
    found = []
    for apart, pieces in sorted(shards.items()):
        held = pool.shape[0] // len(pieces)
        found += [(apart, place * held, piece) for place, piece in enumerate(pieces)]
    return found


def per_device(queries, keys, values, seg_ids, lengths, live, page_table, pool):
    steps = live.shape[2]
    blocks = lax.axis_size("blk")
    far = [shifted(keys, 2), shifted(values, 2)]
    for step in range(3, steps + 1):
        far += [shifted(keys, step), shifted(values, step)]
    swap = [(j, j ^ 1) for j in range(blocks)]
    even = lax.rem(lax.axis_index("blk"), 2) == 0
    swapped_value = lax.ppermute(values, "blk", swap)
    integers = jnp.concatenate([lengths.ravel(), live.ravel(), jnp.swapaxes(page_table, 1, 2).ravel()])
    (
        table, cos_own, sin_own, cos_last, sin_last, cos_far, sin_far, own_bias, last_bias, far_bias
    ) = tables(keys.shape[1], pool.shape[1], integers, lengths.shape[1], steps, page_table.shape)
    query, key, near_key, near_value, own_shard = prepare(
        cos_own, sin_own, queries, keys, values, pool
    )
    to_swap = jnp.where(even, keys, far[0])
    far_key = lax.ppermute(to_swap, "blk", swap)
    split = values.shape[1] * 3 // 4
    passed_value = lax.ppermute(
        swapped_value[:, :split], "blk", [(j, j + 2) for j in range(0, blocks - 2, 2)]
    )
    mean, level = attend_own(own_bias, query, near_key, near_value)
    shards = pool_shards(pool, (level, to_swap, swapped_value))
    pieces, later_values = lax.optimization_barrier(
        ([shard[2] for shard in shards], values[:, split:])
    )
    shards = [(*shard[:2], piece) for shard, piece in zip(shards, pieces)]
    direct_value = lax.ppermute(
        later_values, "blk", [(j, j + 1) for j in range(1, blocks - 1, 2)]
    )
    mean, level = join(
        cos_far, sin_far, far_bias, level, mean, query, [*far[::2], *far[1::2]],
        pages=gather_pages(table, [(0, 0, own_shard), *shards]),
    )
    result = join(
        cos_last, sin_last, last_bias, level, mean, query,
        [far_key, swapped_value, passed_value, direct_value],
    )
    return (result, key)


def solution(mesh):
    in_specs = (
        P("batch", "blk", None),
        P("batch", "blk", None),
        P("batch", "blk", None),
        P("batch", "blk"),
        P("batch", None),
        P("batch", "blk", None),
        P(),
        P("batch", None, None),
    )
    out_specs = (P("batch", "blk", None), P("batch", "blk", None))
    return jax.shard_map(
        per_device, mesh=mesh, in_specs=in_specs, out_specs=out_specs, check_vma=False
    )
```

```python
import math

import jax
import jax.numpy as jnp
import numpy as np
from jax import lax
from jax.experimental import pallas as pl
from jax.experimental.pallas import tpu as pltpu
from jax.sharding import PartitionSpec as P

QUERY_HEADS = 16
KEY_VALUE_HEADS = 8
HEAD_SIZE = 128
GROUP = QUERY_HEADS // KEY_VALUE_HEADS
HALF = HEAD_SIZE // 2
ROPE_BASE = 1000000.0
HIDDEN = -1e30
LANES = 128
ROW_TILE = 64
SOFTMAX_TILE = 16
HEADS_PER_STEP = 2
PREPARE_STEPS = 2


def cost(flops):
    return pl.CostEstimate(flops=flops, bytes_accessed=0, transcendentals=0)


TABLES_COST = cost(2_000_000_000)
PREPARE_COST = cost(0)
OWN_COST = cost(0)
JOIN_COST = cost(0)
GATHER_COST = cost(0)
EXP2_SCALE = math.log2(math.e) / math.sqrt(HEAD_SIZE)

FREQ_POWERS = [float(ROPE_BASE ** (-(2**k) / HALF)) for k in range(HALF.bit_length() - 1)]

PIO2_A = float(np.float32(1.5703125))
PIO2_B = float(np.float32(4.837512969970703125e-4))
PIO2_C = float(np.float32(math.pi / 2 - 1.5703125 - 4.837512969970703125e-4))


def shifted(value, steps):
    count = lax.axis_size("blk")
    return lax.ppermute(value, "blk", [(source, source + steps) for source in range(count - steps)])


def padded_keys(count):
    return -(-count // LANES) * LANES


def vmem_bytes(key_count):
    return 16 * 1024 * (1024 + key_count)


def sine_cosine(angle):
    turns = jnp.floor(angle * (2.0 / math.pi) + 0.5)
    rest = ((angle - turns * PIO2_A) - turns * PIO2_B) - turns * PIO2_C
    square = rest * rest
    sine = rest + rest * square * (
        -1.6666654611e-1 + square * (8.3321608736e-3 - square * 1.9515295891e-4)
    )
    cosine = 1.0 - 0.5 * square + square * square * (
        4.166664568298827e-2 + square * (-1.388731625493765e-3 + square * 2.443315711809948e-5)
    )
    quadrant = turns.astype(jnp.int32) & 3
    swapped = (quadrant & 1) == 1
    sine_out = jnp.where(swapped, cosine, sine)
    cosine_out = jnp.where(swapped, sine, cosine)
    sine_out = jnp.where(quadrant >= 2, -sine_out, sine_out)
    cosine_out = jnp.where((quadrant == 1) | (quadrant == 2), -cosine_out, cosine_out)
    return sine_out, cosine_out


def rotate(head, cosine, signed_sine):
    wide = head.astype(jnp.float32)
    return (wide * cosine + pltpu.roll(wide, HALF, 1) * signed_sine).astype(jnp.bfloat16)


def tables_kernel(
    rows, steps, segs, prefix_len, table_shape, integers_ref,
    page_out, cos_own, sin_own, cos_last, sin_last, cos_far, sin_far, own_bias, last_bias, far_bias,
):
    block_start = lax.axis_index("blk") * rows
    starts = [jnp.int32(0)]
    for seg in range(1, segs):
        starts.append(starts[-1] + integers_ref[seg - 1])
    lane = lax.broadcasted_iota(jnp.int32, (ROW_TILE, LANES), 1)
    row = lax.broadcasted_iota(jnp.int32, (ROW_TILE, LANES), 0)
    freq = jnp.ones((ROW_TILE, LANES), jnp.float32)
    for bit, power in enumerate(FREQ_POWERS):
        freq = jnp.where((lane >> bit) & 1 == 1, freq * power, freq)
    column = lax.axis_index("batch")
    seg_pages = table_shape[2]
    first = segs + steps + column * segs * seg_pages
    for page in range(segs * seg_pages):
        seg, place = divmod(page, seg_pages)
        page_out[page] = integers_ref[first + place * segs + seg]
    for step in range(steps + 1):
        for tile in range(0, rows, ROW_TILE):
            index = block_start + (tile - step * rows) + row
            own_start = jnp.zeros(index.shape, jnp.int32)
            for seg in range(1, segs):
                own_start = jnp.where(index >= starts[seg], starts[seg], own_start)
            place = (prefix_len + index - own_start).astype(jnp.float32)
            sine, cosine = sine_cosine(place * freq)
            sine = jnp.where(lane < HALF, -sine, sine)
            cos_out, sin_out = ((cos_own, sin_own), (cos_last, sin_last), (cos_far, sin_far))[
                min(step, 2)
            ]
            span = pl.ds(max(step - 2, 0) * rows + tile, ROW_TILE)
            cos_out[span, :] = cosine
            sin_out[span, :] = sine
    for tile in range(0, rows, ROW_TILE):
        span = pl.ds(tile, ROW_TILE)
        query_index = block_start + tile + row
        own_start = jnp.zeros(query_index.shape, jnp.int32)
        first_page_token = jnp.zeros(query_index.shape, jnp.int32)
        for seg in range(1, segs):
            later = query_index >= starts[seg]
            own_start = jnp.where(later, starts[seg], own_start)
            first_page_token = jnp.where(later, seg * prefix_len, first_page_token)
        for step in range(steps + 1):
            limit = query_index
            if step > 0:
                limit = jnp.where(integers_ref[segs + step - 1] > 0, limit, -1)
            for column in range(0, rows, LANES):
                key_index = block_start + (column - step * rows) + lane
                seen = (key_index >= own_start) & (key_index <= limit)
                bias = jnp.where(seen, 0.0, HIDDEN)
                if step == 0:
                    own_bias[span, pl.ds(column, LANES)] = bias
                elif step == 1:
                    last_bias[span, pl.ds(column, LANES)] = bias
                else:
                    far_bias[span, pl.ds((step - 2) * rows + column, LANES)] = bias
        base = (steps - 1) * rows
        for column in range(0, far_bias.shape[1] - base, LANES):
            offset = column + lane - first_page_token
            seen = (offset >= 0) & (offset < prefix_len)
            far_bias[span, pl.ds(base + column, LANES)] = jnp.where(seen, 0.0, HIDDEN)


def tables(rows, pool_page, integers, segs, steps, table_shape):
    prefix_len = table_shape[2] * pool_page
    pages = table_shape[1] * table_shape[2]
    far_rows = (steps - 1) * rows
    far_keys = padded_keys(far_rows + segs * prefix_len)
    block = jax.ShapeDtypeStruct((rows, HEAD_SIZE), jnp.float32)
    far = jax.ShapeDtypeStruct((far_rows, HEAD_SIZE), jnp.float32)
    shapes = [
        jax.ShapeDtypeStruct((pages,), jnp.int32),
        *[block] * 4,
        far,
        far,
        *[jax.ShapeDtypeStruct((rows, rows), jnp.float32)] * 2,
        jax.ShapeDtypeStruct((rows, far_keys), jnp.float32),
    ]
    return pl.pallas_call(
        lambda *refs: tables_kernel(rows, steps, segs, prefix_len, table_shape, *refs),
        in_specs=[pl.BlockSpec(memory_space=pltpu.SMEM)],
        out_specs=[pl.BlockSpec(memory_space=pltpu.SMEM)]
        + [pl.BlockSpec(memory_space=pltpu.VMEM)] * (len(shapes) - 1),
        out_shape=shapes,
        compiler_params=pltpu.CompilerParams(vmem_limit_bytes=vmem_bytes(far_keys + far_rows)),
        cost_estimate=TABLES_COST,
        name="tables",
    )(integers)


def prepare_kernel(
    rows, cos_own, sin_own, q_ref, k_ref, v_ref, pool_ref, q_out, k_out, k_copy, v_copy, pool_copy
):
    for tile in range(0, rows, ROW_TILE):
        span = pl.ds(tile, ROW_TILE)
        cosine = cos_own[span, :]
        signed_sine = sin_own[span, :]
        for source, target in ((q_ref, q_out), (k_ref, k_out)):
            for start in range(0, source.shape[2], HEAD_SIZE):
                columns = pl.ds(start, HEAD_SIZE)
                turned = rotate(source[0, span, columns], cosine, signed_sine)
                target[0, span, columns] = turned
                if source is k_ref:
                    k_copy[0, span, columns] = turned
    v_copy[...] = v_ref[...]
    pool_copy[...] = pool_ref[...]


def prepare(cosine, signed_sine, queries, keys, values, pool):
    rows = queries.shape[1]
    whole = lambda part: (0, 0)
    by_part = lambda part: (0, 0, part)
    wide = pl.BlockSpec((1, rows, queries.shape[2] // PREPARE_STEPS), by_part)
    narrow = pl.BlockSpec((1, rows, keys.shape[2] // PREPARE_STEPS), by_part)
    some_pages = pl.BlockSpec(
        (pool.shape[0] // PREPARE_STEPS, *pool.shape[1:]), lambda part: (part, 0, 0)
    )
    table = pl.BlockSpec(cosine.shape, whole)
    return pl.pallas_call(
        lambda *refs: prepare_kernel(rows, *refs),
        grid=(PREPARE_STEPS,),
        in_specs=[table, table, wide, narrow, narrow, some_pages],
        out_specs=[wide, narrow, narrow, narrow, some_pages],
        out_shape=[
            jax.ShapeDtypeStruct(array.shape, array.dtype)
            for array in (queries, keys, keys, values, pool)
        ],
        compiler_params=pltpu.CompilerParams(vmem_limit_bytes=vmem_bytes(rows)),
        cost_estimate=PREPARE_COST,
        name="prepare",
    )(cosine, signed_sine, queries, keys, values, pool)


def stacked_queries(q_ref, part):
    return jnp.concatenate(
        [q_ref[0, :, pl.ds((part * GROUP + h) * HEAD_SIZE, HEAD_SIZE)] for h in range(GROUP)],
        axis=0,
    )


def rotate_rows(target, first, source, lanes, cos_ref, sin_ref):
    rows = source.shape[1]
    for tile in range(0, rows, ROW_TILE):
        span = pl.ds(first + tile, ROW_TILE)
        target[span, :] = rotate(
            source[0, pl.ds(tile, ROW_TILE), lanes], cos_ref[span, :], sin_ref[span, :]
        )


def own_kernel(rows, bias_ref, q_ref, k_ref, v_ref, mean_ref, level_ref, *work):
    k_parts, v_parts, scores, weights, tops = split_work(work)
    group = pl.program_id(0)

    @pl.when(group == 0)
    def _():
        fill_ones(v_parts)
        level_ref[...] = jnp.zeros(level_ref.shape, jnp.float32)

    for part in range(HEADS_PER_STEP):
        lanes = pl.ds(part * HEAD_SIZE, HEAD_SIZE)
        k_parts[part][...] = k_ref[0, :, lanes]
        v_parts[part][:, pl.ds(0, HEAD_SIZE)] = v_ref[0, :, lanes]

    for part in range(HEADS_PER_STEP):
        score_part(part, q_ref, k_parts, scores)
    lane = lax.broadcasted_iota(jnp.int32, (rows, LANES), 1)
    for part in range(HEADS_PER_STEP):
        for start in range(0, GROUP * rows, SOFTMAX_TILE):
            span = pl.ds(start, SOFTMAX_TILE)
            bias = bias_ref[pl.ds(start % rows, SOFTMAX_TILE), :]
            score = scores[part][span, :] * EXP2_SCALE + bias
            highest = jnp.max(score, axis=1, keepdims=True)
            weights[part][span, :] = jnp.exp2(score - highest).astype(jnp.bfloat16)
            tops[part][span, :] = jnp.broadcast_to(highest, (SOFTMAX_TILE, LANES))
        summed = jnp.dot(weights[part][...], v_parts[part][...], preferred_element_type=jnp.float32)
        total = summed[:, HEAD_SIZE:]
        store_part(part, group, rows, lane, summed[:, :HEAD_SIZE] / total,
                   tops[part][...] + jnp.log2(total), mean_ref, level_ref)


def fill_ones(v_parts):
    for v_all in v_parts:
        v_all[:, pl.ds(HEAD_SIZE, HEAD_SIZE)] = jnp.ones((v_all.shape[0], HEAD_SIZE), jnp.bfloat16)


def split_work(work):
    return [work[i : i + HEADS_PER_STEP] for i in range(0, len(work), HEADS_PER_STEP)]


def score_part(part, q_ref, k_parts, scores):
    scores[part][...] = lax.dot_general(
        stacked_queries(q_ref, part), k_parts[part][...], (((1,), (1,)), ((), ())),
        preferred_element_type=jnp.float32,
    )


def store_part(part, group, rows, lane, mean, level, mean_ref, level_ref):
    for h in range(GROUP):
        own = part * GROUP + h
        span = slice(h * rows, (h + 1) * rows)
        mean_ref[:, pl.ds(own * HEAD_SIZE, HEAD_SIZE)] = mean[span]
        head = group * (HEADS_PER_STEP * GROUP) + own
        level_ref[...] = jnp.where(lane == head, level[span], level_ref[...])


def work_shapes(rows, key_count):
    shapes = [
        pltpu.VMEM((key_count, HEAD_SIZE), jnp.bfloat16),
        pltpu.VMEM((key_count, 2 * HEAD_SIZE), jnp.bfloat16),
        pltpu.VMEM((GROUP * rows, key_count), jnp.float32),
        pltpu.VMEM((GROUP * rows, key_count), jnp.bfloat16),
        pltpu.VMEM((GROUP * rows, LANES), jnp.float32),
    ]
    return [shape for shape in shapes for _ in range(HEADS_PER_STEP)]


def attend_own(bias, query, key, value):
    rows, q_width = query.shape[1:]
    by_group = lambda group: (0, 0, group)
    narrow = pl.BlockSpec((1, rows, HEADS_PER_STEP * HEAD_SIZE), by_group)
    wide = HEADS_PER_STEP * GROUP * HEAD_SIZE
    return pl.pallas_call(
        lambda *refs: own_kernel(rows, *refs),
        grid=(KEY_VALUE_HEADS // HEADS_PER_STEP,),
        in_specs=[
            pl.BlockSpec(bias.shape, lambda group: (0, 0)),
            pl.BlockSpec((1, rows, wide), by_group),
            narrow,
            narrow,
        ],
        out_specs=[
            pl.BlockSpec((rows, wide), lambda group: (0, group)),
            pl.BlockSpec((rows, LANES), lambda group: (0, 0)),
        ],
        out_shape=[
            jax.ShapeDtypeStruct((rows, q_width), jnp.float32),
            jax.ShapeDtypeStruct((rows, LANES), jnp.float32),
        ],
        scratch_shapes=work_shapes(rows, rows),
        compiler_params=pltpu.CompilerParams(vmem_limit_bytes=vmem_bytes(rows)),
        cost_estimate=OWN_COST,
        name="own",
    )(bias, query, key, value)


def gather_kernel(pool_rows, places, table_ref, *refs):
    *shards, paged, sem = refs
    column = lax.axis_index("batch")

    def copy(shard, place, page):
        return pltpu.make_async_copy(shard.at[place], paged.at[page], sem.at[page])

    for page in range(paged.shape[0]):
        number = table_ref[page]
        apart = lax.div(number, jnp.int32(pool_rows)) ^ column
        place = lax.rem(number, jnp.int32(pool_rows))
        for (which, first), shard in zip(places, shards):
            inside = place - first

            @pl.when((apart == which) & (inside >= 0) & (inside < shard.shape[0]))
            def _(shard=shard, inside=inside, page=page):
                copy(shard, inside, page).start()

    for page in range(paged.shape[0]):
        copy(shards[0], 0, page).wait()


def gather_pages(numbers, found):
    places, shards = [shard[:2] for shard in found], [shard[2] for shard in found]
    pool_rows = shards[0].shape[0]
    return pl.pallas_call(
        lambda *refs: gather_kernel(pool_rows, places, *refs),
        in_specs=[pl.BlockSpec(memory_space=pltpu.SMEM)]
        + [pl.BlockSpec(memory_space=pl.ANY)] * len(shards),
        out_specs=pl.BlockSpec(memory_space=pltpu.VMEM),
        out_shape=jax.ShapeDtypeStruct(numbers.shape + shards[0].shape[1:], jnp.bfloat16),
        scratch_shapes=[pltpu.SemaphoreType.DMA(numbers.shape)],
        compiler_params=pltpu.CompilerParams(vmem_limit_bytes=vmem_bytes(0)),
        cost_estimate=GATHER_COST,
        name="gather",
    )(numbers, *shards)


def join_heads(
    final, group, rows, k_parts, v_parts, scores, weights, tops,
    bias_ref, level_ref, mean_ref, q_ref, out_ref, level_out,
):
    for part in range(HEADS_PER_STEP):
        score_part(part, q_ref, k_parts, scores)
    lane = lax.broadcasted_iota(jnp.int32, (SOFTMAX_TILE, LANES), 1)
    wide_lane = lax.broadcasted_iota(jnp.int32, (rows, LANES), 1)
    for part in range(HEADS_PER_STEP):
        for start in range(0, GROUP * rows, SOFTMAX_TILE):
            span = pl.ds(start, SOFTMAX_TILE)
            row_span = pl.ds(start % rows, SOFTMAX_TILE)
            head = group * (HEADS_PER_STEP * GROUP) + part * GROUP + start // rows
            score = scores[part][span, :] * EXP2_SCALE + bias_ref[row_span, :]
            level = jnp.sum(
                jnp.where(lane == head, level_ref[row_span, :], 0.0), axis=1, keepdims=True
            )
            highest = jnp.maximum(jnp.max(score, axis=1, keepdims=True), level)
            weights[part][span, :] = jnp.exp2(score - highest).astype(jnp.bfloat16)
            if final:
                shrink = jnp.exp2(level - highest)
                tops[part][span, :] = jnp.broadcast_to(shrink, (SOFTMAX_TILE, LANES))
            else:
                tops[part][span, :] = jnp.where(lane < HALF, highest, level)
        summed = jnp.dot(weights[part][...], v_parts[part][...], preferred_element_type=jnp.float32)
        if final:
            shrink = tops[part][...]
        else:
            both = tops[part][...]
            turned = pltpu.roll(both, HALF, 1)
            low = lax.broadcasted_iota(jnp.int32, both.shape, 1) < HALF
            highest = jnp.where(low, both, turned)
            shrink = jnp.exp2(jnp.where(low, turned, both) - highest)
        total = summed[:, HEAD_SIZE:] + shrink
        before = jnp.concatenate(
            [mean_ref[:, pl.ds((part * GROUP + h) * HEAD_SIZE, HEAD_SIZE)] for h in range(GROUP)],
            axis=0,
        )
        mean = (before * shrink + summed[:, :HEAD_SIZE]) / total
        if final:
            for h in range(GROUP):
                lanes = pl.ds((part * GROUP + h) * HEAD_SIZE, HEAD_SIZE)
                out_ref[0, :, lanes] = mean[h * rows : (h + 1) * rows].astype(jnp.bfloat16)
        else:
            level = highest + jnp.log2(total)
            store_part(part, group, rows, wide_lane, mean, level, out_ref, level_out)


def far_kernel(
    rows, blocks, cos_ref, sin_ref, bias_ref, level_ref, mean_ref, q_ref, page_keys, page_values, *refs
):
    keys, values, refs = refs[:blocks], refs[blocks : 2 * blocks], refs[2 * blocks :]
    mean_out, level_out = refs[:2]
    work = split_work(refs[2:])
    k_parts, v_parts = work[:2]
    group = pl.program_id(0)
    prefix_rows = page_keys.shape[0] * page_keys.shape[1]
    base = blocks * rows

    @pl.when(group == 0)
    def _():
        fill_ones(v_parts)
        level_out[...] = jnp.zeros(level_out.shape, jnp.float32)
        rest = k_parts[0].shape[0] - base - prefix_rows
        if rest:
            blank = jnp.zeros((rest, HEAD_SIZE), jnp.bfloat16)
            for k_all, v_all in zip(k_parts, v_parts):
                k_all[pl.ds(base + prefix_rows, rest), :] = blank
                v_all[pl.ds(base + prefix_rows, rest), pl.ds(0, HEAD_SIZE)] = blank

    for part in range(HEADS_PER_STEP):
        lanes = pl.ds(part * HEAD_SIZE, HEAD_SIZE)
        for block in range(blocks):
            rotate_rows(k_parts[part], block * rows, keys[block], lanes, cos_ref, sin_ref)
            span = pl.ds(block * rows, rows)
            v_parts[part][span, pl.ds(0, HEAD_SIZE)] = values[block][0, :, lanes]
        span = pl.ds(base, prefix_rows)
        k_parts[part][span, :] = page_keys[:, :, lanes].reshape(prefix_rows, HEAD_SIZE)
        v_parts[part][span, pl.ds(0, HEAD_SIZE)] = page_values[:, :, lanes].reshape(
            prefix_rows, HEAD_SIZE
        )
    join_heads(
        False, group, rows, *work, bias_ref, level_ref, mean_ref, q_ref, mean_out, level_out
    )


def last_kernel(
    rows, cos_ref, sin_ref, bias_ref, level_ref, mean_ref, q_ref, key_ref, swapped_value,
    passed_value, direct_value, out_ref, *refs,
):
    work = split_work(refs)
    k_parts, v_parts = work[:2]
    group = pl.program_id(0)
    even = lax.rem(lax.axis_index("blk"), 2) == 0

    @pl.when(group == 0)
    def _():
        fill_ones(v_parts)

    for part in range(HEADS_PER_STEP):
        lanes = pl.ds(part * HEAD_SIZE, HEAD_SIZE)
        rotate_rows(k_parts[part], 0, key_ref, lanes, cos_ref, sin_ref)
        start = 0
        for arrived in (passed_value, direct_value):
            span = pl.ds(start, arrived.shape[1])
            v_parts[part][span, pl.ds(0, HEAD_SIZE)] = jnp.where(
                even, arrived[0, :, lanes], swapped_value[0, span, lanes]
            )
            start += arrived.shape[1]
    join_heads(True, group, rows, *work, bias_ref, level_ref, mean_ref, q_ref, out_ref, None)


def join(cosine, signed_sine, bias, level, mean, query, arrived, pages=None):
    rows = query.shape[1]
    whole = lambda group: (0, 0)
    by_group = lambda group: (0, 0, group)
    width = HEADS_PER_STEP * GROUP * HEAD_SIZE
    wide = pl.BlockSpec((1, rows, width), by_group)
    flat = pl.BlockSpec((rows, width), lambda group: (0, group))
    level_spec = pl.BlockSpec(level.shape, whole)
    table = pl.BlockSpec(cosine.shape, whole)
    in_specs = [table, table, pl.BlockSpec(bias.shape, whole), level_spec, flat, wide]
    arrived_specs = [
        pl.BlockSpec((1, array.shape[1], HEADS_PER_STEP * HEAD_SIZE), by_group)
        for array in arrived
    ]
    operands = [cosine, signed_sine, bias, level, mean, query]
    scratch = work_shapes(rows, bias.shape[1])
    if pages is None:
        kernel = lambda *refs: last_kernel(rows, *refs)
        out_specs, out_shape = wide, jax.ShapeDtypeStruct(query.shape, jnp.bfloat16)
    else:
        kernel = lambda *refs: far_kernel(rows, len(arrived) // 2, *refs)
        groups = KEY_VALUE_HEADS // HEADS_PER_STEP
        for first in (0, groups):
            in_specs.append(
                pl.BlockSpec(
                    (*pages.shape[:2], HEADS_PER_STEP * HEAD_SIZE),
                    lambda group, first=first: (0, 0, first + group),
                )
            )
            operands.append(pages)
        out_specs = [flat, level_spec]
        out_shape = [
            jax.ShapeDtypeStruct(array.shape, jnp.float32) for array in (mean, level)
        ]
    return pl.pallas_call(
        kernel,
        grid=(KEY_VALUE_HEADS // HEADS_PER_STEP,),
        in_specs=in_specs + arrived_specs,
        out_specs=out_specs,
        out_shape=out_shape,
        scratch_shapes=scratch,
        compiler_params=pltpu.CompilerParams(vmem_limit_bytes=vmem_bytes(bias.shape[1])),
        cost_estimate=JOIN_COST,
        name="last" if pages is None else "far",
    )(*operands, *arrived)


def pool_shards(pool, after):
    count = lax.axis_size("batch")

    def swapped(shard, bit):
        return lax.ppermute(shard, "batch", [(c, c ^ bit) for c in range(count)])

    bits = [count >> (step + 1) for step in range(count.bit_length() - 1)]
    shards = {bit: swapped(pool, bit) for bit in bits}
    shards, after = lax.optimization_barrier((shards, after))
    shards = {apart: [shard] for apart, shard in shards.items()}
    for bit in reversed(bits):
        for apart, pieces in list(shards.items()):
            if apart ^ bit not in shards and apart != bit:
                if len(pieces) == 1:
                    middle = pool.shape[0] // 2
                    pieces = [pieces[0][:middle], pieces[0][middle:]]
                shards[apart ^ bit] = [swapped(piece, bit) for piece in pieces]
    found = []
    for apart, pieces in sorted(shards.items()):
        held = pool.shape[0] // len(pieces)
        found += [(apart, place * held, piece) for place, piece in enumerate(pieces)]
    return found


def per_device(queries, keys, values, seg_ids, lengths, live, page_table, pool):
    steps = live.shape[2]
    blocks = lax.axis_size("blk")
    far = [shifted(keys, 2), shifted(values, 2)]
    for step in range(3, steps + 1):
        far += [shifted(keys, step), shifted(values, step)]
    swap = [(j, j ^ 1) for j in range(blocks)]
    even = lax.rem(lax.axis_index("blk"), 2) == 0
    swapped_value = lax.ppermute(values, "blk", swap)
    integers = jnp.concatenate([lengths.ravel(), live.ravel(), jnp.swapaxes(page_table, 1, 2).ravel()])
    (
        table, cos_own, sin_own, cos_last, sin_last, cos_far, sin_far, own_bias, last_bias, far_bias
    ) = tables(keys.shape[1], pool.shape[1], integers, lengths.shape[1], steps, page_table.shape)
    query, key, near_key, near_value, own_shard = prepare(
        cos_own, sin_own, queries, keys, values, pool
    )
    to_swap = jnp.where(even, keys, far[0])
    far_key = lax.ppermute(to_swap, "blk", swap)
    split = values.shape[1] // 2
    passed_value = lax.ppermute(
        swapped_value[:, :split], "blk", [(j, j + 2) for j in range(0, blocks - 2, 2)]
    )
    mean, level = attend_own(own_bias, query, near_key, near_value)
    shards = pool_shards(pool, (level, to_swap, swapped_value))
    pieces, later_values = lax.optimization_barrier(
        ([shard[2] for shard in shards], values[:, split:])
    )
    shards = [(*shard[:2], piece) for shard, piece in zip(shards, pieces)]
    direct_value = lax.ppermute(
        later_values, "blk", [(j, j + 1) for j in range(1, blocks - 1, 2)]
    )
    mean, level = join(
        cos_far, sin_far, far_bias, level, mean, query, [*far[::2], *far[1::2]],
        pages=gather_pages(table, [(0, 0, own_shard), *shards]),
    )
    result = join(
        cos_last, sin_last, last_bias, level, mean, query,
        [far_key, swapped_value, passed_value, direct_value],
    )
    return (result, key)


def solution(mesh):
    in_specs = (
        P("batch", "blk", None),
        P("batch", "blk", None),
        P("batch", "blk", None),
        P("batch", "blk"),
        P("batch", None),
        P("batch", "blk", None),
        P(),
        P("batch", None, None),
    )
    out_specs = (P("batch", "blk", None), P("batch", "blk", None))
    return jax.shard_map(
        per_device, mesh=mesh, in_specs=in_specs, out_specs=out_specs, check_vma=False
    )
```

```python
import math

import jax
import jax.numpy as jnp
import numpy as np
from jax import lax
from jax.experimental import pallas as pl
from jax.experimental.pallas import tpu as pltpu
from jax.sharding import PartitionSpec as P

QUERY_HEADS = 16
KEY_VALUE_HEADS = 8
HEAD_SIZE = 128
GROUP = QUERY_HEADS // KEY_VALUE_HEADS
HALF = HEAD_SIZE // 2
ROPE_BASE = 1000000.0
HIDDEN = -1e30
LANES = 128
ROW_TILE = 64
SOFTMAX_TILE = 16
HEADS_PER_STEP = 2
PREPARE_STEPS = 2


def cost(flops):
    return pl.CostEstimate(flops=flops, bytes_accessed=0, transcendentals=0)


TABLES_COST = cost(2_000_000_000)
PREPARE_COST = cost(0)
OWN_COST = cost(0)
JOIN_COST = cost(0)
GATHER_COST = cost(0)
EXP2_SCALE = math.log2(math.e) / math.sqrt(HEAD_SIZE)

FREQ_POWERS = [float(ROPE_BASE ** (-(2**k) / HALF)) for k in range(HALF.bit_length() - 1)]

PIO2_A = float(np.float32(1.5703125))
PIO2_B = float(np.float32(4.837512969970703125e-4))
PIO2_C = float(np.float32(math.pi / 2 - 1.5703125 - 4.837512969970703125e-4))


def shifted(value, steps):
    count = lax.axis_size("blk")
    return lax.ppermute(value, "blk", [(source, source + steps) for source in range(count - steps)])


def padded_keys(count):
    return -(-count // LANES) * LANES


def vmem_bytes(key_count):
    return 16 * 1024 * (1024 + key_count)


def sine_cosine(angle):
    turns = jnp.floor(angle * (2.0 / math.pi) + 0.5)
    rest = ((angle - turns * PIO2_A) - turns * PIO2_B) - turns * PIO2_C
    square = rest * rest
    sine = rest + rest * square * (
        -1.6666654611e-1 + square * (8.3321608736e-3 - square * 1.9515295891e-4)
    )
    cosine = 1.0 - 0.5 * square + square * square * (
        4.166664568298827e-2 + square * (-1.388731625493765e-3 + square * 2.443315711809948e-5)
    )
    quadrant = turns.astype(jnp.int32) & 3
    swapped = (quadrant & 1) == 1
    sine_out = jnp.where(swapped, cosine, sine)
    cosine_out = jnp.where(swapped, sine, cosine)
    sine_out = jnp.where(quadrant >= 2, -sine_out, sine_out)
    cosine_out = jnp.where((quadrant == 1) | (quadrant == 2), -cosine_out, cosine_out)
    return sine_out, cosine_out


def rotate(head, cosine, signed_sine):
    wide = head.astype(jnp.float32)
    return (wide * cosine + pltpu.roll(wide, HALF, 1) * signed_sine).astype(jnp.bfloat16)


def tables_kernel(
    rows, steps, segs, prefix_len, table_shape, integers_ref,
    page_out, cos_own, sin_own, cos_last, sin_last, cos_far, sin_far, own_bias, last_bias, far_bias,
):
    block_start = lax.axis_index("blk") * rows
    starts = [jnp.int32(0)]
    for seg in range(1, segs):
        starts.append(starts[-1] + integers_ref[seg - 1])
    lane = lax.broadcasted_iota(jnp.int32, (ROW_TILE, LANES), 1)
    row = lax.broadcasted_iota(jnp.int32, (ROW_TILE, LANES), 0)
    freq = jnp.ones((ROW_TILE, LANES), jnp.float32)
    for bit, power in enumerate(FREQ_POWERS):
        freq = jnp.where((lane >> bit) & 1 == 1, freq * power, freq)
    column = lax.axis_index("batch")
    seg_pages = table_shape[2]
    first = segs + steps + column * segs * seg_pages
    for page in range(segs * seg_pages):
        seg, place = divmod(page, seg_pages)
        page_out[page] = integers_ref[first + place * segs + seg]
    for step in range(steps + 1):
        for tile in range(0, rows, ROW_TILE):
            index = block_start + (tile - step * rows) + row
            own_start = jnp.zeros(index.shape, jnp.int32)
            for seg in range(1, segs):
                own_start = jnp.where(index >= starts[seg], starts[seg], own_start)
            place = (prefix_len + index - own_start).astype(jnp.float32)
            sine, cosine = sine_cosine(place * freq)
            sine = jnp.where(lane < HALF, -sine, sine)
            cos_out, sin_out = ((cos_own, sin_own), (cos_last, sin_last), (cos_far, sin_far))[
                min(step, 2)
            ]
            span = pl.ds(max(step - 2, 0) * rows + tile, ROW_TILE)
            cos_out[span, :] = cosine
            sin_out[span, :] = sine
    for tile in range(0, rows, ROW_TILE):
        span = pl.ds(tile, ROW_TILE)
        query_index = block_start + tile + row
        own_start = jnp.zeros(query_index.shape, jnp.int32)
        first_page_token = jnp.zeros(query_index.shape, jnp.int32)
        for seg in range(1, segs):
            later = query_index >= starts[seg]
            own_start = jnp.where(later, starts[seg], own_start)
            first_page_token = jnp.where(later, seg * prefix_len, first_page_token)
        for step in range(steps + 1):
            limit = query_index
            if step > 0:
                limit = jnp.where(integers_ref[segs + step - 1] > 0, limit, -1)
            for column in range(0, rows, LANES):
                key_index = block_start + (column - step * rows) + lane
                seen = (key_index >= own_start) & (key_index <= limit)
                bias = jnp.where(seen, 0.0, HIDDEN)
                if step == 0:
                    own_bias[span, pl.ds(column, LANES)] = bias
                elif step == 1:
                    last_bias[span, pl.ds(column, LANES)] = bias
                else:
                    far_bias[span, pl.ds((step - 2) * rows + column, LANES)] = bias
        base = (steps - 1) * rows
        for column in range(0, far_bias.shape[1] - base, LANES):
            offset = column + lane - first_page_token
            seen = (offset >= 0) & (offset < prefix_len)
            far_bias[span, pl.ds(base + column, LANES)] = jnp.where(seen, 0.0, HIDDEN)


def tables(rows, pool_page, integers, segs, steps, table_shape):
    prefix_len = table_shape[2] * pool_page
    pages = table_shape[1] * table_shape[2]
    far_rows = (steps - 1) * rows
    far_keys = padded_keys(far_rows + segs * prefix_len)
    block = jax.ShapeDtypeStruct((rows, HEAD_SIZE), jnp.float32)
    far = jax.ShapeDtypeStruct((far_rows, HEAD_SIZE), jnp.float32)
    shapes = [
        jax.ShapeDtypeStruct((pages,), jnp.int32),
        *[block] * 4,
        far,
        far,
        *[jax.ShapeDtypeStruct((rows, rows), jnp.float32)] * 2,
        jax.ShapeDtypeStruct((rows, far_keys), jnp.float32),
    ]
    return pl.pallas_call(
        lambda *refs: tables_kernel(rows, steps, segs, prefix_len, table_shape, *refs),
        in_specs=[pl.BlockSpec(memory_space=pltpu.SMEM)],
        out_specs=[pl.BlockSpec(memory_space=pltpu.SMEM)]
        + [pl.BlockSpec(memory_space=pltpu.VMEM)] * (len(shapes) - 1),
        out_shape=shapes,
        compiler_params=pltpu.CompilerParams(vmem_limit_bytes=vmem_bytes(far_keys + far_rows)),
        cost_estimate=TABLES_COST,
        name="tables",
    )(integers)


def prepare_kernel(
    rows, cos_own, sin_own, q_ref, k_ref, v_ref, pool_ref, q_out, k_out, k_copy, v_copy, pool_copy
):
    for tile in range(0, rows, ROW_TILE):
        span = pl.ds(tile, ROW_TILE)
        cosine = cos_own[span, :]
        signed_sine = sin_own[span, :]
        for source, target in ((q_ref, q_out), (k_ref, k_out)):
            for start in range(0, source.shape[2], HEAD_SIZE):
                columns = pl.ds(start, HEAD_SIZE)
                turned = rotate(source[0, span, columns], cosine, signed_sine)
                target[0, span, columns] = turned
                if source is k_ref:
                    k_copy[0, span, columns] = turned
    v_copy[...] = v_ref[...]
    pool_copy[...] = pool_ref[...]


def prepare(cosine, signed_sine, queries, keys, values, pool):
    rows = queries.shape[1]
    whole = lambda part: (0, 0)
    by_part = lambda part: (0, 0, part)
    wide = pl.BlockSpec((1, rows, queries.shape[2] // PREPARE_STEPS), by_part)
    narrow = pl.BlockSpec((1, rows, keys.shape[2] // PREPARE_STEPS), by_part)
    some_pages = pl.BlockSpec(
        (pool.shape[0] // PREPARE_STEPS, *pool.shape[1:]), lambda part: (part, 0, 0)
    )
    table = pl.BlockSpec(cosine.shape, whole)
    return pl.pallas_call(
        lambda *refs: prepare_kernel(rows, *refs),
        grid=(PREPARE_STEPS,),
        in_specs=[table, table, wide, narrow, narrow, some_pages],
        out_specs=[wide, narrow, narrow, narrow, some_pages],
        out_shape=[
            jax.ShapeDtypeStruct(array.shape, array.dtype)
            for array in (queries, keys, keys, values, pool)
        ],
        compiler_params=pltpu.CompilerParams(vmem_limit_bytes=vmem_bytes(rows)),
        cost_estimate=PREPARE_COST,
        name="prepare",
    )(cosine, signed_sine, queries, keys, values, pool)


def stacked_queries(q_ref, part):
    return jnp.concatenate(
        [q_ref[0, :, pl.ds((part * GROUP + h) * HEAD_SIZE, HEAD_SIZE)] for h in range(GROUP)],
        axis=0,
    )


def rotate_rows(target, first, source, lanes, cos_ref, sin_ref):
    rows = source.shape[1]
    for tile in range(0, rows, ROW_TILE):
        span = pl.ds(first + tile, ROW_TILE)
        target[span, :] = rotate(
            source[0, pl.ds(tile, ROW_TILE), lanes], cos_ref[span, :], sin_ref[span, :]
        )


def own_kernel(rows, bias_ref, q_ref, k_ref, v_ref, mean_ref, level_ref, *work):
    k_parts, v_parts, scores, weights, tops = split_work(work)
    group = pl.program_id(0)

    @pl.when(group == 0)
    def _():
        fill_ones(v_parts)
        level_ref[...] = jnp.zeros(level_ref.shape, jnp.float32)

    for part in range(HEADS_PER_STEP):
        lanes = pl.ds(part * HEAD_SIZE, HEAD_SIZE)
        k_parts[part][...] = k_ref[0, :, lanes]
        v_parts[part][:, pl.ds(0, HEAD_SIZE)] = v_ref[0, :, lanes]

    for part in range(HEADS_PER_STEP):
        score_part(part, q_ref, k_parts, scores)
    lane = lax.broadcasted_iota(jnp.int32, (rows, LANES), 1)
    for part in range(HEADS_PER_STEP):
        for start in range(0, GROUP * rows, SOFTMAX_TILE):
            span = pl.ds(start, SOFTMAX_TILE)
            bias = bias_ref[pl.ds(start % rows, SOFTMAX_TILE), :]
            score = scores[part][span, :] * EXP2_SCALE + bias
            highest = jnp.max(score, axis=1, keepdims=True)
            weights[part][span, :] = jnp.exp2(score - highest).astype(jnp.bfloat16)
            tops[part][span, :] = jnp.broadcast_to(highest, (SOFTMAX_TILE, LANES))
        summed = jnp.dot(weights[part][...], v_parts[part][...], preferred_element_type=jnp.float32)
        total = summed[:, HEAD_SIZE:]
        store_part(part, group, rows, lane, summed[:, :HEAD_SIZE] / total,
                   tops[part][...] + jnp.log2(total), mean_ref, level_ref)


def fill_ones(v_parts):
    for v_all in v_parts:
        v_all[:, pl.ds(HEAD_SIZE, HEAD_SIZE)] = jnp.ones((v_all.shape[0], HEAD_SIZE), jnp.bfloat16)


def split_work(work):
    return [work[i : i + HEADS_PER_STEP] for i in range(0, len(work), HEADS_PER_STEP)]


def score_part(part, q_ref, k_parts, scores):
    scores[part][...] = lax.dot_general(
        stacked_queries(q_ref, part), k_parts[part][...], (((1,), (1,)), ((), ())),
        preferred_element_type=jnp.float32,
    )


def store_part(part, group, rows, lane, mean, level, mean_ref, level_ref):
    for h in range(GROUP):
        own = part * GROUP + h
        span = slice(h * rows, (h + 1) * rows)
        mean_ref[:, pl.ds(own * HEAD_SIZE, HEAD_SIZE)] = mean[span]
        head = group * (HEADS_PER_STEP * GROUP) + own
        level_ref[...] = jnp.where(lane == head, level[span], level_ref[...])


def work_shapes(rows, key_count):
    shapes = [
        pltpu.VMEM((key_count, HEAD_SIZE), jnp.bfloat16),
        pltpu.VMEM((key_count, 2 * HEAD_SIZE), jnp.bfloat16),
        pltpu.VMEM((GROUP * rows, key_count), jnp.float32),
        pltpu.VMEM((GROUP * rows, key_count), jnp.bfloat16),
        pltpu.VMEM((GROUP * rows, LANES), jnp.float32),
    ]
    return [shape for shape in shapes for _ in range(HEADS_PER_STEP)]


def attend_own(bias, query, key, value):
    rows, q_width = query.shape[1:]
    by_group = lambda group: (0, 0, group)
    narrow = pl.BlockSpec((1, rows, HEADS_PER_STEP * HEAD_SIZE), by_group)
    wide = HEADS_PER_STEP * GROUP * HEAD_SIZE
    return pl.pallas_call(
        lambda *refs: own_kernel(rows, *refs),
        grid=(KEY_VALUE_HEADS // HEADS_PER_STEP,),
        in_specs=[
            pl.BlockSpec(bias.shape, lambda group: (0, 0)),
            pl.BlockSpec((1, rows, wide), by_group),
            narrow,
            narrow,
        ],
        out_specs=[
            pl.BlockSpec((rows, wide), lambda group: (0, group)),
            pl.BlockSpec((rows, LANES), lambda group: (0, 0)),
        ],
        out_shape=[
            jax.ShapeDtypeStruct((rows, q_width), jnp.float32),
            jax.ShapeDtypeStruct((rows, LANES), jnp.float32),
        ],
        scratch_shapes=work_shapes(rows, rows),
        compiler_params=pltpu.CompilerParams(vmem_limit_bytes=vmem_bytes(rows)),
        cost_estimate=OWN_COST,
        name="own",
    )(bias, query, key, value)


def gather_kernel(pool_rows, places, table_ref, *refs):
    *shards, paged, sem = refs
    column = lax.axis_index("batch")

    def copy(shard, place, page):
        return pltpu.make_async_copy(shard.at[place], paged.at[page], sem.at[page])

    for page in range(paged.shape[0]):
        number = table_ref[page]
        apart = lax.div(number, jnp.int32(pool_rows)) ^ column
        place = lax.rem(number, jnp.int32(pool_rows))
        for (which, first), shard in zip(places, shards):
            inside = place - first

            @pl.when((apart == which) & (inside >= 0) & (inside < shard.shape[0]))
            def _(shard=shard, inside=inside, page=page):
                copy(shard, inside, page).start()

    for page in range(paged.shape[0]):
        copy(shards[0], 0, page).wait()


def gather_pages(numbers, found):
    places, shards = [shard[:2] for shard in found], [shard[2] for shard in found]
    pool_rows = shards[0].shape[0]
    return pl.pallas_call(
        lambda *refs: gather_kernel(pool_rows, places, *refs),
        in_specs=[pl.BlockSpec(memory_space=pltpu.SMEM)]
        + [pl.BlockSpec(memory_space=pl.ANY)] * len(shards),
        out_specs=pl.BlockSpec(memory_space=pltpu.VMEM),
        out_shape=jax.ShapeDtypeStruct(numbers.shape + shards[0].shape[1:], jnp.bfloat16),
        scratch_shapes=[pltpu.SemaphoreType.DMA(numbers.shape)],
        compiler_params=pltpu.CompilerParams(vmem_limit_bytes=vmem_bytes(0)),
        cost_estimate=GATHER_COST,
        name="gather",
    )(numbers, *shards)


def join_heads(
    final, group, rows, k_parts, v_parts, scores, weights, tops,
    bias_ref, level_ref, mean_ref, q_ref, out_ref, level_out,
):
    for part in range(HEADS_PER_STEP):
        score_part(part, q_ref, k_parts, scores)
    lane = lax.broadcasted_iota(jnp.int32, (SOFTMAX_TILE, LANES), 1)
    wide_lane = lax.broadcasted_iota(jnp.int32, (rows, LANES), 1)
    for part in range(HEADS_PER_STEP):
        for start in range(0, GROUP * rows, SOFTMAX_TILE):
            span = pl.ds(start, SOFTMAX_TILE)
            row_span = pl.ds(start % rows, SOFTMAX_TILE)
            head = group * (HEADS_PER_STEP * GROUP) + part * GROUP + start // rows
            score = scores[part][span, :] * EXP2_SCALE + bias_ref[row_span, :]
            level = jnp.sum(
                jnp.where(lane == head, level_ref[row_span, :], 0.0), axis=1, keepdims=True
            )
            highest = jnp.maximum(jnp.max(score, axis=1, keepdims=True), level)
            weights[part][span, :] = jnp.exp2(score - highest).astype(jnp.bfloat16)
            if final:
                shrink = jnp.exp2(level - highest)
                tops[part][span, :] = jnp.broadcast_to(shrink, (SOFTMAX_TILE, LANES))
            else:
                tops[part][span, :] = jnp.where(lane < HALF, highest, level)
        summed = jnp.dot(weights[part][...], v_parts[part][...], preferred_element_type=jnp.float32)
        if final:
            shrink = tops[part][...]
        else:
            both = tops[part][...]
            turned = pltpu.roll(both, HALF, 1)
            low = lax.broadcasted_iota(jnp.int32, both.shape, 1) < HALF
            highest = jnp.where(low, both, turned)
            shrink = jnp.exp2(jnp.where(low, turned, both) - highest)
        total = summed[:, HEAD_SIZE:] + shrink
        before = jnp.concatenate(
            [mean_ref[:, pl.ds((part * GROUP + h) * HEAD_SIZE, HEAD_SIZE)] for h in range(GROUP)],
            axis=0,
        )
        mean = (before * shrink + summed[:, :HEAD_SIZE]) / total
        if final:
            for h in range(GROUP):
                lanes = pl.ds((part * GROUP + h) * HEAD_SIZE, HEAD_SIZE)
                out_ref[0, :, lanes] = mean[h * rows : (h + 1) * rows].astype(jnp.bfloat16)
        else:
            level = highest + jnp.log2(total)
            store_part(part, group, rows, wide_lane, mean, level, out_ref, level_out)


def far_kernel(
    rows, blocks, cos_ref, sin_ref, bias_ref, level_ref, mean_ref, q_ref, page_keys, page_values, *refs
):
    keys, values, refs = refs[:blocks], refs[blocks : 2 * blocks], refs[2 * blocks :]
    mean_out, level_out = refs[:2]
    work = split_work(refs[2:])
    k_parts, v_parts = work[:2]
    group = pl.program_id(0)
    prefix_rows = page_keys.shape[0] * page_keys.shape[1]
    base = blocks * rows

    @pl.when(group == 0)
    def _():
        fill_ones(v_parts)
        level_out[...] = jnp.zeros(level_out.shape, jnp.float32)
        rest = k_parts[0].shape[0] - base - prefix_rows
        if rest:
            blank = jnp.zeros((rest, HEAD_SIZE), jnp.bfloat16)
            for k_all, v_all in zip(k_parts, v_parts):
                k_all[pl.ds(base + prefix_rows, rest), :] = blank
                v_all[pl.ds(base + prefix_rows, rest), pl.ds(0, HEAD_SIZE)] = blank

    for part in range(HEADS_PER_STEP):
        lanes = pl.ds(part * HEAD_SIZE, HEAD_SIZE)
        for block in range(blocks):
            rotate_rows(k_parts[part], block * rows, keys[block], lanes, cos_ref, sin_ref)
            span = pl.ds(block * rows, rows)
            v_parts[part][span, pl.ds(0, HEAD_SIZE)] = values[block][0, :, lanes]
        span = pl.ds(base, prefix_rows)
        k_parts[part][span, :] = page_keys[:, :, lanes].reshape(prefix_rows, HEAD_SIZE)
        v_parts[part][span, pl.ds(0, HEAD_SIZE)] = page_values[:, :, lanes].reshape(
            prefix_rows, HEAD_SIZE
        )
    join_heads(
        False, group, rows, *work, bias_ref, level_ref, mean_ref, q_ref, mean_out, level_out
    )


def last_kernel(
    rows, cos_ref, sin_ref, bias_ref, level_ref, mean_ref, q_ref, key_ref, swapped_value,
    passed_value, direct_value, out_ref, *refs,
):
    work = split_work(refs)
    k_parts, v_parts = work[:2]
    group = pl.program_id(0)
    even = lax.rem(lax.axis_index("blk"), 2) == 0

    @pl.when(group == 0)
    def _():
        fill_ones(v_parts)

    for part in range(HEADS_PER_STEP):
        lanes = pl.ds(part * HEAD_SIZE, HEAD_SIZE)
        rotate_rows(k_parts[part], 0, key_ref, lanes, cos_ref, sin_ref)
        start = 0
        for arrived in (passed_value, direct_value):
            span = pl.ds(start, arrived.shape[1])
            v_parts[part][span, pl.ds(0, HEAD_SIZE)] = jnp.where(
                even, arrived[0, :, lanes], swapped_value[0, span, lanes]
            )
            start += arrived.shape[1]
    join_heads(True, group, rows, *work, bias_ref, level_ref, mean_ref, q_ref, out_ref, None)


def join(cosine, signed_sine, bias, level, mean, query, arrived, pages=None):
    rows = query.shape[1]
    whole = lambda group: (0, 0)
    by_group = lambda group: (0, 0, group)
    width = HEADS_PER_STEP * GROUP * HEAD_SIZE
    wide = pl.BlockSpec((1, rows, width), by_group)
    flat = pl.BlockSpec((rows, width), lambda group: (0, group))
    level_spec = pl.BlockSpec(level.shape, whole)
    table = pl.BlockSpec(cosine.shape, whole)
    in_specs = [table, table, pl.BlockSpec(bias.shape, whole), level_spec, flat, wide]
    arrived_specs = [
        pl.BlockSpec((1, array.shape[1], HEADS_PER_STEP * HEAD_SIZE), by_group)
        for array in arrived
    ]
    operands = [cosine, signed_sine, bias, level, mean, query]
    scratch = work_shapes(rows, bias.shape[1])
    if pages is None:
        kernel = lambda *refs: last_kernel(rows, *refs)
        out_specs, out_shape = wide, jax.ShapeDtypeStruct(query.shape, jnp.bfloat16)
    else:
        kernel = lambda *refs: far_kernel(rows, len(arrived) // 2, *refs)
        groups = KEY_VALUE_HEADS // HEADS_PER_STEP
        for first in (0, groups):
            in_specs.append(
                pl.BlockSpec(
                    (*pages.shape[:2], HEADS_PER_STEP * HEAD_SIZE),
                    lambda group, first=first: (0, 0, first + group),
                )
            )
            operands.append(pages)
        out_specs = [flat, level_spec]
        out_shape = [
            jax.ShapeDtypeStruct(array.shape, jnp.float32) for array in (mean, level)
        ]
    return pl.pallas_call(
        kernel,
        grid=(KEY_VALUE_HEADS // HEADS_PER_STEP,),
        in_specs=in_specs + arrived_specs,
        out_specs=out_specs,
        out_shape=out_shape,
        scratch_shapes=scratch,
        compiler_params=pltpu.CompilerParams(vmem_limit_bytes=vmem_bytes(bias.shape[1])),
        cost_estimate=JOIN_COST,
        name="last" if pages is None else "far",
    )(*operands, *arrived)


def pool_shards(pool, after):
    count = lax.axis_size("batch")

    def swapped(shard, bit):
        return lax.ppermute(shard, "batch", [(c, c ^ bit) for c in range(count)])

    bits = [count >> (step + 1) for step in range(count.bit_length() - 1)]
    shards = {bit: swapped(pool, bit) for bit in bits}
    shards, after = lax.optimization_barrier((shards, after))
    shards = {apart: [shard] for apart, shard in shards.items()}
    for bit in reversed(bits):
        for apart, pieces in list(shards.items()):
            if apart ^ bit not in shards and apart != bit:
                if len(pieces) == 1:
                    middle = pool.shape[0] // 2
                    pieces = [pieces[0][:middle], pieces[0][middle:]]
                shards[apart ^ bit] = [swapped(piece, bit) for piece in pieces]
    found = []
    for apart, pieces in sorted(shards.items()):
        held = pool.shape[0] // len(pieces)
        found += [(apart, place * held, piece) for place, piece in enumerate(pieces)]
    return found


def per_device(queries, keys, values, seg_ids, lengths, live, page_table, pool):
    steps = live.shape[2]
    blocks = lax.axis_size("blk")
    far = [shifted(keys, 2), shifted(values, 2)]
    for step in range(3, steps + 1):
        far += [shifted(keys, step), shifted(values, step)]
    swap = [(j, j ^ 1) for j in range(blocks)]
    even = lax.rem(lax.axis_index("blk"), 2) == 0
    swapped_value = lax.ppermute(values, "blk", swap)
    integers = jnp.concatenate([lengths.ravel(), live.ravel(), jnp.swapaxes(page_table, 1, 2).ravel()])
    (
        table, cos_own, sin_own, cos_last, sin_last, cos_far, sin_far, own_bias, last_bias, far_bias
    ) = tables(keys.shape[1], pool.shape[1], integers, lengths.shape[1], steps, page_table.shape)
    query, key, near_key, near_value, own_shard = prepare(
        cos_own, sin_own, queries, keys, values, pool
    )
    to_swap = jnp.where(even, keys, far[0])
    far_key = lax.ppermute(to_swap, "blk", swap)
    split = values.shape[1] * 9 // 16
    passed_value = lax.ppermute(
        swapped_value[:, :split], "blk", [(j, j + 2) for j in range(0, blocks - 2, 2)]
    )
    mean, level = attend_own(own_bias, query, near_key, near_value)
    shards = pool_shards(pool, (level, to_swap, swapped_value))
    pieces, later_values = lax.optimization_barrier(
        ([shard[2] for shard in shards], values[:, split:])
    )
    shards = [(*shard[:2], piece) for shard, piece in zip(shards, pieces)]
    direct_value = lax.ppermute(
        later_values, "blk", [(j, j + 1) for j in range(1, blocks - 1, 2)]
    )
    mean, level = join(
        cos_far, sin_far, far_bias, level, mean, query, [*far[::2], *far[1::2]],
        pages=gather_pages(table, [(0, 0, own_shard), *shards]),
    )
    result = join(
        cos_last, sin_last, last_bias, level, mean, query,
        [far_key, swapped_value, passed_value, direct_value],
    )
    return (result, key)


def solution(mesh):
    in_specs = (
        P("batch", "blk", None),
        P("batch", "blk", None),
        P("batch", "blk", None),
        P("batch", "blk"),
        P("batch", None),
        P("batch", "blk", None),
        P(),
        P("batch", None, None),
    )
    out_specs = (P("batch", "blk", None), P("batch", "blk", None))
    return jax.shard_map(
        per_device, mesh=mesh, in_specs=in_specs, out_specs=out_specs, check_vma=False
    )
```

```python
import math

import jax
import jax.numpy as jnp
import numpy as np
from jax import lax
from jax.experimental import pallas as pl
from jax.experimental.pallas import tpu as pltpu
from jax.sharding import PartitionSpec as P

QUERY_HEADS = 16
KEY_VALUE_HEADS = 8
HEAD_SIZE = 128
GROUP = QUERY_HEADS // KEY_VALUE_HEADS
HALF = HEAD_SIZE // 2
ROPE_BASE = 1000000.0
HIDDEN = -1e30
LANES = 128
ROW_TILE = 64
SOFTMAX_TILE = 16
HEADS_PER_STEP = 2
PREPARE_STEPS = 2


def cost(flops):
    return pl.CostEstimate(flops=flops, bytes_accessed=0, transcendentals=0)


TABLES_COST = cost(2_000_000_000)
PREPARE_COST = cost(0)
OWN_COST = cost(0)
JOIN_COST = cost(0)
GATHER_COST = cost(0)
EXP2_SCALE = math.log2(math.e) / math.sqrt(HEAD_SIZE)

FREQ_POWERS = [float(ROPE_BASE ** (-(2**k) / HALF)) for k in range(HALF.bit_length() - 1)]

PIO2_A = float(np.float32(1.5703125))
PIO2_B = float(np.float32(4.837512969970703125e-4))
PIO2_C = float(np.float32(math.pi / 2 - 1.5703125 - 4.837512969970703125e-4))


def shifted(value, steps):
    count = lax.axis_size("blk")
    return lax.ppermute(value, "blk", [(source, source + steps) for source in range(count - steps)])


def padded_keys(count):
    return -(-count // LANES) * LANES


def vmem_bytes(key_count):
    return 16 * 1024 * (1024 + key_count)


def sine_cosine(angle):
    turns = jnp.floor(angle * (2.0 / math.pi) + 0.5)
    rest = ((angle - turns * PIO2_A) - turns * PIO2_B) - turns * PIO2_C
    square = rest * rest
    sine = rest + rest * square * (
        -1.6666654611e-1 + square * (8.3321608736e-3 - square * 1.9515295891e-4)
    )
    cosine = 1.0 - 0.5 * square + square * square * (
        4.166664568298827e-2 + square * (-1.388731625493765e-3 + square * 2.443315711809948e-5)
    )
    quadrant = turns.astype(jnp.int32) & 3
    swapped = (quadrant & 1) == 1
    sine_out = jnp.where(swapped, cosine, sine)
    cosine_out = jnp.where(swapped, sine, cosine)
    sine_out = jnp.where(quadrant >= 2, -sine_out, sine_out)
    cosine_out = jnp.where((quadrant == 1) | (quadrant == 2), -cosine_out, cosine_out)
    return sine_out, cosine_out


def rotate(head, cosine, signed_sine):
    wide = head.astype(jnp.float32)
    return (wide * cosine + pltpu.roll(wide, HALF, 1) * signed_sine).astype(jnp.bfloat16)


def tables_kernel(
    rows, steps, segs, prefix_len, table_shape, integers_ref,
    page_out, cos_own, sin_own, cos_last, sin_last, cos_far, sin_far, own_bias, last_bias, far_bias,
):
    block_start = lax.axis_index("blk") * rows
    starts = [jnp.int32(0)]
    for seg in range(1, segs):
        starts.append(starts[-1] + integers_ref[seg - 1])
    lane = lax.broadcasted_iota(jnp.int32, (ROW_TILE, LANES), 1)
    row = lax.broadcasted_iota(jnp.int32, (ROW_TILE, LANES), 0)
    freq = jnp.ones((ROW_TILE, LANES), jnp.float32)
    for bit, power in enumerate(FREQ_POWERS):
        freq = jnp.where((lane >> bit) & 1 == 1, freq * power, freq)
    column = lax.axis_index("batch")
    seg_pages = table_shape[2]
    first = segs + steps + column * segs * seg_pages
    for page in range(segs * seg_pages):
        seg, place = divmod(page, seg_pages)
        page_out[page] = integers_ref[first + place * segs + seg]
    for step in range(steps + 1):
        for tile in range(0, rows, ROW_TILE):
            index = block_start + (tile - step * rows) + row
            own_start = jnp.zeros(index.shape, jnp.int32)
            for seg in range(1, segs):
                own_start = jnp.where(index >= starts[seg], starts[seg], own_start)
            place = (prefix_len + index - own_start).astype(jnp.float32)
            sine, cosine = sine_cosine(place * freq)
            sine = jnp.where(lane < HALF, -sine, sine)
            cos_out, sin_out = ((cos_own, sin_own), (cos_last, sin_last), (cos_far, sin_far))[
                min(step, 2)
            ]
            span = pl.ds(max(step - 2, 0) * rows + tile, ROW_TILE)
            cos_out[span, :] = cosine
            sin_out[span, :] = sine
    for tile in range(0, rows, ROW_TILE):
        span = pl.ds(tile, ROW_TILE)
        query_index = block_start + tile + row
        own_start = jnp.zeros(query_index.shape, jnp.int32)
        first_page_token = jnp.zeros(query_index.shape, jnp.int32)
        for seg in range(1, segs):
            later = query_index >= starts[seg]
            own_start = jnp.where(later, starts[seg], own_start)
            first_page_token = jnp.where(later, seg * prefix_len, first_page_token)
        for step in range(steps + 1):
            limit = query_index
            if step > 0:
                limit = jnp.where(integers_ref[segs + step - 1] > 0, limit, -1)
            for column in range(0, rows, LANES):
                key_index = block_start + (column - step * rows) + lane
                seen = (key_index >= own_start) & (key_index <= limit)
                bias = jnp.where(seen, 0.0, HIDDEN)
                if step == 0:
                    own_bias[span, pl.ds(column, LANES)] = bias
                elif step == 1:
                    last_bias[span, pl.ds(column, LANES)] = bias
                else:
                    far_bias[span, pl.ds((step - 2) * rows + column, LANES)] = bias
        base = (steps - 1) * rows
        for column in range(0, far_bias.shape[1] - base, LANES):
            offset = column + lane - first_page_token
            seen = (offset >= 0) & (offset < prefix_len)
            far_bias[span, pl.ds(base + column, LANES)] = jnp.where(seen, 0.0, HIDDEN)


def tables(rows, pool_page, integers, segs, steps, table_shape):
    prefix_len = table_shape[2] * pool_page
    pages = table_shape[1] * table_shape[2]
    far_rows = (steps - 1) * rows
    far_keys = padded_keys(far_rows + segs * prefix_len)
    block = jax.ShapeDtypeStruct((rows, HEAD_SIZE), jnp.float32)
    far = jax.ShapeDtypeStruct((far_rows, HEAD_SIZE), jnp.float32)
    shapes = [
        jax.ShapeDtypeStruct((pages,), jnp.int32),
        *[block] * 4,
        far,
        far,
        *[jax.ShapeDtypeStruct((rows, rows), jnp.float32)] * 2,
        jax.ShapeDtypeStruct((rows, far_keys), jnp.float32),
    ]
    return pl.pallas_call(
        lambda *refs: tables_kernel(rows, steps, segs, prefix_len, table_shape, *refs),
        in_specs=[pl.BlockSpec(memory_space=pltpu.SMEM)],
        out_specs=[pl.BlockSpec(memory_space=pltpu.SMEM)]
        + [pl.BlockSpec(memory_space=pltpu.VMEM)] * (len(shapes) - 1),
        out_shape=shapes,
        compiler_params=pltpu.CompilerParams(vmem_limit_bytes=vmem_bytes(far_keys + far_rows)),
        cost_estimate=TABLES_COST,
        name="tables",
    )(integers)


def prepare_kernel(
    rows, cos_own, sin_own, q_ref, k_ref, v_ref, pool_ref, q_out, k_out, k_copy, v_copy, pool_copy
):
    for tile in range(0, rows, ROW_TILE):
        span = pl.ds(tile, ROW_TILE)
        cosine = cos_own[span, :]
        signed_sine = sin_own[span, :]
        for source, target in ((q_ref, q_out), (k_ref, k_out)):
            for start in range(0, source.shape[2], HEAD_SIZE):
                columns = pl.ds(start, HEAD_SIZE)
                turned = rotate(source[0, span, columns], cosine, signed_sine)
                target[0, span, columns] = turned
                if source is k_ref:
                    k_copy[0, span, columns] = turned
    v_copy[...] = v_ref[...]
    pool_copy[...] = pool_ref[...]


def prepare(cosine, signed_sine, queries, keys, values, pool):
    rows = queries.shape[1]
    whole = lambda part: (0, 0)
    by_part = lambda part: (0, 0, part)
    wide = pl.BlockSpec((1, rows, queries.shape[2] // PREPARE_STEPS), by_part)
    narrow = pl.BlockSpec((1, rows, keys.shape[2] // PREPARE_STEPS), by_part)
    some_pages = pl.BlockSpec(
        (pool.shape[0] // PREPARE_STEPS, *pool.shape[1:]), lambda part: (part, 0, 0)
    )
    table = pl.BlockSpec(cosine.shape, whole)
    return pl.pallas_call(
        lambda *refs: prepare_kernel(rows, *refs),
        grid=(PREPARE_STEPS,),
        in_specs=[table, table, wide, narrow, narrow, some_pages],
        out_specs=[wide, narrow, narrow, narrow, some_pages],
        out_shape=[
            jax.ShapeDtypeStruct(array.shape, array.dtype)
            for array in (queries, keys, keys, values, pool)
        ],
        compiler_params=pltpu.CompilerParams(vmem_limit_bytes=vmem_bytes(rows)),
        cost_estimate=PREPARE_COST,
        name="prepare",
    )(cosine, signed_sine, queries, keys, values, pool)


def stacked_queries(q_ref, part):
    return jnp.concatenate(
        [q_ref[0, :, pl.ds((part * GROUP + h) * HEAD_SIZE, HEAD_SIZE)] for h in range(GROUP)],
        axis=0,
    )


def rotate_rows(target, first, source, lanes, cos_ref, sin_ref):
    rows = source.shape[1]
    for tile in range(0, rows, ROW_TILE):
        span = pl.ds(first + tile, ROW_TILE)
        target[span, :] = rotate(
            source[0, pl.ds(tile, ROW_TILE), lanes], cos_ref[span, :], sin_ref[span, :]
        )


def own_kernel(rows, bias_ref, q_ref, k_ref, v_ref, mean_ref, level_ref, *work):
    k_parts, v_parts, scores, weights, tops = split_work(work)
    group = pl.program_id(0)

    @pl.when(group == 0)
    def _():
        fill_ones(v_parts)
        level_ref[...] = jnp.zeros(level_ref.shape, jnp.float32)

    for part in range(HEADS_PER_STEP):
        lanes = pl.ds(part * HEAD_SIZE, HEAD_SIZE)
        k_parts[part][...] = k_ref[0, :, lanes]
        v_parts[part][:, pl.ds(0, HEAD_SIZE)] = v_ref[0, :, lanes]

    for part in range(HEADS_PER_STEP):
        score_part(part, q_ref, k_parts, scores)
    lane = lax.broadcasted_iota(jnp.int32, (rows, LANES), 1)
    for part in range(HEADS_PER_STEP):
        for start in range(0, GROUP * rows, SOFTMAX_TILE):
            span = pl.ds(start, SOFTMAX_TILE)
            bias = bias_ref[pl.ds(start % rows, SOFTMAX_TILE), :]
            score = scores[part][span, :] * EXP2_SCALE + bias
            highest = jnp.max(score, axis=1, keepdims=True)
            weights[part][span, :] = jnp.exp2(score - highest).astype(jnp.bfloat16)
            tops[part][span, :] = jnp.broadcast_to(highest, (SOFTMAX_TILE, LANES))
        summed = jnp.dot(weights[part][...], v_parts[part][...], preferred_element_type=jnp.float32)
        total = summed[:, HEAD_SIZE:]
        store_part(part, group, rows, lane, summed[:, :HEAD_SIZE] / total,
                   tops[part][...] + jnp.log2(total), mean_ref, level_ref)


def fill_ones(v_parts):
    for v_all in v_parts:
        v_all[:, pl.ds(HEAD_SIZE, HEAD_SIZE)] = jnp.ones((v_all.shape[0], HEAD_SIZE), jnp.bfloat16)


def split_work(work):
    return [work[i : i + HEADS_PER_STEP] for i in range(0, len(work), HEADS_PER_STEP)]


def score_part(part, q_ref, k_parts, scores):
    scores[part][...] = lax.dot_general(
        stacked_queries(q_ref, part), k_parts[part][...], (((1,), (1,)), ((), ())),
        preferred_element_type=jnp.float32,
    )


def store_part(part, group, rows, lane, mean, level, mean_ref, level_ref):
    for h in range(GROUP):
        own = part * GROUP + h
        span = slice(h * rows, (h + 1) * rows)
        mean_ref[:, pl.ds(own * HEAD_SIZE, HEAD_SIZE)] = mean[span]
        head = group * (HEADS_PER_STEP * GROUP) + own
        level_ref[...] = jnp.where(lane == head, level[span], level_ref[...])


def work_shapes(rows, key_count):
    shapes = [
        pltpu.VMEM((key_count, HEAD_SIZE), jnp.bfloat16),
        pltpu.VMEM((key_count, 2 * HEAD_SIZE), jnp.bfloat16),
        pltpu.VMEM((GROUP * rows, key_count), jnp.float32),
        pltpu.VMEM((GROUP * rows, key_count), jnp.bfloat16),
        pltpu.VMEM((GROUP * rows, LANES), jnp.float32),
    ]
    return [shape for shape in shapes for _ in range(HEADS_PER_STEP)]


def attend_own(bias, query, key, value):
    rows, q_width = query.shape[1:]
    by_group = lambda group: (0, 0, group)
    narrow = pl.BlockSpec((1, rows, HEADS_PER_STEP * HEAD_SIZE), by_group)
    wide = HEADS_PER_STEP * GROUP * HEAD_SIZE
    return pl.pallas_call(
        lambda *refs: own_kernel(rows, *refs),
        grid=(KEY_VALUE_HEADS // HEADS_PER_STEP,),
        in_specs=[
            pl.BlockSpec(bias.shape, lambda group: (0, 0)),
            pl.BlockSpec((1, rows, wide), by_group),
            narrow,
            narrow,
        ],
        out_specs=[
            pl.BlockSpec((rows, wide), lambda group: (0, group)),
            pl.BlockSpec((rows, LANES), lambda group: (0, 0)),
        ],
        out_shape=[
            jax.ShapeDtypeStruct((rows, q_width), jnp.float32),
            jax.ShapeDtypeStruct((rows, LANES), jnp.float32),
        ],
        scratch_shapes=work_shapes(rows, rows),
        compiler_params=pltpu.CompilerParams(vmem_limit_bytes=vmem_bytes(rows)),
        cost_estimate=OWN_COST,
        name="own",
    )(bias, query, key, value)


def gather_kernel(pool_rows, places, table_ref, *refs):
    *shards, paged, sem = refs
    column = lax.axis_index("batch")

    def copy(shard, place, page):
        return pltpu.make_async_copy(shard.at[place], paged.at[page], sem.at[page])

    for page in range(paged.shape[0]):
        number = table_ref[page]
        apart = lax.div(number, jnp.int32(pool_rows)) ^ column
        place = lax.rem(number, jnp.int32(pool_rows))
        for (which, first), shard in zip(places, shards):
            inside = place - first

            @pl.when((apart == which) & (inside >= 0) & (inside < shard.shape[0]))
            def _(shard=shard, inside=inside, page=page):
                copy(shard, inside, page).start()

    for page in range(paged.shape[0]):
        copy(shards[0], 0, page).wait()


def gather_pages(numbers, found):
    places, shards = [shard[:2] for shard in found], [shard[2] for shard in found]
    pool_rows = shards[0].shape[0]
    return pl.pallas_call(
        lambda *refs: gather_kernel(pool_rows, places, *refs),
        in_specs=[pl.BlockSpec(memory_space=pltpu.SMEM)]
        + [pl.BlockSpec(memory_space=pl.ANY)] * len(shards),
        out_specs=pl.BlockSpec(memory_space=pltpu.VMEM),
        out_shape=jax.ShapeDtypeStruct(numbers.shape + shards[0].shape[1:], jnp.bfloat16),
        scratch_shapes=[pltpu.SemaphoreType.DMA(numbers.shape)],
        compiler_params=pltpu.CompilerParams(vmem_limit_bytes=vmem_bytes(0)),
        cost_estimate=GATHER_COST,
        name="gather",
    )(numbers, *shards)


def join_heads(
    final, group, rows, k_parts, v_parts, scores, weights, tops,
    bias_ref, level_ref, mean_ref, q_ref, out_ref, level_out,
):
    for part in range(HEADS_PER_STEP):
        score_part(part, q_ref, k_parts, scores)
    lane = lax.broadcasted_iota(jnp.int32, (SOFTMAX_TILE, LANES), 1)
    wide_lane = lax.broadcasted_iota(jnp.int32, (rows, LANES), 1)
    for part in range(HEADS_PER_STEP):
        for start in range(0, GROUP * rows, SOFTMAX_TILE):
            span = pl.ds(start, SOFTMAX_TILE)
            row_span = pl.ds(start % rows, SOFTMAX_TILE)
            head = group * (HEADS_PER_STEP * GROUP) + part * GROUP + start // rows
            score = scores[part][span, :] * EXP2_SCALE + bias_ref[row_span, :]
            level = jnp.sum(
                jnp.where(lane == head, level_ref[row_span, :], 0.0), axis=1, keepdims=True
            )
            highest = jnp.maximum(jnp.max(score, axis=1, keepdims=True), level)
            weights[part][span, :] = jnp.exp2(score - highest).astype(jnp.bfloat16)
            if final:
                shrink = jnp.exp2(level - highest)
                tops[part][span, :] = jnp.broadcast_to(shrink, (SOFTMAX_TILE, LANES))
            else:
                tops[part][span, :] = jnp.where(lane < HALF, highest, level)
        summed = jnp.dot(weights[part][...], v_parts[part][...], preferred_element_type=jnp.float32)
        if final:
            shrink = tops[part][...]
        else:
            both = tops[part][...]
            turned = pltpu.roll(both, HALF, 1)
            low = lax.broadcasted_iota(jnp.int32, both.shape, 1) < HALF
            highest = jnp.where(low, both, turned)
            shrink = jnp.exp2(jnp.where(low, turned, both) - highest)
        total = summed[:, HEAD_SIZE:] + shrink
        before = jnp.concatenate(
            [mean_ref[:, pl.ds((part * GROUP + h) * HEAD_SIZE, HEAD_SIZE)] for h in range(GROUP)],
            axis=0,
        )
        mean = (before * shrink + summed[:, :HEAD_SIZE]) / total
        if final:
            for h in range(GROUP):
                lanes = pl.ds((part * GROUP + h) * HEAD_SIZE, HEAD_SIZE)
                out_ref[0, :, lanes] = mean[h * rows : (h + 1) * rows].astype(jnp.bfloat16)
        else:
            level = highest + jnp.log2(total)
            store_part(part, group, rows, wide_lane, mean, level, out_ref, level_out)


def far_kernel(
    rows, blocks, cos_ref, sin_ref, bias_ref, level_ref, mean_ref, q_ref, page_keys, page_values, *refs
):
    keys, values, refs = refs[:blocks], refs[blocks : 2 * blocks], refs[2 * blocks :]
    mean_out, level_out = refs[:2]
    work = split_work(refs[2:])
    k_parts, v_parts = work[:2]
    group = pl.program_id(0)
    prefix_rows = page_keys.shape[0] * page_keys.shape[1]
    base = blocks * rows

    @pl.when(group == 0)
    def _():
        fill_ones(v_parts)
        level_out[...] = jnp.zeros(level_out.shape, jnp.float32)
        rest = k_parts[0].shape[0] - base - prefix_rows
        if rest:
            blank = jnp.zeros((rest, HEAD_SIZE), jnp.bfloat16)
            for k_all, v_all in zip(k_parts, v_parts):
                k_all[pl.ds(base + prefix_rows, rest), :] = blank
                v_all[pl.ds(base + prefix_rows, rest), pl.ds(0, HEAD_SIZE)] = blank

    for part in range(HEADS_PER_STEP):
        lanes = pl.ds(part * HEAD_SIZE, HEAD_SIZE)
        for block in range(blocks):
            rotate_rows(k_parts[part], block * rows, keys[block], lanes, cos_ref, sin_ref)
            span = pl.ds(block * rows, rows)
            v_parts[part][span, pl.ds(0, HEAD_SIZE)] = values[block][0, :, lanes]
        span = pl.ds(base, prefix_rows)
        k_parts[part][span, :] = page_keys[:, :, lanes].reshape(prefix_rows, HEAD_SIZE)
        v_parts[part][span, pl.ds(0, HEAD_SIZE)] = page_values[:, :, lanes].reshape(
            prefix_rows, HEAD_SIZE
        )
    join_heads(
        False, group, rows, *work, bias_ref, level_ref, mean_ref, q_ref, mean_out, level_out
    )


def last_kernel(
    rows, cos_ref, sin_ref, bias_ref, level_ref, mean_ref, q_ref, key_ref, swapped_value,
    passed_value, direct_value, out_ref, held, sem, *refs,
):
    work = split_work(refs)
    k_parts, v_parts = work[:2]
    even = lax.rem(lax.axis_index("blk"), 2) == 0
    fill_ones(v_parts)
    copies = []
    for group in range(KEY_VALUE_HEADS // HEADS_PER_STEP):
        for part in range(HEADS_PER_STEP):
            lanes = pl.ds((group * HEADS_PER_STEP + part) * HEAD_SIZE, HEAD_SIZE)
            rotate_rows(k_parts[part], 0, key_ref, lanes, cos_ref, sin_ref)
            start = 0
            for arrived in (passed_value, direct_value):
                span = pl.ds(start, arrived.shape[1])
                v_parts[part][span, pl.ds(0, HEAD_SIZE)] = jnp.where(
                    even, arrived[0, :, lanes], swapped_value[0, span, lanes]
                )
                start += arrived.shape[1]
        query, mean, out = (
            of_group(ref, group, HEADS_PER_STEP * GROUP) for ref in (q_ref, mean_ref, held)
        )
        join_heads(True, group, rows, *work, bias_ref, level_ref, mean, query, out, None)
        copies.append(
            pltpu.make_async_copy(
                out, of_group(out_ref, group, HEADS_PER_STEP * GROUP), sem.at[group]
            )
        )
        copies[-1].start()
    for copy in copies:
        copy.wait()


def of_group(ref, group, heads):
    lanes = pl.ds(group * heads * HEAD_SIZE, heads * HEAD_SIZE)
    return ref.at[:, :, lanes] if len(ref.shape) == 3 else ref.at[:, lanes]


def attend_last(cosine, signed_sine, bias, level, mean, query, arrived):
    rows = query.shape[1]
    operands = [cosine, signed_sine, bias, level, mean, query, *arrived]
    return pl.pallas_call(
        lambda *refs: last_kernel(rows, *refs),
        in_specs=[pl.BlockSpec(memory_space=pltpu.VMEM)] * len(operands),
        out_specs=pl.BlockSpec(memory_space=pl.ANY),
        out_shape=jax.ShapeDtypeStruct(query.shape, jnp.bfloat16),
        scratch_shapes=[
            pltpu.VMEM(query.shape, jnp.bfloat16),
            pltpu.SemaphoreType.DMA((KEY_VALUE_HEADS // HEADS_PER_STEP,)),
            *work_shapes(rows, bias.shape[1]),
        ],
        compiler_params=pltpu.CompilerParams(vmem_limit_bytes=vmem_bytes(bias.shape[1])),
        cost_estimate=JOIN_COST,
        name="last",
    )(*operands)


def attend_far(cosine, signed_sine, bias, level, mean, query, arrived, pages):
    rows = query.shape[1]
    whole = lambda group: (0, 0)
    by_group = lambda group: (0, 0, group)
    width = HEADS_PER_STEP * GROUP * HEAD_SIZE
    wide = pl.BlockSpec((1, rows, width), by_group)
    flat = pl.BlockSpec((rows, width), lambda group: (0, group))
    level_spec = pl.BlockSpec(level.shape, whole)
    table = pl.BlockSpec(cosine.shape, whole)
    in_specs = [table, table, pl.BlockSpec(bias.shape, whole), level_spec, flat, wide]
    arrived_specs = [
        pl.BlockSpec((1, array.shape[1], HEADS_PER_STEP * HEAD_SIZE), by_group)
        for array in arrived
    ]
    operands = [cosine, signed_sine, bias, level, mean, query]
    scratch = work_shapes(rows, bias.shape[1])
    kernel = lambda *refs: far_kernel(rows, len(arrived) // 2, *refs)
    groups = KEY_VALUE_HEADS // HEADS_PER_STEP
    for first in (0, groups):
        in_specs.append(
            pl.BlockSpec(
                (*pages.shape[:2], HEADS_PER_STEP * HEAD_SIZE),
                lambda group, first=first: (0, 0, first + group),
            )
        )
        operands.append(pages)
    out_specs = [flat, level_spec]
    out_shape = [
        jax.ShapeDtypeStruct(array.shape, jnp.float32) for array in (mean, level)
    ]
    return pl.pallas_call(
        kernel,
        grid=(KEY_VALUE_HEADS // HEADS_PER_STEP,),
        in_specs=in_specs + arrived_specs,
        out_specs=out_specs,
        out_shape=out_shape,
        scratch_shapes=scratch,
        compiler_params=pltpu.CompilerParams(vmem_limit_bytes=vmem_bytes(bias.shape[1])),
        cost_estimate=JOIN_COST,
        name="far",
    )(*operands, *arrived)


def pool_shards(pool, after):
    count = lax.axis_size("batch")

    def swapped(shard, bit):
        return lax.ppermute(shard, "batch", [(c, c ^ bit) for c in range(count)])

    bits = [count >> (step + 1) for step in range(count.bit_length() - 1)]
    shards = {bit: swapped(pool, bit) for bit in bits}
    shards, after = lax.optimization_barrier((shards, after))
    shards = {apart: [shard] for apart, shard in shards.items()}
    for bit in reversed(bits):
        for apart, pieces in list(shards.items()):
            if apart ^ bit not in shards and apart != bit:
                if len(pieces) == 1:
                    middle = pool.shape[0] // 2
                    pieces = [pieces[0][:middle], pieces[0][middle:]]
                shards[apart ^ bit] = [swapped(piece, bit) for piece in pieces]
    found = []
    for apart, pieces in sorted(shards.items()):
        held = pool.shape[0] // len(pieces)
        found += [(apart, place * held, piece) for place, piece in enumerate(pieces)]
    return found


def per_device(queries, keys, values, seg_ids, lengths, live, page_table, pool):
    steps = live.shape[2]
    blocks = lax.axis_size("blk")
    far = [shifted(keys, 2), shifted(values, 2)]
    for step in range(3, steps + 1):
        far += [shifted(keys, step), shifted(values, step)]
    swap = [(j, j ^ 1) for j in range(blocks)]
    even = lax.rem(lax.axis_index("blk"), 2) == 0
    swapped_value = lax.ppermute(values, "blk", swap)
    integers = jnp.concatenate([lengths.ravel(), live.ravel(), jnp.swapaxes(page_table, 1, 2).ravel()])
    (
        table, cos_own, sin_own, cos_last, sin_last, cos_far, sin_far, own_bias, last_bias, far_bias
    ) = tables(keys.shape[1], pool.shape[1], integers, lengths.shape[1], steps, page_table.shape)
    query, key, near_key, near_value, own_shard = prepare(
        cos_own, sin_own, queries, keys, values, pool
    )
    to_swap = jnp.where(even, keys, far[0])
    far_key = lax.ppermute(to_swap, "blk", swap)
    split = values.shape[1] * 3 // 4
    passed_value = lax.ppermute(
        swapped_value[:, :split], "blk", [(j, j + 2) for j in range(0, blocks - 2, 2)]
    )
    mean, level = attend_own(own_bias, query, near_key, near_value)
    shards = pool_shards(pool, (level, to_swap, swapped_value))
    pieces, later_values = lax.optimization_barrier(
        ([shard[2] for shard in shards], values[:, split:])
    )
    shards = [(*shard[:2], piece) for shard, piece in zip(shards, pieces)]
    direct_value = lax.ppermute(
        later_values, "blk", [(j, j + 1) for j in range(1, blocks - 1, 2)]
    )
    mean, level = attend_far(
        cos_far, sin_far, far_bias, level, mean, query, [*far[::2], *far[1::2]],
        pages=gather_pages(table, [(0, 0, own_shard), *shards]),
    )
    result = attend_last(
        cos_last, sin_last, last_bias, level, mean, query,
        [far_key, swapped_value, passed_value, direct_value],
    )
    return (result, key)


def solution(mesh):
    in_specs = (
        P("batch", "blk", None),
        P("batch", "blk", None),
        P("batch", "blk", None),
        P("batch", "blk"),
        P("batch", None),
        P("batch", "blk", None),
        P(),
        P("batch", None, None),
    )
    out_specs = (P("batch", "blk", None), P("batch", "blk", None))
    return jax.shard_map(
        per_device, mesh=mesh, in_specs=in_specs, out_specs=out_specs, check_vma=False
    )
```

```python
import math

import jax
import jax.numpy as jnp
import numpy as np
from jax import lax
from jax.experimental import pallas as pl
from jax.experimental.pallas import tpu as pltpu
from jax.sharding import PartitionSpec as P

QUERY_HEADS = 16
KEY_VALUE_HEADS = 8
HEAD_SIZE = 128
GROUP = QUERY_HEADS // KEY_VALUE_HEADS
HALF = HEAD_SIZE // 2
ROPE_BASE = 1000000.0
HIDDEN = -1e30
LANES = 128
ROW_TILE = 64
SOFTMAX_TILE = 16
HEADS_PER_STEP = 2
PREPARE_STEPS = 2


def cost(flops):
    return pl.CostEstimate(flops=flops, bytes_accessed=0, transcendentals=0)


TABLES_COST = cost(2_000_000_000)
PREPARE_COST = cost(0)
OWN_COST = cost(0)
JOIN_COST = cost(0)
GATHER_COST = cost(0)
EXP2_SCALE = math.log2(math.e) / math.sqrt(HEAD_SIZE)

FREQ_POWERS = [float(ROPE_BASE ** (-(2**k) / HALF)) for k in range(HALF.bit_length() - 1)]

PIO2_A = float(np.float32(1.5703125))
PIO2_B = float(np.float32(4.837512969970703125e-4))
PIO2_C = float(np.float32(math.pi / 2 - 1.5703125 - 4.837512969970703125e-4))


def shifted(value, steps):
    count = lax.axis_size("blk")
    return lax.ppermute(value, "blk", [(source, source + steps) for source in range(count - steps)])


def padded_keys(count):
    return -(-count // LANES) * LANES


def vmem_bytes(key_count):
    return 16 * 1024 * (1024 + key_count)


def sine_cosine(angle):
    turns = jnp.floor(angle * (2.0 / math.pi) + 0.5)
    rest = ((angle - turns * PIO2_A) - turns * PIO2_B) - turns * PIO2_C
    square = rest * rest
    sine = rest + rest * square * (
        -1.6666654611e-1 + square * (8.3321608736e-3 - square * 1.9515295891e-4)
    )
    cosine = 1.0 - 0.5 * square + square * square * (
        4.166664568298827e-2 + square * (-1.388731625493765e-3 + square * 2.443315711809948e-5)
    )
    quadrant = turns.astype(jnp.int32) & 3
    swapped = (quadrant & 1) == 1
    sine_out = jnp.where(swapped, cosine, sine)
    cosine_out = jnp.where(swapped, sine, cosine)
    sine_out = jnp.where(quadrant >= 2, -sine_out, sine_out)
    cosine_out = jnp.where((quadrant == 1) | (quadrant == 2), -cosine_out, cosine_out)
    return sine_out, cosine_out


def rotate(head, cosine, signed_sine):
    wide = head.astype(jnp.float32)
    return (wide * cosine + pltpu.roll(wide, HALF, 1) * signed_sine).astype(jnp.bfloat16)


def tables_kernel(
    rows, steps, segs, prefix_len, table_shape, integers_ref,
    page_out, cos_own, sin_own, cos_last, sin_last, cos_far, sin_far, own_bias, last_bias, far_bias,
):
    block_start = lax.axis_index("blk") * rows
    starts = [jnp.int32(0)]
    for seg in range(1, segs):
        starts.append(starts[-1] + integers_ref[seg - 1])
    lane = lax.broadcasted_iota(jnp.int32, (ROW_TILE, LANES), 1)
    row = lax.broadcasted_iota(jnp.int32, (ROW_TILE, LANES), 0)
    freq = jnp.ones((ROW_TILE, LANES), jnp.float32)
    for bit, power in enumerate(FREQ_POWERS):
        freq = jnp.where((lane >> bit) & 1 == 1, freq * power, freq)
    column = lax.axis_index("batch")
    seg_pages = table_shape[2]
    first = segs + steps + column * segs * seg_pages
    for page in range(segs * seg_pages):
        seg, place = divmod(page, seg_pages)
        page_out[page] = integers_ref[first + place * segs + seg]
    for step in range(steps + 1):
        for tile in range(0, rows, ROW_TILE):
            index = block_start + (tile - step * rows) + row
            own_start = jnp.zeros(index.shape, jnp.int32)
            for seg in range(1, segs):
                own_start = jnp.where(index >= starts[seg], starts[seg], own_start)
            place = (prefix_len + index - own_start).astype(jnp.float32)
            sine, cosine = sine_cosine(place * freq)
            sine = jnp.where(lane < HALF, -sine, sine)
            cos_out, sin_out = ((cos_own, sin_own), (cos_last, sin_last), (cos_far, sin_far))[
                min(step, 2)
            ]
            span = pl.ds(max(step - 2, 0) * rows + tile, ROW_TILE)
            cos_out[span, :] = cosine
            sin_out[span, :] = sine
    for tile in range(0, rows, ROW_TILE):
        span = pl.ds(tile, ROW_TILE)
        query_index = block_start + tile + row
        own_start = jnp.zeros(query_index.shape, jnp.int32)
        first_page_token = jnp.zeros(query_index.shape, jnp.int32)
        for seg in range(1, segs):
            later = query_index >= starts[seg]
            own_start = jnp.where(later, starts[seg], own_start)
            first_page_token = jnp.where(later, seg * prefix_len, first_page_token)
        for step in range(steps + 1):
            limit = query_index
            if step > 0:
                limit = jnp.where(integers_ref[segs + step - 1] > 0, limit, -1)
            for column in range(0, rows, LANES):
                key_index = block_start + (column - step * rows) + lane
                seen = (key_index >= own_start) & (key_index <= limit)
                bias = jnp.where(seen, 0.0, HIDDEN)
                if step == 0:
                    own_bias[span, pl.ds(column, LANES)] = bias
                elif step == 1:
                    last_bias[span, pl.ds(column, LANES)] = bias
                else:
                    far_bias[span, pl.ds((step - 2) * rows + column, LANES)] = bias
        base = (steps - 1) * rows
        for column in range(0, far_bias.shape[1] - base, LANES):
            offset = column + lane - first_page_token
            seen = (offset >= 0) & (offset < prefix_len)
            far_bias[span, pl.ds(base + column, LANES)] = jnp.where(seen, 0.0, HIDDEN)


def tables(rows, pool_page, integers, segs, steps, table_shape):
    prefix_len = table_shape[2] * pool_page
    pages = table_shape[1] * table_shape[2]
    far_rows = (steps - 1) * rows
    far_keys = padded_keys(far_rows + segs * prefix_len)
    block = jax.ShapeDtypeStruct((rows, HEAD_SIZE), jnp.float32)
    far = jax.ShapeDtypeStruct((far_rows, HEAD_SIZE), jnp.float32)
    shapes = [
        jax.ShapeDtypeStruct((pages,), jnp.int32),
        *[block] * 4,
        far,
        far,
        *[jax.ShapeDtypeStruct((rows, rows), jnp.float32)] * 2,
        jax.ShapeDtypeStruct((rows, far_keys), jnp.float32),
    ]
    return pl.pallas_call(
        lambda *refs: tables_kernel(rows, steps, segs, prefix_len, table_shape, *refs),
        in_specs=[pl.BlockSpec(memory_space=pltpu.SMEM)],
        out_specs=[pl.BlockSpec(memory_space=pltpu.SMEM)]
        + [pl.BlockSpec(memory_space=pltpu.VMEM)] * (len(shapes) - 1),
        out_shape=shapes,
        compiler_params=pltpu.CompilerParams(vmem_limit_bytes=vmem_bytes(far_keys + far_rows)),
        cost_estimate=TABLES_COST,
        name="tables",
    )(integers)


def prepare_kernel(
    rows, cos_own, sin_own, q_ref, k_ref, v_ref, pool_ref, q_out, k_out, k_copy, v_copy, pool_copy
):
    for tile in range(0, rows, ROW_TILE):
        span = pl.ds(tile, ROW_TILE)
        cosine = cos_own[span, :]
        signed_sine = sin_own[span, :]
        for source, target in ((q_ref, q_out), (k_ref, k_out)):
            for start in range(0, source.shape[2], HEAD_SIZE):
                columns = pl.ds(start, HEAD_SIZE)
                turned = rotate(source[0, span, columns], cosine, signed_sine)
                target[0, span, columns] = turned
                if source is k_ref:
                    k_copy[0, span, columns] = turned
    v_copy[...] = v_ref[...]
    pool_copy[...] = pool_ref[...]


def prepare(cosine, signed_sine, queries, keys, values, pool):
    rows = queries.shape[1]
    whole = lambda part: (0, 0)
    by_part = lambda part: (0, 0, part)
    wide = pl.BlockSpec((1, rows, queries.shape[2] // PREPARE_STEPS), by_part)
    narrow = pl.BlockSpec((1, rows, keys.shape[2] // PREPARE_STEPS), by_part)
    some_pages = pl.BlockSpec(
        (pool.shape[0] // PREPARE_STEPS, *pool.shape[1:]), lambda part: (part, 0, 0)
    )
    table = pl.BlockSpec(cosine.shape, whole)
    return pl.pallas_call(
        lambda *refs: prepare_kernel(rows, *refs),
        grid=(PREPARE_STEPS,),
        in_specs=[table, table, wide, narrow, narrow, some_pages],
        out_specs=[wide, narrow, narrow, narrow, some_pages],
        out_shape=[
            jax.ShapeDtypeStruct(array.shape, array.dtype)
            for array in (queries, keys, keys, values, pool)
        ],
        compiler_params=pltpu.CompilerParams(vmem_limit_bytes=vmem_bytes(rows)),
        cost_estimate=PREPARE_COST,
        name="prepare",
    )(cosine, signed_sine, queries, keys, values, pool)


def stacked_queries(q_ref, part):
    return jnp.concatenate(
        [q_ref[0, :, pl.ds((part * GROUP + h) * HEAD_SIZE, HEAD_SIZE)] for h in range(GROUP)],
        axis=0,
    )


def rotate_rows(target, first, source, lanes, cos_ref, sin_ref):
    rows = source.shape[1]
    for tile in range(0, rows, ROW_TILE):
        span = pl.ds(first + tile, ROW_TILE)
        target[span, :] = rotate(
            source[0, pl.ds(tile, ROW_TILE), lanes], cos_ref[span, :], sin_ref[span, :]
        )


def own_kernel(rows, bias_ref, q_ref, k_ref, v_ref, mean_ref, level_ref, *work):
    k_parts, v_parts, scores, weights, tops = split_work(work)
    group = pl.program_id(0)

    @pl.when(group == 0)
    def _():
        fill_ones(v_parts)
        level_ref[...] = jnp.zeros(level_ref.shape, jnp.float32)

    for part in range(HEADS_PER_STEP):
        lanes = pl.ds(part * HEAD_SIZE, HEAD_SIZE)
        k_parts[part][...] = k_ref[0, :, lanes]
        v_parts[part][:, pl.ds(0, HEAD_SIZE)] = v_ref[0, :, lanes]

    for part in range(HEADS_PER_STEP):
        score_part(part, q_ref, k_parts, scores)
    lane = lax.broadcasted_iota(jnp.int32, (rows, LANES), 1)
    for part in range(HEADS_PER_STEP):
        for start in range(0, GROUP * rows, SOFTMAX_TILE):
            span = pl.ds(start, SOFTMAX_TILE)
            bias = bias_ref[pl.ds(start % rows, SOFTMAX_TILE), :]
            score = scores[part][span, :] * EXP2_SCALE + bias
            highest = jnp.max(score, axis=1, keepdims=True)
            weights[part][span, :] = jnp.exp2(score - highest).astype(jnp.bfloat16)
            tops[part][span, :] = jnp.broadcast_to(highest, (SOFTMAX_TILE, LANES))
        summed = jnp.dot(weights[part][...], v_parts[part][...], preferred_element_type=jnp.float32)
        total = summed[:, HEAD_SIZE:]
        store_part(part, group, rows, lane, summed[:, :HEAD_SIZE] / total,
                   tops[part][...] + jnp.log2(total), mean_ref, level_ref)


def fill_ones(v_parts):
    for v_all in v_parts:
        v_all[:, pl.ds(HEAD_SIZE, HEAD_SIZE)] = jnp.ones((v_all.shape[0], HEAD_SIZE), jnp.bfloat16)


def split_work(work):
    return [work[i : i + HEADS_PER_STEP] for i in range(0, len(work), HEADS_PER_STEP)]


def score_part(part, q_ref, k_parts, scores):
    scores[part][...] = lax.dot_general(
        stacked_queries(q_ref, part), k_parts[part][...], (((1,), (1,)), ((), ())),
        preferred_element_type=jnp.float32,
    )


def store_part(part, group, rows, lane, mean, level, mean_ref, level_ref):
    for h in range(GROUP):
        own = part * GROUP + h
        span = slice(h * rows, (h + 1) * rows)
        mean_ref[:, pl.ds(own * HEAD_SIZE, HEAD_SIZE)] = mean[span]
        head = group * (HEADS_PER_STEP * GROUP) + own
        level_ref[...] = jnp.where(lane == head, level[span], level_ref[...])


def work_shapes(rows, key_count):
    shapes = [
        pltpu.VMEM((key_count, HEAD_SIZE), jnp.bfloat16),
        pltpu.VMEM((key_count, 2 * HEAD_SIZE), jnp.bfloat16),
        pltpu.VMEM((GROUP * rows, key_count), jnp.float32),
        pltpu.VMEM((GROUP * rows, key_count), jnp.bfloat16),
        pltpu.VMEM((GROUP * rows, LANES), jnp.float32),
    ]
    return [shape for shape in shapes for _ in range(HEADS_PER_STEP)]


def attend_own(bias, query, key, value):
    rows, q_width = query.shape[1:]
    by_group = lambda group: (0, 0, group)
    narrow = pl.BlockSpec((1, rows, HEADS_PER_STEP * HEAD_SIZE), by_group)
    wide = HEADS_PER_STEP * GROUP * HEAD_SIZE
    return pl.pallas_call(
        lambda *refs: own_kernel(rows, *refs),
        grid=(KEY_VALUE_HEADS // HEADS_PER_STEP,),
        in_specs=[
            pl.BlockSpec(bias.shape, lambda group: (0, 0)),
            pl.BlockSpec((1, rows, wide), by_group),
            narrow,
            narrow,
        ],
        out_specs=[
            pl.BlockSpec((rows, wide), lambda group: (0, group)),
            pl.BlockSpec((rows, LANES), lambda group: (0, 0)),
        ],
        out_shape=[
            jax.ShapeDtypeStruct((rows, q_width), jnp.float32),
            jax.ShapeDtypeStruct((rows, LANES), jnp.float32),
        ],
        scratch_shapes=work_shapes(rows, rows),
        compiler_params=pltpu.CompilerParams(vmem_limit_bytes=vmem_bytes(rows)),
        cost_estimate=OWN_COST,
        name="own",
    )(bias, query, key, value)


def gather_kernel(pool_rows, places, table_ref, *refs):
    *shards, paged, sem = refs
    column = lax.axis_index("batch")

    def copy(shard, place, page):
        return pltpu.make_async_copy(shard.at[place], paged.at[page], sem.at[page])

    for page in range(paged.shape[0]):
        number = table_ref[page]
        apart = lax.div(number, jnp.int32(pool_rows)) ^ column
        place = lax.rem(number, jnp.int32(pool_rows))
        for (which, first), shard in zip(places, shards):
            inside = place - first

            @pl.when((apart == which) & (inside >= 0) & (inside < shard.shape[0]))
            def _(shard=shard, inside=inside, page=page):
                copy(shard, inside, page).start()

    for page in range(paged.shape[0]):
        copy(shards[0], 0, page).wait()


def gather_pages(numbers, found):
    places, shards = [shard[:2] for shard in found], [shard[2] for shard in found]
    pool_rows = shards[0].shape[0]
    return pl.pallas_call(
        lambda *refs: gather_kernel(pool_rows, places, *refs),
        in_specs=[pl.BlockSpec(memory_space=pltpu.SMEM)]
        + [pl.BlockSpec(memory_space=pl.ANY)] * len(shards),
        out_specs=pl.BlockSpec(memory_space=pltpu.VMEM),
        out_shape=jax.ShapeDtypeStruct(numbers.shape + shards[0].shape[1:], jnp.bfloat16),
        scratch_shapes=[pltpu.SemaphoreType.DMA(numbers.shape)],
        compiler_params=pltpu.CompilerParams(vmem_limit_bytes=vmem_bytes(0)),
        cost_estimate=GATHER_COST,
        name="gather",
    )(numbers, *shards)


def join_heads(
    final, group, rows, k_parts, v_parts, scores, weights, tops,
    bias_ref, level_ref, mean_ref, q_ref, out_ref, level_out,
):
    for part in range(HEADS_PER_STEP):
        score_part(part, q_ref, k_parts, scores)
    lane = lax.broadcasted_iota(jnp.int32, (SOFTMAX_TILE, LANES), 1)
    wide_lane = lax.broadcasted_iota(jnp.int32, (rows, LANES), 1)
    for part in range(HEADS_PER_STEP):
        for start in range(0, GROUP * rows, SOFTMAX_TILE):
            span = pl.ds(start, SOFTMAX_TILE)
            row_span = pl.ds(start % rows, SOFTMAX_TILE)
            head = group * (HEADS_PER_STEP * GROUP) + part * GROUP + start // rows
            score = scores[part][span, :] * EXP2_SCALE + bias_ref[row_span, :]
            level = jnp.sum(
                jnp.where(lane == head, level_ref[row_span, :], 0.0), axis=1, keepdims=True
            )
            highest = jnp.maximum(jnp.max(score, axis=1, keepdims=True), level)
            weights[part][span, :] = jnp.exp2(score - highest).astype(jnp.bfloat16)
            if final:
                shrink = jnp.exp2(level - highest)
                tops[part][span, :] = jnp.broadcast_to(shrink, (SOFTMAX_TILE, LANES))
            else:
                tops[part][span, :] = jnp.where(lane < HALF, highest, level)
        summed = jnp.dot(weights[part][...], v_parts[part][...], preferred_element_type=jnp.float32)
        if final:
            shrink = tops[part][...]
        else:
            both = tops[part][...]
            turned = pltpu.roll(both, HALF, 1)
            low = lax.broadcasted_iota(jnp.int32, both.shape, 1) < HALF
            highest = jnp.where(low, both, turned)
            shrink = jnp.exp2(jnp.where(low, turned, both) - highest)
        total = summed[:, HEAD_SIZE:] + shrink
        before = jnp.concatenate(
            [mean_ref[:, pl.ds((part * GROUP + h) * HEAD_SIZE, HEAD_SIZE)] for h in range(GROUP)],
            axis=0,
        )
        mean = (before * shrink + summed[:, :HEAD_SIZE]) / total
        if final:
            for h in range(GROUP):
                lanes = pl.ds((part * GROUP + h) * HEAD_SIZE, HEAD_SIZE)
                out_ref[0, :, lanes] = mean[h * rows : (h + 1) * rows].astype(jnp.bfloat16)
        else:
            level = highest + jnp.log2(total)
            store_part(part, group, rows, wide_lane, mean, level, out_ref, level_out)


def far_kernel(
    rows, blocks, cos_ref, sin_ref, bias_ref, level_ref, mean_ref, q_ref, page_keys, page_values, *refs
):
    keys, values, refs = refs[:blocks], refs[blocks : 2 * blocks], refs[2 * blocks :]
    mean_out, level_out = refs[:2]
    work = split_work(refs[2:])
    k_parts, v_parts = work[:2]
    group = pl.program_id(0)
    prefix_rows = page_keys.shape[0] * page_keys.shape[1]
    base = blocks * rows

    @pl.when(group == 0)
    def _():
        fill_ones(v_parts)
        level_out[...] = jnp.zeros(level_out.shape, jnp.float32)
        rest = k_parts[0].shape[0] - base - prefix_rows
        if rest:
            blank = jnp.zeros((rest, HEAD_SIZE), jnp.bfloat16)
            for k_all, v_all in zip(k_parts, v_parts):
                k_all[pl.ds(base + prefix_rows, rest), :] = blank
                v_all[pl.ds(base + prefix_rows, rest), pl.ds(0, HEAD_SIZE)] = blank

    for part in range(HEADS_PER_STEP):
        lanes = pl.ds(part * HEAD_SIZE, HEAD_SIZE)
        for block in range(blocks):
            rotate_rows(k_parts[part], block * rows, keys[block], lanes, cos_ref, sin_ref)
            span = pl.ds(block * rows, rows)
            v_parts[part][span, pl.ds(0, HEAD_SIZE)] = values[block][0, :, lanes]
        span = pl.ds(base, prefix_rows)
        k_parts[part][span, :] = page_keys[:, :, lanes].reshape(prefix_rows, HEAD_SIZE)
        v_parts[part][span, pl.ds(0, HEAD_SIZE)] = page_values[:, :, lanes].reshape(
            prefix_rows, HEAD_SIZE
        )
    join_heads(
        False, group, rows, *work, bias_ref, level_ref, mean_ref, q_ref, mean_out, level_out
    )


def last_kernel(
    rows, cos_ref, sin_ref, bias_ref, level_ref, mean_ref, q_ref, key_ref, swapped_value,
    passed_value, direct_value, out_ref, held, sem, *refs,
):
    work = split_work(refs)
    k_parts, v_parts = work[:2]
    even = lax.rem(lax.axis_index("blk"), 2) == 0
    fill_ones(v_parts)
    copies = []
    for group in range(KEY_VALUE_HEADS // HEADS_PER_STEP):
        for part in range(HEADS_PER_STEP):
            lanes = pl.ds((group * HEADS_PER_STEP + part) * HEAD_SIZE, HEAD_SIZE)
            rotate_rows(k_parts[part], 0, key_ref, lanes, cos_ref, sin_ref)
            start = 0
            for arrived in (passed_value, direct_value):
                span = pl.ds(start, arrived.shape[1])
                v_parts[part][span, pl.ds(0, HEAD_SIZE)] = jnp.where(
                    even, arrived[0, :, lanes], swapped_value[0, span, lanes]
                )
                start += arrived.shape[1]
        query, mean, out = (
            of_group(ref, group, HEADS_PER_STEP * GROUP) for ref in (q_ref, mean_ref, held)
        )
        join_heads(True, group, rows, *work, bias_ref, level_ref, mean, query, out, None)
        copies.append(
            pltpu.make_async_copy(
                out, of_group(out_ref, group, HEADS_PER_STEP * GROUP), sem.at[group]
            )
        )
        copies[-1].start()
    for copy in copies:
        copy.wait()


def of_group(ref, group, heads):
    lanes = pl.ds(group * heads * HEAD_SIZE, heads * HEAD_SIZE)
    return ref.at[:, :, lanes] if len(ref.shape) == 3 else ref.at[:, lanes]


def attend_last(cosine, signed_sine, bias, level, mean, query, arrived):
    rows = query.shape[1]
    operands = [cosine, signed_sine, bias, level, mean, query, *arrived]
    return pl.pallas_call(
        lambda *refs: last_kernel(rows, *refs),
        in_specs=[pl.BlockSpec(memory_space=pltpu.VMEM)] * len(operands),
        out_specs=pl.BlockSpec(memory_space=pl.ANY),
        out_shape=jax.ShapeDtypeStruct(query.shape, jnp.bfloat16),
        scratch_shapes=[
            pltpu.VMEM(query.shape, jnp.bfloat16),
            pltpu.SemaphoreType.DMA((KEY_VALUE_HEADS // HEADS_PER_STEP,)),
            *work_shapes(rows, bias.shape[1]),
        ],
        compiler_params=pltpu.CompilerParams(vmem_limit_bytes=vmem_bytes(bias.shape[1])),
        cost_estimate=JOIN_COST,
        name="last",
    )(*operands)


def attend_far(cosine, signed_sine, bias, level, mean, query, arrived, pages):
    rows = query.shape[1]
    whole = lambda group: (0, 0)
    by_group = lambda group: (0, 0, group)
    width = HEADS_PER_STEP * GROUP * HEAD_SIZE
    wide = pl.BlockSpec((1, rows, width), by_group)
    flat = pl.BlockSpec((rows, width), lambda group: (0, group))
    level_spec = pl.BlockSpec(level.shape, whole)
    table = pl.BlockSpec(cosine.shape, whole)
    in_specs = [table, table, pl.BlockSpec(bias.shape, whole), level_spec, flat, wide]
    arrived_specs = [
        pl.BlockSpec((1, array.shape[1], HEADS_PER_STEP * HEAD_SIZE), by_group)
        for array in arrived
    ]
    operands = [cosine, signed_sine, bias, level, mean, query]
    scratch = work_shapes(rows, bias.shape[1])
    kernel = lambda *refs: far_kernel(rows, len(arrived) // 2, *refs)
    groups = KEY_VALUE_HEADS // HEADS_PER_STEP
    for first in (0, groups):
        in_specs.append(
            pl.BlockSpec(
                (*pages.shape[:2], HEADS_PER_STEP * HEAD_SIZE),
                lambda group, first=first: (0, 0, first + group),
            )
        )
        operands.append(pages)
    out_specs = [flat, level_spec]
    out_shape = [
        jax.ShapeDtypeStruct(array.shape, jnp.float32) for array in (mean, level)
    ]
    return pl.pallas_call(
        kernel,
        grid=(KEY_VALUE_HEADS // HEADS_PER_STEP,),
        in_specs=in_specs + arrived_specs,
        out_specs=out_specs,
        out_shape=out_shape,
        scratch_shapes=scratch,
        compiler_params=pltpu.CompilerParams(vmem_limit_bytes=vmem_bytes(bias.shape[1])),
        cost_estimate=JOIN_COST,
        name="far",
    )(*operands, *arrived)


def pool_shards(pool, after):
    count = lax.axis_size("batch")

    def swapped(shard, bit):
        return lax.ppermute(shard, "batch", [(c, c ^ bit) for c in range(count)])

    bits = [count >> (step + 1) for step in range(count.bit_length() - 1)]
    shards = {bit: swapped(pool, bit) for bit in bits}
    shards, after = lax.optimization_barrier((shards, after))
    shards = {apart: [shard] for apart, shard in shards.items()}
    for bit in reversed(bits):
        for apart, pieces in list(shards.items()):
            if apart ^ bit not in shards and apart != bit:
                if len(pieces) == 1:
                    middle = pool.shape[0] // 2
                    pieces = [pieces[0][:middle], pieces[0][middle:]]
                shards[apart ^ bit] = [swapped(piece, bit) for piece in pieces]
    found = []
    for apart, pieces in sorted(shards.items()):
        held = pool.shape[0] // len(pieces)
        found += [(apart, place * held, piece) for place, piece in enumerate(pieces)]
    return found


def per_device(queries, keys, values, seg_ids, lengths, live, page_table, pool):
    steps = live.shape[2]
    blocks = lax.axis_size("blk")
    far = [shifted(keys, 2), shifted(values, 2)]
    for step in range(3, steps + 1):
        far += [shifted(keys, step), shifted(values, step)]
    swap = [(j, j ^ 1) for j in range(blocks)]
    even = lax.rem(lax.axis_index("blk"), 2) == 0
    swapped_value = lax.ppermute(values, "blk", swap)
    integers = jnp.concatenate([lengths.ravel(), live.ravel(), jnp.swapaxes(page_table, 1, 2).ravel()])
    (
        table, cos_own, sin_own, cos_last, sin_last, cos_far, sin_far, own_bias, last_bias, far_bias
    ) = tables(keys.shape[1], pool.shape[1], integers, lengths.shape[1], steps, page_table.shape)
    query, key, near_key, near_value, own_shard = prepare(
        cos_own, sin_own, queries, keys, values, pool
    )
    to_swap = jnp.where(even, keys, far[0])
    far_key = lax.ppermute(to_swap, "blk", swap)
    split = values.shape[1] * 11 // 16
    passed_value = lax.ppermute(
        swapped_value[:, :split], "blk", [(j, j + 2) for j in range(0, blocks - 2, 2)]
    )
    mean, level = attend_own(own_bias, query, near_key, near_value)
    shards = pool_shards(pool, (level, to_swap, swapped_value))
    pieces, later_values = lax.optimization_barrier(
        ([shard[2] for shard in shards], values[:, split:])
    )
    shards = [(*shard[:2], piece) for shard, piece in zip(shards, pieces)]
    direct_value = lax.ppermute(
        later_values, "blk", [(j, j + 1) for j in range(1, blocks - 1, 2)]
    )
    mean, level = attend_far(
        cos_far, sin_far, far_bias, level, mean, query, [*far[::2], *far[1::2]],
        pages=gather_pages(table, [(0, 0, own_shard), *shards]),
    )
    result = attend_last(
        cos_last, sin_last, last_bias, level, mean, query,
        [far_key, swapped_value, passed_value, direct_value],
    )
    return (result, key)


def solution(mesh):
    in_specs = (
        P("batch", "blk", None),
        P("batch", "blk", None),
        P("batch", "blk", None),
        P("batch", "blk"),
        P("batch", None),
        P("batch", "blk", None),
        P(),
        P("batch", None, None),
    )
    out_specs = (P("batch", "blk", None), P("batch", "blk", None))
    return jax.shard_map(
        per_device, mesh=mesh, in_specs=in_specs, out_specs=out_specs, check_vma=False
    )
```

```python
import math

import jax
import jax.numpy as jnp
import numpy as np
from jax import lax
from jax.experimental import pallas as pl
from jax.experimental.pallas import tpu as pltpu
from jax.sharding import PartitionSpec as P

QUERY_HEADS = 16
KEY_VALUE_HEADS = 8
HEAD_SIZE = 128
GROUP = QUERY_HEADS // KEY_VALUE_HEADS
HALF = HEAD_SIZE // 2
ROPE_BASE = 1000000.0
HIDDEN = -1e30
LANES = 128
ROW_TILE = 64
SOFTMAX_TILE = 16
HEADS_PER_STEP = 2
PREPARE_STEPS = 2


def cost(flops):
    return pl.CostEstimate(flops=flops, bytes_accessed=0, transcendentals=0)


TABLES_COST = cost(2_000_000_000)
PREPARE_COST = cost(0)
OWN_COST = cost(0)
JOIN_COST = cost(0)
GATHER_COST = cost(0)
EXP2_SCALE = math.log2(math.e) / math.sqrt(HEAD_SIZE)

FREQ_POWERS = [float(ROPE_BASE ** (-(2**k) / HALF)) for k in range(HALF.bit_length() - 1)]

PIO2_A = float(np.float32(1.5703125))
PIO2_B = float(np.float32(4.837512969970703125e-4))
PIO2_C = float(np.float32(math.pi / 2 - 1.5703125 - 4.837512969970703125e-4))


def shifted(value, steps):
    count = lax.axis_size("blk")
    return lax.ppermute(value, "blk", [(source, source + steps) for source in range(count - steps)])


def padded_keys(count):
    return -(-count // LANES) * LANES


def vmem_bytes(key_count):
    return 16 * 1024 * (1024 + key_count)


def sine_cosine(angle):
    turns = jnp.floor(angle * (2.0 / math.pi) + 0.5)
    rest = ((angle - turns * PIO2_A) - turns * PIO2_B) - turns * PIO2_C
    square = rest * rest
    sine = rest + rest * square * (
        -1.6666654611e-1 + square * (8.3321608736e-3 - square * 1.9515295891e-4)
    )
    cosine = 1.0 - 0.5 * square + square * square * (
        4.166664568298827e-2 + square * (-1.388731625493765e-3 + square * 2.443315711809948e-5)
    )
    quadrant = turns.astype(jnp.int32) & 3
    swapped = (quadrant & 1) == 1
    sine_out = jnp.where(swapped, cosine, sine)
    cosine_out = jnp.where(swapped, sine, cosine)
    sine_out = jnp.where(quadrant >= 2, -sine_out, sine_out)
    cosine_out = jnp.where((quadrant == 1) | (quadrant == 2), -cosine_out, cosine_out)
    return sine_out, cosine_out


def rotate(head, cosine, signed_sine):
    wide = head.astype(jnp.float32)
    return (wide * cosine + pltpu.roll(wide, HALF, 1) * signed_sine).astype(jnp.bfloat16)


def tables_kernel(
    rows, steps, segs, prefix_len, table_shape, integers_ref,
    page_out, cos_own, sin_own, cos_last, sin_last, cos_far, sin_far, own_bias, last_bias, far_bias,
):
    block_start = lax.axis_index("blk") * rows
    starts = [jnp.int32(0)]
    for seg in range(1, segs):
        starts.append(starts[-1] + integers_ref[seg - 1])
    lane = lax.broadcasted_iota(jnp.int32, (ROW_TILE, LANES), 1)
    row = lax.broadcasted_iota(jnp.int32, (ROW_TILE, LANES), 0)
    freq = jnp.ones((ROW_TILE, LANES), jnp.float32)
    for bit, power in enumerate(FREQ_POWERS):
        freq = jnp.where((lane >> bit) & 1 == 1, freq * power, freq)
    column = lax.axis_index("batch")
    seg_pages = table_shape[2]
    first = segs + steps + column * segs * seg_pages
    for page in range(segs * seg_pages):
        seg, place = divmod(page, seg_pages)
        page_out[page] = integers_ref[first + place * segs + seg]
    for step in range(steps + 1):
        for tile in range(0, rows, ROW_TILE):
            index = block_start + (tile - step * rows) + row
            own_start = jnp.zeros(index.shape, jnp.int32)
            for seg in range(1, segs):
                own_start = jnp.where(index >= starts[seg], starts[seg], own_start)
            place = (prefix_len + index - own_start).astype(jnp.float32)
            sine, cosine = sine_cosine(place * freq)
            sine = jnp.where(lane < HALF, -sine, sine)
            cos_out, sin_out = ((cos_own, sin_own), (cos_last, sin_last), (cos_far, sin_far))[
                min(step, 2)
            ]
            span = pl.ds(max(step - 2, 0) * rows + tile, ROW_TILE)
            cos_out[span, :] = cosine
            sin_out[span, :] = sine
    for tile in range(0, rows, ROW_TILE):
        span = pl.ds(tile, ROW_TILE)
        query_index = block_start + tile + row
        own_start = jnp.zeros(query_index.shape, jnp.int32)
        first_page_token = jnp.zeros(query_index.shape, jnp.int32)
        for seg in range(1, segs):
            later = query_index >= starts[seg]
            own_start = jnp.where(later, starts[seg], own_start)
            first_page_token = jnp.where(later, seg * prefix_len, first_page_token)
        for step in range(steps + 1):
            limit = query_index
            if step > 0:
                limit = jnp.where(integers_ref[segs + step - 1] > 0, limit, -1)
            for column in range(0, rows, LANES):
                key_index = block_start + (column - step * rows) + lane
                seen = (key_index >= own_start) & (key_index <= limit)
                bias = jnp.where(seen, 0.0, HIDDEN)
                if step == 0:
                    own_bias[span, pl.ds(column, LANES)] = bias
                elif step == 1:
                    last_bias[span, pl.ds(column, LANES)] = bias
                else:
                    far_bias[span, pl.ds((step - 2) * rows + column, LANES)] = bias
        base = (steps - 1) * rows
        for column in range(0, far_bias.shape[1] - base, LANES):
            offset = column + lane - first_page_token
            seen = (offset >= 0) & (offset < prefix_len)
            far_bias[span, pl.ds(base + column, LANES)] = jnp.where(seen, 0.0, HIDDEN)


def tables(rows, pool_page, integers, segs, steps, table_shape):
    prefix_len = table_shape[2] * pool_page
    pages = table_shape[1] * table_shape[2]
    far_rows = (steps - 1) * rows
    far_keys = padded_keys(far_rows + segs * prefix_len)
    block = jax.ShapeDtypeStruct((rows, HEAD_SIZE), jnp.float32)
    far = jax.ShapeDtypeStruct((far_rows, HEAD_SIZE), jnp.float32)
    shapes = [
        jax.ShapeDtypeStruct((pages,), jnp.int32),
        *[block] * 4,
        far,
        far,
        *[jax.ShapeDtypeStruct((rows, rows), jnp.float32)] * 2,
        jax.ShapeDtypeStruct((rows, far_keys), jnp.float32),
    ]
    return pl.pallas_call(
        lambda *refs: tables_kernel(rows, steps, segs, prefix_len, table_shape, *refs),
        in_specs=[pl.BlockSpec(memory_space=pltpu.SMEM)],
        out_specs=[pl.BlockSpec(memory_space=pltpu.SMEM)]
        + [pl.BlockSpec(memory_space=pltpu.VMEM)] * (len(shapes) - 1),
        out_shape=shapes,
        compiler_params=pltpu.CompilerParams(vmem_limit_bytes=vmem_bytes(far_keys + far_rows)),
        cost_estimate=TABLES_COST,
        name="tables",
    )(integers)


def prepare_kernel(
    rows, cos_own, sin_own, q_ref, k_ref, v_ref, pool_ref, q_out, k_out, k_copy, v_copy, pool_copy
):
    for tile in range(0, rows, ROW_TILE):
        span = pl.ds(tile, ROW_TILE)
        cosine = cos_own[span, :]
        signed_sine = sin_own[span, :]
        for source, target in ((q_ref, q_out), (k_ref, k_out)):
            for start in range(0, source.shape[2], HEAD_SIZE):
                columns = pl.ds(start, HEAD_SIZE)
                turned = rotate(source[0, span, columns], cosine, signed_sine)
                target[0, span, columns] = turned
                if source is k_ref:
                    k_copy[0, span, columns] = turned
    v_copy[...] = v_ref[...]
    pool_copy[...] = pool_ref[...]


def prepare(cosine, signed_sine, queries, keys, values, pool):
    rows = queries.shape[1]
    whole = lambda part: (0, 0)
    by_part = lambda part: (0, 0, part)
    wide = pl.BlockSpec((1, rows, queries.shape[2] // PREPARE_STEPS), by_part)
    narrow = pl.BlockSpec((1, rows, keys.shape[2] // PREPARE_STEPS), by_part)
    some_pages = pl.BlockSpec(
        (pool.shape[0] // PREPARE_STEPS, *pool.shape[1:]), lambda part: (part, 0, 0)
    )
    table = pl.BlockSpec(cosine.shape, whole)
    return pl.pallas_call(
        lambda *refs: prepare_kernel(rows, *refs),
        grid=(PREPARE_STEPS,),
        in_specs=[table, table, wide, narrow, narrow, some_pages],
        out_specs=[wide, narrow, narrow, narrow, some_pages],
        out_shape=[
            jax.ShapeDtypeStruct(array.shape, array.dtype)
            for array in (queries, keys, keys, values, pool)
        ],
        compiler_params=pltpu.CompilerParams(vmem_limit_bytes=vmem_bytes(rows)),
        cost_estimate=PREPARE_COST,
        name="prepare",
    )(cosine, signed_sine, queries, keys, values, pool)


def stacked_queries(q_ref, part):
    return jnp.concatenate(
        [q_ref[0, :, pl.ds((part * GROUP + h) * HEAD_SIZE, HEAD_SIZE)] for h in range(GROUP)],
        axis=0,
    )


def rotate_rows(target, first, source, lanes, cos_ref, sin_ref):
    rows = source.shape[1]
    for tile in range(0, rows, ROW_TILE):
        span = pl.ds(first + tile, ROW_TILE)
        target[span, :] = rotate(
            source[0, pl.ds(tile, ROW_TILE), lanes], cos_ref[span, :], sin_ref[span, :]
        )


def own_kernel(rows, bias_ref, q_ref, k_ref, v_ref, mean_ref, level_ref, *work):
    k_parts, v_parts, scores, weights, tops = split_work(work)
    group = pl.program_id(0)

    @pl.when(group == 0)
    def _():
        fill_ones(v_parts)
        level_ref[...] = jnp.zeros(level_ref.shape, jnp.float32)

    for part in range(HEADS_PER_STEP):
        lanes = pl.ds(part * HEAD_SIZE, HEAD_SIZE)
        k_parts[part][...] = k_ref[0, :, lanes]
        v_parts[part][:, pl.ds(0, HEAD_SIZE)] = v_ref[0, :, lanes]

    for part in range(HEADS_PER_STEP):
        score_part(part, q_ref, k_parts, scores)
    lane = lax.broadcasted_iota(jnp.int32, (rows, LANES), 1)
    for part in range(HEADS_PER_STEP):
        for start in range(0, GROUP * rows, SOFTMAX_TILE):
            span = pl.ds(start, SOFTMAX_TILE)
            bias = bias_ref[pl.ds(start % rows, SOFTMAX_TILE), :]
            score = scores[part][span, :] * EXP2_SCALE + bias
            highest = jnp.max(score, axis=1, keepdims=True)
            weights[part][span, :] = jnp.exp2(score - highest).astype(jnp.bfloat16)
            tops[part][span, :] = jnp.broadcast_to(highest, (SOFTMAX_TILE, LANES))
        summed = jnp.dot(weights[part][...], v_parts[part][...], preferred_element_type=jnp.float32)
        total = summed[:, HEAD_SIZE:]
        store_part(part, group, rows, lane, summed[:, :HEAD_SIZE] / total,
                   tops[part][...] + jnp.log2(total), mean_ref, level_ref)


def fill_ones(v_parts):
    for v_all in v_parts:
        v_all[:, pl.ds(HEAD_SIZE, HEAD_SIZE)] = jnp.ones((v_all.shape[0], HEAD_SIZE), jnp.bfloat16)


def split_work(work):
    return [work[i : i + HEADS_PER_STEP] for i in range(0, len(work), HEADS_PER_STEP)]


def score_part(part, q_ref, k_parts, scores):
    scores[part][...] = lax.dot_general(
        stacked_queries(q_ref, part), k_parts[part][...], (((1,), (1,)), ((), ())),
        preferred_element_type=jnp.float32,
    )


def store_part(part, group, rows, lane, mean, level, mean_ref, level_ref):
    for h in range(GROUP):
        own = part * GROUP + h
        span = slice(h * rows, (h + 1) * rows)
        mean_ref[:, pl.ds(own * HEAD_SIZE, HEAD_SIZE)] = mean[span]
        head = group * (HEADS_PER_STEP * GROUP) + own
        level_ref[...] = jnp.where(lane == head, level[span], level_ref[...])


def work_shapes(rows, key_count):
    shapes = [
        pltpu.VMEM((key_count, HEAD_SIZE), jnp.bfloat16),
        pltpu.VMEM((key_count, 2 * HEAD_SIZE), jnp.bfloat16),
        pltpu.VMEM((GROUP * rows, key_count), jnp.float32),
        pltpu.VMEM((GROUP * rows, key_count), jnp.bfloat16),
        pltpu.VMEM((GROUP * rows, LANES), jnp.float32),
    ]
    return [shape for shape in shapes for _ in range(HEADS_PER_STEP)]


def attend_own(bias, query, key, value):
    rows, q_width = query.shape[1:]
    by_group = lambda group: (0, 0, group)
    narrow = pl.BlockSpec((1, rows, HEADS_PER_STEP * HEAD_SIZE), by_group)
    wide = HEADS_PER_STEP * GROUP * HEAD_SIZE
    return pl.pallas_call(
        lambda *refs: own_kernel(rows, *refs),
        grid=(KEY_VALUE_HEADS // HEADS_PER_STEP,),
        in_specs=[
            pl.BlockSpec(bias.shape, lambda group: (0, 0)),
            pl.BlockSpec((1, rows, wide), by_group),
            narrow,
            narrow,
        ],
        out_specs=[
            pl.BlockSpec((rows, wide), lambda group: (0, group)),
            pl.BlockSpec((rows, LANES), lambda group: (0, 0)),
        ],
        out_shape=[
            jax.ShapeDtypeStruct((rows, q_width), jnp.float32),
            jax.ShapeDtypeStruct((rows, LANES), jnp.float32),
        ],
        scratch_shapes=work_shapes(rows, rows),
        compiler_params=pltpu.CompilerParams(vmem_limit_bytes=vmem_bytes(rows)),
        cost_estimate=OWN_COST,
        name="own",
    )(bias, query, key, value)


def gather_kernel(pool_rows, places, table_ref, *refs):
    *shards, paged, sem = refs
    column = lax.axis_index("batch")

    def copy(shard, place, page):
        return pltpu.make_async_copy(shard.at[place], paged.at[page], sem.at[page])

    for page in range(paged.shape[0]):
        number = table_ref[page]
        apart = lax.div(number, jnp.int32(pool_rows)) ^ column
        place = lax.rem(number, jnp.int32(pool_rows))
        for (which, first), shard in zip(places, shards):
            inside = place - first

            @pl.when((apart == which) & (inside >= 0) & (inside < shard.shape[0]))
            def _(shard=shard, inside=inside, page=page):
                copy(shard, inside, page).start()

    for page in range(paged.shape[0]):
        copy(shards[0], 0, page).wait()


def gather_pages(numbers, found):
    places, shards = [shard[:2] for shard in found], [shard[2] for shard in found]
    pool_rows = shards[0].shape[0]
    return pl.pallas_call(
        lambda *refs: gather_kernel(pool_rows, places, *refs),
        in_specs=[pl.BlockSpec(memory_space=pltpu.SMEM)]
        + [pl.BlockSpec(memory_space=pl.ANY)] * len(shards),
        out_specs=pl.BlockSpec(memory_space=pltpu.VMEM),
        out_shape=jax.ShapeDtypeStruct(numbers.shape + shards[0].shape[1:], jnp.bfloat16),
        scratch_shapes=[pltpu.SemaphoreType.DMA(numbers.shape)],
        compiler_params=pltpu.CompilerParams(vmem_limit_bytes=vmem_bytes(0)),
        cost_estimate=GATHER_COST,
        name="gather",
    )(numbers, *shards)


def join_heads(
    final, group, rows, k_parts, v_parts, scores, weights, tops,
    bias_ref, level_ref, mean_ref, q_ref, out_ref, level_out,
):
    for part in range(HEADS_PER_STEP):
        score_part(part, q_ref, k_parts, scores)
    lane = lax.broadcasted_iota(jnp.int32, (SOFTMAX_TILE, LANES), 1)
    wide_lane = lax.broadcasted_iota(jnp.int32, (rows, LANES), 1)
    for part in range(HEADS_PER_STEP):
        for start in range(0, GROUP * rows, SOFTMAX_TILE):
            span = pl.ds(start, SOFTMAX_TILE)
            row_span = pl.ds(start % rows, SOFTMAX_TILE)
            head = group * (HEADS_PER_STEP * GROUP) + part * GROUP + start // rows
            score = scores[part][span, :] * EXP2_SCALE + bias_ref[row_span, :]
            level = jnp.sum(
                jnp.where(lane == head, level_ref[row_span, :], 0.0), axis=1, keepdims=True
            )
            highest = jnp.maximum(jnp.max(score, axis=1, keepdims=True), level)
            weights[part][span, :] = jnp.exp2(score - highest).astype(jnp.bfloat16)
            if final:
                shrink = jnp.exp2(level - highest)
                tops[part][span, :] = jnp.broadcast_to(shrink, (SOFTMAX_TILE, LANES))
            else:
                tops[part][span, :] = jnp.where(lane < HALF, highest, level)
        summed = jnp.dot(weights[part][...], v_parts[part][...], preferred_element_type=jnp.float32)
        if final:
            shrink = tops[part][...]
        else:
            both = tops[part][...]
            turned = pltpu.roll(both, HALF, 1)
            low = lax.broadcasted_iota(jnp.int32, both.shape, 1) < HALF
            highest = jnp.where(low, both, turned)
            shrink = jnp.exp2(jnp.where(low, turned, both) - highest)
        total = summed[:, HEAD_SIZE:] + shrink
        before = jnp.concatenate(
            [mean_ref[:, pl.ds((part * GROUP + h) * HEAD_SIZE, HEAD_SIZE)] for h in range(GROUP)],
            axis=0,
        )
        mean = (before * shrink + summed[:, :HEAD_SIZE]) / total
        if final:
            for h in range(GROUP):
                lanes = pl.ds((part * GROUP + h) * HEAD_SIZE, HEAD_SIZE)
                out_ref[0, :, lanes] = mean[h * rows : (h + 1) * rows].astype(jnp.bfloat16)
        else:
            level = highest + jnp.log2(total)
            store_part(part, group, rows, wide_lane, mean, level, out_ref, level_out)


def far_kernel(
    rows, blocks, cos_ref, sin_ref, bias_ref, level_ref, mean_ref, q_ref, page_keys, page_values, *refs
):
    keys, values, refs = refs[:blocks], refs[blocks : 2 * blocks], refs[2 * blocks :]
    mean_out, level_out = refs[:2]
    work = split_work(refs[2:])
    k_parts, v_parts = work[:2]
    group = pl.program_id(0)
    prefix_rows = page_keys.shape[0] * page_keys.shape[1]
    base = blocks * rows

    @pl.when(group == 0)
    def _():
        fill_ones(v_parts)
        level_out[...] = jnp.zeros(level_out.shape, jnp.float32)
        rest = k_parts[0].shape[0] - base - prefix_rows
        if rest:
            blank = jnp.zeros((rest, HEAD_SIZE), jnp.bfloat16)
            for k_all, v_all in zip(k_parts, v_parts):
                k_all[pl.ds(base + prefix_rows, rest), :] = blank
                v_all[pl.ds(base + prefix_rows, rest), pl.ds(0, HEAD_SIZE)] = blank

    for part in range(HEADS_PER_STEP):
        lanes = pl.ds(part * HEAD_SIZE, HEAD_SIZE)
        for block in range(blocks):
            rotate_rows(k_parts[part], block * rows, keys[block], lanes, cos_ref, sin_ref)
            span = pl.ds(block * rows, rows)
            v_parts[part][span, pl.ds(0, HEAD_SIZE)] = values[block][0, :, lanes]
        span = pl.ds(base, prefix_rows)
        k_parts[part][span, :] = page_keys[:, :, lanes].reshape(prefix_rows, HEAD_SIZE)
        v_parts[part][span, pl.ds(0, HEAD_SIZE)] = page_values[:, :, lanes].reshape(
            prefix_rows, HEAD_SIZE
        )
    join_heads(
        False, group, rows, *work, bias_ref, level_ref, mean_ref, q_ref, mean_out, level_out
    )


def last_kernel(
    rows, bias_ref, level_ref, mean_ref, q_ref, key_ref, swapped_value,
    passed_value, direct_value, out_ref, held, sem, *refs,
):
    work = split_work(refs)
    k_parts, v_parts = work[:2]
    even = lax.rem(lax.axis_index("blk"), 2) == 0
    fill_ones(v_parts)
    copies = []
    for group in range(KEY_VALUE_HEADS // HEADS_PER_STEP):
        for part in range(HEADS_PER_STEP):
            lanes = pl.ds((group * HEADS_PER_STEP + part) * HEAD_SIZE, HEAD_SIZE)
            k_parts[part][...] = key_ref[0, :, lanes]
            start = 0
            for arrived in (passed_value, direct_value):
                span = pl.ds(start, arrived.shape[1])
                v_parts[part][span, pl.ds(0, HEAD_SIZE)] = jnp.where(
                    even, arrived[0, :, lanes], swapped_value[0, span, lanes]
                )
                start += arrived.shape[1]
        query, mean, out = (
            of_group(ref, group, HEADS_PER_STEP * GROUP) for ref in (q_ref, mean_ref, held)
        )
        join_heads(True, group, rows, *work, bias_ref, level_ref, mean, query, out, None)
        copies.append(
            pltpu.make_async_copy(
                out, of_group(out_ref, group, HEADS_PER_STEP * GROUP), sem.at[group]
            )
        )
        copies[-1].start()
    for copy in copies:
        copy.wait()


def of_group(ref, group, heads):
    lanes = pl.ds(group * heads * HEAD_SIZE, heads * HEAD_SIZE)
    return ref.at[:, :, lanes] if len(ref.shape) == 3 else ref.at[:, lanes]


def turn_kernel(cos_ref, sin_ref, key_ref, out_ref):
    for start in range(0, key_ref.shape[2], HEAD_SIZE):
        lanes = pl.ds(start, HEAD_SIZE)
        rotate_rows(out_ref.at[0, :, lanes], 0, key_ref, lanes, cos_ref, sin_ref)


def turn(cosine, signed_sine, key):
    return pl.pallas_call(
        turn_kernel,
        in_specs=[pl.BlockSpec(memory_space=pltpu.VMEM)] * 3,
        out_specs=pl.BlockSpec(memory_space=pltpu.VMEM),
        out_shape=jax.ShapeDtypeStruct(key.shape, key.dtype),
        compiler_params=pltpu.CompilerParams(vmem_limit_bytes=vmem_bytes(key.shape[1])),
        cost_estimate=cost(0),
        name="turn",
    )(cosine, signed_sine, key)


def attend_last(bias, level, mean, query, arrived):
    rows = query.shape[1]
    operands = [bias, level, mean, query, *arrived]
    return pl.pallas_call(
        lambda *refs: last_kernel(rows, *refs),
        in_specs=[pl.BlockSpec(memory_space=pltpu.VMEM)] * len(operands),
        out_specs=pl.BlockSpec(memory_space=pl.ANY),
        out_shape=jax.ShapeDtypeStruct(query.shape, jnp.bfloat16),
        scratch_shapes=[
            pltpu.VMEM(query.shape, jnp.bfloat16),
            pltpu.SemaphoreType.DMA((KEY_VALUE_HEADS // HEADS_PER_STEP,)),
            *work_shapes(rows, bias.shape[1]),
        ],
        compiler_params=pltpu.CompilerParams(vmem_limit_bytes=vmem_bytes(bias.shape[1])),
        cost_estimate=JOIN_COST,
        name="last",
    )(*operands)


def attend_far(cosine, signed_sine, bias, level, mean, query, arrived, pages):
    rows = query.shape[1]
    whole = lambda group: (0, 0)
    by_group = lambda group: (0, 0, group)
    width = HEADS_PER_STEP * GROUP * HEAD_SIZE
    wide = pl.BlockSpec((1, rows, width), by_group)
    flat = pl.BlockSpec((rows, width), lambda group: (0, group))
    level_spec = pl.BlockSpec(level.shape, whole)
    table = pl.BlockSpec(cosine.shape, whole)
    in_specs = [table, table, pl.BlockSpec(bias.shape, whole), level_spec, flat, wide]
    arrived_specs = [
        pl.BlockSpec((1, array.shape[1], HEADS_PER_STEP * HEAD_SIZE), by_group)
        for array in arrived
    ]
    operands = [cosine, signed_sine, bias, level, mean, query]
    scratch = work_shapes(rows, bias.shape[1])
    kernel = lambda *refs: far_kernel(rows, len(arrived) // 2, *refs)
    groups = KEY_VALUE_HEADS // HEADS_PER_STEP
    for first in (0, groups):
        in_specs.append(
            pl.BlockSpec(
                (*pages.shape[:2], HEADS_PER_STEP * HEAD_SIZE),
                lambda group, first=first: (0, 0, first + group),
            )
        )
        operands.append(pages)
    out_specs = [flat, level_spec]
    out_shape = [
        jax.ShapeDtypeStruct(array.shape, jnp.float32) for array in (mean, level)
    ]
    return pl.pallas_call(
        kernel,
        grid=(KEY_VALUE_HEADS // HEADS_PER_STEP,),
        in_specs=in_specs + arrived_specs,
        out_specs=out_specs,
        out_shape=out_shape,
        scratch_shapes=scratch,
        compiler_params=pltpu.CompilerParams(vmem_limit_bytes=vmem_bytes(bias.shape[1])),
        cost_estimate=JOIN_COST,
        name="far",
    )(*operands, *arrived)


def pool_shards(pool, after):
    count = lax.axis_size("batch")

    def swapped(shard, bit):
        return lax.ppermute(shard, "batch", [(c, c ^ bit) for c in range(count)])

    bits = [count >> (step + 1) for step in range(count.bit_length() - 1)]
    shards = {bit: swapped(pool, bit) for bit in bits}
    shards, after = lax.optimization_barrier((shards, after))
    shards = {apart: [shard] for apart, shard in shards.items()}
    for bit in reversed(bits):
        for apart, pieces in list(shards.items()):
            if apart ^ bit not in shards and apart != bit:
                if len(pieces) == 1:
                    middle = pool.shape[0] // 2
                    pieces = [pieces[0][:middle], pieces[0][middle:]]
                shards[apart ^ bit] = [swapped(piece, bit) for piece in pieces]
    found = []
    for apart, pieces in sorted(shards.items()):
        held = pool.shape[0] // len(pieces)
        found += [(apart, place * held, piece) for place, piece in enumerate(pieces)]
    return found


def per_device(queries, keys, values, seg_ids, lengths, live, page_table, pool):
    steps = live.shape[2]
    blocks = lax.axis_size("blk")
    far = [shifted(keys, 2), shifted(values, 2)]
    for step in range(3, steps + 1):
        far += [shifted(keys, step), shifted(values, step)]
    swap = [(j, j ^ 1) for j in range(blocks)]
    even = lax.rem(lax.axis_index("blk"), 2) == 0
    swapped_value = lax.ppermute(values, "blk", swap)
    integers = jnp.concatenate([lengths.ravel(), live.ravel(), jnp.swapaxes(page_table, 1, 2).ravel()])
    (
        table, cos_own, sin_own, cos_last, sin_last, cos_far, sin_far, own_bias, last_bias, far_bias
    ) = tables(keys.shape[1], pool.shape[1], integers, lengths.shape[1], steps, page_table.shape)
    query, key, near_key, near_value, own_shard = prepare(
        cos_own, sin_own, queries, keys, values, pool
    )
    to_swap = jnp.where(even, keys, far[0])
    far_key = lax.ppermute(to_swap, "blk", swap)
    split = values.shape[1] * 11 // 16
    passed_value = lax.ppermute(
        swapped_value[:, :split], "blk", [(j, j + 2) for j in range(0, blocks - 2, 2)]
    )
    mean, level = attend_own(own_bias, query, near_key, near_value)
    shards = pool_shards(pool, (level, to_swap, swapped_value))
    pieces, later_values = lax.optimization_barrier(
        ([shard[2] for shard in shards], values[:, split:])
    )
    shards = [(*shard[:2], piece) for shard, piece in zip(shards, pieces)]
    direct_value = lax.ppermute(
        later_values, "blk", [(j, j + 1) for j in range(1, blocks - 1, 2)]
    )
    mean, level = attend_far(
        cos_far, sin_far, far_bias, level, mean, query, [*far[::2], *far[1::2]],
        pages=gather_pages(table, [(0, 0, own_shard), *shards]),
    )
    result = attend_last(
        last_bias, level, mean, query,
        [turn(cos_last, sin_last, far_key), swapped_value, passed_value, direct_value],
    )
    return (result, key)


def solution(mesh):
    in_specs = (
        P("batch", "blk", None),
        P("batch", "blk", None),
        P("batch", "blk", None),
        P("batch", "blk"),
        P("batch", None),
        P("batch", "blk", None),
        P(),
        P("batch", None, None),
    )
    out_specs = (P("batch", "blk", None), P("batch", "blk", None))
    return jax.shard_map(
        per_device, mesh=mesh, in_specs=in_specs, out_specs=out_specs, check_vma=False
    )
```
